32 devices in a mesh: dp: 8 (over z, y), mp: 4 (over x, core).
Axes of the slice: x: 2, y: 2, z: 4, core: 2. Of those that a mesh axis runs over, the one named last changes fastest.
Arguments:
- token_ids: int32 [4096], P('dp'), may hold values from 0 to 127
- prefix_lengths: int32 [8], P('dp'), may hold values from 1 to 511
- cluster_ids: int32 [8], replicated, may hold values from 0 to 3
- embedding: bfloat16 [128, 2048], replicated, may hold values from -6 to 6
- w_query: bfloat16 [2048, 2048], P(None, 'mp'), may hold values from -0.125 to 0.125
- w_key: bfloat16 [2048, 2048], P(None, 'mp'), may hold values from -0.125 to 0.125
- w_value: bfloat16 [2048, 2048], P(None, 'mp'), may hold values from -0.125 to 0.125
- w_dense: bfloat16 [2048, 2048], P(None, 'mp'), may hold values from -6 to 6
- w_gate: bfloat16 [2048, 5472], P(None, 'mp'), may hold values from -0.125 to 0.125
- w_up: bfloat16 [2048, 5472], P(None, 'mp'), may hold values from -0.125 to 0.125
- w_down: bfloat16 [2048, 5472], P(None, 'mp'), may hold values from -0.75 to 0.75
- norm1_gain: float32 [2048], replicated, may hold values from 0.5 to 1.5
- norm1_bias: float32 [2048], replicated, may hold values from -4 to 4
- norm2_gain: float32 [2048], replicated, may hold values from 0.5 to 1.5
- norm2_bias: float32 [2048], replicated, may hold values from -4 to 4
- cotangent: bfloat16 [4096, 2048], P('dp'), may hold values from -6 to 6
Outputs:
- block_out: bfloat16 [4096, 2048], P('dp')
- grad_embedding: float32 [128, 2048], P('dp')
- grad_w_query: float32 [2048, 2048], P('dp', 'mp')
- grad_w_key: float32 [2048, 2048], P('dp', 'mp')
- grad_w_value: float32 [2048, 2048], P('dp', 'mp')
- grad_w_dense: float32 [2048, 2048], P('dp', 'mp')
- grad_w_gate: float32 [2048, 5472], P('dp', 'mp')
- grad_w_up: float32 [2048, 5472], P('dp', 'mp')
- grad_w_down: float32 [2048, 5472], P('dp', 'mp')
- grad_norm1_gain: float32 [2048], P('dp')
- grad_norm1_bias: float32 [2048], P('dp')
- grad_norm2_gain: float32 [2048], P('dp')
- grad_norm2_bias: float32 [2048], P('dp')
The draws below stay inside these ranges and needn't reach their ends.
All inputs are finite; a program needn't handle non-finite values.
Results may differ from the reference program's by a relative error of at most 0.014.
Values sent between devices are 32-bit elements; how exact they have to be, the bound alone decides.
A program may use at most 192 MiB of HBM per device.

```python
import math
import jax
import jax.numpy as jnp
from jax import lax

D = 2048
H = 16
HD = 128
FF = 5472
FF_USED = 5461
V = 128
TOK_DEV = 512
SEQS = 8
TOKENS = 4096


def with_ends(array, rng, low, high):
    longest = array.shape.index(max(array.shape))
    spots = []
    for shift in (0, 1):
        where = [jax.random.randint(jax.random.fold_in(rng, axis), (), 0, length) for axis, length in enumerate(array.shape)]
        where[longest] = (where[longest] + shift) % array.shape[longest]
        spots.append(tuple(where))
    return array.at[spots[0]].set(low).at[spots[1]].set(high)


def steps_of(key, extent, pieces, least, largest):
    def one(position, parts):
        draws = jax.random.uniform(jax.random.fold_in(jax.random.fold_in(key, 6), position), (parts,), jnp.float32, least / len(pieces), largest / len(pieces))
        return jnp.repeat(jnp.exp(draws), extent[position] // parts).reshape((-1,) + (1,) * (len(extent) - position - 1))

    level = one(*pieces[0])
    for cut in pieces[1:]:
        level = level * one(*cut)
    return level


def bell_draw(stream_key, extent, scale, reach, split=(), kind=jnp.bfloat16):
    array = scale * jax.random.normal(stream_key, extent, jnp.float32)
    if split:
        array = array * steps_of(stream_key, extent, split, -0.22, 0.18)
    return jnp.clip(array, -reach, reach).astype(kind)


def setup_inputs(seed: int = 0) -> dict:
    key_of = jax.random.split(jax.random.key(seed), 17)
    return {
        "token_ids": with_ends(jax.random.randint(key_of[0], (TOKENS,), 0, V), jax.random.fold_in(key_of[0], 1), 0, V - 1).astype(jnp.int32),
        "prefix_lengths": with_ends(jax.random.randint(key_of[1], (SEQS,), 1, TOK_DEV), jax.random.fold_in(key_of[1], 1), 1, TOK_DEV - 1).astype(jnp.int32),
        "cluster_ids": with_ends(jax.random.randint(key_of[2], (SEQS,), 0, SEQS // 2), jax.random.fold_in(key_of[2], 1), 0, (SEQS // 2) - 1).astype(jnp.int32),
        "embedding": bell_draw(key_of[3], (V, D), 1.0, 6.0),
        "w_query": bell_draw(key_of[4], (D, H * HD), D ** -0.5, 0.125, ((1, 4),)),
        "w_key": bell_draw(key_of[5], (D, H * HD), D ** -0.5, 0.125, ((1, 4),)),
        "w_value": bell_draw(key_of[6], (D, H * HD), D ** -0.5, 0.125, ((1, 4),)),
        "w_dense": bell_draw(key_of[7], (D, H * HD), (24.0 / (H * HD) ** 0.5), 6.0, ((1, 4),)),
        "w_gate": bell_draw(key_of[8], (D, FF), D ** -0.5, 0.125, ((1, 4),)),
        "w_up": bell_draw(key_of[9], (D, FF), D ** -0.5, 0.125, ((1, 4),)),
        "w_down": bell_draw(key_of[10], (D, FF), (4.0 / FF ** 0.5), 0.75, ((1, 4),)),
        "norm1_gain": jnp.clip(1.0 + 0.1 * jax.random.normal(key_of[11], (D,), jnp.float32), 0.5, 1.5),
        "norm1_bias": bell_draw(key_of[12], (D,), 0.3, 4.0, (), jnp.float32),
        "norm2_gain": jnp.clip(1.0 + 0.1 * jax.random.normal(key_of[13], (D,), jnp.float32), 0.5, 1.5),
        "norm2_bias": bell_draw(key_of[14], (D,), 0.3, 4.0, (), jnp.float32),
        "cotangent": bell_draw(key_of[15], (TOKENS, D), 1.0, 6.0, ((0, 8),)),
    }


@jax.custom_vjp
def low(v):
    return lax.optimization_barrier(v.astype(jnp.bfloat16)).astype(jnp.float32)

@jax.custom_vjp
def low_back(v):
    return v

def low_keep(v):
    return (low(v), None)

def low_pass(kept, grad):
    return (grad,)

def back_keep(v):
    return (v, None)

def back_low(kept, grad):
    return (low(grad),)
low.defvjp(low_keep, low_pass)
low_back.defvjp(back_keep, back_low)
deep_alpha = math.sqrt(48.0)
norm_eps = 1e-05
highest = lax.Precision.HIGHEST

def layer_norm(inputs, norm_gain, norm_bias):
    center = lax.optimization_barrier(jnp.mean(inputs, axis=-1, keepdims=True))
    centered = inputs - center
    spread = lax.optimization_barrier(jnp.mean(centered * centered, axis=-1, keepdims=True))
    return centered * lax.rsqrt(spread + norm_eps) * norm_gain + norm_bias

def rotary_tables(length, head_width):
    half_width = head_width // 2
    frequency = jnp.exp(jnp.arange(half_width, dtype=jnp.float32) * (-2.0 * math.log(10000.0) / head_width))
    angles = jnp.arange(length, dtype=jnp.float32)[:, None] * frequency[None, :]
    return (jnp.cos(angles), jnp.sin(angles))

def rotate(inputs, cosine, sine):
    half_width = inputs.shape[-1] // 2
    first = inputs[..., :half_width]
    second = inputs[..., half_width:]
    cosine = cosine[:, None, :]
    sine = sine[:, None, :]
    return jnp.concatenate([first * cosine - second * sine, second * cosine + first * sine], axis=-1)

def attend(queries, keys_rot, values_in, prefix):
    length = queries.shape[0]
    row_block = min(512, length)
    score_scale = 1.0 / math.sqrt(HD)
    columns = jnp.arange(length).astype(jnp.int32)

    def one_block(row_begin):
        query_block = lax.dynamic_slice_in_dim(queries, row_begin, row_block, 0)
        row_index = row_begin + jnp.arange(row_block).astype(jnp.int32)
        scores = jnp.einsum('bhd,khd->hbk', query_block, keys_rot, precision=highest) * score_scale
        scores = low_back(scores)
        visible = (columns[None, :] < prefix) | (columns[None, :] <= row_index[:, None])
        scores = jnp.where(visible[None, :, :], scores, -1e+30)
        row_max = lax.optimization_barrier(jnp.max(scores, axis=-1, keepdims=True))
        weights = jnp.exp(scores - row_max)
        probability = weights / lax.optimization_barrier(jnp.sum(weights, axis=-1, keepdims=True))
        return jnp.einsum('hbk,khd->bhd', low(probability), values_in, precision=highest)
    starts = jnp.arange(length // row_block).astype(jnp.int32) * row_block
    outputs = lax.map(jax.checkpoint(one_block), starts)
    return outputs.reshape(length, -1)

def forward(params, group_ids, group_prefix):
    embed_table, w_query, w_key, w_value, w_dense, w_gate, w_up, w_down, gain_one, bias_one, gain_two, bias_two = params
    length = group_ids.shape[1]
    embedded = embed_table[group_ids]
    cosine, sine = rotary_tables(length, HD)

    def sequence_mix(tokens_in, prefix):

        def project(weight_in):
            return low_back(jnp.dot(tokens_in, weight_in, precision=highest)).reshape(length, -1, HD)
        queries = low(rotate(project(w_query), cosine, sine))
        keys_rot = low(rotate(project(w_key), cosine, sine))
        values_in = low(project(w_value))
        return low(low_back(attend(queries, keys_rot, values_in, prefix)))
    attended = jax.vmap(sequence_mix)(embedded, group_prefix)
    branch = low_back(jnp.einsum('glh,dh->gld', attended, w_dense, precision=highest))
    residual_one = deep_alpha * embedded + branch
    hidden = layer_norm(residual_one, gain_one, bias_one)
    hidden_low = low(hidden)
    gate_proj = low_back(jnp.einsum('gld,df->glf', hidden_low, w_gate, precision=highest))
    up_proj = low_back(jnp.einsum('gld,df->glf', hidden_low, w_up, precision=highest))
    used_mask = (jnp.arange(FF) < FF_USED).astype(jnp.float32)
    activation = low(jax.nn.gelu(gate_proj, approximate=True) * up_proj * used_mask)
    branch_two = low_back(jnp.einsum('glf,df->gld', activation, w_down, precision=highest))
    return layer_norm(deep_alpha * hidden + branch_two, gain_two, bias_two)

def reference(token_ids, prefix_lengths, cluster_ids, embedding, w_query, w_key, w_value, w_dense, w_gate, w_up, w_down, norm1_gain, norm1_bias, norm2_gain, norm2_bias, cotangent):
    params = tuple((member.astype(jnp.float32) for member in (embedding, w_query, w_key, w_value, w_dense, w_gate, w_up, w_down, norm1_gain, norm1_bias, norm2_gain, norm2_bias)))
    same_cluster = (cluster_ids[:, None] == cluster_ids[None, :]).astype(jnp.float32)
    seq_weight = 1.0 / lax.optimization_barrier(jnp.sum(same_cluster, axis=1))
    per_group = math.gcd(SEQS, max(1, 4096 // TOK_DEV))
    groups = SEQS // per_group
    group_ids = token_ids.reshape(groups, per_group, TOK_DEV)
    group_prefix = prefix_lengths.reshape(groups, per_group)
    group_cot = cotangent.astype(jnp.float32).reshape(groups, per_group, TOK_DEV, D) * seq_weight.reshape(groups, per_group, 1, 1)

    def one_group(totals, inputs):
        ids_here, prefix_here, cot_here = inputs

        def closed(*weights):
            return forward(weights, ids_here, prefix_here)
        result, pullback = jax.vjp(closed, *params)
        gradients = pullback(cot_here)
        return (jax.tree.map(jnp.add, totals, tuple(gradients)), result.astype(jnp.bfloat16))
    initial = tuple((jnp.zeros_like(member) for member in params))
    totals, outputs = lax.scan(one_group, initial, (group_ids, group_prefix, group_cot))
    block_out = outputs.reshape(TOKENS, D)
    return (block_out, 0.1 * totals[0], totals[1], totals[2], totals[3], totals[4], totals[5], totals[6], totals[7], totals[8], totals[9], totals[10], totals[11])
```

```python
import math

import jax
import jax.numpy as jnp
from jax import lax
from jax.sharding import PartitionSpec as P

HD = 128
FF_USED = 5461


deep_alpha = math.sqrt(48.0)
norm_eps = 1e-05
highest = lax.Precision.HIGHEST


def layer_norm(inputs, norm_gain, norm_bias):
    center = jnp.mean(inputs, axis=-1, keepdims=True)
    centered = inputs - center
    spread = jnp.mean(centered * centered, axis=-1, keepdims=True)
    return centered * lax.rsqrt(spread + norm_eps) * norm_gain + norm_bias


def rotary_tables(length, head_width):
    half_width = head_width // 2
    frequency = jnp.exp(
        jnp.arange(half_width, dtype=jnp.float32) * (-2.0 * math.log(10000.0) / head_width)
    )
    angles = jnp.arange(length, dtype=jnp.float32)[:, None] * frequency[None, :]
    return (jnp.cos(angles), jnp.sin(angles))


def rotate(inputs, cosine, sine):
    half_width = inputs.shape[-1] // 2
    first = inputs[..., :half_width]
    second = inputs[..., half_width:]
    cosine = cosine[:, None, :]
    sine = sine[:, None, :]
    return jnp.concatenate(
        [first * cosine - second * sine, second * cosine + first * sine], axis=-1
    )


def row_mask(row_begin, row_count, length, prefix):
    columns = jnp.arange(length, dtype=jnp.int32)
    row_index = row_begin + jnp.arange(row_count, dtype=jnp.int32)
    return (columns[None, :] < prefix) | (columns[None, :] <= row_index[:, None])


def block_scores(query_block, keys_rot, visible, score_scale):
    scores = (
        jnp.einsum("bhd,khd->hbk", query_block, keys_rot, preferred_element_type=jnp.float32)
        * score_scale
    )
    return jnp.where(visible[None, :, :], scores, -1e30)


def attention_forward(queries, keys_rot, values_in, prefix, row_block):
    length = queries.shape[0]
    score_scale = 1.0 / math.sqrt(HD)

    def one_block(row_begin):
        scores = block_scores(
            queries, keys_rot, row_mask(row_begin, row_block, length, prefix), score_scale
        )
        row_max = jnp.max(scores, axis=-1, keepdims=True)
        weights = jnp.exp(scores - row_max)
        total_weight = jnp.sum(weights, axis=-1, keepdims=True)
        probability = (weights / total_weight).astype(jnp.bfloat16)
        mixed_block = jnp.einsum(
            "hbk,khd->bhd", probability, values_in, preferred_element_type=jnp.float32
        )
        return (mixed_block, row_max + jnp.log(total_weight))

    starts = jnp.arange(length // row_block, dtype=jnp.int32) * row_block
    attended, log_total = lax.map(one_block, starts)
    return (attended.reshape(length, -1), log_total)


def attention_backward(queries, keys_rot, values_in, prefix, row_block, log_total, grad_mixed):
    length = queries.shape[0]
    score_scale = 1.0 / math.sqrt(HD)

    def one_block(carried, inputs):
        grad_keys, grad_values = carried
        row_begin, block_total = inputs
        scores = block_scores(
            queries, keys_rot, row_mask(row_begin, row_block, length, prefix), score_scale
        )
        probability = jnp.exp(scores - block_total)
        prob_low = probability.astype(jnp.bfloat16)
        grad_prob = jnp.einsum(
            "bhd,khd->hbk", grad_mixed, values_in, preferred_element_type=jnp.float32
        )
        centre = jnp.sum(grad_prob * probability, axis=-1, keepdims=True)
        grad_scores = (probability * (grad_prob - centre)).astype(jnp.bfloat16)
        grad_query = (
            jnp.einsum("hbk,khd->bhd", grad_scores, keys_rot, preferred_element_type=jnp.float32)
            * score_scale
        )
        grad_keys = (
            grad_keys
            + jnp.einsum("hbk,bhd->khd", grad_scores, queries, preferred_element_type=jnp.float32)
            * score_scale
        )
        grad_values = grad_values + jnp.einsum(
            "hbk,bhd->khd", prob_low, grad_mixed, preferred_element_type=jnp.float32
        )
        return ((grad_keys, grad_values), grad_query)

    starts = jnp.arange(length // row_block, dtype=jnp.int32) * row_block
    zeros_kv = jnp.zeros(keys_rot.shape, jnp.float32)
    (grad_keys, grad_values), grad_queries = lax.scan(
        one_block, (zeros_kv, zeros_kv), (starts, log_total)
    )
    return (grad_queries.reshape(queries.shape), grad_keys, grad_values)


def flip_pairs(count, bit):
    return [(index, index ^ bit) for index in range(count)]


def swap(value, axis, count, bit):
    moved = lax.ppermute(value, axis, flip_pairs(count, bit))
    return moved


def sum_over_groups(part, count):
    if count != 4:
        return lax.psum(part, "mp")
    rows = part.shape[0] // 2
    core = lax.axis_index("mp") % 2
    mine = lax.dynamic_slice_in_dim(part, core * rows, rows, 0)
    other = lax.dynamic_slice_in_dim(part, (1 - core) * rows, rows, 0)
    half = mine + lax.ppermute(other, "mp", flip_pairs(count, 1))
    half = half + lax.ppermute(half, "mp", flip_pairs(count, 2))
    back = lax.ppermute(half, "mp", flip_pairs(count, 1))
    return jnp.where(
        core == 0,
        jnp.concatenate([half, back], axis=0),
        jnp.concatenate([back, half], axis=0),
    )


def line_scatter(shards, outer):
    if outer != 4:
        flat = shards.reshape((-1,) + shards.shape[2:])
        groups = [[2 * place + parity for place in range(outer)] for parity in range(2)]
        return lax.psum_scatter(
            flat, "dp", scatter_dimension=0, tiled=True, axis_index_groups=groups
        )
    here = lax.axis_index("dp") // 2

    def shard(place):
        return lax.dynamic_index_in_dim(shards, jnp.clip(place, 0, outer - 1), 0, keepdims=False)

    from_below = None
    from_above = None
    for slot in range(1, outer):
        up = shard(outer - slot + here)
        down = shard(slot - outer + here)
        if from_below is not None:
            up = up + from_below
            down = down + from_above
        up_pairs = [(2 * z + y, 2 * z + 2 + y) for z in range(slot) for y in range(2)]
        down_pairs = [
            (2 * (outer - 1 - z) + y, 2 * (outer - 2 - z) + y) for z in range(slot) for y in range(2)
        ]
        from_below = lax.ppermute(up, "dp", up_pairs)
        from_above = lax.ppermute(down, "dp", down_pairs)
    return shard(here) + from_below + from_above


def half_columns(value, parity, outer):
    rows, width = value.shape
    parts = value.reshape(rows, outer, 2, width // (2 * outer))
    return lax.dynamic_index_in_dim(parts, parity, 2, keepdims=False).reshape(rows, width // 2)


def local(
    token_ids,
    prefix_lengths,
    cluster_ids,
    embedding,
    w_query,
    w_key,
    w_value,
    w_dense,
    w_gate,
    w_up,
    w_down,
    norm1_gain,
    norm1_bias,
    norm2_gain,
    norm2_bias,
    cotangent,
):
    length = token_ids.shape[0]
    vocab_rows = embedding.shape[0]
    row_block = min(512, length)
    local_heads = w_query.shape[1] // HD
    local_hidden = w_gate.shape[1]
    one_hot = (token_ids[:, None] == jnp.arange(vocab_rows, dtype=jnp.int32)[None, :]).astype(
        jnp.bfloat16
    )
    embedded_low = jnp.dot(one_hot, embedding, preferred_element_type=jnp.float32).astype(
        jnp.bfloat16
    )
    embedded = embedded_low.astype(jnp.float32)
    their_ids = lax.ppermute(token_ids, "dp", flip_pairs(lax.axis_size("dp"), 1))
    their_hot = (their_ids[:, None] == jnp.arange(vocab_rows, dtype=jnp.int32)[None, :]).astype(
        jnp.bfloat16
    )
    their_embedded = jnp.dot(their_hot, embedding, preferred_element_type=jnp.float32).astype(
        jnp.bfloat16
    )
    cosine, sine = rotary_tables(length, HD)
    prefix = prefix_lengths[0]
    dp_count = lax.axis_size("dp")
    mp_count = lax.axis_size("mp")
    outer = dp_count // 2
    parity = lax.axis_index("dp") % 2
    own_cluster = cluster_ids[lax.axis_index("dp")]
    seq_weight = 1.0 / jnp.sum((cluster_ids == own_cluster).astype(jnp.float32))

    unit = (prefix_lengths[0] > 0).astype(jnp.float32)

    def exchange(value):
        return (swap(value.astype(jnp.float32), "dp", dp_count, 1) * unit).astype(jnp.bfloat16)

    def exchange_half(value):
        theirs = half_columns(value, 1 - parity, outer)
        if mp_count != 4:
            return exchange(theirs)
        rows = length // 2
        core = lax.axis_index("mp") % 2
        part = lax.dynamic_slice_in_dim(theirs, core * rows, rows, 0)
        got = swap(part.astype(jnp.float32), "dp", dp_count, 1) * unit
        rest = swap(got, "mp", mp_count, 1) * unit
        got, rest = got.astype(jnp.bfloat16), rest.astype(jnp.bfloat16)
        return jnp.where(
            core == 0,
            jnp.concatenate([got, rest], axis=0),
            jnp.concatenate([rest, got], axis=0),
        )

    def pair_product(left, right, left_theirs, right_theirs):
        both = jnp.einsum(
            "ld,lf->df", left, right, preferred_element_type=jnp.float32
        ) + jnp.einsum("ld,lf->df", left_theirs, right_theirs, preferred_element_type=jnp.float32)
        return line_scatter(both.reshape((outer, -1) + both.shape[1:]), outer)

    def project(weight_in):
        return jnp.dot(embedded_low, weight_in, preferred_element_type=jnp.float32).reshape(
            length, local_heads, HD
        )

    queries = rotate(project(w_query), cosine, sine).astype(jnp.bfloat16)
    keys_rot = rotate(project(w_key), cosine, sine).astype(jnp.bfloat16)
    values_in = project(w_value).astype(jnp.bfloat16)
    attended, log_total = attention_forward(queries, keys_rot, values_in, prefix, row_block)
    attended_low = attended.astype(jnp.bfloat16)
    branch = sum_over_groups(
        jnp.einsum("lh,dh->ld", attended_low, w_dense, preferred_element_type=jnp.float32), mp_count
    )
    residual_one = deep_alpha * embedded + branch
    hidden, norm_one_pull = jax.vjp(layer_norm, residual_one, norm1_gain, norm1_bias)
    hidden_low = hidden.astype(jnp.bfloat16)
    gate_proj = jnp.dot(hidden_low, w_gate, preferred_element_type=jnp.float32)
    up_proj = jnp.dot(hidden_low, w_up, preferred_element_type=jnp.float32)
    unit_index = lax.axis_index("mp") * local_hidden + jnp.arange(local_hidden, dtype=jnp.int32)
    used_mask = (unit_index < FF_USED).astype(jnp.float32)

    def gated_unit(gate_in, up_in):
        return jax.nn.gelu(gate_in, approximate=True) * up_in * used_mask

    activation, gated_pull = jax.vjp(gated_unit, gate_proj, up_proj)
    activation_low = activation.astype(jnp.bfloat16)
    branch_two = sum_over_groups(
        jnp.einsum("lf,df->ld", activation_low, w_down, preferred_element_type=jnp.float32), mp_count
    )
    residual_two = deep_alpha * hidden + branch_two
    final, norm_two_pull = jax.vjp(layer_norm, residual_two, norm2_gain, norm2_bias)
    grad_out = cotangent.astype(jnp.float32) * seq_weight
    grad_two, grad_gain_two, grad_bias_two = norm_two_pull(grad_out)
    grad_branch_two = grad_two.astype(jnp.bfloat16)
    grad_act = jnp.dot(grad_branch_two, w_down, preferred_element_type=jnp.float32)
    grad_gate, grad_up = gated_pull(grad_act)
    grad_gate_low = grad_gate.astype(jnp.bfloat16)
    grad_up_low = grad_up.astype(jnp.bfloat16)
    hidden_part = jnp.einsum(
        "lf,df->ld", grad_gate_low, w_gate, preferred_element_type=jnp.float32
    ) + jnp.einsum("lf,df->ld", grad_up_low, w_up, preferred_element_type=jnp.float32)
    grad_hidden = deep_alpha * grad_two + sum_over_groups(hidden_part, mp_count)
    hidden_half = half_columns(hidden_low, parity, outer)
    out_w_down = pair_product(
        half_columns(grad_branch_two, parity, outer),
        activation_low,
        exchange_half(grad_branch_two),
        exchange(activation_low),
    )
    hidden_theirs = exchange_half(hidden_low)
    out_w_gate = pair_product(hidden_half, grad_gate_low, hidden_theirs, exchange(grad_gate_low))
    out_w_up = pair_product(hidden_half, grad_up_low, hidden_theirs, exchange(grad_up_low))
    grad_one, grad_gain_one, grad_bias_one = norm_one_pull(grad_hidden)
    grad_branch = grad_one.astype(jnp.bfloat16)
    out_w_dense = pair_product(
        half_columns(grad_branch, parity, outer),
        attended_low,
        exchange_half(grad_branch),
        exchange(attended_low),
    )
    grad_attended = jnp.dot(grad_branch, w_dense, preferred_element_type=jnp.float32).astype(
        jnp.bfloat16
    )
    grad_attended = grad_attended.reshape(length, local_heads, HD)
    grad_queries, grad_keys, grad_values = attention_backward(
        queries, keys_rot, values_in, prefix, row_block, log_total, grad_attended
    )
    grad_query_lin = rotate(grad_queries, cosine, -sine).astype(jnp.bfloat16).reshape(length, -1)
    grad_key_lin = rotate(grad_keys, cosine, -sine).astype(jnp.bfloat16).reshape(length, -1)
    grad_value_lin = grad_values.astype(jnp.bfloat16).reshape(length, -1)
    input_part = (
        jnp.einsum("lh,dh->ld", grad_query_lin, w_query, preferred_element_type=jnp.float32)
        + jnp.einsum("lh,dh->ld", grad_key_lin, w_key, preferred_element_type=jnp.float32)
        + jnp.einsum("lh,dh->ld", grad_value_lin, w_value, preferred_element_type=jnp.float32)
    )
    embedded_half = half_columns(embedded_low, parity, outer)
    embedded_theirs = half_columns(their_embedded, parity, outer)
    out_w_query = pair_product(
        embedded_half, grad_query_lin, embedded_theirs, exchange(grad_query_lin)
    )
    out_w_key = pair_product(embedded_half, grad_key_lin, embedded_theirs, exchange(grad_key_lin))
    out_w_value = pair_product(
        embedded_half, grad_value_lin, embedded_theirs, exchange(grad_value_lin)
    )
    own_share = jnp.where(lax.axis_index("mp") == 0, deep_alpha, 0.0)
    table_part = 0.1 * jnp.dot(
        one_hot.astype(jnp.float32).T, own_share * grad_one + input_part, precision=highest
    )
    table_part = lax.psum_scatter(table_part, "mp", scatter_dimension=1, tiled=True)
    table_rows = vocab_rows // dp_count
    width = grad_gain_one.shape[0] // dp_count
    small = jnp.concatenate(
        [
            vector.reshape(dp_count, width)
            for vector in (grad_gain_one, grad_bias_one, grad_gain_two, grad_bias_two)
        ]
        + [table_part.reshape(dp_count, -1)],
        axis=1,
    ).reshape(outer, 2, -1)
    keep = lax.dynamic_index_in_dim(small, parity, 1, keepdims=False)
    give = lax.dynamic_index_in_dim(small, 1 - parity, 1, keepdims=False)
    small = keep + lax.ppermute(give, "dp", flip_pairs(dp_count, 1))
    small = line_scatter(small.reshape(outer, -1, 128), outer).reshape(-1)
    out_norms = [small[place * width : (place + 1) * width] for place in range(4)]
    out_table = small[4 * width :].reshape(table_rows, -1)
    out_table = lax.all_gather(out_table, "mp", axis=1, tiled=True)
    return (
        final.astype(jnp.bfloat16),
        out_table,
        out_w_query,
        out_w_key,
        out_w_value,
        out_w_dense,
        out_w_gate,
        out_w_up,
        out_w_down,
        out_norms[0],
        out_norms[1],
        out_norms[2],
        out_norms[3],
    )


def solution(mesh):
    return jax.shard_map(
        local,
        mesh=mesh,
        in_specs=(
            P("dp"),
            P("dp"),
            P(),
            P(),
            P(None, "mp"),
            P(None, "mp"),
            P(None, "mp"),
            P(None, "mp"),
            P(None, "mp"),
            P(None, "mp"),
            P(None, "mp"),
            P(),
            P(),
            P(),
            P(),
            P("dp", None),
        ),
        out_specs=(
            P("dp", None),
            P("dp", None),
            P("dp", "mp"),
            P("dp", "mp"),
            P("dp", "mp"),
            P("dp", "mp"),
            P("dp", "mp"),
            P("dp", "mp"),
            P("dp", "mp"),
            P("dp"),
            P("dp"),
            P("dp"),
            P("dp"),
        ),
        check_vma=False,
    )
```

```python
import functools
import math

import jax
import jax.numpy as jnp
from jax import lax
from jax.experimental import pallas as pl
from jax.experimental.pallas import tpu as pltpu
from jax.sharding import PartitionSpec as P

HD = 128
FF_USED = 5461


deep_alpha = math.sqrt(48.0)
norm_eps = 1e-05
highest = lax.Precision.HIGHEST


def layer_norm(inputs, norm_gain, norm_bias):
    center = jnp.mean(inputs, axis=-1, keepdims=True)
    centered = inputs - center
    spread = jnp.mean(centered * centered, axis=-1, keepdims=True)
    return centered * lax.rsqrt(spread + norm_eps) * norm_gain + norm_bias


def rotary_tables(length, head_width):
    half_width = head_width // 2
    frequency = jnp.exp(
        jnp.arange(half_width, dtype=jnp.float32) * (-2.0 * math.log(10000.0) / head_width)
    )
    angles = jnp.arange(length, dtype=jnp.float32)[:, None] * frequency[None, :]
    return (jnp.cos(angles), jnp.sin(angles))


def rotate(inputs, cosine, sine):
    half_width = inputs.shape[-1] // 2
    first = inputs[..., :half_width]
    second = inputs[..., half_width:]
    cosine = cosine[:, None, :]
    sine = sine[:, None, :]
    return jnp.concatenate(
        [first * cosine - second * sine, second * cosine + first * sine], axis=-1
    )


def row_mask(row_begin, row_count, length, prefix):
    columns = jnp.arange(length, dtype=jnp.int32)
    row_index = row_begin + jnp.arange(row_count, dtype=jnp.int32)
    return (columns[None, :] < prefix) | (columns[None, :] <= row_index[:, None])


def block_scores(query_block, keys_rot, visible, score_scale):
    scores = (
        jnp.einsum("bhd,khd->hbk", query_block, keys_rot, preferred_element_type=jnp.float32)
        * score_scale
    )
    return jnp.where(visible[None, :, :], scores, -1e30)


def attention_forward(queries, keys_rot, values_in, prefix, row_block):
    length = queries.shape[0]
    score_scale = 1.0 / math.sqrt(HD)

    def one_block(row_begin):
        scores = block_scores(
            queries, keys_rot, row_mask(row_begin, row_block, length, prefix), score_scale
        )
        row_max = jnp.max(scores, axis=-1, keepdims=True)
        weights = jnp.exp(scores - row_max)
        total_weight = jnp.sum(weights, axis=-1, keepdims=True)
        probability = (weights / total_weight).astype(jnp.bfloat16)
        mixed_block = jnp.einsum(
            "hbk,khd->bhd", probability, values_in, preferred_element_type=jnp.float32
        )
        return (mixed_block, row_max + jnp.log(total_weight))

    starts = jnp.arange(length // row_block, dtype=jnp.int32) * row_block
    attended, log_total = lax.map(one_block, starts)
    return (attended.reshape(length, -1), log_total)


def attention_backward(queries, keys_rot, values_in, prefix, row_block, log_total, grad_mixed):
    length = queries.shape[0]
    score_scale = 1.0 / math.sqrt(HD)

    def one_block(carried, inputs):
        grad_keys, grad_values = carried
        row_begin, block_total = inputs
        scores = block_scores(
            queries, keys_rot, row_mask(row_begin, row_block, length, prefix), score_scale
        )
        probability = jnp.exp(scores - block_total)
        prob_low = probability.astype(jnp.bfloat16)
        grad_prob = jnp.einsum(
            "bhd,khd->hbk", grad_mixed, values_in, preferred_element_type=jnp.float32
        )
        centre = jnp.sum(grad_prob * probability, axis=-1, keepdims=True)
        grad_scores = (probability * (grad_prob - centre)).astype(jnp.bfloat16)
        grad_query = (
            jnp.einsum("hbk,khd->bhd", grad_scores, keys_rot, preferred_element_type=jnp.float32)
            * score_scale
        )
        grad_keys = (
            grad_keys
            + jnp.einsum("hbk,bhd->khd", grad_scores, queries, preferred_element_type=jnp.float32)
            * score_scale
        )
        grad_values = grad_values + jnp.einsum(
            "hbk,bhd->khd", prob_low, grad_mixed, preferred_element_type=jnp.float32
        )
        return ((grad_keys, grad_values), grad_query)

    starts = jnp.arange(length // row_block, dtype=jnp.int32) * row_block
    zeros_kv = jnp.zeros(keys_rot.shape, jnp.float32)
    (grad_keys, grad_values), grad_queries = lax.scan(
        one_block, (zeros_kv, zeros_kv), (starts, log_total)
    )
    return (grad_queries.reshape(queries.shape), grad_keys, grad_values)


def local_general(
    token_ids,
    prefix_lengths,
    cluster_ids,
    embedding,
    w_query,
    w_key,
    w_value,
    w_dense,
    w_gate,
    w_up,
    w_down,
    norm1_gain,
    norm1_bias,
    norm2_gain,
    norm2_bias,
    cotangent,
):
    length = token_ids.shape[0]
    vocab_rows = embedding.shape[0]
    row_block = min(512, length)
    local_heads = w_query.shape[1] // HD
    local_hidden = w_gate.shape[1]
    one_hot = (token_ids[:, None] == jnp.arange(vocab_rows, dtype=jnp.int32)[None, :]).astype(
        jnp.bfloat16
    )
    embedded_low = jnp.dot(one_hot, embedding, preferred_element_type=jnp.float32).astype(
        jnp.bfloat16
    )
    embedded = embedded_low.astype(jnp.float32)
    cosine, sine = rotary_tables(length, HD)
    prefix = prefix_lengths[0]
    own_cluster = cluster_ids[lax.axis_index("dp")]
    seq_weight = 1.0 / jnp.sum((cluster_ids == own_cluster).astype(jnp.float32))

    def project(weight_in):
        return jnp.dot(embedded_low, weight_in, preferred_element_type=jnp.float32).reshape(
            length, local_heads, HD
        )

    queries = rotate(project(w_query), cosine, sine).astype(jnp.bfloat16)
    keys_rot = rotate(project(w_key), cosine, sine).astype(jnp.bfloat16)
    values_in = project(w_value).astype(jnp.bfloat16)
    attended, log_total = attention_forward(queries, keys_rot, values_in, prefix, row_block)
    attended_low = attended.astype(jnp.bfloat16)
    branch = lax.psum(
        jnp.einsum("lh,dh->ld", attended_low, w_dense, preferred_element_type=jnp.float32), "mp"
    )
    residual_one = deep_alpha * embedded + branch
    hidden, norm_one_pull = jax.vjp(layer_norm, residual_one, norm1_gain, norm1_bias)
    hidden_low = hidden.astype(jnp.bfloat16)
    gate_proj = jnp.dot(hidden_low, w_gate, preferred_element_type=jnp.float32)
    up_proj = jnp.dot(hidden_low, w_up, preferred_element_type=jnp.float32)
    unit_index = lax.axis_index("mp") * local_hidden + jnp.arange(local_hidden, dtype=jnp.int32)
    used_mask = (unit_index < FF_USED).astype(jnp.float32)

    def gated_unit(gate_in, up_in):
        return jax.nn.gelu(gate_in, approximate=True) * up_in * used_mask

    activation, gated_pull = jax.vjp(gated_unit, gate_proj, up_proj)
    activation_low = activation.astype(jnp.bfloat16)
    branch_two = lax.psum(
        jnp.einsum("lf,df->ld", activation_low, w_down, preferred_element_type=jnp.float32), "mp"
    )
    residual_two = deep_alpha * hidden + branch_two
    final, norm_two_pull = jax.vjp(layer_norm, residual_two, norm2_gain, norm2_bias)
    grad_out = cotangent.astype(jnp.float32) * seq_weight
    grad_two, grad_gain_two, grad_bias_two = norm_two_pull(grad_out)
    grad_branch_two = grad_two.astype(jnp.bfloat16)
    grad_w_down = jnp.einsum(
        "ld,lf->df", grad_branch_two, activation_low, preferred_element_type=jnp.float32
    )
    grad_act = jnp.dot(grad_branch_two, w_down, preferred_element_type=jnp.float32)
    grad_gate, grad_up = gated_pull(grad_act)
    grad_gate_low = grad_gate.astype(jnp.bfloat16)
    grad_up_low = grad_up.astype(jnp.bfloat16)
    grad_w_gate = jnp.einsum(
        "ld,lf->df", hidden_low, grad_gate_low, preferred_element_type=jnp.float32
    )
    grad_w_up = jnp.einsum("ld,lf->df", hidden_low, grad_up_low, preferred_element_type=jnp.float32)
    hidden_part = jnp.einsum(
        "lf,df->ld", grad_gate_low, w_gate, preferred_element_type=jnp.float32
    ) + jnp.einsum("lf,df->ld", grad_up_low, w_up, preferred_element_type=jnp.float32)
    grad_hidden = deep_alpha * grad_two + lax.psum(hidden_part, "mp")
    feed_sums = (
        lax.psum_scatter(grad_w_gate, "dp", scatter_dimension=0, tiled=True),
        lax.psum_scatter(grad_w_up, "dp", scatter_dimension=0, tiled=True),
        lax.psum_scatter(grad_w_down, "dp", scatter_dimension=0, tiled=True),
        lax.psum_scatter(grad_gain_two, "dp", scatter_dimension=0, tiled=True),
        lax.psum_scatter(grad_bias_two, "dp", scatter_dimension=0, tiled=True),
    )
    grad_one, grad_gain_one, grad_bias_one = norm_one_pull(grad_hidden)
    grad_branch = grad_one.astype(jnp.bfloat16)
    grad_w_dense = jnp.einsum(
        "ld,lh->dh", grad_branch, attended_low, preferred_element_type=jnp.float32
    )
    grad_attended = jnp.dot(grad_branch, w_dense, preferred_element_type=jnp.float32).astype(
        jnp.bfloat16
    )
    grad_attended = grad_attended.reshape(length, local_heads, HD)
    grad_queries, grad_keys, grad_values = attention_backward(
        queries, keys_rot, values_in, prefix, row_block, log_total, grad_attended
    )
    grad_query_lin = rotate(grad_queries, cosine, -sine).astype(jnp.bfloat16).reshape(length, -1)
    grad_key_lin = rotate(grad_keys, cosine, -sine).astype(jnp.bfloat16).reshape(length, -1)
    grad_value_lin = grad_values.astype(jnp.bfloat16).reshape(length, -1)
    grad_w_query = jnp.einsum(
        "ld,lh->dh", embedded_low, grad_query_lin, preferred_element_type=jnp.float32
    )
    grad_w_key = jnp.einsum(
        "ld,lh->dh", embedded_low, grad_key_lin, preferred_element_type=jnp.float32
    )
    grad_w_value = jnp.einsum(
        "ld,lh->dh", embedded_low, grad_value_lin, preferred_element_type=jnp.float32
    )
    input_part = (
        jnp.einsum("lh,dh->ld", grad_query_lin, w_query, preferred_element_type=jnp.float32)
        + jnp.einsum("lh,dh->ld", grad_key_lin, w_key, preferred_element_type=jnp.float32)
        + jnp.einsum("lh,dh->ld", grad_value_lin, w_value, preferred_element_type=jnp.float32)
    )
    grad_embedded = deep_alpha * grad_one + lax.psum(input_part, "mp")
    grad_table = 0.1 * jnp.dot(one_hot.astype(jnp.float32).T, grad_embedded, precision=highest)
    attn_sums = (
        lax.psum_scatter(grad_table, "dp", scatter_dimension=0, tiled=True),
        lax.psum_scatter(grad_w_query, "dp", scatter_dimension=0, tiled=True),
        lax.psum_scatter(grad_w_key, "dp", scatter_dimension=0, tiled=True),
        lax.psum_scatter(grad_w_value, "dp", scatter_dimension=0, tiled=True),
        lax.psum_scatter(grad_w_dense, "dp", scatter_dimension=0, tiled=True),
        lax.psum_scatter(grad_gain_one, "dp", scatter_dimension=0, tiled=True),
        lax.psum_scatter(grad_bias_one, "dp", scatter_dimension=0, tiled=True),
    )
    summed = (
        attn_sums[0],
        attn_sums[1],
        attn_sums[2],
        attn_sums[3],
        attn_sums[4],
        feed_sums[0],
        feed_sums[1],
        feed_sums[2],
        attn_sums[5],
        attn_sums[6],
        feed_sums[3],
        feed_sums[4],
    )
    return (
        final.astype(jnp.bfloat16),
        summed[0],
        summed[1],
        summed[2],
        summed[3],
        summed[4],
        summed[5],
        summed[6],
        summed[7],
        summed[8],
        summed[9],
        summed[10],
        summed[11],
    )


LINE = 4
MESH = pl.DeviceIdType.MESH
CHUNKS = 4
LOW = jnp.bfloat16
FULL = jnp.float32
TANH_SCALE = math.sqrt(2.0 / math.pi)


def dot(left, right):
    return jnp.dot(left, right, preferred_element_type=FULL)


def dot_nt(left, right):
    return lax.dot_general(left, right, (((1,), (1,)), ((), ())), preferred_element_type=FULL)


def dot_tn(left, right):
    return lax.dot_general(left, right, (((0,), (0,)), ((), ())), preferred_element_type=FULL)


def split_low(value):
    high = value.astype(LOW)
    return high, (value - high.astype(FULL)).astype(LOW)


def row_mean(value):
    return jnp.mean(value, axis=-1, keepdims=True)


def column_tiles(width, tile=512):
    return [(start, min(tile, width - start)) for start in range(0, width, tile)]


def layer_kernel(
    length, width, local_hidden,
    prefix_ref, weight_ref, ids_col, ids_row, emb, tab, cos_ref, sin_ref, norms, w_dense_hbm, w_gate_hbm, w_up_hbm,
    w_down_hbm, cot_hbm,
    block_out, out_gate, out_up, out_down, out_dense, out_sums,
    r_act, r_y, r_cols, r_att, xhat_park, grad_two_park, dnx, r_dny, dnv, r_dnz, r_rs, r_rsd,
    parts, core_in, x_in, back_in, blocks, xbuf, gbuf, obuf, gate_up, grads_low, act_low, send_a, cols_own, cols_send, att_low,
    heads, w_dense, one_hot, rstd_one, vectors, sums, sums_y, sums_below, sums_above, sums_other,
    core_s, core_r, x_s, x_r, back_s, back_r, act_s, act_r, cols_s, cols_r, fwd_s, fwd_r, ys_s, ys_r, gb1_s, gb1_r,
    att_s, att_r, dny_s, dny_r, dnz_s, dnz_r, rs_s, rs_r, sums_s, sums_r, load_sem, weight_sem,
):
    dp, mp = lax.axis_index("dp"), lax.axis_index("mp")
    z, y = lax.div(dp, 2), lax.rem(dp, 2)
    x, core = lax.div(mp, 2), lax.rem(mp, 2)
    half = lax.rem(z, 2)
    rows = length // CHUNKS
    heads_here = heads.shape[1]
    block = width // (2 * LINE)
    alpha = jnp.float32(deep_alpha)

    def at(z_to=None, y_to=None, x_to=None, core_to=None):
        z_to = z if z_to is None else z_to
        y_to = y if y_to is None else y_to
        x_to = x if x_to is None else x_to
        core_to = core if core_to is None else core_to
        return (2 * z_to + y_to, 2 * x_to + core_to)

    core_peer = at(core_to=1 - core)
    x_peer = at(x_to=1 - x)
    y_peer = at(y_to=1 - y)
    z_pair = z + 1 - 2 * half
    z_peer = at(z_to=z_pair)

    def remote(source, target, send, receive, device):
        return pltpu.make_async_remote_copy(
            src_ref=source, dst_ref=target, send_sem=send, recv_sem=receive,
            device_id=device, device_id_type=MESH,
        )

    def load_all(pairs):
        copies = [
            pltpu.make_async_copy(source, target, load_sem.at[place])
            for place, (source, target) in enumerate(pairs)
        ]
        for copy in copies:
            copy.start()
        return copies

    def moved(pairs):
        for copy in load_all(pairs):
            copy.wait()

    barrier = pltpu.get_barrier_semaphore()
    greeted = [core_peer, x_peer, y_peer] + [at(z_to=lax.rem(z + step, LINE)) for step in range(1, LINE)]
    for device in greeted:
        pl.semaphore_signal(barrier, inc=1, device_id=device, device_id_type=MESH)

    def chunk_rows(chunk):
        return pl.ds(pl.multiple_of(chunk * rows, rows), rows)

    def core_copy(turn, chunk):
        return remote(
            parts.at[chunk, 1 - core], core_in.at[chunk], core_s.at[turn, chunk], core_r.at[turn, chunk], core_peer
        )

    def x_copy(turn, chunk):
        return remote(
            parts.at[chunk, core], x_in.at[turn % 2, chunk], x_s.at[turn, chunk], x_r.at[turn, chunk], x_peer
        )

    def back_copy(turn, chunk):
        return remote(
            parts.at[chunk, core], back_in.at[chunk], back_s.at[turn, chunk], back_r.at[turn, chunk], core_peer
        )

    def send_part(turn, chunk):
        core_copy(turn, chunk).wait()
        parts[chunk, core] = parts[chunk, core] + core_in[chunk]
        x_copy(turn, chunk).start()

    def take_part(turn, chunk):
        x_copy(turn, chunk).wait()
        parts[chunk, core] = parts[chunk, core] + x_in[turn % 2, chunk]
        back = back_copy(turn, chunk)
        back.start()
        mine = parts[chunk, core]
        back.wait()
        other = back_in[chunk]
        return jnp.concatenate([jnp.where(core == 0, mine, other), jnp.where(core == 0, other, mine)], axis=1)

    def put_blocks(value):
        for place in range(2 * LINE):
            blocks[place] = value[:, place * block : (place + 1) * block]

    def own_pair_blocks(place):
        return 2 * place + y

    def sent_pair_block(place):
        return 2 * (2 * core + place) + 1 - y

    def own_z_block(place):
        return 4 * half + place

    def sent_z_block(place):
        return 4 * (1 - half) + 2 * core + place

    def keep_columns(kind, chunk, own_block, sent_block, target):
        for place in range(LINE):
            piece = blocks[own_block(place)].T.astype(LOW)
            cols_own[min(kind, 1), place, :, chunk_rows(chunk)] = piece
        for place in range(2):
            target[place, chunk] = blocks[sent_block(place)]

    def cols_copy(kind, chunk, device):
        return remote(
            cols_send.at[min(kind, 1), :, chunk], r_cols.at[kind, pl.ds(2 * core, 2), chunk],
            cols_s.at[kind, chunk], cols_r.at[kind, chunk], device,
        )

    def forward_copy(kind):
        view = r_cols.at[kind, pl.ds(2 * core, 2)]
        return remote(view, view, fwd_s.at[kind], fwd_r.at[kind], core_peer)

    def act_copy(chunk):
        source = send_a.at[lax.div(chunk, 2), pl.ds(pl.multiple_of(lax.rem(chunk, 2) * rows, rows), rows)]
        return remote(source, r_act.at[chunk_rows(chunk)], act_s.at[chunk], act_r.at[chunk], z_peer)

    def pair_copy(which, chunk):
        return remote(
            gate_up.at[which, chunk_rows(chunk)], r_y.at[which, chunk_rows(chunk)],
            ys_s.at[which, chunk], ys_r.at[which, chunk], y_peer,
        )

    def every_chunk(body):
        lax.fori_loop(0, CHUNKS, lambda chunk, carried: (body(chunk), carried)[1], 0)

    column = lax.broadcasted_iota(jnp.int32, (length, length), 1)
    row = lax.broadcasted_iota(jnp.int32, (length, length), 0)
    score_scale = 1.0 / math.sqrt(HD)

    def probabilities(queries, keys):
        visible = (column < prefix_ref[0]) | (column <= row)
        scores = jnp.where(visible, dot_nt(queries, keys) * score_scale, -1e30)
        weights = jnp.exp(scores - jnp.max(scores, axis=-1, keepdims=True))
        return weights / jnp.sum(weights, axis=-1, keepdims=True)

    def turn_by(value, sine):
        return value * cos_ref[...] + pltpu.roll(value, HD // 2, 1) * sine

    def head_lanes(place, offset=0):
        return pl.ds(pl.multiple_of(offset + place * HD, HD), HD)

    def attend_head(place, carried):
        hot = one_hot[...]
        lin = []
        for kind in range(3):
            high, rest = split_low(tab[kind * heads_here + place])
            lin.append(dot(hot, high) + dot(hot, rest))
        queries = turn_by(lin[0], sin_ref[...]).astype(LOW)
        keys = turn_by(lin[1], sin_ref[...]).astype(LOW)
        values = lin[2].astype(LOW)
        heads[0, place], heads[1, place], heads[2, place] = queries, keys, values
        probability = probabilities(queries, keys).astype(LOW)
        att_low[:, head_lanes(place)] = dot(probability, values).astype(LOW)
        return carried

    def first_scope(w_gate, w_up, w_down, cotbuf):
        weight_copies = [
            pltpu.make_async_copy(source, target, weight_sem.at[place])
            for place, (source, target) in enumerate(
                ((w_dense_hbm, w_dense), (w_gate_hbm, w_gate), (w_up_hbm, w_up), (w_down_hbm, w_down))
            )
        ]
        for copy in weight_copies:
            copy.start()
        vocab = emb.shape[0]
        lanes = lax.broadcasted_iota(jnp.int32, (length, vocab), 1)
        one_hot[...] = jnp.where(ids_col[...] == lanes, 1.0, 0.0).astype(LOW)
        vectors[...] = jnp.zeros_like(vectors)
        lax.fori_loop(0, heads_here, attend_head, 0)
        weight_copies[0].wait()
        pl.semaphore_wait(barrier, len(greeted))

        def project(chunk):
            mixed = att_low[chunk_rows(chunk), :]
            for side in range(2):
                for start, size in column_tiles(width // 2, 256):
                    weight = w_dense[side * (width // 2) + start : side * (width // 2) + start + size, :]
                    parts[chunk, side, :, start : start + size] = dot_nt(mixed, weight)
            core_copy(0, chunk).start()

        every_chunk(project)
        every_chunk(lambda chunk: send_part(0, chunk))
        for copy in weight_copies[1:]:
            copy.wait()

        def feed_forward(chunk):
            branch = take_part(0, chunk)
            residual = alpha * dot(one_hot[chunk_rows(chunk), :], emb[...]) + branch
            centered = residual - row_mean(residual)
            rstd = lax.rsqrt(row_mean(centered * centered) + norm_eps)
            xhat = centered * rstd
            rstd_one[chunk] = rstd
            xbuf[...] = xhat
            park = pltpu.make_async_copy(xbuf, xhat_park.at[chunk], load_sem.at[0])
            park.start()
            hidden_low = (xhat * norms[0:1, :] + norms[1:2, :]).astype(LOW)
            put_blocks(hidden_low.astype(FULL))
            keep_columns(0, chunk, own_pair_blocks, sent_pair_block, cols_send.at[0])
            cols_copy(0, chunk, y_peer).start()
            base = lax.rem(chunk, 2) * rows
            for start, size in column_tiles(local_hidden):
                cut = slice(start, start + size)
                gate = dot(hidden_low, w_gate[:, cut])
                up = dot(hidden_low, w_up[:, cut])
                units = mp * local_hidden + start + lax.broadcasted_iota(jnp.int32, (rows, size), 1)
                used = jnp.where(units < FF_USED, 1.0, 0.0)
                square = gate * gate
                bend = jnp.tanh(TANH_SCALE * gate * (1.0 + 0.044715 * square))
                gelu = 0.5 * gate * (1.0 + bend) * used
                slope = 0.5 * (1.0 + bend) + 0.5 * gate * (1.0 - bend * bend) * (
                    TANH_SCALE * (1.0 + 3.0 * 0.044715 * square)
                )
                gate_up[0, chunk_rows(chunk), cut] = slope * up * used
                gate_up[1, chunk_rows(chunk), cut] = gelu
                active = (gelu * up).astype(LOW)
                act_low[chunk_rows(chunk), cut] = active
                send_a[lax.div(chunk, 2), pl.ds(pl.multiple_of(base, rows), rows), cut] = active.astype(FULL)
            act_copy(chunk).start()
            active = act_low[chunk_rows(chunk), :]
            for side in range(2):
                for start, size in column_tiles(width // 2, 256):
                    weight = w_down[side * (width // 2) + start : side * (width // 2) + start + size, :]
                    parts[chunk, side, :, start : start + size] = dot_nt(active, weight)
            core_copy(1, chunk).start()
            park.wait()
            send_part(1, chunk)

        every_chunk(feed_forward)

        def feed_backward(chunk):
            loads = load_all(
                ((xhat_park.at[chunk], xbuf), (cot_hbm.at[chunk_rows(chunk)], cotbuf))
            )
            branch = take_part(1, chunk)
            for copy in loads:
                copy.wait()
            residual = alpha * (xbuf[...] * norms[0:1, :] + norms[1:2, :]) + branch
            centered = residual - row_mean(residual)
            rstd = lax.rsqrt(row_mean(centered * centered) + norm_eps)
            xhat = centered * rstd
            obuf[...] = (xhat * norms[2:3, :] + norms[3:4, :]).astype(LOW)
            grad_out = cotbuf[...].astype(FULL) * weight_ref[...]
            vectors[2:3, :] += jnp.sum(grad_out * xhat, axis=0, keepdims=True)
            vectors[3:4, :] += jnp.sum(grad_out, axis=0, keepdims=True)
            grad_x = grad_out * norms[2:3, :]
            grad_two = (grad_x - row_mean(grad_x) - xhat * row_mean(grad_x * xhat)) * rstd
            gbuf[...] = grad_two
            stores = load_all(
                ((obuf, block_out.at[chunk_rows(chunk)]), (gbuf, grad_two_park.at[chunk]))
            )
            grad_low = grad_two.astype(LOW)
            put_blocks(grad_low.astype(FULL))
            keep_columns(1, chunk, own_z_block, sent_z_block, cols_send.at[1])
            cols_copy(1, chunk, z_peer).start()
            for start, size in column_tiles(local_hidden):
                cut = slice(start, start + size)
                grad_act = dot(grad_low, w_down[:, cut])
                for which in range(2):
                    low = (grad_act * gate_up[which, chunk_rows(chunk), cut]).astype(LOW)
                    grads_low[which, chunk_rows(chunk), cut] = low
                    gate_up[which, chunk_rows(chunk), cut] = low.astype(FULL)
            pair_copy(0, chunk).start()
            grad_gate = grads_low[0, chunk_rows(chunk), :]
            grad_up = grads_low[1, chunk_rows(chunk), :]
            for side in range(2):
                for start, size in column_tiles(width // 2, 256):
                    cut = slice(side * (width // 2) + start, side * (width // 2) + start + size)
                    parts[chunk, side, :, start : start + size] = dot_nt(grad_gate, w_gate[cut, :]) + dot_nt(
                        grad_up, w_up[cut, :]
                    )
            core_copy(2, chunk).start()
            for copy in stores:
                copy.wait()
            send_part(2, chunk)

        every_chunk(feed_backward)

    pl.run_scoped(
        first_scope,
        pltpu.VMEM((width, local_hidden), LOW),
        pltpu.VMEM((width, local_hidden), LOW),
        pltpu.VMEM((width, local_hidden), LOW),
        pltpu.VMEM((rows, width), LOW),
    )

    def second_scope(theirs, cols_theirs, att_theirs, send_b, stage, att_send, grad_att, grad_one_own, sums_up, sums_down):
        def norm_backward(chunk):
            loads = load_all(((xhat_park.at[chunk], xbuf), (grad_two_park.at[chunk], gbuf)))
            branch = take_part(2, chunk)
            for copy in loads:
                copy.wait()
            grad_hidden = alpha * gbuf[...] + branch
            xhat = xbuf[...]
            vectors[0:1, :] += jnp.sum(grad_hidden * xhat, axis=0, keepdims=True)
            vectors[1:2, :] += jnp.sum(grad_hidden, axis=0, keepdims=True)
            grad_x = grad_hidden * norms[0:1, :]
            grad_one = (grad_x - row_mean(grad_x) - xhat * row_mean(grad_x * xhat)) * rstd_one[chunk]
            put_blocks(grad_one)
            for place in range(2):
                grad_one_own[chunk_rows(chunk), place * block : (place + 1) * block] = blocks[2 * mp + place]
            grad_low = grad_one.astype(LOW)
            put_blocks(grad_low.astype(FULL))
            keep_columns(2, chunk, own_pair_blocks, sent_pair_block, cols_send.at[1])
            grad_mixed = dot(grad_low, w_dense[...]).astype(LOW)
            for place in range(heads_here):
                grad_att[place, chunk_rows(chunk), :] = grad_mixed[:, place * HD : (place + 1) * HD]

        def fetch_columns(kind):
            forward = forward_copy(kind)
            forward.start()
            forward.wait()
            for pair in range(2):
                moved(
                    [(r_cols.at[kind, 2 * pair + place], blocks.at[pl.ds(CHUNKS * place, CHUNKS)]) for place in range(2)]
                )
                for place in range(2):
                    for chunk in range(CHUNKS):
                        cols_theirs[min(kind, 1), 2 * pair + place, :, chunk * rows : (chunk + 1) * rows] = blocks[
                            CHUNKS * place + chunk
                        ].T.astype(LOW)

        def fetch_rows(source, target):
            size = stage.shape[1]
            moved([(source.at[pl.ds(size * place, size)], stage.at[place]) for place in range(2)])
            for place in range(2):
                target[size * place : size * (place + 1), :] = stage[place].astype(LOW)

        def outer_product(target, kind, place, own, other):
            left, left_theirs = cols_own[min(kind, 1), place], cols_theirs[min(kind, 1), place]
            for start, size in column_tiles(own.shape[-1]):
                cut = slice(start, start + size)
                target[:, cut] = dot(left, own[:, cut]) + dot(left_theirs, other[:, cut])

        def down_products():
            for chunk in range(CHUNKS):
                act_copy(chunk).wait()
                cols_copy(1, chunk, z_peer).wait()
            fetch_columns(1)
            fetch_rows(r_act, theirs.at[0])
            homes = [send_a.at[0], send_a.at[1], send_b.at[0], send_b.at[1]]
            copies = []
            for place in range(LINE):
                outer_product(homes[place], 1, place, act_low, theirs.at[0])
                copies.append(pltpu.make_async_copy(homes[place], dnx.at[place], load_sem.at[place]))
                copies[-1].start()
            for copy in copies:
                copy.wait()
            for place in range(2):
                down_pair_copy(place).start()

        def down_pair_copy(place):
            return remote(dnx.at[2 * place + 1 - y], r_dny.at[place], dny_s.at[place], dny_r.at[place], y_peer)

        def down_line_copy(place):
            goal = 2 * half + place
            slot = jnp.where(((z == 2) & (goal == 1)) | ((z == 3) & (goal == 2)), 1, 0)
            return goal != z, remote(
                dnv.at[place], r_dnz.at[slot], dnz_s.at[place], dnz_r.at[slot], at(z_to=goal)
            )

        def down_sums():
            for place in range(2):
                down_pair_copy(place).wait()
                moved([(dnx.at[2 * place + y], stage.at[0]), (r_dny.at[place], stage.at[1])])
                stage[0] = stage[0] + stage[1]
                moved([(stage.at[0], dnv.at[place])])
                leaves, copy = down_line_copy(place)
                pl.when(leaves)(copy.start)

        def down_landed(slot):
            return remote(dnv.at[0], r_dnz.at[slot], dnz_s.at[0], dnz_r.at[slot], core_peer)

        def down_end():
            @pl.when((z == 0) | (z == LINE - 1))
            def _():
                down_landed(0).wait_recv()
                moved([(dnv.at[half], stage.at[0]), (r_dnz.at[0], stage.at[1])])

            @pl.when((z > 0) & (z < LINE - 1))
            def _():
                down_landed(0).wait_recv()
                down_landed(1).wait_recv()
                moved([(r_dnz.at[0], stage.at[0]), (r_dnz.at[1], stage.at[1])])

            stage[0] = stage[0] + stage[1]
            moved([(stage.at[0], out_down)])
            for place in range(2):
                leaves, copy = down_line_copy(place)
                pl.when(leaves)(copy.wait_send)

        sent = {0: [], 1: []}

        def line_terms(kind):
            if kind < 2:
                return 0, grads_low.at[kind], theirs.at[1 + kind], out_gate if kind == 0 else out_up, local_hidden
            return 2, att_low, att_theirs, out_dense, att_low.shape[1]

        def line_land(kind, slot, way):
            return r_rs.at[kind, slot - 1, way] if kind < 2 else r_rsd.at[slot - 1, way]

        def cut_to(ref, size):
            return ref if size == ref.shape[-1] else ref.at[:, pl.ds(0, size)]

        def line_copy(kind, slot, way, home):
            size = line_terms(kind)[4]
            goal = jnp.clip(z + 1 - 2 * way, 0, LINE - 1)
            return remote(
                cut_to(home, size), line_land(kind, slot, way), rs_s.at[kind, slot - 1, way],
                rs_r.at[kind, slot - 1, way], at(z_to=goal),
            )

        def line_slot(kind, slot):
            column_kind, own, other, _, size = line_terms(kind)
            for way in range(2):
                home = (send_a, send_b)[way].at[len(sent[way]) % 2]
                if len(sent[way]) >= 2:
                    active, copy = sent[way][-2]
                    pl.when(active)(copy.wait_send)
                active = z < slot if way == 0 else z > LINE - 1 - slot
                inner = z > 0 if way == 0 else z < LINE - 1
                copy = line_copy(kind, slot, way, home)
                sent[way].append((active, copy))

                @pl.when(active)
                def _():
                    place = LINE - slot + z if way == 0 else slot - LINE + z
                    target = cut_to(home, size)
                    outer_product(target, column_kind, place, own, other)
                    if slot > 1:

                        @pl.when(inner)
                        def _():
                            line_copy(kind, slot - 1, way, home).wait_recv()
                            arrived = cut_to(stage.at[way], size)
                            moved([(line_land(kind, slot - 1, way), arrived)])
                            target[...] = target[...] + arrived[...]

                    copy.start()

        def line_end(kind):
            column_kind, own, other, result, size = line_terms(kind)
            total, arrived = cut_to(stage.at[0], size), cut_to(stage.at[1], size)
            outer_product(total, column_kind, z, own, other)
            for way in range(2):

                @pl.when(z > 0 if way == 0 else z < LINE - 1)
                def _():
                    line_copy(kind, LINE - 1, way, send_a.at[0]).wait_recv()
                    moved([(line_land(kind, LINE - 1, way), arrived)])
                    total[...] = total[...] + arrived[...]

            moved([(total, result)])

        def attention_backward(place, carried):
            queries, keys, values = heads[0, place], heads[1, place], heads[2, place]
            grad_mixed = grad_att[place]
            probability = probabilities(queries, keys)
            grad_prob = dot_nt(grad_mixed, values)
            centre = jnp.sum(grad_prob * probability, axis=-1, keepdims=True)
            grad_scores = (probability * (grad_prob - centre)).astype(LOW)
            grad_queries = dot(grad_scores, keys) * score_scale
            grad_keys = dot_tn(grad_scores, queries) * score_scale
            grad_values = dot_tn(probability.astype(LOW), grad_mixed)
            vocab = emb.shape[0]
            named = lax.broadcasted_iota(jnp.int32, (vocab, length), 0) == ids_row[...]
            hot_t = jnp.where(named, 1.0, 0.0).astype(LOW)
            inner = heads_here * HD
            sums[0, 0:vocab, head_lanes(place)] = dot(hot_t, turn_by(grad_queries, -sin_ref[...]).astype(LOW))
            sums[0, 0:vocab, head_lanes(place, inner)] = dot(hot_t, turn_by(grad_keys, -sin_ref[...]).astype(LOW))
            sums[1, 0:vocab, head_lanes(place)] = dot(hot_t, grad_values.astype(LOW))
            return carried

        def small_sums():
            lax.fori_loop(0, heads_here, attention_backward, 0)
            vocab = emb.shape[0]
            named = lax.broadcasted_iota(jnp.int32, (vocab, length), 0) == ids_row[...]
            hot_t = jnp.where(named, 1.0, 0.0).astype(LOW)
            high, rest = split_low(grad_one_own[...])
            sums[1, 0:vocab, heads_here * HD :] = dot(hot_t, high) + dot(hot_t, rest)
            for side in range(2):
                sums[side, vocab:, :] = vectors[:, side * (width // 2) : (side + 1) * (width // 2)]
            sums_pair().start()

        def sums_pair():
            return remote(sums.at[1 - y], sums_y, sums_s.at[0], sums_r.at[0], y_peer)

        def sums_line(way):
            source, target = ((sums_up, sums_below), (sums_down, sums_above))[way]
            goal = jnp.clip(z + 1 - 2 * way, 0, LINE - 1)
            return remote(source, target, sums_s.at[1 + way], sums_r.at[1 + way], at(z_to=goal))

        def sums_back():
            return remote(sums.at[y], sums_other, sums_s.at[3], sums_r.at[3], y_peer)

        def sums_first():
            sums_pair().wait()
            sums[y] = sums[y] + sums_y[...]

            @pl.when(z == 0)
            def _():
                sums_up[...] = sums[y]
                sums_line(0).start()

            @pl.when(z == LINE - 1)
            def _():
                sums_down[...] = sums[y]
                sums_line(1).start()

        def sums_middle():
            @pl.when(z > 0)
            def _():
                sums_line(0).wait_recv()

            @pl.when((z > 0) & (z < LINE - 1))
            def _():
                sums_up[...] = sums[y] + sums_below[...]
                sums_line(0).start()

            @pl.when(z < LINE - 1)
            def _():
                sums_line(1).wait_recv()

            @pl.when((z > 0) & (z < LINE - 1))
            def _():
                sums_down[...] = sums[y] + sums_above[...]
                sums_line(1).start()

            @pl.when(z > 0)
            def _():
                sums[y] = sums[y] + sums_below[...]

            @pl.when(z < LINE - 1)
            def _():
                sums[y] = sums[y] + sums_above[...]

            sums_back().start()

        def sums_end():
            sums_back().wait()
            pl.when(z < LINE - 1)(sums_line(0).wait_send)
            pl.when(z > 0)(sums_line(1).wait_send)
            moved([(sums.at[y], out_sums.at[y]), (sums_other, out_sums.at[1 - y])])

        def rows_copy():
            return remote(att_send, r_att, att_s, att_r, y_peer)

        down_products()
        norm_backward(0)
        norm_backward(1)
        for chunk in range(CHUNKS):
            cols_copy(0, chunk, y_peer).wait()
        fetch_columns(0)
        for chunk in range(CHUNKS):
            pair_copy(0, chunk).wait()
        fetch_rows(r_y.at[0], theirs.at[1])
        line_slot(0, 1)
        for chunk in range(CHUNKS):
            pair_copy(1, chunk).start()
        norm_backward(2)
        norm_backward(3)
        for chunk in range(CHUNKS):
            cols_copy(2, chunk, y_peer).start()
        att_send[...] = att_low[...].astype(FULL)
        rows_copy().start()
        line_slot(0, 2)
        small_sums()
        line_slot(0, 3)
        sums_first()
        for chunk in range(CHUNKS):
            pair_copy(1, chunk).wait()
        fetch_rows(r_y.at[1], theirs.at[2])
        line_slot(1, 1)
        sums_middle()
        line_end(0)
        line_slot(1, 2)
        down_sums()
        line_slot(1, 3)
        for chunk in range(CHUNKS):
            cols_copy(2, chunk, y_peer).wait()
        fetch_columns(2)
        rows_copy().wait()
        moved([(r_att, att_send)])
        att_theirs[...] = att_send[...].astype(LOW)
        line_slot(2, 1)
        line_slot(2, 2)
        line_end(1)
        line_slot(2, 3)
        sums_end()
        down_end()
        line_end(2)
        for way in range(2):
            for active, copy in sent[way][-2:]:
                pl.when(active)(copy.wait_send)

    shard = width // (2 * LINE)
    pl.run_scoped(
        second_scope,
        pltpu.VMEM((3, length, local_hidden), LOW),
        pltpu.VMEM((2, LINE, block, length), LOW),
        pltpu.VMEM(att_low.shape, LOW),
        pltpu.VMEM((2, shard, local_hidden), FULL),
        pltpu.VMEM((2, shard, local_hidden), FULL),
        pltpu.VMEM(att_low.shape, FULL),
        pltpu.VMEM((heads_here, length, HD), LOW),
        pltpu.VMEM((length, 2 * block), FULL),
        pltpu.VMEM(sums_y.shape, FULL),
        pltpu.VMEM(sums_y.shape, FULL),
    )


def local_fast(
    token_ids,
    prefix_lengths,
    cluster_ids,
    embedding,
    w_query,
    w_key,
    w_value,
    w_dense,
    w_gate,
    w_up,
    w_down,
    norm1_gain,
    norm1_bias,
    norm2_gain,
    norm2_bias,
    cotangent,
):
    length = token_ids.shape[0]
    vocab, width = embedding.shape
    inner = w_query.shape[1]
    heads_here = inner // HD
    local_hidden = w_gate.shape[1]
    rows = length // CHUNKS
    block = width // (2 * LINE)
    dp, mp = lax.axis_index("dp"), lax.axis_index("mp")
    own_cluster = cluster_ids[dp]
    seq_weight = 1.0 / jnp.sum((cluster_ids == own_cluster).astype(FULL))
    tables = [
        dot(embedding, weight).reshape(vocab, heads_here, HD).transpose(1, 0, 2)
        for weight in (w_query, w_key, w_value)
    ]
    cosine, sine = rotary_tables(length, HD)
    cosine = jnp.concatenate([cosine, cosine], axis=1)
    sine = jnp.concatenate([-sine, sine], axis=1)
    norms = jnp.stack([norm1_gain, norm1_bias, norm2_gain, norm2_bias])

    hbm = pl.BlockSpec(memory_space=pl.ANY)
    vmem = pl.BlockSpec(memory_space=pltpu.VMEM)
    sums_rows = vocab + 8
    shapes = [
        ((length, width), LOW),
        ((block, local_hidden), FULL),
        ((block, local_hidden), FULL),
        ((block, local_hidden), FULL),
        ((block, inner), FULL),
        ((2, sums_rows, width // 2), FULL),
        ((length, local_hidden), FULL),
        ((2, length, local_hidden), FULL),
        ((3, LINE, CHUNKS, rows, block), FULL),
        ((length, inner), FULL),
        ((CHUNKS, rows, width), FULL),
        ((CHUNKS, rows, width), FULL),
        ((LINE, block, local_hidden), FULL),
        ((2, block, local_hidden), FULL),
        ((2, block, local_hidden), FULL),
        ((2, block, local_hidden), FULL),
        ((2, LINE - 1, 2, block, local_hidden), FULL),
        ((LINE - 1, 2, block, inner), FULL),
    ]
    scratch = [
        ((CHUNKS, 2, rows, width // 2), FULL),
        ((CHUNKS, rows, width // 2), FULL),
        ((2, CHUNKS, rows, width // 2), FULL),
        ((CHUNKS, rows, width // 2), FULL),
        ((2 * LINE, rows, block), FULL),
        ((rows, width), FULL),
        ((rows, width), FULL),
        ((rows, width), LOW),
        ((2, length, local_hidden), FULL),
        ((2, length, local_hidden), LOW),
        ((length, local_hidden), LOW),
        ((2, block, local_hidden), FULL),
        ((2, LINE, block, length), LOW),
        ((2, 2, CHUNKS, rows, block), FULL),
        ((length, inner), LOW),
        ((3, heads_here, length, HD), LOW),
        ((width, inner), LOW),
        ((length, vocab), LOW),
        ((CHUNKS, rows, 1), FULL),
        ((8, width), FULL),
        ((2, sums_rows, width // 2), FULL),
        ((sums_rows, width // 2), FULL),
        ((sums_rows, width // 2), FULL),
        ((sums_rows, width // 2), FULL),
        ((sums_rows, width // 2), FULL),
    ]
    dma = pltpu.SemaphoreType.DMA
    semaphores = [
        (3, CHUNKS), (3, CHUNKS), (3, CHUNKS), (3, CHUNKS), (3, CHUNKS), (3, CHUNKS), (CHUNKS,), (CHUNKS,),
        (3, CHUNKS), (3, CHUNKS), (3,), (3,), (2, CHUNKS), (2, CHUNKS), (1,), (1,),
        None, None, (2,), (2,), (2,), (2,), (3, LINE - 1, 2), (3, LINE - 1, 2), (4,), (4,), (4,), (4,),
    ]
    results = pl.pallas_call(
        functools.partial(layer_kernel, length, width, local_hidden),
        out_shape=[jax.ShapeDtypeStruct(shape, dtype) for shape, dtype in shapes],
        in_specs=[pl.BlockSpec(memory_space=pltpu.SMEM)] + [vmem] * 8 + [hbm] * 5,
        out_specs=[hbm] * len(shapes),
        scratch_shapes=[pltpu.VMEM(shape, dtype) for shape, dtype in scratch]
        + [dma if shape is None else dma(shape) for shape in semaphores],
        compiler_params=pltpu.CompilerParams(
            collective_id=0, has_side_effects=True, vmem_limit_bytes=62 * 2**20
        ),
    )(
        prefix_lengths,
        seq_weight.reshape(1, 1),
        token_ids.reshape(length, 1),
        token_ids.reshape(1, length),
        embedding,
        jnp.concatenate(tables, axis=0),
        cosine,
        sine,
        norms,
        w_dense,
        w_gate,
        w_up,
        w_down,
        cotangent,
    )
    block_out, out_gate, out_up, out_down, out_dense, sums = results[:6]
    sums = jnp.concatenate([sums[0], sums[1]], axis=1)
    own_columns = lax.dynamic_slice_in_dim(embedding, dp * block, block, 1).astype(FULL)
    by_token = [sums[:vocab, kind * inner : (kind + 1) * inner] for kind in range(3)]
    out_lin = [
        lax.dot_general(
            own_columns, part, (((0,), (0,)), ((), ())), precision=highest, preferred_element_type=FULL
        )
        for part in by_token
    ]
    table_rows = vocab // (2 * LINE)
    mine = lax.dynamic_slice_in_dim(sums, dp * table_rows, table_rows, 0)
    high = lax.reduce_precision(mine, 8, 7)
    pieces = jnp.concatenate([high, mine - high], axis=0).astype(LOW)
    table = sum(
        dot_nt(pieces[:, kind * inner : (kind + 1) * inner], weight)
        for kind, weight in enumerate((w_query, w_key, w_value))
    )
    table = table[:table_rows] + table[table_rows:]
    quarter = lax.dynamic_slice_in_dim(table, mp * inner, inner, 1) + deep_alpha * mine[:, 3 * inner :]
    table = lax.psum(lax.dynamic_update_slice_in_dim(table, quarter, mp * inner, 1), "mp")
    norm_rows = lax.dynamic_slice_in_dim(sums[vocab : vocab + 4], dp * block, block, 1)
    return (
        block_out,
        0.1 * table,
        out_lin[0],
        out_lin[1],
        out_lin[2],
        out_dense,
        out_gate,
        out_up,
        out_down,
        norm_rows[0],
        norm_rows[1],
        norm_rows[2],
        norm_rows[3],
    )


def solution(mesh):
    fast = mesh.shape["dp"] == 2 * LINE and mesh.shape["mp"] == 4
    return jax.shard_map(
        local_fast if fast else local_general,
        mesh=mesh,
        in_specs=(
            P("dp"),
            P("dp"),
            P(),
            P(),
            P(None, "mp"),
            P(None, "mp"),
            P(None, "mp"),
            P(None, "mp"),
            P(None, "mp"),
            P(None, "mp"),
            P(None, "mp"),
            P(),
            P(),
            P(),
            P(),
            P("dp", None),
        ),
        out_specs=(
            P("dp", None),
            P("dp", None),
            P("dp", "mp"),
            P("dp", "mp"),
            P("dp", "mp"),
            P("dp", "mp"),
            P("dp", "mp"),
            P("dp", "mp"),
            P("dp", "mp"),
            P("dp"),
            P("dp"),
            P("dp"),
            P("dp"),
        ),
        check_vma=False,
    )
```

```python
import functools
import math

import jax
import jax.numpy as jnp
import numpy as np
from jax import lax
from jax.experimental import pallas as pl
from jax.experimental.pallas import tpu as pltpu
from jax.sharding import PartitionSpec as P

HD = 128
FF_USED = 5461


deep_alpha = math.sqrt(48.0)
norm_eps = 1e-05
highest = lax.Precision.HIGHEST


def layer_norm(inputs, norm_gain, norm_bias):
    center = jnp.mean(inputs, axis=-1, keepdims=True)
    centered = inputs - center
    spread = jnp.mean(centered * centered, axis=-1, keepdims=True)
    return centered * lax.rsqrt(spread + norm_eps) * norm_gain + norm_bias


def rotary_tables(length, head_width):
    half_width = head_width // 2
    frequency = jnp.exp(
        jnp.arange(half_width, dtype=jnp.float32) * (-2.0 * math.log(10000.0) / head_width)
    )
    angles = jnp.arange(length, dtype=jnp.float32)[:, None] * frequency[None, :]
    return (jnp.cos(angles), jnp.sin(angles))


def rotate(inputs, cosine, sine):
    half_width = inputs.shape[-1] // 2
    first = inputs[..., :half_width]
    second = inputs[..., half_width:]
    cosine = cosine[:, None, :]
    sine = sine[:, None, :]
    return jnp.concatenate(
        [first * cosine - second * sine, second * cosine + first * sine], axis=-1
    )


def row_mask(row_begin, row_count, length, prefix):
    columns = jnp.arange(length, dtype=jnp.int32)
    row_index = row_begin + jnp.arange(row_count, dtype=jnp.int32)
    return (columns[None, :] < prefix) | (columns[None, :] <= row_index[:, None])


def block_scores(query_block, keys_rot, visible, score_scale):
    scores = (
        jnp.einsum("bhd,khd->hbk", query_block, keys_rot, preferred_element_type=jnp.float32)
        * score_scale
    )
    return jnp.where(visible[None, :, :], scores, -1e30)


def attention_forward(queries, keys_rot, values_in, prefix, row_block):
    length = queries.shape[0]
    score_scale = 1.0 / math.sqrt(HD)

    def one_block(row_begin):
        scores = block_scores(
            queries, keys_rot, row_mask(row_begin, row_block, length, prefix), score_scale
        )
        row_max = jnp.max(scores, axis=-1, keepdims=True)
        weights = jnp.exp(scores - row_max)
        total_weight = jnp.sum(weights, axis=-1, keepdims=True)
        probability = (weights / total_weight).astype(jnp.bfloat16)
        mixed_block = jnp.einsum(
            "hbk,khd->bhd", probability, values_in, preferred_element_type=jnp.float32
        )
        return (mixed_block, row_max + jnp.log(total_weight))

    starts = jnp.arange(length // row_block, dtype=jnp.int32) * row_block
    attended, log_total = lax.map(one_block, starts)
    return (attended.reshape(length, -1), log_total)


def attention_backward(queries, keys_rot, values_in, prefix, row_block, log_total, grad_mixed):
    length = queries.shape[0]
    score_scale = 1.0 / math.sqrt(HD)

    def one_block(carried, inputs):
        grad_keys, grad_values = carried
        row_begin, block_total = inputs
        scores = block_scores(
            queries, keys_rot, row_mask(row_begin, row_block, length, prefix), score_scale
        )
        probability = jnp.exp(scores - block_total)
        prob_low = probability.astype(jnp.bfloat16)
        grad_prob = jnp.einsum(
            "bhd,khd->hbk", grad_mixed, values_in, preferred_element_type=jnp.float32
        )
        centre = jnp.sum(grad_prob * probability, axis=-1, keepdims=True)
        grad_scores = (probability * (grad_prob - centre)).astype(jnp.bfloat16)
        grad_query = (
            jnp.einsum("hbk,khd->bhd", grad_scores, keys_rot, preferred_element_type=jnp.float32)
            * score_scale
        )
        grad_keys = (
            grad_keys
            + jnp.einsum("hbk,bhd->khd", grad_scores, queries, preferred_element_type=jnp.float32)
            * score_scale
        )
        grad_values = grad_values + jnp.einsum(
            "hbk,bhd->khd", prob_low, grad_mixed, preferred_element_type=jnp.float32
        )
        return ((grad_keys, grad_values), grad_query)

    starts = jnp.arange(length // row_block, dtype=jnp.int32) * row_block
    zeros_kv = jnp.zeros(keys_rot.shape, jnp.float32)
    (grad_keys, grad_values), grad_queries = lax.scan(
        one_block, (zeros_kv, zeros_kv), (starts, log_total)
    )
    return (grad_queries.reshape(queries.shape), grad_keys, grad_values)


def local_general(
    token_ids,
    prefix_lengths,
    cluster_ids,
    embedding,
    w_query,
    w_key,
    w_value,
    w_dense,
    w_gate,
    w_up,
    w_down,
    norm1_gain,
    norm1_bias,
    norm2_gain,
    norm2_bias,
    cotangent,
):
    length = token_ids.shape[0]
    vocab_rows = embedding.shape[0]
    row_block = min(512, length)
    local_heads = w_query.shape[1] // HD
    local_hidden = w_gate.shape[1]
    one_hot = (token_ids[:, None] == jnp.arange(vocab_rows, dtype=jnp.int32)[None, :]).astype(
        jnp.bfloat16
    )
    embedded_low = jnp.dot(one_hot, embedding, preferred_element_type=jnp.float32).astype(
        jnp.bfloat16
    )
    embedded = embedded_low.astype(jnp.float32)
    cosine, sine = rotary_tables(length, HD)
    prefix = prefix_lengths[0]
    own_cluster = cluster_ids[lax.axis_index("dp")]
    seq_weight = 1.0 / jnp.sum((cluster_ids == own_cluster).astype(jnp.float32))

    def project(weight_in):
        return jnp.dot(embedded_low, weight_in, preferred_element_type=jnp.float32).reshape(
            length, local_heads, HD
        )

    queries = rotate(project(w_query), cosine, sine).astype(jnp.bfloat16)
    keys_rot = rotate(project(w_key), cosine, sine).astype(jnp.bfloat16)
    values_in = project(w_value).astype(jnp.bfloat16)
    attended, log_total = attention_forward(queries, keys_rot, values_in, prefix, row_block)
    attended_low = attended.astype(jnp.bfloat16)
    branch = lax.psum(
        jnp.einsum("lh,dh->ld", attended_low, w_dense, preferred_element_type=jnp.float32), "mp"
    )
    residual_one = deep_alpha * embedded + branch
    hidden, norm_one_pull = jax.vjp(layer_norm, residual_one, norm1_gain, norm1_bias)
    hidden_low = hidden.astype(jnp.bfloat16)
    gate_proj = jnp.dot(hidden_low, w_gate, preferred_element_type=jnp.float32)
    up_proj = jnp.dot(hidden_low, w_up, preferred_element_type=jnp.float32)
    unit_index = lax.axis_index("mp") * local_hidden + jnp.arange(local_hidden, dtype=jnp.int32)
    used_mask = (unit_index < FF_USED).astype(jnp.float32)

    def gated_unit(gate_in, up_in):
        return jax.nn.gelu(gate_in, approximate=True) * up_in * used_mask

    activation, gated_pull = jax.vjp(gated_unit, gate_proj, up_proj)
    activation_low = activation.astype(jnp.bfloat16)
    branch_two = lax.psum(
        jnp.einsum("lf,df->ld", activation_low, w_down, preferred_element_type=jnp.float32), "mp"
    )
    residual_two = deep_alpha * hidden + branch_two
    final, norm_two_pull = jax.vjp(layer_norm, residual_two, norm2_gain, norm2_bias)
    grad_out = cotangent.astype(jnp.float32) * seq_weight
    grad_two, grad_gain_two, grad_bias_two = norm_two_pull(grad_out)
    grad_branch_two = grad_two.astype(jnp.bfloat16)
    grad_w_down = jnp.einsum(
        "ld,lf->df", grad_branch_two, activation_low, preferred_element_type=jnp.float32
    )
    grad_act = jnp.dot(grad_branch_two, w_down, preferred_element_type=jnp.float32)
    grad_gate, grad_up = gated_pull(grad_act)
    grad_gate_low = grad_gate.astype(jnp.bfloat16)
    grad_up_low = grad_up.astype(jnp.bfloat16)
    grad_w_gate = jnp.einsum(
        "ld,lf->df", hidden_low, grad_gate_low, preferred_element_type=jnp.float32
    )
    grad_w_up = jnp.einsum("ld,lf->df", hidden_low, grad_up_low, preferred_element_type=jnp.float32)
    hidden_part = jnp.einsum(
        "lf,df->ld", grad_gate_low, w_gate, preferred_element_type=jnp.float32
    ) + jnp.einsum("lf,df->ld", grad_up_low, w_up, preferred_element_type=jnp.float32)
    grad_hidden = deep_alpha * grad_two + lax.psum(hidden_part, "mp")
    feed_sums = (
        lax.psum_scatter(grad_w_gate, "dp", scatter_dimension=0, tiled=True),
        lax.psum_scatter(grad_w_up, "dp", scatter_dimension=0, tiled=True),
        lax.psum_scatter(grad_w_down, "dp", scatter_dimension=0, tiled=True),
        lax.psum_scatter(grad_gain_two, "dp", scatter_dimension=0, tiled=True),
        lax.psum_scatter(grad_bias_two, "dp", scatter_dimension=0, tiled=True),
    )
    grad_one, grad_gain_one, grad_bias_one = norm_one_pull(grad_hidden)
    grad_branch = grad_one.astype(jnp.bfloat16)
    grad_w_dense = jnp.einsum(
        "ld,lh->dh", grad_branch, attended_low, preferred_element_type=jnp.float32
    )
    grad_attended = jnp.dot(grad_branch, w_dense, preferred_element_type=jnp.float32).astype(
        jnp.bfloat16
    )
    grad_attended = grad_attended.reshape(length, local_heads, HD)
    grad_queries, grad_keys, grad_values = attention_backward(
        queries, keys_rot, values_in, prefix, row_block, log_total, grad_attended
    )
    grad_query_lin = rotate(grad_queries, cosine, -sine).astype(jnp.bfloat16).reshape(length, -1)
    grad_key_lin = rotate(grad_keys, cosine, -sine).astype(jnp.bfloat16).reshape(length, -1)
    grad_value_lin = grad_values.astype(jnp.bfloat16).reshape(length, -1)
    grad_w_query = jnp.einsum(
        "ld,lh->dh", embedded_low, grad_query_lin, preferred_element_type=jnp.float32
    )
    grad_w_key = jnp.einsum(
        "ld,lh->dh", embedded_low, grad_key_lin, preferred_element_type=jnp.float32
    )
    grad_w_value = jnp.einsum(
        "ld,lh->dh", embedded_low, grad_value_lin, preferred_element_type=jnp.float32
    )
    input_part = (
        jnp.einsum("lh,dh->ld", grad_query_lin, w_query, preferred_element_type=jnp.float32)
        + jnp.einsum("lh,dh->ld", grad_key_lin, w_key, preferred_element_type=jnp.float32)
        + jnp.einsum("lh,dh->ld", grad_value_lin, w_value, preferred_element_type=jnp.float32)
    )
    grad_embedded = deep_alpha * grad_one + lax.psum(input_part, "mp")
    grad_table = 0.1 * jnp.dot(one_hot.astype(jnp.float32).T, grad_embedded, precision=highest)
    attn_sums = (
        lax.psum_scatter(grad_table, "dp", scatter_dimension=0, tiled=True),
        lax.psum_scatter(grad_w_query, "dp", scatter_dimension=0, tiled=True),
        lax.psum_scatter(grad_w_key, "dp", scatter_dimension=0, tiled=True),
        lax.psum_scatter(grad_w_value, "dp", scatter_dimension=0, tiled=True),
        lax.psum_scatter(grad_w_dense, "dp", scatter_dimension=0, tiled=True),
        lax.psum_scatter(grad_gain_one, "dp", scatter_dimension=0, tiled=True),
        lax.psum_scatter(grad_bias_one, "dp", scatter_dimension=0, tiled=True),
    )
    summed = (
        attn_sums[0],
        attn_sums[1],
        attn_sums[2],
        attn_sums[3],
        attn_sums[4],
        feed_sums[0],
        feed_sums[1],
        feed_sums[2],
        attn_sums[5],
        attn_sums[6],
        feed_sums[3],
        feed_sums[4],
    )
    return (
        final.astype(jnp.bfloat16),
        summed[0],
        summed[1],
        summed[2],
        summed[3],
        summed[4],
        summed[5],
        summed[6],
        summed[7],
        summed[8],
        summed[9],
        summed[10],
        summed[11],
    )


LINE = 4
MESH = pl.DeviceIdType.MESH
CHUNKS = 4
LOW = jnp.bfloat16
FULL = jnp.float32
TANH_SCALE = math.sqrt(2.0 / math.pi)


def dot(left, right):
    return jnp.dot(left, right, preferred_element_type=FULL)


def dot_nt(left, right):
    return lax.dot_general(left, right, (((1,), (1,)), ((), ())), preferred_element_type=FULL)


def dot_tn(left, right):
    return lax.dot_general(left, right, (((0,), (0,)), ((), ())), preferred_element_type=FULL)


def split_low(value):
    high = value.astype(LOW)
    return high, (value - high.astype(FULL)).astype(LOW)


def row_mean(value):
    return jnp.mean(value, axis=-1, keepdims=True)


def column_tiles(width, tile=512):
    return [(start, min(tile, width - start)) for start in range(0, width, tile)]


def layer_kernel(
    length, width, local_hidden,
    prefix_ref, cluster_ref, ids_row, emb, cos_ref, sin_ref, norms, w_query_hbm, w_key_hbm, w_value_hbm, w_dense_hbm,
    w_gate_hbm, w_up_hbm, w_down_hbm, cot_hbm,
    block_out, out_table, out_query, out_key, out_value, out_dense, out_gate, out_up, out_down, out_norms,
    r_act, r_two, r_y, r_cols, r_att, xhat_park, grad_two_park, r_dny, r_rs, r_rsd, r_sums,
    parts, core_in, x_in, back_in, blocks, xbuf, gbuf, obuf, gate_up, grads_low, act_low, send_a, cols_own, cols_send,
    two_own, two_send, att_low, att_turned, heads, w_dense, one_hot, hot_turned, rstd_one, vectors, table_core, table_x,
    core_s, core_r, x_s, x_r, back_s, back_r, act_s, act_r, two_s, two_r, fwd_two_s, fwd_two_r, cols_s, cols_r, fwd_s,
    fwd_r, ys_s, ys_r, att_s, att_r, dny_s, dny_r, rs_s, rs_r, sums_s, sums_r, table_s, table_r, load_sem, weight_sem,
):
    dp, mp = lax.axis_index("dp"), lax.axis_index("mp")
    z, y = lax.div(dp, 2), lax.rem(dp, 2)
    x, core = lax.div(mp, 2), lax.rem(mp, 2)
    rows = length // CHUNKS
    heads_here = heads.shape[1]
    inner = heads_here * HD
    vocab = emb.shape[0]
    shift = (local_hidden + 15) // 16 * 16
    block = width // (2 * LINE)
    alpha = jnp.float32(deep_alpha)

    def at(z_to=None, y_to=None, x_to=None, core_to=None):
        z_to = z if z_to is None else z_to
        y_to = y if y_to is None else y_to
        x_to = x if x_to is None else x_to
        core_to = core if core_to is None else core_to
        return (2 * z_to + y_to, 2 * x_to + core_to)

    core_peer = at(core_to=1 - core)
    x_peer = at(x_to=1 - x)
    y_peer = at(y_to=1 - y)

    def remote(source, target, send, receive, device):
        return pltpu.make_async_remote_copy(
            src_ref=source, dst_ref=target, send_sem=send, recv_sem=receive,
            device_id=device, device_id_type=MESH,
        )

    def load_all(pairs):
        copies = [
            pltpu.make_async_copy(source, target, load_sem.at[place])
            for place, (source, target) in enumerate(pairs)
        ]
        for copy in copies:
            copy.start()
        return copies

    def moved(pairs):
        for copy in load_all(pairs):
            copy.wait()

    barrier = pltpu.get_barrier_semaphore()
    greeted = [core_peer, x_peer, y_peer] + [at(z_to=lax.rem(z + step, LINE)) for step in range(1, LINE)]
    for device in greeted:
        pl.semaphore_signal(barrier, inc=1, device_id=device, device_id_type=MESH)

    def chunk_rows(chunk):
        return pl.ds(pl.multiple_of(chunk * rows, rows), rows)

    def core_copy(turn, chunk):
        return remote(
            parts.at[chunk, 1 - core], core_in.at[chunk], core_s.at[turn, chunk], core_r.at[turn, chunk], core_peer
        )

    def x_copy(turn, chunk):
        return remote(
            parts.at[chunk, core], x_in.at[turn % 2, chunk], x_s.at[turn, chunk], x_r.at[turn, chunk], x_peer
        )

    def back_copy(turn, chunk):
        return remote(
            parts.at[chunk, core], back_in.at[chunk], back_s.at[turn, chunk], back_r.at[turn, chunk], core_peer
        )

    def send_part(turn, chunk):
        core_copy(turn, chunk).wait()
        parts[chunk, core] = parts[chunk, core] + core_in[chunk]
        x_copy(turn, chunk).start()

    def take_part(turn, chunk):
        x_copy(turn, chunk).wait()
        parts[chunk, core] = parts[chunk, core] + x_in[turn % 2, chunk]
        back = back_copy(turn, chunk)
        back.start()
        mine = parts[chunk, core]
        back.wait()
        other = back_in[chunk]
        return jnp.concatenate([jnp.where(core == 0, mine, other), jnp.where(core == 0, other, mine)], axis=1)

    def put_blocks(value):
        for place in range(2 * LINE):
            blocks[place] = value[:, place * block : (place + 1) * block]

    def chunk_lanes(chunk):
        return pl.ds(pl.multiple_of(chunk * rows, rows), rows)

    def half_lanes(side):
        return pl.ds(pl.multiple_of(side * block, block), block)

    def keep_columns(own, chunk):
        for place in range(LINE):
            own[place, chunk_rows(chunk), :] = blocks[2 * place + y].astype(LOW)
        for place in range(2):
            cols_send[place, chunk] = blocks[2 * (2 * core + place) + 1 - y]

    def cols_copy(kind, chunk):
        return remote(
            cols_send.at[:, chunk], r_cols.at[kind, pl.ds(2 * core, 2), chunk],
            cols_s.at[kind, chunk], cols_r.at[kind, chunk], y_peer,
        )

    def forward_copy(kind):
        view = r_cols.at[kind, pl.ds(2 * core, 2)]
        return remote(view, view, fwd_s.at[kind], fwd_r.at[kind], core_peer)

    def act_copy(way, hop, chunk):
        goal = jnp.clip(z + 1 - 2 * way, 0, LINE - 1)
        owner = z - hop if way == 0 else z + hop
        active = (owner >= 0) & (z < LINE - 1) if way == 0 else (owner < LINE) & (z > 0)
        owner = jnp.clip(owner, 0, LINE - 1)
        landed = r_act.at[owner, :, chunk_lanes(chunk)]
        source = send_a.at[lax.div(chunk, 2), :, half_chunk(chunk)] if hop == 0 else landed
        return active, remote(
            source, landed, act_s.at[way, hop, chunk], act_r.at[way, hop, chunk], at(z_to=goal)
        )

    def act_landed(way, hop):
        return z - 1 - hop >= 0 if way == 0 else z + 1 + hop < LINE

    def half_chunk(chunk):
        return pl.ds(pl.multiple_of(lax.rem(chunk, 2) * rows, rows), rows)

    def act_send(hop, chunk):
        for way in range(2):
            active, copy = act_copy(way, hop, chunk)
            pl.when(active)(copy.start)

    def act_take(hop, chunk):
        for way in range(2):
            _, copy = act_copy(way, hop, chunk)
            pl.when(act_landed(way, hop))(copy.wait_recv)

    def two_copy(step, chunk):
        goal = lax.rem(z + step, LINE)
        return remote(
            two_send.at[goal, chunk], r_two.at[z, core, chunk],
            two_s.at[step - 1, chunk], two_r.at[step - 1, chunk], at(z_to=goal),
        )

    def two_forward(step):
        view = r_two.at[lax.rem(z + step, LINE), core]
        return remote(view, view, fwd_two_s.at[step - 1], fwd_two_r.at[step - 1], core_peer)

    def pair_copy(which, chunk):
        return remote(
            gate_up.at[which, :, chunk_lanes(chunk)], r_y.at[which, :, chunk_lanes(chunk)],
            ys_s.at[which, chunk], ys_r.at[which, chunk], y_peer,
        )

    def rows_copy():
        return remote(gbuf, r_att, att_s, att_r, y_peer)

    def every_chunk(body):
        lax.fori_loop(0, CHUNKS, lambda chunk, carried: (body(chunk), carried)[1], 0)

    column = lax.broadcasted_iota(jnp.int32, (length, length), 1)
    row = lax.broadcasted_iota(jnp.int32, (length, length), 0)
    score_scale = 1.0 / math.sqrt(HD)

    def probabilities(queries, keys):
        visible = (column < prefix_ref[0]) | (column <= row)
        scores = jnp.where(visible, dot_nt(queries, keys) * score_scale, -1e30)
        weights = jnp.exp(scores - jnp.max(scores, axis=-1, keepdims=True))
        return weights / jnp.sum(weights, axis=-1, keepdims=True)

    def turn_by(value, sine):
        return value * cos_ref[...] + pltpu.roll(value, HD // 2, 1) * sine

    def head_lanes(place, offset=0):
        return pl.ds(pl.multiple_of(offset + place * HD, HD), HD)

    def first_scope(w_heads, tab):
        loads = [
            pltpu.make_async_copy(source, target, weight_sem.at[place])
            for place, (source, target) in enumerate(
                (
                    (w_query_hbm, w_heads.at[0]),
                    (w_key_hbm, w_heads.at[1]),
                    (w_value_hbm, w_heads.at[2]),
                    (w_dense_hbm, w_dense),
                )
            )
        ]
        for copy in loads:
            copy.start()
        named = lax.broadcasted_iota(jnp.int32, (vocab, length), 0) == ids_row[...]
        hot = jnp.where(named, 1.0, 0.0)
        hot_turned[...] = hot.astype(LOW)
        one_hot[...] = hot.T.astype(LOW)
        vectors[...] = jnp.zeros_like(vectors)
        for kind in range(3):
            loads[kind].wait()
            table = dot(emb[...], w_heads[kind])
            for place in range(heads_here):
                tab[kind * heads_here + place] = table[:, place * HD : (place + 1) * HD]

        def attend_head(place, carried):
            hot = one_hot[...]
            lin = []
            for kind in range(3):
                high, rest = split_low(tab[kind * heads_here + place])
                lin.append(dot(hot, high) + dot(hot, rest))
            queries = turn_by(lin[0], sin_ref[...]).astype(LOW)
            keys = turn_by(lin[1], sin_ref[...]).astype(LOW)
            values = lin[2].astype(LOW)
            heads[0, place], heads[1, place], heads[2, place] = queries, keys, values
            probability = probabilities(queries, keys).astype(LOW)
            mixed = dot(probability, values).astype(LOW)
            att_low[:, head_lanes(place)] = mixed
            turned = mixed.astype(FULL).T
            head_rows = pl.ds(pl.multiple_of(place * HD, HD), HD)
            att_turned[head_rows, :] = turned.astype(LOW)
            gbuf[head_rows, :] = turned
            return carried

        lax.fori_loop(0, heads_here, attend_head, 0)
        loads[3].wait()
        pl.semaphore_wait(barrier, len(greeted))

        def project(chunk):
            mixed = att_low[chunk_rows(chunk), :]
            for side in range(2):
                for start, size in column_tiles(width // 2, 256):
                    weight = w_dense[side * (width // 2) + start : side * (width // 2) + start + size, :]
                    parts[chunk, side, :, start : start + size] = dot_nt(mixed, weight)
            core_copy(0, chunk).start()

        every_chunk(project)
        every_chunk(lambda chunk: send_part(0, chunk))
        rows_copy().start()

    pl.run_scoped(first_scope, pltpu.VMEM((3, width, inner), LOW), pltpu.VMEM((3 * heads_here, vocab, HD), FULL))

    def middle_scope(w_gate, w_up, w_down, cotbuf):
        weight_copies = [
            pltpu.make_async_copy(source, target, weight_sem.at[place])
            for place, (source, target) in enumerate(((w_gate_hbm, w_gate), (w_up_hbm, w_up), (w_down_hbm, w_down)))
        ]
        for copy in weight_copies:
            copy.start()
        for copy in weight_copies:
            copy.wait()

        def feed_forward(chunk):
            branch = take_part(0, chunk)
            residual = alpha * dot(one_hot[chunk_rows(chunk), :], emb[...]) + branch
            centered = residual - row_mean(residual)
            rstd = lax.rsqrt(row_mean(centered * centered) + norm_eps)
            xhat = centered * rstd
            rstd_one[chunk] = rstd
            xbuf[...] = xhat
            park = pltpu.make_async_copy(xbuf, xhat_park.at[chunk], load_sem.at[0])
            park.start()
            hidden_low = (xhat * norms[0:1, :] + norms[1:2, :]).astype(LOW)
            put_blocks(hidden_low.astype(FULL))
            keep_columns(cols_own, chunk)
            cols_copy(0, chunk).start()
            for start, size in column_tiles(local_hidden):
                cut = slice(start, start + size)
                gate = dot_nt(w_gate[cut, :], hidden_low)
                up = dot_nt(w_up[cut, :], hidden_low)
                units = mp * local_hidden + start + lax.broadcasted_iota(jnp.int32, (size, rows), 0)
                used = jnp.where(units < FF_USED, 1.0, 0.0)
                square = gate * gate
                bend = jnp.tanh(TANH_SCALE * gate * (1.0 + 0.044715 * square))
                gelu = 0.5 * gate * (1.0 + bend) * used
                slope = 0.5 * (1.0 + bend) + 0.5 * gate * (1.0 - bend * bend) * (
                    TANH_SCALE * (1.0 + 3.0 * 0.044715 * square)
                )
                gate_up[0, cut, chunk_lanes(chunk)] = slope * up * used
                gate_up[1, cut, chunk_lanes(chunk)] = gelu
                active = (gelu * up).astype(LOW)
                act_low[cut, chunk_lanes(chunk)] = active
                send_a[lax.div(chunk, 2), cut, half_chunk(chunk)] = active.astype(FULL)
            act_send(0, chunk)
            active = send_a[lax.div(chunk, 2), :, half_chunk(chunk)].T.astype(LOW)
            for side in range(2):
                for start, size in column_tiles(width // 2, 256):
                    cut = slice(side * (width // 2) + start, side * (width // 2) + start + size)
                    parts[chunk, side, :, start : start + size] = dot(active, w_down[:, cut])
            core_copy(1, chunk).start()
            park.wait()
            send_part(1, chunk)

        every_chunk(feed_forward)
        rows_copy().wait()
        same = jnp.int32(0)
        for place in range(2 * LINE):
            same = same + jnp.where(cluster_ref[place] == cluster_ref[dp], 1, 0)
        weight_row = 1.0 / jnp.full((1, width), same, jnp.int32).astype(FULL)

        def feed_backward(chunk):
            loads = load_all(
                ((xhat_park.at[chunk], xbuf), (cot_hbm.at[chunk_rows(chunk)], cotbuf))
            )
            branch = take_part(1, chunk)
            for copy in loads:
                copy.wait()
            residual = alpha * (xbuf[...] * norms[0:1, :] + norms[1:2, :]) + branch
            centered = residual - row_mean(residual)
            rstd = lax.rsqrt(row_mean(centered * centered) + norm_eps)
            xhat = centered * rstd
            obuf[...] = (xhat * norms[2:3, :] + norms[3:4, :]).astype(LOW)
            grad_out = cotbuf[...].astype(FULL) * weight_row
            vectors[2:3, :] += jnp.sum(grad_out * xhat, axis=0, keepdims=True)
            vectors[3:4, :] += jnp.sum(grad_out, axis=0, keepdims=True)
            grad_x = grad_out * norms[2:3, :]
            grad_two = (grad_x - row_mean(grad_x) - xhat * row_mean(grad_x * xhat)) * rstd
            for place in range(width // inner):
                gbuf[place * rows : (place + 1) * rows, :] = grad_two[:, place * inner : (place + 1) * inner]
            stores = load_all(
                ((obuf, block_out.at[chunk_rows(chunk)]), (gbuf, grad_two_park.at[chunk]))
            )
            grad_low = grad_two.astype(LOW)
            put_blocks(grad_low.astype(FULL))
            for place in range(2):
                two_own[place, chunk_rows(chunk), :] = blocks[2 * z + place].astype(LOW)
            for place in range(LINE):
                two_send[place, chunk] = blocks[2 * place + core]
            for step in range(1, LINE):
                two_copy(step, chunk).start()
            for start, size in column_tiles(local_hidden):
                cut = slice(start, start + size)
                grad_act = dot_nt(w_down[cut, :], grad_low)
                for which in range(2):
                    low = (grad_act * gate_up[which, cut, chunk_lanes(chunk)]).astype(LOW)
                    grads_low[which * shift + start : which * shift + start + size, chunk_lanes(chunk)] = low
                    gate_up[which, cut, chunk_lanes(chunk)] = low.astype(FULL)
            pair_copy(0, chunk).start()
            act_take(0, chunk)
            act_send(1, chunk)
            grad_gate = gate_up[0, :, chunk_lanes(chunk)].T.astype(LOW)
            grad_up = gate_up[1, :, chunk_lanes(chunk)].T.astype(LOW)
            for side in range(2):
                for start, size in column_tiles(width // 2, 256):
                    cut = slice(side * (width // 2) + start, side * (width // 2) + start + size)
                    parts[chunk, side, :, start : start + size] = dot(grad_gate, w_gate[:, cut]) + dot(
                        grad_up, w_up[:, cut]
                    )
            core_copy(2, chunk).start()
            for copy in stores:
                copy.wait()
            send_part(2, chunk)

        every_chunk(feed_backward)

    pl.run_scoped(
        middle_scope,
        pltpu.VMEM((local_hidden, width), LOW),
        pltpu.VMEM((local_hidden, width), LOW),
        pltpu.VMEM((local_hidden, width), LOW),
        pltpu.VMEM((rows, width), LOW),
    )

    def last_scope(theirs, cols_theirs, two_theirs, att_theirs, send_b, stage, grad_att, grad_one_own, sums, sums_up, sums_down, sums_below, sums_above, late_own):
        def norm_backward(chunk):
            loads = load_all(((xhat_park.at[chunk], xbuf), (grad_two_park.at[chunk], gbuf)))
            branch = take_part(2, chunk)
            for copy in loads:
                copy.wait()
            grad_two = [gbuf[place * rows : (place + 1) * rows, :] for place in range(width // inner)]
            grad_hidden = alpha * jnp.concatenate(grad_two, axis=1) + branch
            xhat = xbuf[...]
            vectors[0:1, :] += jnp.sum(grad_hidden * xhat, axis=0, keepdims=True)
            vectors[1:2, :] += jnp.sum(grad_hidden, axis=0, keepdims=True)
            grad_x = grad_hidden * norms[0:1, :]
            grad_one = (grad_x - row_mean(grad_x) - xhat * row_mean(grad_x * xhat)) * rstd_one[chunk]
            put_blocks(grad_one)
            for place in range(2):
                grad_one_own[chunk_rows(chunk), place * block : (place + 1) * block] = blocks[2 * mp + place]
            grad_low = grad_one.astype(LOW)
            put_blocks(grad_low.astype(FULL))
            keep_columns(late_own, chunk)
            grad_mixed = dot(grad_low, w_dense[...]).astype(LOW)
            for place in range(heads_here):
                grad_att[place, chunk_rows(chunk), :] = grad_mixed[:, place * HD : (place + 1) * HD]

        def fetch_columns(kind):
            forward = forward_copy(kind)
            forward.start()
            forward.wait()
            for pair in range(2):
                moved(
                    [(r_cols.at[kind, 2 * pair + place], blocks.at[pl.ds(CHUNKS * place, CHUNKS)]) for place in range(2)]
                )
                for place in range(2):
                    for chunk in range(CHUNKS):
                        piece = blocks[CHUNKS * place + chunk].astype(LOW)
                        cols_theirs[kind, 2 * pair + place, chunk * rows : (chunk + 1) * rows, :] = piece

        def fetch_rows(source, target):
            size = source.shape[0]
            views = [stage.at[place, pl.ds(0, size)] for place in range(2)]
            moved([(source.at[:, pl.ds(block * place, block)], views[place]) for place in range(2)])
            for place in range(2):
                target[:, block * place : block * (place + 1)] = views[place][...].astype(LOW)

        def row_tiles(size):
            return column_tiles(size)

        def outer_product(target, kind, place, own, other):
            right, right_theirs = (cols_own, late_own)[kind][place], cols_theirs[kind, place]
            for start, size in row_tiles(target.shape[0]):
                cut = slice(start, start + size)
                target[cut, :] = dot(own[cut, :], right) + dot(other[cut, :], right_theirs)

        def down_products():
            for step in range(1, LINE):
                for chunk in range(CHUNKS):
                    two_copy(step, chunk).wait()
            for step in range(1, LINE):
                two_forward(step).start()
            for step in range(1, LINE):
                two_forward(step).wait()
            for chunk in range(CHUNKS):
                act_take(2, chunk)
            for step in range(LINE):
                owner = lax.rem(z + step, LINE)
                if step:
                    moved(
                        [
                            (r_two.at[owner, place], blocks.at[pl.ds(CHUNKS * place, CHUNKS)])
                            for place in range(2)
                        ]
                    )
                    for place in range(2):
                        for chunk in range(CHUNKS):
                            piece = blocks[CHUNKS * place + chunk].astype(LOW)
                            two_theirs[place, chunk * rows : (chunk + 1) * rows, :] = piece
                    fetch_rows(r_act.at[owner], theirs.at[0])
                left, right = (theirs.at[0], two_theirs) if step else (act_low, two_own)
                for place in range(2):
                    for start, size in row_tiles(local_hidden):
                        cut = slice(start, start + size)
                        lanes = slice(place * block, (place + 1) * block)
                        product = dot(left[cut, :], right[place])
                        gate_up[0, cut, lanes] = gate_up[0, cut, lanes] + product if step else product

        def down_copy():
            return remote(gate_up.at[0, :, half_lanes(1 - y)], r_dny, dny_s, dny_r, y_peer)

        def down_end():
            down_copy().wait()
            moved([(r_dny, stage.at[0])])
            stage[0] = stage[0] + gate_up[0, :, half_lanes(y)]
            moved([(stage.at[0], out_down)])
            for chunk in range(CHUNKS):
                for way in range(2):
                    for hop in range(1, LINE - 1):
                        active, copy = act_copy(way, hop, chunk)
                        pl.when(active)(copy.wait_send)

        sent = {0: [], 1: []}

        def line_terms(kind):
            if kind < 2:
                own = grads_low.at[pl.ds(kind * shift, local_hidden)]
                return 0, own, theirs.at[1 + kind], out_gate if kind == 0 else out_up, local_hidden
            return 1, att_turned, att_theirs, out_dense, inner

        def line_land(kind, slot, way):
            return r_rs.at[kind, slot - 1, way] if kind < 2 else r_rsd.at[slot - 1, way]

        def cut_to(ref, size):
            return ref if size == ref.shape[0] else ref.at[pl.ds(0, size)]

        def line_copy(kind, slot, way, home):
            size = line_terms(kind)[4]
            goal = jnp.clip(z + 1 - 2 * way, 0, LINE - 1)
            return remote(
                cut_to(home, size), line_land(kind, slot, way), rs_s.at[kind, slot - 1, way],
                rs_r.at[kind, slot - 1, way], at(z_to=goal),
            )

        def line_slot(kind, slot):
            column_kind, own, other, _, size = line_terms(kind)
            for way in range(2):
                home = (send_a, send_b)[way].at[len(sent[way]) % 2]
                if len(sent[way]) >= 2:
                    active, copy = sent[way][-2]
                    pl.when(active)(copy.wait_send)
                active = z < slot if way == 0 else z > LINE - 1 - slot
                inner = z > 0 if way == 0 else z < LINE - 1
                copy = line_copy(kind, slot, way, home)
                sent[way].append((active, copy))

                @pl.when(active)
                def _():
                    place = LINE - slot + z if way == 0 else slot - LINE + z
                    target = cut_to(home, size)
                    outer_product(target, column_kind, place, own, other)
                    if slot > 1:

                        @pl.when(inner)
                        def _():
                            line_copy(kind, slot - 1, way, home).wait_recv()
                            arrived = cut_to(stage.at[way], size)
                            moved([(line_land(kind, slot - 1, way), arrived)])
                            target[...] = target[...] + arrived[...]

                    copy.start()

        def line_end(kind):
            column_kind, own, other, result, size = line_terms(kind)
            total, arrived = cut_to(stage.at[0], size), cut_to(stage.at[1], size)
            outer_product(total, column_kind, z, own, other)
            for way in range(2):

                @pl.when(z > 0 if way == 0 else z < LINE - 1)
                def _():
                    line_copy(kind, LINE - 1, way, send_a.at[0]).wait_recv()
                    moved([(line_land(kind, LINE - 1, way), arrived)])
                    total[...] = total[...] + arrived[...]

            if kind == 2:
                gbuf[0:block, :] = total[...].T
                total = gbuf.at[pl.ds(0, block)]
            moved([(total, result)])

        def attention_backward(place, carried):
            hot_t = hot_turned[...]
            queries, keys, values = heads[0, place], heads[1, place], heads[2, place]
            grad_mixed = grad_att[place]
            probability = probabilities(queries, keys)
            grad_prob = dot_nt(grad_mixed, values)
            centre = jnp.sum(grad_prob * probability, axis=-1, keepdims=True)
            grad_scores = (probability * (grad_prob - centre)).astype(LOW)
            grad_queries = dot(grad_scores, keys) * score_scale
            grad_keys = dot_tn(grad_scores, queries) * score_scale
            grad_values = dot_tn(probability.astype(LOW), grad_mixed)
            sums[0, 0:vocab, head_lanes(place)] = dot(hot_t, turn_by(grad_queries, -sin_ref[...]).astype(LOW))
            sums[0, 0:vocab, head_lanes(place, inner)] = dot(hot_t, turn_by(grad_keys, -sin_ref[...]).astype(LOW))
            sums[1, 0:vocab, head_lanes(place)] = dot(hot_t, grad_values.astype(LOW))
            return carried

        def small_sums():
            lax.fori_loop(0, heads_here, attention_backward, 0)
            hot_t = hot_turned[...]
            high, rest = split_low(grad_one_own[...])
            sums[1, 0:vocab, heads_here * HD :] = dot(hot_t, high) + dot(hot_t, rest)
            for side in range(2):
                sums[side, vocab:, :] = vectors[:, side * (width // 2) : (side + 1) * (width // 2)]
            sums_pair().start()

        def sums_pair():
            return remote(sums.at[1 - y], r_sums.at[0], sums_s.at[0], sums_r.at[0], y_peer)

        def sums_line(way):
            source = (sums_up, sums_down)[way]
            goal = jnp.clip(z + 1 - 2 * way, 0, LINE - 1)
            return remote(source, r_sums.at[1 + way], sums_s.at[1 + way], sums_r.at[1 + way], at(z_to=goal))

        def sums_back():
            return remote(sums.at[y], r_sums.at[3], sums_s.at[3], sums_r.at[3], y_peer)

        def sums_first():
            sums_pair().wait()
            moved([(r_sums.at[0], sums_below)])
            sums[y] = sums[y] + sums_below[...]

            @pl.when(z == 0)
            def _():
                sums_up[...] = sums[y]
                sums_line(0).start()

            @pl.when(z == LINE - 1)
            def _():
                sums_down[...] = sums[y]
                sums_line(1).start()

        def sums_middle():
            @pl.when(z > 0)
            def _():
                sums_line(0).wait_recv()
                moved([(r_sums.at[1], sums_below)])

            @pl.when((z > 0) & (z < LINE - 1))
            def _():
                sums_up[...] = sums[y] + sums_below[...]
                sums_line(0).start()

            @pl.when(z < LINE - 1)
            def _():
                sums_line(1).wait_recv()
                moved([(r_sums.at[2], sums_above)])

            @pl.when((z > 0) & (z < LINE - 1))
            def _():
                sums_down[...] = sums[y] + sums_above[...]
                sums_line(1).start()

            @pl.when(z > 0)
            def _():
                sums[y] = sums[y] + sums_below[...]

            @pl.when(z < LINE - 1)
            def _():
                sums[y] = sums[y] + sums_above[...]

            sums_back().start()

        def sums_end():
            sums_back().wait()
            pl.when(z < LINE - 1)(sums_line(0).wait_send)
            pl.when(z > 0)(sums_line(1).wait_send)
            moved([(r_sums.at[3], sums.at[1 - y])])
            lanes = pl.ds(pl.multiple_of(lax.rem(dp, LINE) * block, block), block)
            moved([(sums.at[lax.div(dp, LINE), pl.ds(vocab, 8), lanes], out_norms)])

        def by_token(kind, rows_of):
            side, start = ((0, 0), (0, inner), (1, 0), (1, inner))[kind]
            return sums[side, rows_of, start : start + inner]

        def head_gradients():
            own_columns = emb[:, pl.ds(pl.multiple_of(dp * block, block), block)]
            for kind, result in enumerate((out_query, out_key, out_value)):
                high, rest = split_low(by_token(kind, slice(0, vocab)))
                gbuf[0:block, :] = dot_tn(own_columns, high) + dot_tn(own_columns, rest)
                moved([(gbuf.at[pl.ds(0, block)], result)])

        table_rows = vocab // (2 * LINE)
        table_own = pl.ds(pl.multiple_of(dp * table_rows, table_rows), table_rows)

        def table_part():
            for kind, weight in enumerate((w_query_hbm, w_key_hbm, w_value_hbm)):
                moved([(weight, w_dense)])
                pieces = jnp.concatenate(split_low(by_token(kind, table_own)), axis=0)
                for start, size in column_tiles(width):
                    cut = slice(start, start + size)
                    both = dot_nt(pieces, w_dense[cut, :])
                    both = both[:table_rows] + both[table_rows:]
                    xbuf[0:table_rows, cut] = both if kind == 0 else xbuf[0:table_rows, cut] + both
            quarter = pl.ds(pl.multiple_of(mp * inner, inner), inner)
            xbuf[0:table_rows, quarter] = xbuf[0:table_rows, quarter] + alpha * by_token(3, table_own)
            table_copy(0).start()

        def table_middle():
            table_copy(0).wait()
            xbuf[table_rows : 2 * table_rows, :] = xbuf[0:table_rows, :] + table_core[...]
            table_copy(1).start()

        def table_end():
            table_copy(1).wait()
            xbuf[0:table_rows, :] = 0.1 * (xbuf[table_rows : 2 * table_rows, :] + table_x[...])
            moved([(xbuf.at[pl.ds(0, table_rows)], out_table)])

        def table_copy(turn):
            target, device = ((table_core, core_peer), (table_x, x_peer))[turn]
            return remote(xbuf.at[pl.ds(turn * table_rows, table_rows)], target, table_s.at[turn], table_r.at[turn], device)

        def act_pass(chunk):
            act_take(1, chunk)
            act_send(2, chunk)

        pair_copy(1, 0).start()
        pair_copy(1, 1).start()
        for chunk in range(CHUNKS):
            cols_copy(0, chunk).wait()
        fetch_columns(0)
        norm_backward(0)
        norm_backward(1)
        for chunk in range(CHUNKS):
            pair_copy(0, chunk).wait()
        fetch_rows(r_y.at[0], theirs.at[1])
        for chunk in range(CHUNKS):
            for way in range(2):
                active, copy = act_copy(way, 0, chunk)
                pl.when(active)(copy.wait_send)
        line_slot(0, 1)
        norm_backward(2)
        norm_backward(3)
        small_sums()
        pair_copy(1, 2).start()
        pair_copy(1, 3).start()
        for chunk in range(CHUNKS):
            cols_copy(1, chunk).start()
        act_pass(0)
        act_pass(1)
        line_slot(0, 2)
        act_pass(2)
        act_pass(3)
        sums_first()
        line_slot(0, 3)
        for chunk in range(CHUNKS):
            pair_copy(1, chunk).wait()
        fetch_rows(r_y.at[1], theirs.at[2])
        line_slot(1, 1)
        down_products()
        down_copy().start()
        sums_middle()
        line_end(0)
        line_slot(1, 2)
        for chunk in range(CHUNKS):
            cols_copy(1, chunk).wait()
        fetch_columns(1)
        fetch_rows(r_att, att_theirs)
        line_slot(1, 3)
        sums_end()
        head_gradients()
        table_part()
        line_slot(2, 1)
        table_middle()
        down_end()
        table_end()
        line_slot(2, 2)
        line_end(1)
        line_slot(2, 3)
        line_end(2)
        for way in range(2):
            for active, copy in sent[way][-2:]:
                pl.when(active)(copy.wait_send)

    pl.run_scoped(
        last_scope,
        pltpu.VMEM((3, local_hidden, length), LOW),
        pltpu.VMEM((2, LINE, length, block), LOW),
        pltpu.VMEM((2, length, block), LOW),
        pltpu.VMEM((inner, length), LOW),
        pltpu.VMEM((2, local_hidden, block), FULL),
        pltpu.VMEM((2, local_hidden, block), FULL),
        pltpu.VMEM((heads_here, length, HD), LOW),
        pltpu.VMEM((length, 2 * block), FULL),
        pltpu.VMEM((2,) + r_sums.shape[1:], FULL),
        pltpu.VMEM(r_sums.shape[1:], FULL),
        pltpu.VMEM(r_sums.shape[1:], FULL),
        pltpu.VMEM(r_sums.shape[1:], FULL),
        pltpu.VMEM(r_sums.shape[1:], FULL),
        pltpu.VMEM(cols_own.shape, LOW),
    )


def local_fast(
    token_ids,
    prefix_lengths,
    cluster_ids,
    embedding,
    w_query,
    w_key,
    w_value,
    w_dense,
    w_gate,
    w_up,
    w_down,
    norm1_gain,
    norm1_bias,
    norm2_gain,
    norm2_bias,
    cotangent,
):
    length = token_ids.shape[0]
    vocab, width = embedding.shape
    inner = w_query.shape[1]
    heads_here = inner // HD
    local_hidden = w_gate.shape[1]
    rows = length // CHUNKS
    block = width // (2 * LINE)
    shift = (local_hidden + 15) // 16 * 16
    frequency = 10000.0 ** (np.arange(HD // 2) * (-2.0 / HD))
    angles = np.arange(length)[:, None] * frequency[None, :]
    cosine = np.concatenate([np.cos(angles)] * 2, axis=1).astype(np.float32)
    sine = np.concatenate([-np.sin(angles), np.sin(angles)], axis=1).astype(np.float32)
    norms = jnp.stack([norm1_gain, norm1_bias, norm2_gain, norm2_bias])

    hbm = pl.BlockSpec(memory_space=pl.ANY)
    vmem = pl.BlockSpec(memory_space=pltpu.VMEM)
    smem = pl.BlockSpec(memory_space=pltpu.SMEM)
    sums_rows = vocab + 8
    table_rows = vocab // (2 * LINE)
    shapes = [
        ((length, width), LOW),
        ((table_rows, width), FULL),
        ((block, inner), FULL),
        ((block, inner), FULL),
        ((block, inner), FULL),
        ((block, inner), FULL),
        ((local_hidden, block), FULL),
        ((local_hidden, block), FULL),
        ((local_hidden, block), FULL),
        ((8, block), FULL),
        ((LINE, local_hidden, length), FULL),
        ((LINE, 2, CHUNKS, rows, block), FULL),
        ((2, local_hidden, length), FULL),
        ((2, LINE, CHUNKS, rows, block), FULL),
        ((inner, length), FULL),
        ((CHUNKS, rows, width), FULL),
        ((CHUNKS, length, inner), FULL),
        ((local_hidden, block), FULL),
        ((2, LINE - 1, 2, local_hidden, block), FULL),
        ((LINE - 1, 2, inner, block), FULL),
        ((4, sums_rows, width // 2), FULL),
    ]
    scratch = [
        ((CHUNKS, 2, rows, width // 2), FULL),
        ((CHUNKS, rows, width // 2), FULL),
        ((2, CHUNKS, rows, width // 2), FULL),
        ((CHUNKS, rows, width // 2), FULL),
        ((2 * LINE, rows, block), FULL),
        ((rows, width), FULL),
        ((length, inner), FULL),
        ((rows, width), LOW),
        ((2, local_hidden, length), FULL),
        ((2 * shift, length), LOW),
        ((local_hidden, length), LOW),
        ((2, local_hidden, block), FULL),
        ((LINE, length, block), LOW),
        ((2, CHUNKS, rows, block), FULL),
        ((2, length, block), LOW),
        ((LINE, CHUNKS, rows, block), FULL),
        ((length, inner), LOW),
        ((inner, length), LOW),
        ((3, heads_here, length, HD), LOW),
        ((width, inner), LOW),
        ((length, vocab), LOW),
        ((vocab, length), LOW),
        ((CHUNKS, rows, 1), FULL),
        ((8, width), FULL),
        ((table_rows, width), FULL),
        ((table_rows, width), FULL),
    ]
    dma = pltpu.SemaphoreType.DMA
    each = (3, CHUNKS)
    semaphores = [
        each, each, each, each, each, each, (2, LINE - 1, CHUNKS), (2, LINE - 1, CHUNKS), each, each, (3,), (3,),
        (2, CHUNKS), (2, CHUNKS), (2,), (2,), (2, CHUNKS), (2, CHUNKS), None, None, None, None,
        (3, LINE - 1, 2), (3, LINE - 1, 2), (4,), (4,), (2,), (2,), (4,), (4,),
    ]
    results = pl.pallas_call(
        functools.partial(layer_kernel, length, width, local_hidden),
        out_shape=[jax.ShapeDtypeStruct(shape, dtype) for shape, dtype in shapes],
        in_specs=[smem] * 2 + [vmem] * 5 + [hbm] * 8,
        out_specs=[hbm] * len(shapes),
        scratch_shapes=[pltpu.VMEM(shape, dtype) for shape, dtype in scratch]
        + [dma if shape is None else dma(shape) for shape in semaphores],
        compiler_params=pltpu.CompilerParams(
            collective_id=0, has_side_effects=True, vmem_limit_bytes=62 * 2**20
        ),
    )(
        prefix_lengths,
        cluster_ids,
        token_ids.reshape(1, length),
        embedding,
        cosine,
        sine,
        norms,
        w_query,
        w_key,
        w_value,
        w_dense,
        w_gate.T,
        w_up.T,
        w_down.T,
        cotangent,
    )
    block_out, table, out_query, out_key, out_value, out_dense, out_gate, out_up, out_down, out_norms = results[:10]
    return (
        block_out,
        table,
        out_query,
        out_key,
        out_value,
        out_dense,
        out_gate.T,
        out_up.T,
        out_down.T,
        out_norms[0],
        out_norms[1],
        out_norms[2],
        out_norms[3],
    )


def solution(mesh):
    fast = mesh.shape["dp"] == 2 * LINE and mesh.shape["mp"] == 4
    return jax.shard_map(
        local_fast if fast else local_general,
        mesh=mesh,
        in_specs=(
            P("dp"),
            P("dp"),
            P(),
            P(),
            P(None, "mp"),
            P(None, "mp"),
            P(None, "mp"),
            P(None, "mp"),
            P(None, "mp"),
            P(None, "mp"),
            P(None, "mp"),
            P(),
            P(),
            P(),
            P(),
            P("dp", None),
        ),
        out_specs=(
            P("dp", None),
            P("dp", None),
            P("dp", "mp"),
            P("dp", "mp"),
            P("dp", "mp"),
            P("dp", "mp"),
            P("dp", "mp"),
            P("dp", "mp"),
            P("dp", "mp"),
            P("dp"),
            P("dp"),
            P("dp"),
            P("dp"),
        ),
        check_vma=False,
    )
```

```python
import functools
import math

import jax
import jax.numpy as jnp
import numpy as np
from jax import lax
from jax.experimental import pallas as pl
from jax.experimental.pallas import tpu as pltpu
from jax.sharding import PartitionSpec as P

HD = 128
FF_USED = 5461


deep_alpha = math.sqrt(48.0)
norm_eps = 1e-05
highest = lax.Precision.HIGHEST


def layer_norm(inputs, norm_gain, norm_bias):
    center = jnp.mean(inputs, axis=-1, keepdims=True)
    centered = inputs - center
    spread = jnp.mean(centered * centered, axis=-1, keepdims=True)
    return centered * lax.rsqrt(spread + norm_eps) * norm_gain + norm_bias


def rotary_tables(length, head_width):
    half_width = head_width // 2
    frequency = jnp.exp(
        jnp.arange(half_width, dtype=jnp.float32) * (-2.0 * math.log(10000.0) / head_width)
    )
    angles = jnp.arange(length, dtype=jnp.float32)[:, None] * frequency[None, :]
    return (jnp.cos(angles), jnp.sin(angles))


def rotate(inputs, cosine, sine):
    half_width = inputs.shape[-1] // 2
    first = inputs[..., :half_width]
    second = inputs[..., half_width:]
    cosine = cosine[:, None, :]
    sine = sine[:, None, :]
    return jnp.concatenate(
        [first * cosine - second * sine, second * cosine + first * sine], axis=-1
    )


def row_mask(row_begin, row_count, length, prefix):
    columns = jnp.arange(length, dtype=jnp.int32)
    row_index = row_begin + jnp.arange(row_count, dtype=jnp.int32)
    return (columns[None, :] < prefix) | (columns[None, :] <= row_index[:, None])


def block_scores(query_block, keys_rot, visible, score_scale):
    scores = (
        jnp.einsum("bhd,khd->hbk", query_block, keys_rot, preferred_element_type=jnp.float32)
        * score_scale
    )
    return jnp.where(visible[None, :, :], scores, -1e30)


def attention_forward(queries, keys_rot, values_in, prefix, row_block):
    length = queries.shape[0]
    score_scale = 1.0 / math.sqrt(HD)

    def one_block(row_begin):
        scores = block_scores(
            queries, keys_rot, row_mask(row_begin, row_block, length, prefix), score_scale
        )
        row_max = jnp.max(scores, axis=-1, keepdims=True)
        weights = jnp.exp(scores - row_max)
        total_weight = jnp.sum(weights, axis=-1, keepdims=True)
        probability = (weights / total_weight).astype(jnp.bfloat16)
        mixed_block = jnp.einsum(
            "hbk,khd->bhd", probability, values_in, preferred_element_type=jnp.float32
        )
        return (mixed_block, row_max + jnp.log(total_weight))

    starts = jnp.arange(length // row_block, dtype=jnp.int32) * row_block
    attended, log_total = lax.map(one_block, starts)
    return (attended.reshape(length, -1), log_total)


def attention_backward(queries, keys_rot, values_in, prefix, row_block, log_total, grad_mixed):
    length = queries.shape[0]
    score_scale = 1.0 / math.sqrt(HD)

    def one_block(carried, inputs):
        grad_keys, grad_values = carried
        row_begin, block_total = inputs
        scores = block_scores(
            queries, keys_rot, row_mask(row_begin, row_block, length, prefix), score_scale
        )
        probability = jnp.exp(scores - block_total)
        prob_low = probability.astype(jnp.bfloat16)
        grad_prob = jnp.einsum(
            "bhd,khd->hbk", grad_mixed, values_in, preferred_element_type=jnp.float32
        )
        centre = jnp.sum(grad_prob * probability, axis=-1, keepdims=True)
        grad_scores = (probability * (grad_prob - centre)).astype(jnp.bfloat16)
        grad_query = (
            jnp.einsum("hbk,khd->bhd", grad_scores, keys_rot, preferred_element_type=jnp.float32)
            * score_scale
        )
        grad_keys = (
            grad_keys
            + jnp.einsum("hbk,bhd->khd", grad_scores, queries, preferred_element_type=jnp.float32)
            * score_scale
        )
        grad_values = grad_values + jnp.einsum(
            "hbk,bhd->khd", prob_low, grad_mixed, preferred_element_type=jnp.float32
        )
        return ((grad_keys, grad_values), grad_query)

    starts = jnp.arange(length // row_block, dtype=jnp.int32) * row_block
    zeros_kv = jnp.zeros(keys_rot.shape, jnp.float32)
    (grad_keys, grad_values), grad_queries = lax.scan(
        one_block, (zeros_kv, zeros_kv), (starts, log_total)
    )
    return (grad_queries.reshape(queries.shape), grad_keys, grad_values)


def local_general(
    token_ids,
    prefix_lengths,
    cluster_ids,
    embedding,
    w_query,
    w_key,
    w_value,
    w_dense,
    w_gate,
    w_up,
    w_down,
    norm1_gain,
    norm1_bias,
    norm2_gain,
    norm2_bias,
    cotangent,
):
    length = token_ids.shape[0]
    vocab_rows = embedding.shape[0]
    row_block = min(512, length)
    local_heads = w_query.shape[1] // HD
    local_hidden = w_gate.shape[1]
    one_hot = (token_ids[:, None] == jnp.arange(vocab_rows, dtype=jnp.int32)[None, :]).astype(
        jnp.bfloat16
    )
    embedded_low = jnp.dot(one_hot, embedding, preferred_element_type=jnp.float32).astype(
        jnp.bfloat16
    )
    embedded = embedded_low.astype(jnp.float32)
    cosine, sine = rotary_tables(length, HD)
    prefix = prefix_lengths[0]
    own_cluster = cluster_ids[lax.axis_index("dp")]
    seq_weight = 1.0 / jnp.sum((cluster_ids == own_cluster).astype(jnp.float32))

    def project(weight_in):
        return jnp.dot(embedded_low, weight_in, preferred_element_type=jnp.float32).reshape(
            length, local_heads, HD
        )

    queries = rotate(project(w_query), cosine, sine).astype(jnp.bfloat16)
    keys_rot = rotate(project(w_key), cosine, sine).astype(jnp.bfloat16)
    values_in = project(w_value).astype(jnp.bfloat16)
    attended, log_total = attention_forward(queries, keys_rot, values_in, prefix, row_block)
    attended_low = attended.astype(jnp.bfloat16)
    branch = lax.psum(
        jnp.einsum("lh,dh->ld", attended_low, w_dense, preferred_element_type=jnp.float32), "mp"
    )
    residual_one = deep_alpha * embedded + branch
    hidden, norm_one_pull = jax.vjp(layer_norm, residual_one, norm1_gain, norm1_bias)
    hidden_low = hidden.astype(jnp.bfloat16)
    gate_proj = jnp.dot(hidden_low, w_gate, preferred_element_type=jnp.float32)
    up_proj = jnp.dot(hidden_low, w_up, preferred_element_type=jnp.float32)
    unit_index = lax.axis_index("mp") * local_hidden + jnp.arange(local_hidden, dtype=jnp.int32)
    used_mask = (unit_index < FF_USED).astype(jnp.float32)

    def gated_unit(gate_in, up_in):
        return jax.nn.gelu(gate_in, approximate=True) * up_in * used_mask

    activation, gated_pull = jax.vjp(gated_unit, gate_proj, up_proj)
    activation_low = activation.astype(jnp.bfloat16)
    branch_two = lax.psum(
        jnp.einsum("lf,df->ld", activation_low, w_down, preferred_element_type=jnp.float32), "mp"
    )
    residual_two = deep_alpha * hidden + branch_two
    final, norm_two_pull = jax.vjp(layer_norm, residual_two, norm2_gain, norm2_bias)
    grad_out = cotangent.astype(jnp.float32) * seq_weight
    grad_two, grad_gain_two, grad_bias_two = norm_two_pull(grad_out)
    grad_branch_two = grad_two.astype(jnp.bfloat16)
    grad_w_down = jnp.einsum(
        "ld,lf->df", grad_branch_two, activation_low, preferred_element_type=jnp.float32
    )
    grad_act = jnp.dot(grad_branch_two, w_down, preferred_element_type=jnp.float32)
    grad_gate, grad_up = gated_pull(grad_act)
    grad_gate_low = grad_gate.astype(jnp.bfloat16)
    grad_up_low = grad_up.astype(jnp.bfloat16)
    grad_w_gate = jnp.einsum(
        "ld,lf->df", hidden_low, grad_gate_low, preferred_element_type=jnp.float32
    )
    grad_w_up = jnp.einsum("ld,lf->df", hidden_low, grad_up_low, preferred_element_type=jnp.float32)
    hidden_part = jnp.einsum(
        "lf,df->ld", grad_gate_low, w_gate, preferred_element_type=jnp.float32
    ) + jnp.einsum("lf,df->ld", grad_up_low, w_up, preferred_element_type=jnp.float32)
    grad_hidden = deep_alpha * grad_two + lax.psum(hidden_part, "mp")
    feed_sums = (
        lax.psum_scatter(grad_w_gate, "dp", scatter_dimension=0, tiled=True),
        lax.psum_scatter(grad_w_up, "dp", scatter_dimension=0, tiled=True),
        lax.psum_scatter(grad_w_down, "dp", scatter_dimension=0, tiled=True),
        lax.psum_scatter(grad_gain_two, "dp", scatter_dimension=0, tiled=True),
        lax.psum_scatter(grad_bias_two, "dp", scatter_dimension=0, tiled=True),
    )
    grad_one, grad_gain_one, grad_bias_one = norm_one_pull(grad_hidden)
    grad_branch = grad_one.astype(jnp.bfloat16)
    grad_w_dense = jnp.einsum(
        "ld,lh->dh", grad_branch, attended_low, preferred_element_type=jnp.float32
    )
    grad_attended = jnp.dot(grad_branch, w_dense, preferred_element_type=jnp.float32).astype(
        jnp.bfloat16
    )
    grad_attended = grad_attended.reshape(length, local_heads, HD)
    grad_queries, grad_keys, grad_values = attention_backward(
        queries, keys_rot, values_in, prefix, row_block, log_total, grad_attended
    )
    grad_query_lin = rotate(grad_queries, cosine, -sine).astype(jnp.bfloat16).reshape(length, -1)
    grad_key_lin = rotate(grad_keys, cosine, -sine).astype(jnp.bfloat16).reshape(length, -1)
    grad_value_lin = grad_values.astype(jnp.bfloat16).reshape(length, -1)
    grad_w_query = jnp.einsum(
        "ld,lh->dh", embedded_low, grad_query_lin, preferred_element_type=jnp.float32
    )
    grad_w_key = jnp.einsum(
        "ld,lh->dh", embedded_low, grad_key_lin, preferred_element_type=jnp.float32
    )
    grad_w_value = jnp.einsum(
        "ld,lh->dh", embedded_low, grad_value_lin, preferred_element_type=jnp.float32
    )
    input_part = (
        jnp.einsum("lh,dh->ld", grad_query_lin, w_query, preferred_element_type=jnp.float32)
        + jnp.einsum("lh,dh->ld", grad_key_lin, w_key, preferred_element_type=jnp.float32)
        + jnp.einsum("lh,dh->ld", grad_value_lin, w_value, preferred_element_type=jnp.float32)
    )
    grad_embedded = deep_alpha * grad_one + lax.psum(input_part, "mp")
    grad_table = 0.1 * jnp.dot(one_hot.astype(jnp.float32).T, grad_embedded, precision=highest)
    attn_sums = (
        lax.psum_scatter(grad_table, "dp", scatter_dimension=0, tiled=True),
        lax.psum_scatter(grad_w_query, "dp", scatter_dimension=0, tiled=True),
        lax.psum_scatter(grad_w_key, "dp", scatter_dimension=0, tiled=True),
        lax.psum_scatter(grad_w_value, "dp", scatter_dimension=0, tiled=True),
        lax.psum_scatter(grad_w_dense, "dp", scatter_dimension=0, tiled=True),
        lax.psum_scatter(grad_gain_one, "dp", scatter_dimension=0, tiled=True),
        lax.psum_scatter(grad_bias_one, "dp", scatter_dimension=0, tiled=True),
    )
    summed = (
        attn_sums[0],
        attn_sums[1],
        attn_sums[2],
        attn_sums[3],
        attn_sums[4],
        feed_sums[0],
        feed_sums[1],
        feed_sums[2],
        attn_sums[5],
        attn_sums[6],
        feed_sums[3],
        feed_sums[4],
    )
    return (
        final.astype(jnp.bfloat16),
        summed[0],
        summed[1],
        summed[2],
        summed[3],
        summed[4],
        summed[5],
        summed[6],
        summed[7],
        summed[8],
        summed[9],
        summed[10],
        summed[11],
    )


LINE = 4
MESH = pl.DeviceIdType.MESH
CHUNKS = 4
AHEAD = 2
LOW = jnp.bfloat16
FULL = jnp.float32
TANH_SCALE = math.sqrt(2.0 / math.pi)


def dot(left, right):
    return jnp.dot(left, right, preferred_element_type=FULL)


def dot_nt(left, right):
    return lax.dot_general(left, right, (((1,), (1,)), ((), ())), preferred_element_type=FULL)


def dot_tn(left, right):
    return lax.dot_general(left, right, (((0,), (0,)), ((), ())), preferred_element_type=FULL)


def split_low(value):
    high = value.astype(LOW)
    return high, (value - high.astype(FULL)).astype(LOW)


def row_mean(value):
    return jnp.mean(value, axis=-1, keepdims=True)


def spread(size, body, tile=512):
    for start in range(0, size, tile):
        body(start, min(tile, size - start))


def tiles(size, body, tile=512):
    whole = size // tile
    lax.fori_loop(0, whole, lambda step, carried: (body(pl.multiple_of(step * tile, tile), tile), carried)[1], 0)
    if size % tile:
        body(whole * tile, size % tile)


def layer_kernel(
    length, width, local_hidden,
    prefix_ref, cluster_ref, ids_row, emb, cos_ref, sin_ref, norms, w_query_hbm, w_key_hbm, w_value_hbm, w_dense_hbm,
    w_gate_hbm, w_up_hbm, w_down_hbm, cot_hbm,
    block_out, out_table, out_query, out_key, out_value, out_dense, out_gate, out_up, out_down, out_norms,
    r_act, r_two, r_y, r_cols, r_att, xhat_park, grad_two_park, r_dny, r_rs, r_rsd, r_sums,
    parts, core_in, x_in, back_in, blocks, xbuf, gbuf, obuf, gate_up, grads_low, act_low, send_a, cols_own, cols_send,
    two_own, two_send, att_low, att_turned, heads, w_dense, one_hot, hot_turned, rstd_one, vectors, table_core, table_x,
    core_s, core_r, x_s, x_r, back_s, back_r, act_s, act_r, two_s, two_r, fwd_two_s, fwd_two_r, cols_s, cols_r, fwd_s,
    fwd_r, ys_s, ys_r, att_s, att_r, dny_s, dny_r, rs_s, rs_r, sums_s, sums_r, table_s, table_r, load_sem, weight_sem,
):
    dp, mp = lax.axis_index("dp"), lax.axis_index("mp")
    z, y = lax.div(dp, 2), lax.rem(dp, 2)
    x, core = lax.div(mp, 2), lax.rem(mp, 2)
    rows = length // CHUNKS
    heads_here = heads.shape[1]
    inner = heads_here * HD
    vocab = emb.shape[0]
    shift = (local_hidden + 15) // 16 * 16
    block = width // (2 * LINE)
    alpha = jnp.float32(deep_alpha)

    def at(z_to=None, y_to=None, x_to=None, core_to=None):
        z_to = z if z_to is None else z_to
        y_to = y if y_to is None else y_to
        x_to = x if x_to is None else x_to
        core_to = core if core_to is None else core_to
        return (2 * z_to + y_to, 2 * x_to + core_to)

    core_peer = at(core_to=1 - core)
    x_peer = at(x_to=1 - x)
    y_peer = at(y_to=1 - y)

    def remote(source, target, send, receive, device):
        return pltpu.make_async_remote_copy(
            src_ref=source, dst_ref=target, send_sem=send, recv_sem=receive,
            device_id=device, device_id_type=MESH,
        )

    def load_all(pairs):
        copies = [
            pltpu.make_async_copy(source, target, load_sem.at[place])
            for place, (source, target) in enumerate(pairs)
        ]
        for copy in copies:
            copy.start()
        return copies

    def moved(pairs):
        for copy in load_all(pairs):
            copy.wait()

    barrier = pltpu.get_barrier_semaphore()
    greeted = [core_peer, x_peer, y_peer] + [at(z_to=lax.rem(z + step, LINE)) for step in range(1, LINE)]
    for device in greeted:
        pl.semaphore_signal(barrier, inc=1, device_id=device, device_id_type=MESH)

    def chunk_rows(chunk):
        return pl.ds(pl.multiple_of(chunk * rows, rows), rows)

    def core_copy(turn, chunk):
        return remote(
            parts.at[chunk, 1 - core], core_in.at[chunk], core_s.at[turn, chunk], core_r.at[turn, chunk], core_peer
        )

    def x_copy(turn, chunk):
        return remote(
            parts.at[chunk, core], x_in.at[turn % 2, chunk], x_s.at[turn, chunk], x_r.at[turn, chunk], x_peer
        )

    def back_copy(turn, chunk):
        return remote(
            parts.at[chunk, core], back_in.at[chunk], back_s.at[turn, chunk], back_r.at[turn, chunk], core_peer
        )

    def put_part(chunk, start, size, value):
        lanes = pl.ds(pl.multiple_of(lax.rem(start, width // 2), size), size)
        parts[chunk, lax.div(start, width // 2), :, lanes] = value

    def send_part(turn, chunk):
        core_copy(turn, chunk).wait()
        parts[chunk, core] = parts[chunk, core] + core_in[chunk]
        x_copy(turn, chunk).start()

    def take_part(turn, chunk):
        x_copy(turn, chunk).wait()
        parts[chunk, core] = parts[chunk, core] + x_in[turn % 2, chunk]
        back = back_copy(turn, chunk)
        back.start()
        mine = parts[chunk, core]
        back.wait()
        other = back_in[chunk]
        return jnp.concatenate([jnp.where(core == 0, mine, other), jnp.where(core == 0, other, mine)], axis=1)

    def put_blocks(value):
        for place in range(2 * LINE):
            blocks[place] = value[:, place * block : (place + 1) * block]

    def chunk_lanes(chunk):
        return pl.ds(pl.multiple_of(chunk * rows, rows), rows)

    def half_lanes(side):
        return pl.ds(pl.multiple_of(side * block, block), block)

    def keep_columns(own, chunk):
        for place in range(LINE):
            own[place, chunk_rows(chunk), :] = blocks[2 * place + y].astype(LOW)
        for place in range(2):
            cols_send[place, chunk] = blocks[2 * (2 * core + place) + 1 - y]

    def cols_copy(kind, chunk):
        return remote(
            cols_send.at[:, chunk], r_cols.at[kind, pl.ds(2 * core, 2), chunk],
            cols_s.at[kind, chunk], cols_r.at[kind, chunk], y_peer,
        )

    def forward_copy(kind):
        view = r_cols.at[kind, pl.ds(2 * core, 2)]
        return remote(view, view, fwd_s.at[kind], fwd_r.at[kind], core_peer)

    def act_copy(way, hop, chunk):
        goal = jnp.clip(z + 1 - 2 * way, 0, LINE - 1)
        owner = z - hop if way == 0 else z + hop
        active = (owner >= 0) & (z < LINE - 1) if way == 0 else (owner < LINE) & (z > 0)
        owner = jnp.clip(owner, 0, LINE - 1)
        landed = r_act.at[owner, :, chunk_lanes(chunk)]
        source = send_a.at[lax.div(chunk, 2), :, half_chunk(chunk)] if hop == 0 else landed
        return active, remote(
            source, landed, act_s.at[way, hop, chunk], act_r.at[way, hop, chunk], at(z_to=goal)
        )

    def act_landed(way, hop):
        return z - 1 - hop >= 0 if way == 0 else z + 1 + hop < LINE

    def half_chunk(chunk):
        return pl.ds(pl.multiple_of(lax.rem(chunk, 2) * rows, rows), rows)

    def act_send(hop, chunk):
        for way in range(2):
            active, copy = act_copy(way, hop, chunk)
            pl.when(active)(copy.start)

    def act_take(hop, chunk):
        for way in range(2):
            _, copy = act_copy(way, hop, chunk)
            pl.when(act_landed(way, hop))(copy.wait_recv)

    def two_copy(step, chunk):
        goal = lax.rem(z + step, LINE)
        return remote(
            two_send.at[goal, chunk], r_two.at[z, core, chunk],
            two_s.at[step - 1, chunk], two_r.at[step - 1, chunk], at(z_to=goal),
        )

    def two_forward(step):
        view = r_two.at[lax.rem(z + step, LINE), core]
        return remote(view, view, fwd_two_s.at[step - 1], fwd_two_r.at[step - 1], core_peer)

    def pair_copy(which, chunk):
        return remote(
            gate_up.at[which, :, chunk_lanes(chunk)], r_y.at[which, :, chunk_lanes(chunk)],
            ys_s.at[which, chunk], ys_r.at[which, chunk], y_peer,
        )

    def rows_copy():
        return remote(gbuf, r_att, att_s, att_r, y_peer)

    def every_chunk(body):
        lax.fori_loop(0, CHUNKS, lambda chunk, carried: (body(chunk), carried)[1], 0)

    column = lax.broadcasted_iota(jnp.int32, (length, length), 1)
    row = lax.broadcasted_iota(jnp.int32, (length, length), 0)
    score_scale = 1.0 / math.sqrt(HD)

    def probabilities(queries, keys):
        visible = (column < prefix_ref[0]) | (column <= row)
        scores = jnp.where(visible, dot_nt(queries, keys) * score_scale, -1e30)
        weights = jnp.exp(scores - jnp.max(scores, axis=-1, keepdims=True))
        return weights / jnp.sum(weights, axis=-1, keepdims=True)

    def turn_by(value, sine):
        return value * cos_ref[...] + pltpu.roll(value, HD // 2, 1) * sine

    def head_lanes(place, offset=0):
        return pl.ds(pl.multiple_of(offset + place * HD, HD), HD)

    def first_scope(w_heads, tab):
        loads = [
            pltpu.make_async_copy(source, target, weight_sem.at[place])
            for place, (source, target) in enumerate(
                (
                    (w_query_hbm, w_heads.at[0]),
                    (w_key_hbm, w_heads.at[1]),
                    (w_value_hbm, w_heads.at[2]),
                    (w_dense_hbm, w_dense),
                )
            )
        ]
        for copy in loads:
            copy.start()
        named = lax.broadcasted_iota(jnp.int32, (vocab, length), 0) == ids_row[...]
        hot = jnp.where(named, 1.0, 0.0)
        hot_turned[...] = hot.astype(LOW)
        one_hot[...] = hot.T.astype(LOW)
        vectors[...] = jnp.zeros_like(vectors)
        for kind in range(3):
            loads[kind].wait()
            table = dot(emb[...], w_heads[kind])
            for place in range(heads_here):
                tab[kind * heads_here + place] = table[:, place * HD : (place + 1) * HD]

        def attend_head(place, carried):
            hot = one_hot[...]
            lin = []
            for kind in range(3):
                high, rest = split_low(tab[kind * heads_here + place])
                lin.append(dot(hot, high) + dot(hot, rest))
            queries = turn_by(lin[0], sin_ref[...]).astype(LOW)
            keys = turn_by(lin[1], sin_ref[...]).astype(LOW)
            values = lin[2].astype(LOW)
            heads[0, place], heads[1, place], heads[2, place] = queries, keys, values
            probability = probabilities(queries, keys).astype(LOW)
            mixed = dot(probability, values).astype(LOW)
            att_low[:, head_lanes(place)] = mixed
            turned = mixed.astype(FULL).T
            head_rows = pl.ds(pl.multiple_of(place * HD, HD), HD)
            att_turned[head_rows, :] = turned.astype(LOW)
            gbuf[head_rows, :] = turned
            return carried

        lax.fori_loop(0, heads_here, attend_head, 0)
        loads[3].wait()
        pl.semaphore_wait(barrier, len(greeted))

        def project(chunk):
            mixed = att_low[chunk_rows(chunk), :]

            def columns(start, size):
                put_part(chunk, start, size, dot_nt(mixed, w_dense[pl.ds(start, size), :]))

            tiles(width, columns)
            core_copy(0, chunk).start()
            pl.when((chunk > 0) & (chunk <= AHEAD))(lambda: send_part(0, chunk - 1))

        every_chunk(project)
        rows_copy().start()

    pl.run_scoped(first_scope, pltpu.VMEM((3, width, inner), LOW), pltpu.VMEM((3 * heads_here, vocab, HD), FULL))

    def middle_scope(w_gate, w_up, w_down, cotbuf):
        weight_copies = [
            pltpu.make_async_copy(source, target, weight_sem.at[place])
            for place, (source, target) in enumerate(((w_gate_hbm, w_gate), (w_up_hbm, w_up), (w_down_hbm, w_down)))
        ]
        for copy in weight_copies:
            copy.start()
        for copy in weight_copies:
            copy.wait()

        def feed_forward(chunk):
            branch = take_part(0, chunk)
            residual = alpha * dot(one_hot[chunk_rows(chunk), :], emb[...]) + branch
            centered = residual - row_mean(residual)
            rstd = lax.rsqrt(row_mean(centered * centered) + norm_eps)
            xhat = centered * rstd
            rstd_one[chunk] = rstd
            xbuf[...] = xhat
            park = pltpu.make_async_copy(xbuf, xhat_park.at[chunk], load_sem.at[0])
            park.start()
            hidden_low = (xhat * norms[0:1, :] + norms[1:2, :]).astype(LOW)
            put_blocks(hidden_low.astype(FULL))
            keep_columns(cols_own, chunk)
            cols_copy(0, chunk).start()

            def units_tile(start, size):
                cut = pl.ds(start, size)
                gate = dot_nt(w_gate[cut, :], hidden_low)
                up = dot_nt(w_up[cut, :], hidden_low)
                units = mp * local_hidden + start + lax.broadcasted_iota(jnp.int32, (size, rows), 0)
                used = jnp.where(units < FF_USED, 1.0, 0.0)
                square = gate * gate
                bend = jnp.tanh(TANH_SCALE * gate * (1.0 + 0.044715 * square))
                gelu = 0.5 * gate * (1.0 + bend) * used
                slope = 0.5 * (1.0 + bend) + 0.5 * gate * (1.0 - bend * bend) * (
                    TANH_SCALE * (1.0 + 3.0 * 0.044715 * square)
                )
                gate_up[0, cut, chunk_lanes(chunk)] = slope * up * used
                gate_up[1, cut, chunk_lanes(chunk)] = gelu
                active = (gelu * up).astype(LOW)
                act_low[cut, chunk_lanes(chunk)] = active
                send_a[lax.div(chunk, 2), cut, half_chunk(chunk)] = active.astype(FULL)

            tiles(local_hidden, units_tile)
            act_send(0, chunk)
            active = send_a[lax.div(chunk, 2), :, half_chunk(chunk)].T.astype(LOW)
            tiles(
                width, lambda start, size: put_part(chunk, start, size, dot(active, w_down[:, pl.ds(start, size)]))
            )
            core_copy(1, chunk).start()
            park.wait()
            send_part(1, chunk)
            pl.when(chunk + AHEAD < CHUNKS)(lambda: send_part(0, chunk + AHEAD))

        same = jnp.int32(0)
        for place in range(2 * LINE):
            same = same + jnp.where(cluster_ref[place] == cluster_ref[dp], 1, 0)
        weight_row = 1.0 / jnp.full((1, width), same, jnp.int32).astype(FULL)

        def feed_backward(chunk):
            loads = load_all(
                ((xhat_park.at[chunk], xbuf), (cot_hbm.at[chunk_rows(chunk)], cotbuf))
            )
            branch = take_part(1, chunk)
            for copy in loads:
                copy.wait()
            residual = alpha * (xbuf[...] * norms[0:1, :] + norms[1:2, :]) + branch
            centered = residual - row_mean(residual)
            rstd = lax.rsqrt(row_mean(centered * centered) + norm_eps)
            xhat = centered * rstd
            obuf[...] = (xhat * norms[2:3, :] + norms[3:4, :]).astype(LOW)
            grad_out = cotbuf[...].astype(FULL) * weight_row
            vectors[2:3, :] += jnp.sum(grad_out * xhat, axis=0, keepdims=True)
            vectors[3:4, :] += jnp.sum(grad_out, axis=0, keepdims=True)
            grad_x = grad_out * norms[2:3, :]
            grad_two = (grad_x - row_mean(grad_x) - xhat * row_mean(grad_x * xhat)) * rstd
            for place in range(width // inner):
                gbuf[place * rows : (place + 1) * rows, :] = grad_two[:, place * inner : (place + 1) * inner]
            stores = load_all(
                ((obuf, block_out.at[chunk_rows(chunk)]), (gbuf, grad_two_park.at[chunk]))
            )
            grad_low = grad_two.astype(LOW)
            put_blocks(grad_low.astype(FULL))
            for place in range(2):
                two_own[place, chunk_rows(chunk), :] = blocks[2 * z + place].astype(LOW)
            for place in range(LINE):
                two_send[place, chunk] = blocks[2 * place + core]
            for step in range(1, LINE):
                two_copy(step, chunk).start()

            def units_tile(start, size):
                cut = pl.ds(start, size)
                grad_act = dot_nt(w_down[cut, :], grad_low)
                for which in range(2):
                    low = (grad_act * gate_up[which, cut, chunk_lanes(chunk)]).astype(LOW)
                    grads_low[pl.ds(which * shift + start, size), chunk_lanes(chunk)] = low
                    gate_up[which, cut, chunk_lanes(chunk)] = low.astype(FULL)

            spread(local_hidden, units_tile)
            pair_copy(0, chunk).start()
            for copy in stores:
                copy.wait()

        def step(turn, carried):
            pl.when(turn < CHUNKS)(lambda: feed_forward(turn))
            pl.when(turn == 1)(lambda: rows_copy().wait())
            pl.when(turn > 0)(lambda: feed_backward(turn - 1))
            return carried

        lax.fori_loop(0, CHUNKS + 1, step, 0)

        def hidden_part(pair):
            both = pl.ds(pl.multiple_of(2 * rows * pair, 2 * rows), 2 * rows)
            grad_gate = gate_up[0, :, both].T.astype(LOW)
            grad_up = gate_up[1, :, both].T.astype(LOW)

            def columns(start, size):
                cut = pl.ds(start, size)
                value = dot(grad_gate, w_gate[:, cut]) + dot(grad_up, w_up[:, cut])
                put_part(2 * pair, start, size, value[:rows])
                put_part(2 * pair + 1, start, size, value[rows:])

            tiles(width, columns)
            for place in range(2):
                core_copy(2, 2 * pair + place).start()
            for place in range(2):
                send_part(2, 2 * pair + place)

        lax.fori_loop(0, CHUNKS // 2, lambda pair, carried: (hidden_part(pair), carried)[1], 0)

    pl.run_scoped(
        middle_scope,
        pltpu.VMEM((local_hidden, width), LOW),
        pltpu.VMEM((local_hidden, width), LOW),
        pltpu.VMEM((local_hidden, width), LOW),
        pltpu.VMEM((rows, width), LOW),
    )

    def last_scope(theirs, cols_theirs, two_theirs, att_theirs, send_b, stage, grad_att, grad_one_own, sums, sums_up, sums_down, sums_below, sums_above, late_own):
        def norm_backward(chunk):
            loads = load_all(((xhat_park.at[chunk], xbuf), (grad_two_park.at[chunk], gbuf)))
            branch = take_part(2, chunk)
            for copy in loads:
                copy.wait()
            grad_two = [gbuf[place * rows : (place + 1) * rows, :] for place in range(width // inner)]
            grad_hidden = alpha * jnp.concatenate(grad_two, axis=1) + branch
            xhat = xbuf[...]
            vectors[0:1, :] += jnp.sum(grad_hidden * xhat, axis=0, keepdims=True)
            vectors[1:2, :] += jnp.sum(grad_hidden, axis=0, keepdims=True)
            grad_x = grad_hidden * norms[0:1, :]
            grad_one = (grad_x - row_mean(grad_x) - xhat * row_mean(grad_x * xhat)) * rstd_one[chunk]
            put_blocks(grad_one)
            for place in range(2):
                grad_one_own[chunk_rows(chunk), place * block : (place + 1) * block] = blocks[2 * mp + place]
            grad_low = grad_one.astype(LOW)
            put_blocks(grad_low.astype(FULL))
            keep_columns(late_own, chunk)
            grad_mixed = dot(grad_low, w_dense[...]).astype(LOW)
            for place in range(heads_here):
                grad_att[place, chunk_rows(chunk), :] = grad_mixed[:, place * HD : (place + 1) * HD]

        def fetch_columns(kind):
            forward = forward_copy(kind)
            forward.start()
            forward.wait()
            for pair in range(2):
                moved(
                    [(r_cols.at[kind, 2 * pair + place], blocks.at[pl.ds(CHUNKS * place, CHUNKS)]) for place in range(2)]
                )
                for place in range(2):
                    for chunk in range(CHUNKS):
                        piece = blocks[CHUNKS * place + chunk].astype(LOW)
                        cols_theirs[kind, 2 * pair + place, chunk * rows : (chunk + 1) * rows, :] = piece

        def fetch_rows(source, target):
            size = source.shape[0]
            views = [stage.at[place, pl.ds(0, size)] for place in range(2)]
            moved([(source.at[:, pl.ds(block * place, block)], views[place]) for place in range(2)])
            for place in range(2):
                target[:, block * place : block * (place + 1)] = views[place][...].astype(LOW)

        def outer_product(target, kind, place, own, other):
            right, right_theirs = (cols_own, late_own)[kind][place], cols_theirs[kind, place]

            def rows_tile(start, size):
                cut = pl.ds(start, size)
                target[cut, :] = dot(own[cut, :], right) + dot(other[cut, :], right_theirs)

            tiles(target.shape[0], rows_tile)

        def down_products():
            for step in range(1, LINE):
                for chunk in range(CHUNKS):
                    two_copy(step, chunk).wait()
            for step in range(1, LINE):
                two_forward(step).start()
            for step in range(1, LINE):
                two_forward(step).wait()
            for chunk in range(CHUNKS):
                pl.when(at_end)(lambda: act_take(1, chunk))
                act_take(2, chunk)
            for step in range(LINE):
                owner = lax.rem(z + step, LINE)
                if step:
                    moved(
                        [
                            (r_two.at[owner, place], blocks.at[pl.ds(CHUNKS * place, CHUNKS)])
                            for place in range(2)
                        ]
                    )
                    for place in range(2):
                        for chunk in range(CHUNKS):
                            piece = blocks[CHUNKS * place + chunk].astype(LOW)
                            two_theirs[place, chunk * rows : (chunk + 1) * rows, :] = piece
                    fetch_rows(r_act.at[owner], theirs.at[0])
                left, right = (theirs.at[0], two_theirs) if step else (act_low, two_own)
                for place in range(2):
                    lanes = slice(place * block, (place + 1) * block)

                    def rows_tile(start, size):
                        cut = pl.ds(start, size)
                        product = dot(left[cut, :], right[place])
                        gate_up[0, cut, lanes] = gate_up[0, cut, lanes] + product if step else product

                    tiles(local_hidden, rows_tile)

        def down_copy():
            return remote(gate_up.at[0, :, half_lanes(1 - y)], r_dny, dny_s, dny_r, y_peer)

        def down_end():
            down_copy().wait()
            moved([(r_dny, stage.at[0])])
            stage[0] = stage[0] + gate_up[0, :, half_lanes(y)]
            moved([(stage.at[0], out_down)])
            for chunk in range(CHUNKS):
                for way in range(2):
                    for hop in range(1, LINE - 1):
                        active, copy = act_copy(way, hop, chunk)
                        pl.when(active)(copy.wait_send)

        def goes(slot, way):
            return z < slot if way == 0 else z > LINE - 1 - slot

        def inner_place(way):
            return z > 0 if way == 0 else z < LINE - 1

        def line_goal(way):
            return at(z_to=jnp.clip(z + 1 - 2 * way, 0, LINE - 1))

        def unit_terms(kind):
            return grads_low.at[pl.ds(pl.multiple_of(kind * shift, 16), local_hidden)], theirs.at[1 + kind]

        def count(way):
            return LINE - 1 - z if way == 0 else z

        def order(kind, slot, way):
            return kind * count(way) + slot - (LINE - count(way))

        def turn_of(number, way):
            many = jnp.maximum(count(way), 1)
            return lax.div(number, many) * (LINE - 1) + lax.rem(number, many) + LINE - 1 - count(way)

        def unit_copy(turn, way):
            kind, slot = lax.div(turn, LINE - 1), lax.rem(turn, LINE - 1)
            home = (send_a, send_b)[way].at[lax.rem(jnp.maximum(order(kind, slot + 1, way), 0), 2)]
            return remote(
                home, r_rs.at[kind, slot, way], rs_s.at[kind, slot, way], rs_r.at[kind, slot, way], line_goal(way)
            )

        def unit_sent(number, way):
            unit_copy(turn_of(jnp.maximum(number, 0), way), way).wait_send()

        def unit_slot(turn):
            kind, slot = lax.div(turn, LINE - 1), lax.rem(turn, LINE - 1) + 1
            own, other = unit_terms(kind)
            for way in range(2):

                @pl.when(goes(slot, way))
                def _():
                    number = order(kind, slot, way)
                    home = (send_a, send_b)[way].at[lax.rem(jnp.maximum(number, 0), 2)]
                    pl.when(number >= 2)(lambda: unit_sent(number - 2, way))
                    place = LINE - slot + z if way == 0 else slot - LINE + z
                    outer_product(home, 0, place, own, other)

                    @pl.when((slot > 1) & inner_place(way))
                    def _():
                        before = jnp.maximum(turn - 1, 0)
                        unit_copy(before, way).wait_recv()
                        landed = r_rs.at[lax.div(before, LINE - 1), lax.rem(before, LINE - 1), way]
                        moved([(landed, stage.at[way])])
                        home[...] = home[...] + stage[way]

                    unit_copy(turn, way).start()

        def unit_end(kind):
            own, other = unit_terms(kind)
            outer_product(stage.at[0], 0, z, own, other)
            for way in range(2):

                @pl.when(inner_place(way))
                def _():
                    unit_copy(kind * (LINE - 1) + LINE - 2, way).wait_recv()
                    moved([(r_rs.at[kind, LINE - 2, way], stage.at[1])])
                    stage[0] = stage[0] + stage[1]

            moved([(stage.at[0], (out_gate, out_up)[kind])])

        def late_home(slot, way):
            number = jnp.maximum(order(2, slot, way), 0)
            return (send_a, send_b)[way].at[lax.rem(number, 2), pl.ds(0, inner)]

        def late_copy(slot, way):
            return remote(
                late_home(slot, way), r_rsd.at[slot - 1, way], rs_s.at[2, slot - 1, way], rs_r.at[2, slot - 1, way],
                line_goal(way),
            )

        def late_slot(slot):
            for way in range(2):

                @pl.when(goes(slot, way))
                def _():
                    home = late_home(slot, way)
                    number = order(2, slot, way)
                    of_units = number - 2 < 2 * count(way)
                    pl.when(of_units)(lambda: unit_sent(number - 2, way))
                    if slot == LINE - 1:
                        pl.when(~of_units)(lambda: late_copy(slot - 2, way).wait_send())
                    place = LINE - slot + z if way == 0 else slot - LINE + z
                    outer_product(home, 1, place, att_turned, att_theirs)
                    if slot > 1:

                        @pl.when(inner_place(way))
                        def _():
                            late_copy(slot - 1, way).wait_recv()
                            arrived = stage.at[way, pl.ds(0, inner)]
                            moved([(r_rsd.at[slot - 2, way], arrived)])
                            home[...] = home[...] + arrived[...]

                    late_copy(slot, way).start()

        def last_sent(way):
            pl.when(goes(LINE - 1, way))(lambda: late_copy(LINE - 1, way).wait_send())
            pl.when(goes(LINE - 2, way))(lambda: late_copy(LINE - 2, way).wait_send())
            pl.when(count(way) == 1)(lambda: unit_sent(1, way))

        def late_end():
            total, arrived = stage.at[0, pl.ds(0, inner)], stage.at[1, pl.ds(0, inner)]
            outer_product(total, 1, z, att_turned, att_theirs)
            for way in range(2):

                @pl.when(inner_place(way))
                def _():
                    late_copy(LINE - 1, way).wait_recv()
                    moved([(r_rsd.at[LINE - 2, way], arrived)])
                    total[...] = total[...] + arrived[...]

            gbuf[0:block, :] = total[...].T
            moved([(gbuf.at[pl.ds(0, block)], out_dense)])
            for way in range(2):
                last_sent(way)

        def attention_backward(place, carried):
            hot_t = hot_turned[...]
            queries, keys, values = heads[0, place], heads[1, place], heads[2, place]
            grad_mixed = grad_att[place]
            probability = probabilities(queries, keys)
            grad_prob = dot_nt(grad_mixed, values)
            centre = jnp.sum(grad_prob * probability, axis=-1, keepdims=True)
            grad_scores = (probability * (grad_prob - centre)).astype(LOW)
            grad_queries = dot(grad_scores, keys) * score_scale
            grad_keys = dot_tn(grad_scores, queries) * score_scale
            grad_values = dot_tn(probability.astype(LOW), grad_mixed)
            sums[0, 0:vocab, head_lanes(place)] = dot(hot_t, turn_by(grad_queries, -sin_ref[...]).astype(LOW))
            sums[0, 0:vocab, head_lanes(place, inner)] = dot(hot_t, turn_by(grad_keys, -sin_ref[...]).astype(LOW))
            sums[1, 0:vocab, head_lanes(place)] = dot(hot_t, grad_values.astype(LOW))
            return carried

        def small_sums():
            lax.fori_loop(0, heads_here, attention_backward, 0)
            hot_t = hot_turned[...]
            high, rest = split_low(grad_one_own[...])
            sums[1, 0:vocab, heads_here * HD :] = dot(hot_t, high) + dot(hot_t, rest)
            for side in range(2):
                sums[side, vocab:, :] = vectors[:, side * (width // 2) : (side + 1) * (width // 2)]
            sums_pair().start()

        def sums_pair():
            return remote(sums.at[1 - y], r_sums.at[0], sums_s.at[0], sums_r.at[0], y_peer)

        def sums_line(way):
            source = (sums_up, sums_down)[way]
            goal = jnp.clip(z + 1 - 2 * way, 0, LINE - 1)
            return remote(source, r_sums.at[1 + way], sums_s.at[1 + way], sums_r.at[1 + way], at(z_to=goal))

        def sums_back():
            return remote(sums.at[y], r_sums.at[3], sums_s.at[3], sums_r.at[3], y_peer)

        def sums_first():
            sums_pair().wait()
            moved([(r_sums.at[0], sums_below)])
            sums[y] = sums[y] + sums_below[...]

            @pl.when(z == 0)
            def _():
                sums_up[...] = sums[y]
                sums_line(0).start()

            @pl.when(z == LINE - 1)
            def _():
                sums_down[...] = sums[y]
                sums_line(1).start()

        def sums_up_step():
            sums_line(0).wait_recv()
            moved([(r_sums.at[1], sums_below)])
            sums_up[...] = sums[y] + sums_below[...]
            sums_line(0).start()

        def sums_down_step():
            sums_line(1).wait_recv()
            moved([(r_sums.at[2], sums_above)])
            sums_down[...] = sums[y] + sums_above[...]
            sums_line(1).start()

        def sums_near():
            pl.when(z == 1)(sums_up_step)
            pl.when(z == LINE - 2)(sums_down_step)

        def sums_far():
            pl.when(z == LINE - 2)(sums_up_step)
            pl.when(z == 1)(sums_down_step)

        def sums_middle():
            @pl.when(z == LINE - 1)
            def _():
                sums_line(0).wait_recv()
                moved([(r_sums.at[1], sums_below)])

            @pl.when(z == 0)
            def _():
                sums_line(1).wait_recv()
                moved([(r_sums.at[2], sums_above)])

            @pl.when(z > 0)
            def _():
                sums[y] = sums[y] + sums_below[...]

            @pl.when(z < LINE - 1)
            def _():
                sums[y] = sums[y] + sums_above[...]

            sums_back().start()

        def sums_end():
            sums_back().wait()
            pl.when(z < LINE - 1)(sums_line(0).wait_send)
            pl.when(z > 0)(sums_line(1).wait_send)
            moved([(r_sums.at[3], sums.at[1 - y])])
            lanes = pl.ds(pl.multiple_of(lax.rem(dp, LINE) * block, block), block)
            moved([(sums.at[lax.div(dp, LINE), pl.ds(vocab, 8), lanes], out_norms)])

        def by_token(kind, rows_of):
            side, start = ((0, 0), (0, inner), (1, 0), (1, inner))[kind]
            return sums[side, rows_of, start : start + inner]

        def head_gradients():
            own_columns = emb[:, pl.ds(pl.multiple_of(dp * block, block), block)]
            for kind, result in enumerate((out_query, out_key, out_value)):
                high, rest = split_low(by_token(kind, slice(0, vocab)))
                gbuf[0:block, :] = dot_tn(own_columns, high) + dot_tn(own_columns, rest)
                moved([(gbuf.at[pl.ds(0, block)], result)])

        table_rows = vocab // (2 * LINE)
        table_own = pl.ds(pl.multiple_of(dp * table_rows, table_rows), table_rows)

        def table_part():
            for kind, weight in enumerate((w_query_hbm, w_key_hbm, w_value_hbm)):
                moved([(weight, w_dense)])
                pieces = jnp.concatenate(split_low(by_token(kind, table_own)), axis=0)

                def columns(start, size):
                    cut = pl.ds(start, size)
                    both = dot_nt(pieces, w_dense[cut, :])
                    both = both[:table_rows] + both[table_rows:]
                    xbuf[0:table_rows, cut] = both if kind == 0 else xbuf[0:table_rows, cut] + both

                tiles(width, columns)
            quarter = pl.ds(pl.multiple_of(mp * inner, inner), inner)
            xbuf[0:table_rows, quarter] = xbuf[0:table_rows, quarter] + alpha * by_token(3, table_own)
            table_copy(0).start()

        def table_middle():
            table_copy(0).wait()
            xbuf[table_rows : 2 * table_rows, :] = xbuf[0:table_rows, :] + table_core[...]
            table_copy(1).start()

        def table_end():
            table_copy(1).wait()
            xbuf[0:table_rows, :] = 0.1 * (xbuf[table_rows : 2 * table_rows, :] + table_x[...])
            moved([(xbuf.at[pl.ds(0, table_rows)], out_table)])

        def table_copy(turn):
            target, device = ((table_core, core_peer), (table_x, x_peer))[turn]
            return remote(xbuf.at[pl.ds(turn * table_rows, table_rows)], target, table_s.at[turn], table_r.at[turn], device)

        def act_pass():
            for chunk in range(CHUNKS):
                act_take(1, chunk)
                act_send(2, chunk)

        def down_all():
            down_products()
            down_copy().start()

        at_end = (z == 0) | (z == LINE - 1)

        for chunk in range(CHUNKS):
            cols_copy(0, chunk).wait()
        fetch_columns(0)
        for chunk in range(CHUNKS):
            pair_copy(0, chunk).wait()
        pair_copy(1, 0).start()
        pair_copy(1, 1).start()
        fetch_rows(r_y.at[0], theirs.at[1])
        for chunk in range(CHUNKS):
            for way in range(2):
                active, copy = act_copy(way, 0, chunk)
                pl.when(active)(copy.wait_send)
        def one_turn(turn, carried):
            unit_slot(turn)

            @pl.when(turn == 0)
            def _():
                for chunk in range(CHUNKS):
                    act_take(0, chunk)
                    act_send(1, chunk)

            @pl.when(turn == 1)
            def _():
                every_chunk(norm_backward)
                small_sums()
                pl.when(~at_end)(act_pass)
                sums_first()
                pair_copy(1, 2).start()
                pair_copy(1, 3).start()
                for chunk in range(CHUNKS):
                    cols_copy(1, chunk).start()

            @pl.when(turn == 2)
            def _():
                for chunk in range(CHUNKS):
                    pair_copy(1, chunk).wait()
                fetch_rows(r_y.at[1], theirs.at[2])

            pl.when(turn == 3)(sums_near)
            pl.when((turn == 3) & ~at_end | (turn == 5) & at_end)(down_all)
            pl.when(turn == 4)(sums_far)
            return carried

        lax.fori_loop(0, 2 * (LINE - 1), one_turn, 0)
        unit_end(0)
        for chunk in range(CHUNKS):
            cols_copy(1, chunk).wait()
        fetch_columns(1)
        fetch_rows(r_att, att_theirs)
        late_slot(1)
        sums_middle()
        sums_end()
        head_gradients()
        table_part()
        late_slot(2)
        table_middle()
        unit_end(1)
        late_slot(3)
        table_end()
        down_end()
        late_end()

    pl.run_scoped(
        last_scope,
        pltpu.VMEM((3, local_hidden, length), LOW),
        pltpu.VMEM((2, LINE, length, block), LOW),
        pltpu.VMEM((2, length, block), LOW),
        pltpu.VMEM((inner, length), LOW),
        pltpu.VMEM((2, local_hidden, block), FULL),
        pltpu.VMEM((2, local_hidden, block), FULL),
        pltpu.VMEM((heads_here, length, HD), LOW),
        pltpu.VMEM((length, 2 * block), FULL),
        pltpu.VMEM((2,) + r_sums.shape[1:], FULL),
        pltpu.VMEM(r_sums.shape[1:], FULL),
        pltpu.VMEM(r_sums.shape[1:], FULL),
        pltpu.VMEM(r_sums.shape[1:], FULL),
        pltpu.VMEM(r_sums.shape[1:], FULL),
        pltpu.VMEM(cols_own.shape, LOW),
    )


def local_fast(
    token_ids,
    prefix_lengths,
    cluster_ids,
    embedding,
    w_query,
    w_key,
    w_value,
    w_dense,
    w_gate,
    w_up,
    w_down,
    norm1_gain,
    norm1_bias,
    norm2_gain,
    norm2_bias,
    cotangent,
):
    length = token_ids.shape[0]
    vocab, width = embedding.shape
    inner = w_query.shape[1]
    heads_here = inner // HD
    local_hidden = w_gate.shape[1]
    rows = length // CHUNKS
    block = width // (2 * LINE)
    shift = (local_hidden + 15) // 16 * 16
    frequency = 10000.0 ** (np.arange(HD // 2) * (-2.0 / HD))
    angles = np.arange(length)[:, None] * frequency[None, :]
    cosine = np.concatenate([np.cos(angles)] * 2, axis=1).astype(np.float32)
    sine = np.concatenate([-np.sin(angles), np.sin(angles)], axis=1).astype(np.float32)
    norms = jnp.stack([norm1_gain, norm1_bias, norm2_gain, norm2_bias])

    hbm = pl.BlockSpec(memory_space=pl.ANY)
    vmem = pl.BlockSpec(memory_space=pltpu.VMEM)
    smem = pl.BlockSpec(memory_space=pltpu.SMEM)
    sums_rows = vocab + 8
    table_rows = vocab // (2 * LINE)
    shapes = [
        ((length, width), LOW),
        ((table_rows, width), FULL),
        ((block, inner), FULL),
        ((block, inner), FULL),
        ((block, inner), FULL),
        ((block, inner), FULL),
        ((local_hidden, block), FULL),
        ((local_hidden, block), FULL),
        ((local_hidden, block), FULL),
        ((8, block), FULL),
        ((LINE, local_hidden, length), FULL),
        ((LINE, 2, CHUNKS, rows, block), FULL),
        ((2, local_hidden, length), FULL),
        ((2, LINE, CHUNKS, rows, block), FULL),
        ((inner, length), FULL),
        ((CHUNKS, rows, width), FULL),
        ((CHUNKS, length, inner), FULL),
        ((local_hidden, block), FULL),
        ((2, LINE - 1, 2, local_hidden, block), FULL),
        ((LINE - 1, 2, inner, block), FULL),
        ((4, sums_rows, width // 2), FULL),
    ]
    scratch = [
        ((CHUNKS, 2, rows, width // 2), FULL),
        ((CHUNKS, rows, width // 2), FULL),
        ((2, CHUNKS, rows, width // 2), FULL),
        ((CHUNKS, rows, width // 2), FULL),
        ((2 * LINE, rows, block), FULL),
        ((rows, width), FULL),
        ((length, inner), FULL),
        ((rows, width), LOW),
        ((2, local_hidden, length), FULL),
        ((2 * shift, length), LOW),
        ((local_hidden, length), LOW),
        ((2, local_hidden, block), FULL),
        ((LINE, length, block), LOW),
        ((2, CHUNKS, rows, block), FULL),
        ((2, length, block), LOW),
        ((LINE, CHUNKS, rows, block), FULL),
        ((length, inner), LOW),
        ((inner, length), LOW),
        ((3, heads_here, length, HD), LOW),
        ((width, inner), LOW),
        ((length, vocab), LOW),
        ((vocab, length), LOW),
        ((CHUNKS, rows, 1), FULL),
        ((8, width), FULL),
        ((table_rows, width), FULL),
        ((table_rows, width), FULL),
    ]
    dma = pltpu.SemaphoreType.DMA
    each = (3, CHUNKS)
    semaphores = [
        each, each, each, each, each, each, (2, LINE - 1, CHUNKS), (2, LINE - 1, CHUNKS), each, each, (3,), (3,),
        (2, CHUNKS), (2, CHUNKS), (2,), (2,), (2, CHUNKS), (2, CHUNKS), None, None, None, None,
        (3, LINE - 1, 2), (3, LINE - 1, 2), (4,), (4,), (2,), (2,), (4,), (4,),
    ]
    results = pl.pallas_call(
        functools.partial(layer_kernel, length, width, local_hidden),
        out_shape=[jax.ShapeDtypeStruct(shape, dtype) for shape, dtype in shapes],
        in_specs=[smem] * 2 + [vmem] * 5 + [hbm] * 8,
        out_specs=[hbm] * len(shapes),
        scratch_shapes=[pltpu.VMEM(shape, dtype) for shape, dtype in scratch]
        + [dma if shape is None else dma(shape) for shape in semaphores],
        compiler_params=pltpu.CompilerParams(
            collective_id=0, has_side_effects=True, vmem_limit_bytes=62 * 2**20
        ),
    )(
        prefix_lengths,
        cluster_ids,
        token_ids.reshape(1, length),
        embedding,
        cosine,
        sine,
        norms,
        w_query,
        w_key,
        w_value,
        w_dense,
        w_gate.T,
        w_up.T,
        w_down.T,
        cotangent,
    )
    block_out, table, out_query, out_key, out_value, out_dense, out_gate, out_up, out_down, out_norms = results[:10]
    return (
        block_out,
        table,
        out_query,
        out_key,
        out_value,
        out_dense,
        out_gate.T,
        out_up.T,
        out_down.T,
        out_norms[0],
        out_norms[1],
        out_norms[2],
        out_norms[3],
    )


def solution(mesh):
    fast = mesh.shape["dp"] == 2 * LINE and mesh.shape["mp"] == 4
    return jax.shard_map(
        local_fast if fast else local_general,
        mesh=mesh,
        in_specs=(
            P("dp"),
            P("dp"),
            P(),
            P(),
            P(None, "mp"),
            P(None, "mp"),
            P(None, "mp"),
            P(None, "mp"),
            P(None, "mp"),
            P(None, "mp"),
            P(None, "mp"),
            P(),
            P(),
            P(),
            P(),
            P("dp", None),
        ),
        out_specs=(
            P("dp", None),
            P("dp", None),
            P("dp", "mp"),
            P("dp", "mp"),
            P("dp", "mp"),
            P("dp", "mp"),
            P("dp", "mp"),
            P("dp", "mp"),
            P("dp", "mp"),
            P("dp"),
            P("dp"),
            P("dp"),
            P("dp"),
        ),
        check_vma=False,
    )
```

```python
import functools
import math

import jax
import jax.numpy as jnp
import numpy as np
from jax import lax
from jax.experimental import pallas as pl
from jax.experimental.pallas import tpu as pltpu
from jax.sharding import PartitionSpec as P

HD = 128
FF_USED = 5461


deep_alpha = math.sqrt(48.0)
norm_eps = 1e-05
highest = lax.Precision.HIGHEST


def layer_norm(inputs, norm_gain, norm_bias):
    center = jnp.mean(inputs, axis=-1, keepdims=True)
    centered = inputs - center
    spread = jnp.mean(centered * centered, axis=-1, keepdims=True)
    return centered * lax.rsqrt(spread + norm_eps) * norm_gain + norm_bias


def rotary_tables(length, head_width):
    half_width = head_width // 2
    frequency = jnp.exp(
        jnp.arange(half_width, dtype=jnp.float32) * (-2.0 * math.log(10000.0) / head_width)
    )
    angles = jnp.arange(length, dtype=jnp.float32)[:, None] * frequency[None, :]
    return (jnp.cos(angles), jnp.sin(angles))


def rotate(inputs, cosine, sine):
    half_width = inputs.shape[-1] // 2
    first = inputs[..., :half_width]
    second = inputs[..., half_width:]
    cosine = cosine[:, None, :]
    sine = sine[:, None, :]
    return jnp.concatenate(
        [first * cosine - second * sine, second * cosine + first * sine], axis=-1
    )


def row_mask(row_begin, row_count, length, prefix):
    columns = jnp.arange(length, dtype=jnp.int32)
    row_index = row_begin + jnp.arange(row_count, dtype=jnp.int32)
    return (columns[None, :] < prefix) | (columns[None, :] <= row_index[:, None])


def block_scores(query_block, keys_rot, visible, score_scale):
    scores = (
        jnp.einsum("bhd,khd->hbk", query_block, keys_rot, preferred_element_type=jnp.float32)
        * score_scale
    )
    return jnp.where(visible[None, :, :], scores, -1e30)


def attention_forward(queries, keys_rot, values_in, prefix, row_block):
    length = queries.shape[0]
    score_scale = 1.0 / math.sqrt(HD)

    def one_block(row_begin):
        scores = block_scores(
            queries, keys_rot, row_mask(row_begin, row_block, length, prefix), score_scale
        )
        row_max = jnp.max(scores, axis=-1, keepdims=True)
        weights = jnp.exp(scores - row_max)
        total_weight = jnp.sum(weights, axis=-1, keepdims=True)
        probability = (weights / total_weight).astype(jnp.bfloat16)
        mixed_block = jnp.einsum(
            "hbk,khd->bhd", probability, values_in, preferred_element_type=jnp.float32
        )
        return (mixed_block, row_max + jnp.log(total_weight))

    starts = jnp.arange(length // row_block, dtype=jnp.int32) * row_block
    attended, log_total = lax.map(one_block, starts)
    return (attended.reshape(length, -1), log_total)


def attention_backward(queries, keys_rot, values_in, prefix, row_block, log_total, grad_mixed):
    length = queries.shape[0]
    score_scale = 1.0 / math.sqrt(HD)

    def one_block(carried, inputs):
        grad_keys, grad_values = carried
        row_begin, block_total = inputs
        scores = block_scores(
            queries, keys_rot, row_mask(row_begin, row_block, length, prefix), score_scale
        )
        probability = jnp.exp(scores - block_total)
        prob_low = probability.astype(jnp.bfloat16)
        grad_prob = jnp.einsum(
            "bhd,khd->hbk", grad_mixed, values_in, preferred_element_type=jnp.float32
        )
        centre = jnp.sum(grad_prob * probability, axis=-1, keepdims=True)
        grad_scores = (probability * (grad_prob - centre)).astype(jnp.bfloat16)
        grad_query = (
            jnp.einsum("hbk,khd->bhd", grad_scores, keys_rot, preferred_element_type=jnp.float32)
            * score_scale
        )
        grad_keys = (
            grad_keys
            + jnp.einsum("hbk,bhd->khd", grad_scores, queries, preferred_element_type=jnp.float32)
            * score_scale
        )
        grad_values = grad_values + jnp.einsum(
            "hbk,bhd->khd", prob_low, grad_mixed, preferred_element_type=jnp.float32
        )
        return ((grad_keys, grad_values), grad_query)

    starts = jnp.arange(length // row_block, dtype=jnp.int32) * row_block
    zeros_kv = jnp.zeros(keys_rot.shape, jnp.float32)
    (grad_keys, grad_values), grad_queries = lax.scan(
        one_block, (zeros_kv, zeros_kv), (starts, log_total)
    )
    return (grad_queries.reshape(queries.shape), grad_keys, grad_values)


def local_general(
    token_ids,
    prefix_lengths,
    cluster_ids,
    embedding,
    w_query,
    w_key,
    w_value,
    w_dense,
    w_gate,
    w_up,
    w_down,
    norm1_gain,
    norm1_bias,
    norm2_gain,
    norm2_bias,
    cotangent,
):
    length = token_ids.shape[0]
    vocab_rows = embedding.shape[0]
    row_block = min(512, length)
    local_heads = w_query.shape[1] // HD
    local_hidden = w_gate.shape[1]
    one_hot = (token_ids[:, None] == jnp.arange(vocab_rows, dtype=jnp.int32)[None, :]).astype(
        jnp.bfloat16
    )
    embedded_low = jnp.dot(one_hot, embedding, preferred_element_type=jnp.float32).astype(
        jnp.bfloat16
    )
    embedded = embedded_low.astype(jnp.float32)
    cosine, sine = rotary_tables(length, HD)
    prefix = prefix_lengths[0]
    own_cluster = cluster_ids[lax.axis_index("dp")]
    seq_weight = 1.0 / jnp.sum((cluster_ids == own_cluster).astype(jnp.float32))

    def project(weight_in):
        return jnp.dot(embedded_low, weight_in, preferred_element_type=jnp.float32).reshape(
            length, local_heads, HD
        )

    queries = rotate(project(w_query), cosine, sine).astype(jnp.bfloat16)
    keys_rot = rotate(project(w_key), cosine, sine).astype(jnp.bfloat16)
    values_in = project(w_value).astype(jnp.bfloat16)
    attended, log_total = attention_forward(queries, keys_rot, values_in, prefix, row_block)
    attended_low = attended.astype(jnp.bfloat16)
    branch = lax.psum(
        jnp.einsum("lh,dh->ld", attended_low, w_dense, preferred_element_type=jnp.float32), "mp"
    )
    residual_one = deep_alpha * embedded + branch
    hidden, norm_one_pull = jax.vjp(layer_norm, residual_one, norm1_gain, norm1_bias)
    hidden_low = hidden.astype(jnp.bfloat16)
    gate_proj = jnp.dot(hidden_low, w_gate, preferred_element_type=jnp.float32)
    up_proj = jnp.dot(hidden_low, w_up, preferred_element_type=jnp.float32)
    unit_index = lax.axis_index("mp") * local_hidden + jnp.arange(local_hidden, dtype=jnp.int32)
    used_mask = (unit_index < FF_USED).astype(jnp.float32)

    def gated_unit(gate_in, up_in):
        return jax.nn.gelu(gate_in, approximate=True) * up_in * used_mask

    activation, gated_pull = jax.vjp(gated_unit, gate_proj, up_proj)
    activation_low = activation.astype(jnp.bfloat16)
    branch_two = lax.psum(
        jnp.einsum("lf,df->ld", activation_low, w_down, preferred_element_type=jnp.float32), "mp"
    )
    residual_two = deep_alpha * hidden + branch_two
    final, norm_two_pull = jax.vjp(layer_norm, residual_two, norm2_gain, norm2_bias)
    grad_out = cotangent.astype(jnp.float32) * seq_weight
    grad_two, grad_gain_two, grad_bias_two = norm_two_pull(grad_out)
    grad_branch_two = grad_two.astype(jnp.bfloat16)
    grad_w_down = jnp.einsum(
        "ld,lf->df", grad_branch_two, activation_low, preferred_element_type=jnp.float32
    )
    grad_act = jnp.dot(grad_branch_two, w_down, preferred_element_type=jnp.float32)
    grad_gate, grad_up = gated_pull(grad_act)
    grad_gate_low = grad_gate.astype(jnp.bfloat16)
    grad_up_low = grad_up.astype(jnp.bfloat16)
    grad_w_gate = jnp.einsum(
        "ld,lf->df", hidden_low, grad_gate_low, preferred_element_type=jnp.float32
    )
    grad_w_up = jnp.einsum("ld,lf->df", hidden_low, grad_up_low, preferred_element_type=jnp.float32)
    hidden_part = jnp.einsum(
        "lf,df->ld", grad_gate_low, w_gate, preferred_element_type=jnp.float32
    ) + jnp.einsum("lf,df->ld", grad_up_low, w_up, preferred_element_type=jnp.float32)
    grad_hidden = deep_alpha * grad_two + lax.psum(hidden_part, "mp")
    feed_sums = (
        lax.psum_scatter(grad_w_gate, "dp", scatter_dimension=0, tiled=True),
        lax.psum_scatter(grad_w_up, "dp", scatter_dimension=0, tiled=True),
        lax.psum_scatter(grad_w_down, "dp", scatter_dimension=0, tiled=True),
        lax.psum_scatter(grad_gain_two, "dp", scatter_dimension=0, tiled=True),
        lax.psum_scatter(grad_bias_two, "dp", scatter_dimension=0, tiled=True),
    )
    grad_one, grad_gain_one, grad_bias_one = norm_one_pull(grad_hidden)
    grad_branch = grad_one.astype(jnp.bfloat16)
    grad_w_dense = jnp.einsum(
        "ld,lh->dh", grad_branch, attended_low, preferred_element_type=jnp.float32
    )
    grad_attended = jnp.dot(grad_branch, w_dense, preferred_element_type=jnp.float32).astype(
        jnp.bfloat16
    )
    grad_attended = grad_attended.reshape(length, local_heads, HD)
    grad_queries, grad_keys, grad_values = attention_backward(
        queries, keys_rot, values_in, prefix, row_block, log_total, grad_attended
    )
    grad_query_lin = rotate(grad_queries, cosine, -sine).astype(jnp.bfloat16).reshape(length, -1)
    grad_key_lin = rotate(grad_keys, cosine, -sine).astype(jnp.bfloat16).reshape(length, -1)
    grad_value_lin = grad_values.astype(jnp.bfloat16).reshape(length, -1)
    grad_w_query = jnp.einsum(
        "ld,lh->dh", embedded_low, grad_query_lin, preferred_element_type=jnp.float32
    )
    grad_w_key = jnp.einsum(
        "ld,lh->dh", embedded_low, grad_key_lin, preferred_element_type=jnp.float32
    )
    grad_w_value = jnp.einsum(
        "ld,lh->dh", embedded_low, grad_value_lin, preferred_element_type=jnp.float32
    )
    input_part = (
        jnp.einsum("lh,dh->ld", grad_query_lin, w_query, preferred_element_type=jnp.float32)
        + jnp.einsum("lh,dh->ld", grad_key_lin, w_key, preferred_element_type=jnp.float32)
        + jnp.einsum("lh,dh->ld", grad_value_lin, w_value, preferred_element_type=jnp.float32)
    )
    grad_embedded = deep_alpha * grad_one + lax.psum(input_part, "mp")
    grad_table = 0.1 * jnp.dot(one_hot.astype(jnp.float32).T, grad_embedded, precision=highest)
    attn_sums = (
        lax.psum_scatter(grad_table, "dp", scatter_dimension=0, tiled=True),
        lax.psum_scatter(grad_w_query, "dp", scatter_dimension=0, tiled=True),
        lax.psum_scatter(grad_w_key, "dp", scatter_dimension=0, tiled=True),
        lax.psum_scatter(grad_w_value, "dp", scatter_dimension=0, tiled=True),
        lax.psum_scatter(grad_w_dense, "dp", scatter_dimension=0, tiled=True),
        lax.psum_scatter(grad_gain_one, "dp", scatter_dimension=0, tiled=True),
        lax.psum_scatter(grad_bias_one, "dp", scatter_dimension=0, tiled=True),
    )
    summed = (
        attn_sums[0],
        attn_sums[1],
        attn_sums[2],
        attn_sums[3],
        attn_sums[4],
        feed_sums[0],
        feed_sums[1],
        feed_sums[2],
        attn_sums[5],
        attn_sums[6],
        feed_sums[3],
        feed_sums[4],
    )
    return (
        final.astype(jnp.bfloat16),
        summed[0],
        summed[1],
        summed[2],
        summed[3],
        summed[4],
        summed[5],
        summed[6],
        summed[7],
        summed[8],
        summed[9],
        summed[10],
        summed[11],
    )


LINE = 4
MESH = pl.DeviceIdType.MESH
CHUNKS = 4
AHEAD = 2
LOW = jnp.bfloat16
FULL = jnp.float32
TANH_SCALE = math.sqrt(2.0 / math.pi)


def dot(left, right):
    return jnp.dot(left, right, preferred_element_type=FULL)


def dot_nt(left, right):
    return lax.dot_general(left, right, (((1,), (1,)), ((), ())), preferred_element_type=FULL)


def dot_tn(left, right):
    return lax.dot_general(left, right, (((0,), (0,)), ((), ())), preferred_element_type=FULL)


def split_low(value):
    high = value.astype(LOW)
    return high, (value - high.astype(FULL)).astype(LOW)


def row_mean(value):
    return jnp.mean(value, axis=-1, keepdims=True)


def spread(size, body, tile=512):
    for start in range(0, size, tile):
        body(start, min(tile, size - start))


def tiles(size, body, tile=512):
    whole = size // tile
    lax.fori_loop(0, whole, lambda step, carried: (body(pl.multiple_of(step * tile, tile), tile), carried)[1], 0)
    if size % tile:
        body(whole * tile, size % tile)


def layer_kernel(
    length, width, local_hidden,
    prefix_ref, cluster_ref, ids_row, emb, cos_ref, sin_ref, gain_one, bias_one, gain_two, bias_two, w_query_hbm, w_key_hbm, w_value_hbm, w_dense_hbm,
    w_gate_hbm, w_up_hbm, w_down_hbm, cot_hbm,
    block_out, out_table, out_query, out_key, out_value, out_dense, out_gate, out_up, out_down, out_norms,
    r_act, r_two, r_y, r_cols, r_att, xhat_park, grad_two_park, r_dny, r_rs, r_rsd, r_sums,
    parts, core_in, x_in, back_in, blocks, xbuf, gbuf, obuf, gate_up, grads_low, act_low, send_a, cols_own, cols_send,
    hidden_theirs, two_own, two_send, att_low, att_turned, heads, w_dense, one_hot, hot_turned, rstd_one, vectors, table_core, table_x,
    core_s, core_r, x_s, x_r, back_s, back_r, act_s, act_r, two_s, two_r, fwd_two_s, fwd_two_r, cols_s, cols_r, fwd_s,
    fwd_r, ys_s, ys_r, att_s, att_r, dny_s, dny_r, rs_s, rs_r, sums_s, sums_r, table_s, table_r, load_sem, weight_sem,
):
    dp, mp = lax.axis_index("dp"), lax.axis_index("mp")
    z, y = lax.div(dp, 2), lax.rem(dp, 2)
    x, core = lax.div(mp, 2), lax.rem(mp, 2)
    rows = length // CHUNKS
    heads_here = heads.shape[1]
    inner = heads_here * HD
    vocab = emb.shape[0]
    shift = (local_hidden + 15) // 16 * 16
    near = (local_hidden // 2 + 15) // 16 * 16
    spans = ((0, near), (near, local_hidden - near))
    block = width // (2 * LINE)
    alpha = jnp.float32(deep_alpha)

    def at(z_to=None, y_to=None, x_to=None, core_to=None):
        z_to = z if z_to is None else z_to
        y_to = y if y_to is None else y_to
        x_to = x if x_to is None else x_to
        core_to = core if core_to is None else core_to
        return (2 * z_to + y_to, 2 * x_to + core_to)

    core_peer = at(core_to=1 - core)
    x_peer = at(x_to=1 - x)
    y_peer = at(y_to=1 - y)

    def remote(source, target, send, receive, device):
        return pltpu.make_async_remote_copy(
            src_ref=source, dst_ref=target, send_sem=send, recv_sem=receive,
            device_id=device, device_id_type=MESH,
        )

    def load_all(pairs):
        copies = [
            pltpu.make_async_copy(source, target, load_sem.at[place])
            for place, (source, target) in enumerate(pairs)
        ]
        for copy in copies:
            copy.start()
        return copies

    def moved(pairs):
        for copy in load_all(pairs):
            copy.wait()

    barrier = pltpu.get_barrier_semaphore()
    greeted = [core_peer, x_peer, y_peer] + [at(z_to=lax.rem(z + step, LINE)) for step in range(1, LINE)]
    for device in greeted:
        pl.semaphore_signal(barrier, inc=1, device_id=device, device_id_type=MESH)

    def chunk_rows(chunk):
        return pl.ds(pl.multiple_of(chunk * rows, rows), rows)

    def core_copy(turn, chunk):
        return remote(
            parts.at[chunk, 1 - core], core_in.at[chunk], core_s.at[turn, chunk], core_r.at[turn, chunk], core_peer
        )

    def x_copy(turn, chunk):
        return remote(
            parts.at[chunk, core], x_in.at[turn % 2, chunk], x_s.at[turn, chunk], x_r.at[turn, chunk], x_peer
        )

    def back_copy(turn, chunk):
        return remote(
            parts.at[chunk, core], back_in.at[chunk], back_s.at[turn, chunk], back_r.at[turn, chunk], core_peer
        )

    def put_part(chunk, start, size, value):
        side, first = lax.div(start, width // 2), lax.rem(start, width // 2)
        parts[chunk, side, :, pl.ds(pl.multiple_of(first, size), size)] = value

    def send_part(turn, chunk):
        core_copy(turn, chunk).wait()
        parts[chunk, core] = parts[chunk, core] + core_in[chunk]
        x_copy(turn, chunk).start()

    def take_part(turn, chunk):
        x_copy(turn, chunk).wait()
        parts[chunk, core] = parts[chunk, core] + x_in[turn % 2, chunk]
        back = back_copy(turn, chunk)
        back.start()
        mine = parts[chunk, core]
        back.wait()
        other = back_in[chunk]
        return jnp.concatenate([jnp.where(core == 0, mine, other), jnp.where(core == 0, other, mine)], axis=1)

    def put_blocks(value):
        for place in range(2 * LINE):
            blocks[place] = value[:, place * block : (place + 1) * block]

    def chunk_lanes(chunk):
        return pl.ds(pl.multiple_of(chunk * rows, rows), rows)

    def half_lanes(side):
        return pl.ds(pl.multiple_of(side * block, block), block)

    def keep_columns(own, chunk):
        for place in range(LINE):
            own[place, chunk_rows(chunk), :] = blocks[2 * place + y].astype(LOW)
        for place in range(2):
            cols_send[place, chunk] = blocks[2 * (2 * core + place) + 1 - y]

    def cols_copy(kind, chunk):
        return remote(
            cols_send.at[:, chunk], r_cols.at[kind, pl.ds(2 * core, 2), chunk],
            cols_s.at[kind, chunk], cols_r.at[kind, chunk], y_peer,
        )

    def forward_copy(kind):
        view = r_cols.at[kind, pl.ds(2 * core, 2)]
        return remote(view, view, fwd_s.at[kind], fwd_r.at[kind], core_peer)

    def act_copy(way, hop, chunk):
        goal = jnp.clip(z + 1 - 2 * way, 0, LINE - 1)
        owner = z - hop if way == 0 else z + hop
        active = (owner >= 0) & (z < LINE - 1) if way == 0 else (owner < LINE) & (z > 0)
        owner = jnp.clip(owner, 0, LINE - 1)
        landed = r_act.at[owner, :, chunk_lanes(chunk)]
        source = send_a.at[lax.div(chunk, 2), :, half_chunk(chunk)] if hop == 0 else landed
        return active, remote(
            source, landed, act_s.at[way, hop, chunk], act_r.at[way, hop, chunk], at(z_to=goal)
        )

    def act_landed(way, hop):
        return z - 1 - hop >= 0 if way == 0 else z + 1 + hop < LINE

    def half_chunk(chunk):
        return pl.ds(pl.multiple_of(lax.rem(chunk, 2) * rows, rows), rows)

    def act_send(hop, chunk):
        for way in range(2):
            active, copy = act_copy(way, hop, chunk)
            pl.when(active)(copy.start)

    def act_take(hop, chunk):
        for way in range(2):
            _, copy = act_copy(way, hop, chunk)
            pl.when(act_landed(way, hop))(copy.wait_recv)

    def two_copy(step, chunk):
        goal = lax.rem(z + step, LINE)
        return remote(
            two_send.at[goal, chunk], r_two.at[z, core, chunk],
            two_s.at[step - 1, chunk], two_r.at[step - 1, chunk], at(z_to=goal),
        )

    def two_forward(step):
        view = r_two.at[lax.rem(z + step, LINE), core]
        return remote(view, view, fwd_two_s.at[step - 1], fwd_two_r.at[step - 1], core_peer)

    def pair_copy(which, chunk, part):
        units = pl.ds(*spans[part])
        return remote(
            gate_up.at[which, units, chunk_lanes(chunk)], r_y.at[which, units, chunk_lanes(chunk)],
            ys_s.at[which, chunk, part], ys_r.at[which, chunk, part], y_peer,
        )

    def pair_send(which, chunk):
        for part in range(2):
            pair_copy(which, chunk, part).start()

    def rows_copy():
        return remote(gbuf, r_att, att_s, att_r, y_peer)

    def fetch_columns(kind, target):
        forward = forward_copy(kind)
        forward.start()
        forward.wait()
        for pair in range(2):
            moved(
                [(r_cols.at[kind, 2 * pair + place], blocks.at[pl.ds(CHUNKS * place, CHUNKS)]) for place in range(2)]
            )
            for place in range(2):
                for chunk in range(CHUNKS):
                    piece = blocks[CHUNKS * place + chunk].astype(LOW)
                    target[2 * pair + place, chunk * rows : (chunk + 1) * rows, :] = piece

    def every_chunk(body):
        lax.fori_loop(0, CHUNKS, lambda chunk, carried: (body(chunk), carried)[1], 0)

    column = lax.broadcasted_iota(jnp.int32, (length, length), 1)
    row = lax.broadcasted_iota(jnp.int32, (length, length), 0)
    score_scale = 1.0 / math.sqrt(HD)

    def probabilities(queries, keys):
        visible = (column < prefix_ref[0]) | (column <= row)
        scores = jnp.where(visible, dot_nt(queries, keys) * score_scale, -1e30)
        weights = jnp.exp(scores - jnp.max(scores, axis=-1, keepdims=True))
        return weights / jnp.sum(weights, axis=-1, keepdims=True)

    def turn_by(value, sine):
        return value * cos_ref[...] + pltpu.roll(value, HD // 2, 1) * sine

    def head_lanes(place, offset=0):
        return pl.ds(pl.multiple_of(offset + place * HD, HD), HD)

    def first_scope(w_heads, tab):
        loads = [
            pltpu.make_async_copy(source, target, weight_sem.at[place])
            for place, (source, target) in enumerate(
                (
                    (w_query_hbm, w_heads.at[0]),
                    (w_key_hbm, w_heads.at[1]),
                    (w_value_hbm, w_heads.at[2]),
                    (w_dense_hbm, w_dense),
                )
            )
        ]
        for copy in loads:
            copy.start()
        named = lax.broadcasted_iota(jnp.int32, (vocab, length), 0) == ids_row[...]
        hot = jnp.where(named, 1.0, 0.0)
        hot_turned[...] = hot.astype(LOW)
        one_hot[...] = hot.T.astype(LOW)
        vectors[...] = jnp.zeros_like(vectors)
        for kind in range(3):
            loads[kind].wait()
            table = dot(emb[...], w_heads[kind])
            for place in range(heads_here):
                tab[kind * heads_here + place] = table[:, place * HD : (place + 1) * HD]

        def attend_head(place, carried):
            hot = one_hot[...]
            lin = []
            for kind in range(3):
                high, rest = split_low(tab[kind * heads_here + place])
                lin.append(dot(hot, high) + dot(hot, rest))
            queries = turn_by(lin[0], sin_ref[...]).astype(LOW)
            keys = turn_by(lin[1], sin_ref[...]).astype(LOW)
            values = lin[2].astype(LOW)
            heads[0, place], heads[1, place], heads[2, place] = queries, keys, values
            probability = probabilities(queries, keys).astype(LOW)
            mixed = dot(probability, values).astype(LOW)
            att_low[:, head_lanes(place)] = mixed
            turned = mixed.astype(FULL).T
            head_rows = pl.ds(pl.multiple_of(place * HD, HD), HD)
            att_turned[head_rows, :] = turned.astype(LOW)
            gbuf[head_rows, :] = turned
            return carried

        lax.fori_loop(0, heads_here, attend_head, 0)
        loads[3].wait()
        pl.semaphore_wait(barrier, len(greeted))

        def project(chunk):
            mixed = att_low[chunk_rows(chunk), :]

            def columns(start, size):
                put_part(chunk, start, size, dot_nt(mixed, w_dense[pl.ds(start, size), :]))

            spread(width, columns, 256)
            core_copy(0, chunk).start()
            pl.when((chunk > 0) & (chunk <= AHEAD))(lambda: send_part(0, chunk - 1))

        every_chunk(project)
        rows_copy().start()

    pl.run_scoped(first_scope, pltpu.VMEM((3, width, inner), LOW), pltpu.VMEM((3 * heads_here, vocab, HD), FULL))

    def middle_scope(w_gate, w_up, w_down, cotbuf):
        weight_copies = [
            pltpu.make_async_copy(source, target, weight_sem.at[place])
            for place, (source, target) in enumerate(((w_gate_hbm, w_gate), (w_up_hbm, w_up), (w_down_hbm, w_down)))
        ]
        for copy in weight_copies:
            copy.start()
        for copy in weight_copies:
            copy.wait()

        def feed_forward(chunk):
            branch = take_part(0, chunk)
            residual = alpha * dot(one_hot[chunk_rows(chunk), :], emb[...]) + branch
            centered = residual - row_mean(residual)
            rstd = lax.rsqrt(row_mean(centered * centered) + norm_eps)
            xhat = centered * rstd
            rstd_one[chunk] = rstd
            xbuf[...] = xhat
            park = pltpu.make_async_copy(xbuf, xhat_park.at[chunk], load_sem.at[0])
            park.start()
            hidden_low = (xhat * gain_one[...] + bias_one[...]).astype(LOW)
            put_blocks(hidden_low.astype(FULL))
            keep_columns(cols_own, chunk)
            cols_copy(0, chunk).start()

            def units_tile(start, size):
                cut = pl.ds(start, size)
                gate = dot_nt(w_gate[cut, :], hidden_low)
                up = dot_nt(w_up[cut, :], hidden_low)
                units = mp * local_hidden + start + lax.broadcasted_iota(jnp.int32, (size, rows), 0)
                used = jnp.where(units < FF_USED, 1.0, 0.0)
                square = gate * gate
                bend = jnp.tanh(TANH_SCALE * gate * (1.0 + 0.044715 * square))
                gelu = 0.5 * gate * (1.0 + bend) * used
                slope = 0.5 * (1.0 + bend) + 0.5 * gate * (1.0 - bend * bend) * (
                    TANH_SCALE * (1.0 + 3.0 * 0.044715 * square)
                )
                gate_up[0, cut, chunk_lanes(chunk)] = slope * up * used
                gate_up[1, cut, chunk_lanes(chunk)] = gelu
                active = (gelu * up).astype(LOW)
                act_low[cut, chunk_lanes(chunk)] = active
                send_a[lax.div(chunk, 2), cut, half_chunk(chunk)] = active.astype(FULL)

            tiles(local_hidden, units_tile)
            act_send(0, chunk)
            active = send_a[lax.div(chunk, 2), :, half_chunk(chunk)].T.astype(LOW)
            tiles(
                width, lambda start, size: put_part(chunk, start, size, dot(active, w_down[:, pl.ds(start, size)]))
            )
            core_copy(1, chunk).start()
            park.wait()
            send_part(1, chunk)
            pl.when(chunk + AHEAD < CHUNKS)(lambda: send_part(0, chunk + AHEAD))

        same = jnp.int32(0)
        for place in range(2 * LINE):
            same = same + jnp.where(cluster_ref[place] == cluster_ref[dp], 1, 0)
        weight_row = 1.0 / jnp.full((1, width), same, jnp.int32).astype(FULL)

        def feed_backward(chunk):
            loads = load_all(
                ((xhat_park.at[chunk], xbuf), (cot_hbm.at[chunk_rows(chunk)], cotbuf))
            )
            branch = take_part(1, chunk)
            for copy in loads:
                copy.wait()
            residual = alpha * (xbuf[...] * gain_one[...] + bias_one[...]) + branch
            centered = residual - row_mean(residual)
            rstd = lax.rsqrt(row_mean(centered * centered) + norm_eps)
            xhat = centered * rstd
            obuf[...] = (xhat * gain_two[...] + bias_two[...]).astype(LOW)
            grad_out = cotbuf[...].astype(FULL) * weight_row
            vectors[2:3, :] += jnp.sum(grad_out * xhat, axis=0, keepdims=True)
            vectors[3:4, :] += jnp.sum(grad_out, axis=0, keepdims=True)
            grad_x = grad_out * gain_two[...]
            grad_two = (grad_x - row_mean(grad_x) - xhat * row_mean(grad_x * xhat)) * rstd
            for place in range(width // inner):
                gbuf[place * rows : (place + 1) * rows, :] = grad_two[:, place * inner : (place + 1) * inner]
            stores = load_all(
                ((obuf, block_out.at[chunk_rows(chunk)]), (gbuf, grad_two_park.at[chunk]))
            )
            grad_low = grad_two.astype(LOW)
            put_blocks(grad_low.astype(FULL))
            for place in range(2):
                two_own[place, chunk_rows(chunk), :] = blocks[2 * z + place].astype(LOW)
            for place in range(LINE):
                two_send[place, chunk] = blocks[2 * place + core]
            for step in range(1, LINE):
                two_copy(step, chunk).start()

            def units_tile(start, size):
                cut = pl.ds(start, size)
                grad_act = dot_nt(w_down[cut, :], grad_low)
                for which in range(2):
                    low = (grad_act * gate_up[which, cut, chunk_lanes(chunk)]).astype(LOW)
                    grads_low[pl.ds(which * shift + start, size), chunk_lanes(chunk)] = low
                    gate_up[which, cut, chunk_lanes(chunk)] = low.astype(FULL)

            spread(local_hidden, units_tile)
            pair_send(0, chunk)
            for copy in stores:
                copy.wait()

        def hidden_part(pair):
            both = pl.ds(pl.multiple_of(2 * rows * pair, 2 * rows), 2 * rows)
            grad_gate = gate_up[0, :, both].T.astype(LOW)
            grad_up = gate_up[1, :, both].T.astype(LOW)

            def columns(start, size):
                cut = pl.ds(start, size)
                value = dot(grad_gate, w_gate[:, cut]) + dot(grad_up, w_up[:, cut])
                put_part(2 * pair, start, size, value[:rows])
                put_part(2 * pair + 1, start, size, value[rows:])

            tiles(width, columns)
            for place in range(2):
                core_copy(2, 2 * pair + place).start()

        def take_hidden():
            for chunk in range(CHUNKS):
                cols_copy(0, chunk).wait()
            fetch_columns(0, hidden_theirs)

        def step(turn, carried):
            pl.when(turn == CHUNKS - 1)(lambda: hidden_part(0))
            pl.when(turn == CHUNKS)(take_hidden)
            pl.when(turn < CHUNKS)(lambda: feed_forward(turn))
            pl.when(turn == 1)(lambda: rows_copy().wait())
            pl.when(turn > 0)(lambda: feed_backward(turn - 1))
            return carried

        lax.fori_loop(0, CHUNKS + 1, step, 0)

        hidden_part(1)
        every_chunk(lambda chunk: send_part(2, chunk))

    pl.run_scoped(
        middle_scope,
        pltpu.VMEM((local_hidden, width), LOW),
        pltpu.VMEM((local_hidden, width), LOW),
        pltpu.VMEM((local_hidden, width), LOW),
        pltpu.VMEM((rows, width), LOW),
    )

    def last_scope(theirs, late_theirs, two_theirs, att_theirs, send_b, stage, grad_att, grad_one_own, sums, sums_up, sums_down, sums_below, sums_above, late_own):
        def norm_backward(chunk):
            loads = load_all(((xhat_park.at[chunk], xbuf), (grad_two_park.at[chunk], gbuf)))
            branch = take_part(2, chunk)
            for copy in loads:
                copy.wait()
            grad_two = [gbuf[place * rows : (place + 1) * rows, :] for place in range(width // inner)]
            grad_hidden = alpha * jnp.concatenate(grad_two, axis=1) + branch
            xhat = xbuf[...]
            vectors[0:1, :] += jnp.sum(grad_hidden * xhat, axis=0, keepdims=True)
            vectors[1:2, :] += jnp.sum(grad_hidden, axis=0, keepdims=True)
            grad_x = grad_hidden * gain_one[...]
            grad_one = (grad_x - row_mean(grad_x) - xhat * row_mean(grad_x * xhat)) * rstd_one[chunk]
            put_blocks(grad_one)
            for place in range(2):
                grad_one_own[chunk_rows(chunk), place * block : (place + 1) * block] = blocks[2 * mp + place]
            grad_low = grad_one.astype(LOW)
            put_blocks(grad_low.astype(FULL))
            keep_columns(late_own, chunk)
            grad_mixed = dot(grad_low, w_dense[...]).astype(LOW)
            for place in range(heads_here):
                grad_att[place, chunk_rows(chunk), :] = grad_mixed[:, place * HD : (place + 1) * HD]

        def fetch_units(which, part):
            start, size = spans[part]
            for chunk in range(CHUNKS):
                pair_copy(which, chunk, part).wait()
            views = [stage.at[side, pl.ds(start, size)] for side in range(2)]
            moved(
                [(r_y.at[which, pl.ds(start, size), pl.ds(block * side, block)], views[side]) for side in range(2)]
            )
            for side in range(2):
                theirs[1 + which, start : start + size, block * side : block * (side + 1)] = views[side][...].astype(LOW)

        def fetch_rows(source, target):
            size = source.shape[0]
            views = [stage.at[place, pl.ds(0, size)] for place in range(2)]
            moved([(source.at[:, pl.ds(block * place, block)], views[place]) for place in range(2)])
            for place in range(2):
                target[:, block * place : block * (place + 1)] = views[place][...].astype(LOW)

        def outer_product(target, kind, place, own, other):
            right, right_theirs = (cols_own, late_own)[kind][place], (hidden_theirs, late_theirs)[kind][place]

            def rows_tile(start, size):
                cut = pl.ds(start, size)
                target[cut, :] = dot(own[cut, :], right) + dot(other[cut, :], right_theirs)

            tiles(target.shape[0], rows_tile)

        def down_products():
            for step in range(1, LINE):
                for chunk in range(CHUNKS):
                    two_copy(step, chunk).wait()
            for step in range(1, LINE):
                two_forward(step).start()
            for step in range(1, LINE):
                two_forward(step).wait()
            for chunk in range(CHUNKS):
                pl.when(at_end)(lambda: act_take(1, chunk))
                act_take(2, chunk)
            for step in range(LINE):
                owner = lax.rem(z + step, LINE)
                if step:
                    moved(
                        [
                            (r_two.at[owner, place], blocks.at[pl.ds(CHUNKS * place, CHUNKS)])
                            for place in range(2)
                        ]
                    )
                    for place in range(2):
                        for chunk in range(CHUNKS):
                            piece = blocks[CHUNKS * place + chunk].astype(LOW)
                            two_theirs[place, chunk * rows : (chunk + 1) * rows, :] = piece
                    fetch_rows(r_act.at[owner], theirs.at[0])
                left, right = (theirs.at[0], two_theirs) if step else (act_low, two_own)
                for place in range(2):
                    lanes = slice(place * block, (place + 1) * block)

                    def rows_tile(start, size):
                        cut = pl.ds(start, size)
                        product = dot(left[cut, :], right[place])
                        gate_up[0, cut, lanes] = gate_up[0, cut, lanes] + product if step else product

                    tiles(local_hidden, rows_tile)

        def down_copy():
            return remote(gate_up.at[0, :, half_lanes(1 - y)], r_dny, dny_s, dny_r, y_peer)

        def down_end():
            down_copy().wait()
            moved([(r_dny, stage.at[0])])
            stage[0] = stage[0] + gate_up[0, :, half_lanes(y)]
            moved([(stage.at[0], out_down)])
            for chunk in range(CHUNKS):
                for way in range(2):
                    for hop in range(1, LINE - 1):
                        active, copy = act_copy(way, hop, chunk)
                        pl.when(active)(copy.wait_send)

        def goes(slot, way):
            return z < slot if way == 0 else z > LINE - 1 - slot

        def inner_place(way):
            return z > 0 if way == 0 else z < LINE - 1

        def line_goal(way):
            return at(z_to=jnp.clip(z + 1 - 2 * way, 0, LINE - 1))

        def unit_terms(kind):
            return grads_low.at[pl.ds(pl.multiple_of(kind * shift, 16), local_hidden)], theirs.at[1 + kind]

        def count(way):
            return LINE - 1 - z if way == 0 else z

        def order(kind, slot, way):
            return kind * count(way) + slot - (LINE - count(way))

        def turn_of(number, way):
            many = jnp.maximum(count(way), 1)
            return lax.div(number, many) * (LINE - 1) + lax.rem(number, many) + LINE - 1 - count(way)

        def unit_copy(turn, way, part):
            kind, slot = lax.div(turn, LINE - 1), lax.rem(turn, LINE - 1)
            units = pl.ds(*spans[part])
            home = (send_a, send_b)[way].at[lax.rem(jnp.maximum(order(kind, slot + 1, way), 0), 2), units]
            return remote(
                home, r_rs.at[kind, slot, way, units], rs_s.at[kind, slot, way, part], rs_r.at[kind, slot, way, part],
                line_goal(way),
            )

        def unit_sent(number, way):
            for part in range(2):
                unit_copy(turn_of(jnp.maximum(number, 0), way), way, part).wait_send()

        def unit_slot(turn, part):
            kind, slot = lax.div(turn, LINE - 1), lax.rem(turn, LINE - 1) + 1
            own, other = unit_terms(kind)
            start, size = spans[part]
            cut = slice(start, start + size)
            for way in range(2):

                @pl.when(goes(slot, way))
                def _():
                    number = order(kind, slot, way)
                    home = (send_a, send_b)[way].at[lax.rem(jnp.maximum(number, 0), 2)]
                    if part == 0:
                        pl.when(number >= 2)(lambda: unit_sent(number - 2, way))
                    place = LINE - slot + z if way == 0 else slot - LINE + z
                    home[cut, :] = dot(own[cut, :], cols_own[place]) + dot(other[cut, :], hidden_theirs[place])

                    @pl.when((slot > 1) & inner_place(way))
                    def _():
                        before = jnp.maximum(turn - 1, 0)
                        unit_copy(before, way, part).wait_recv()
                        landed = r_rs.at[lax.div(before, LINE - 1), lax.rem(before, LINE - 1), way, pl.ds(start, size)]
                        moved([(landed, stage.at[way, pl.ds(start, size)])])
                        home[cut, :] = home[cut, :] + stage[way, cut, :]

                    unit_copy(turn, way, part).start()

        def unit_end(kind):
            own, other = unit_terms(kind)
            outer_product(stage.at[0], 0, z, own, other)
            for way in range(2):

                @pl.when(inner_place(way))
                def _():
                    for part in range(2):
                        unit_copy(kind * (LINE - 1) + LINE - 2, way, part).wait_recv()
                    moved([(r_rs.at[kind, LINE - 2, way], stage.at[1])])
                    stage[0] = stage[0] + stage[1]

            moved([(stage.at[0], (out_gate, out_up)[kind])])

        def late_home(slot, way):
            return parts.at[:, way, :, pl.ds(block * (slot - 1), block)]

        def late_copy(slot, way):
            return remote(
                late_home(slot, way), r_rsd.at[slot - 1, way], rs_s.at[2, slot - 1, way, 0],
                rs_r.at[2, slot - 1, way, 0], line_goal(way),
            )

        def late_product(place, piece):
            cut = slice(piece * rows, (piece + 1) * rows)
            return dot(att_turned[cut, :], late_own[place]) + dot(att_theirs[cut, :], late_theirs[place])

        def late_slot(slot):
            for way in range(2):

                @pl.when(goes(slot, way))
                def _():
                    home = late_home(slot, way)
                    place = LINE - slot + z if way == 0 else slot - LINE + z
                    for piece in range(CHUNKS):
                        home[piece] = late_product(place, piece)
                    if slot > 1:

                        @pl.when(inner_place(way))
                        def _():
                            late_copy(slot - 1, way).wait_recv()
                            arrived = blocks.at[pl.ds(0, CHUNKS)]
                            moved([(r_rsd.at[slot - 2, way], arrived)])
                            home[...] = home[...] + arrived[...]

                    late_copy(slot, way).start()

        def late_end():
            total, arrived = blocks.at[pl.ds(0, CHUNKS)], blocks.at[pl.ds(CHUNKS, CHUNKS)]
            for piece in range(CHUNKS):
                total[piece] = late_product(z, piece)
            for way in range(2):

                @pl.when(inner_place(way))
                def _():
                    late_copy(LINE - 1, way).wait_recv()
                    moved([(r_rsd.at[LINE - 2, way], arrived)])
                    total[...] = total[...] + arrived[...]

            for piece in range(CHUNKS):
                gbuf[0:block, piece * rows : (piece + 1) * rows] = total[piece].T
            moved([(gbuf.at[pl.ds(0, block)], out_dense)])

        def last_sent():
            for way in range(2):
                for slot in range(1, LINE):
                    pl.when(goes(slot, way))(late_copy(slot, way).wait_send)
                pl.when(count(way) > 0)(lambda: unit_sent(2 * count(way) - 1, way))
                pl.when(count(way) > 0)(lambda: unit_sent(2 * count(way) - 2, way))

        def attention_backward(place, carried):
            hot_t = hot_turned[...]
            queries, keys, values = heads[0, place], heads[1, place], heads[2, place]
            grad_mixed = grad_att[place]
            probability = probabilities(queries, keys)
            grad_prob = dot_nt(grad_mixed, values)
            centre = jnp.sum(grad_prob * probability, axis=-1, keepdims=True)
            grad_scores = (probability * (grad_prob - centre)).astype(LOW)
            grad_queries = dot(grad_scores, keys) * score_scale
            grad_keys = dot_tn(grad_scores, queries) * score_scale
            grad_values = dot_tn(probability.astype(LOW), grad_mixed)
            sums[0, 0:vocab, head_lanes(place)] = dot(hot_t, turn_by(grad_queries, -sin_ref[...]).astype(LOW))
            sums[0, 0:vocab, head_lanes(place, inner)] = dot(hot_t, turn_by(grad_keys, -sin_ref[...]).astype(LOW))
            sums[1, 0:vocab, head_lanes(place)] = dot(hot_t, grad_values.astype(LOW))
            return carried

        def small_sums():
            lax.fori_loop(0, heads_here, attention_backward, 0)
            hot_t = hot_turned[...]
            high, rest = split_low(grad_one_own[...])
            sums[1, 0:vocab, heads_here * HD :] = dot(hot_t, high) + dot(hot_t, rest)
            for side in range(2):
                sums[side, vocab:, :] = vectors[:, side * (width // 2) : (side + 1) * (width // 2)]
            sums_pair().start()

        def sums_pair():
            return remote(sums.at[1 - y], r_sums.at[0], sums_s.at[0], sums_r.at[0], y_peer)

        def sums_line(way):
            source = (sums_up, sums_down)[way]
            goal = jnp.clip(z + 1 - 2 * way, 0, LINE - 1)
            return remote(source, r_sums.at[1 + way], sums_s.at[1 + way], sums_r.at[1 + way], at(z_to=goal))

        def sums_back():
            return remote(sums.at[y], r_sums.at[3], sums_s.at[3], sums_r.at[3], y_peer)

        def sums_first():
            sums_pair().wait()
            moved([(r_sums.at[0], sums_below)])
            sums[y] = sums[y] + sums_below[...]

            @pl.when(z == 0)
            def _():
                sums_up[...] = sums[y]
                sums_line(0).start()

            @pl.when(z == LINE - 1)
            def _():
                sums_down[...] = sums[y]
                sums_line(1).start()

        def sums_up_step():
            sums_line(0).wait_recv()
            moved([(r_sums.at[1], sums_below)])
            sums_up[...] = sums[y] + sums_below[...]
            sums_line(0).start()

        def sums_down_step():
            sums_line(1).wait_recv()
            moved([(r_sums.at[2], sums_above)])
            sums_down[...] = sums[y] + sums_above[...]
            sums_line(1).start()

        def sums_near():
            pl.when(z == 1)(sums_up_step)
            pl.when(z == LINE - 2)(sums_down_step)

        def sums_far():
            pl.when(z == LINE - 2)(sums_up_step)
            pl.when(z == 1)(sums_down_step)

        def sums_middle():
            @pl.when(z == LINE - 1)
            def _():
                sums_line(0).wait_recv()
                moved([(r_sums.at[1], sums_below)])

            @pl.when(z == 0)
            def _():
                sums_line(1).wait_recv()
                moved([(r_sums.at[2], sums_above)])

            @pl.when(z > 0)
            def _():
                sums[y] = sums[y] + sums_below[...]

            @pl.when(z < LINE - 1)
            def _():
                sums[y] = sums[y] + sums_above[...]

            sums_back().start()

        def sums_end():
            sums_back().wait()
            pl.when(z < LINE - 1)(sums_line(0).wait_send)
            pl.when(z > 0)(sums_line(1).wait_send)
            moved([(r_sums.at[3], sums.at[1 - y])])
            lanes = pl.ds(pl.multiple_of(lax.rem(dp, LINE) * block, block), block)
            moved([(sums.at[lax.div(dp, LINE), pl.ds(vocab, 8), lanes], out_norms)])

        def by_token(kind, rows_of):
            side, start = ((0, 0), (0, inner), (1, 0), (1, inner))[kind]
            return sums[side, rows_of, start : start + inner]

        def head_gradients():
            own_columns = emb[:, pl.ds(pl.multiple_of(dp * block, block), block)]
            for kind, result in enumerate((out_query, out_key, out_value)):
                high, rest = split_low(by_token(kind, slice(0, vocab)))
                gbuf[0:block, :] = dot_tn(own_columns, high) + dot_tn(own_columns, rest)
                moved([(gbuf.at[pl.ds(0, block)], result)])

        table_rows = vocab // (2 * LINE)
        table_own = pl.ds(pl.multiple_of(dp * table_rows, table_rows), table_rows)

        def table_part():
            for kind, weight in enumerate((w_query_hbm, w_key_hbm, w_value_hbm)):
                moved([(weight, w_dense)])
                pieces = jnp.concatenate(split_low(by_token(kind, table_own)), axis=0)

                def columns(start, size):
                    cut = pl.ds(start, size)
                    both = dot_nt(pieces, w_dense[cut, :])
                    both = both[:table_rows] + both[table_rows:]
                    xbuf[0:table_rows, cut] = both if kind == 0 else xbuf[0:table_rows, cut] + both

                tiles(width, columns)
            quarter = pl.ds(pl.multiple_of(mp * inner, inner), inner)
            xbuf[0:table_rows, quarter] = xbuf[0:table_rows, quarter] + alpha * by_token(3, table_own)
            table_copy(0).start()

        def table_middle():
            table_copy(0).wait()
            xbuf[table_rows : 2 * table_rows, :] = xbuf[0:table_rows, :] + table_core[...]
            table_copy(1).start()

        def table_end():
            table_copy(1).wait()
            xbuf[0:table_rows, :] = 0.1 * (xbuf[table_rows : 2 * table_rows, :] + table_x[...])
            moved([(xbuf.at[pl.ds(0, table_rows)], out_table)])

        def table_copy(turn):
            target, device = ((table_core, core_peer), (table_x, x_peer))[turn]
            return remote(xbuf.at[pl.ds(turn * table_rows, table_rows)], target, table_s.at[turn], table_r.at[turn], device)

        def act_pass():
            for chunk in range(CHUNKS):
                act_take(1, chunk)
                act_send(2, chunk)

        at_end = (z == 0) | (z == LINE - 1)

        for chunk in range(CHUNKS):
            for way in range(2):
                active, copy = act_copy(way, 0, chunk)
                pl.when(active)(copy.wait_send)
        def one_turn(turn, carried):
            for part in range(2):
                pl.when(turn == 0)(lambda: fetch_units(0, part))
                unit_slot(turn, part)

            @pl.when(turn == 0)
            def _():
                pair_send(1, 0)
                pair_send(1, 1)
                for chunk in range(CHUNKS):
                    act_take(0, chunk)
                    act_send(1, chunk)

            @pl.when(turn == 1)
            def _():
                every_chunk(norm_backward)
                small_sums()
                pl.when(~at_end)(act_pass)
                sums_first()
                for chunk in range(CHUNKS):
                    cols_copy(1, chunk).start()
                pair_send(1, 2)
                pair_send(1, 3)

            @pl.when(turn == 2)
            def _():
                sums_near()
                for chunk in range(CHUNKS):
                    cols_copy(1, chunk).wait()
                fetch_columns(1, late_theirs)
                fetch_rows(r_att, att_theirs)
                late_slot(1)

            lately = (turn == 3) & ~at_end | (turn == 2) & at_end
            pl.when(lately)(lambda: late_slot(2))
            pl.when((turn == 3) & ~at_end | (turn == 4) & at_end)(down_products)
            pl.when(lately)(lambda: late_slot(3))

            @pl.when(turn == 2)
            def _():
                for part in range(2):
                    fetch_units(1, part)

            @pl.when((turn == 3) & ~at_end | (turn == 5) & at_end)
            def _():
                sums_far()
                sums_middle()
                down_copy().start()

            @pl.when((turn == 4) & ~at_end | (turn == 5) & at_end)
            def _():
                sums_end()
                head_gradients()
                table_part()

            return carried

        lax.fori_loop(0, 2 * (LINE - 1), one_turn, 0)
        unit_end(0)
        late_end()
        table_middle()
        table_end()
        down_end()
        unit_end(1)
        last_sent()

    pl.run_scoped(
        last_scope,
        pltpu.VMEM((3, local_hidden, length), LOW),
        pltpu.VMEM((LINE, length, block), LOW),
        pltpu.VMEM((2, length, block), LOW),
        pltpu.VMEM((inner, length), LOW),
        pltpu.VMEM((2, local_hidden, block), FULL),
        pltpu.VMEM((2, local_hidden, block), FULL),
        pltpu.VMEM((heads_here, length, HD), LOW),
        pltpu.VMEM((length, 2 * block), FULL),
        pltpu.VMEM((2,) + r_sums.shape[1:], FULL),
        pltpu.VMEM(r_sums.shape[1:], FULL),
        pltpu.VMEM(r_sums.shape[1:], FULL),
        pltpu.VMEM(r_sums.shape[1:], FULL),
        pltpu.VMEM(r_sums.shape[1:], FULL),
        pltpu.VMEM(cols_own.shape, LOW),
    )


def local_fast(
    token_ids,
    prefix_lengths,
    cluster_ids,
    embedding,
    w_query,
    w_key,
    w_value,
    w_dense,
    w_gate,
    w_up,
    w_down,
    norm1_gain,
    norm1_bias,
    norm2_gain,
    norm2_bias,
    cotangent,
):
    length = token_ids.shape[0]
    vocab, width = embedding.shape
    inner = w_query.shape[1]
    heads_here = inner // HD
    local_hidden = w_gate.shape[1]
    rows = length // CHUNKS
    block = width // (2 * LINE)
    shift = (local_hidden + 15) // 16 * 16
    frequency = 10000.0 ** (np.arange(HD // 2) * (-2.0 / HD))
    angles = np.arange(length)[:, None] * frequency[None, :]
    cosine = np.concatenate([np.cos(angles)] * 2, axis=1).astype(np.float32)
    sine = np.concatenate([-np.sin(angles), np.sin(angles)], axis=1).astype(np.float32)
    norms = [vector.reshape(1, width) for vector in (norm1_gain, norm1_bias, norm2_gain, norm2_bias)]

    hbm = pl.BlockSpec(memory_space=pl.ANY)
    vmem = pl.BlockSpec(memory_space=pltpu.VMEM)
    smem = pl.BlockSpec(memory_space=pltpu.SMEM)
    sums_rows = vocab + 8
    table_rows = vocab // (2 * LINE)
    shapes = [
        ((length, width), LOW),
        ((table_rows, width), FULL),
        ((block, inner), FULL),
        ((block, inner), FULL),
        ((block, inner), FULL),
        ((block, inner), FULL),
        ((local_hidden, block), FULL),
        ((local_hidden, block), FULL),
        ((local_hidden, block), FULL),
        ((8, block), FULL),
        ((LINE, local_hidden, length), FULL),
        ((LINE, 2, CHUNKS, rows, block), FULL),
        ((2, local_hidden, length), FULL),
        ((2, LINE, CHUNKS, rows, block), FULL),
        ((inner, length), FULL),
        ((CHUNKS, rows, width), FULL),
        ((CHUNKS, length, inner), FULL),
        ((local_hidden, block), FULL),
        ((2, LINE - 1, 2, local_hidden, block), FULL),
        ((LINE - 1, 2, CHUNKS, rows, block), FULL),
        ((4, sums_rows, width // 2), FULL),
    ]
    scratch = [
        ((CHUNKS, 2, rows, width // 2), FULL),
        ((CHUNKS, rows, width // 2), FULL),
        ((2, CHUNKS, rows, width // 2), FULL),
        ((CHUNKS, rows, width // 2), FULL),
        ((2 * LINE, rows, block), FULL),
        ((rows, width), FULL),
        ((length, inner), FULL),
        ((rows, width), LOW),
        ((2, local_hidden, length), FULL),
        ((2 * shift, length), LOW),
        ((local_hidden, length), LOW),
        ((2, local_hidden, block), FULL),
        ((LINE, length, block), LOW),
        ((2, CHUNKS, rows, block), FULL),
        ((LINE, length, block), LOW),
        ((2, length, block), LOW),
        ((LINE, CHUNKS, rows, block), FULL),
        ((length, inner), LOW),
        ((inner, length), LOW),
        ((3, heads_here, length, HD), LOW),
        ((width, inner), LOW),
        ((length, vocab), LOW),
        ((vocab, length), LOW),
        ((CHUNKS, rows, 1), FULL),
        ((8, width), FULL),
        ((table_rows, width), FULL),
        ((table_rows, width), FULL),
    ]
    dma = pltpu.SemaphoreType.DMA
    each = (3, CHUNKS)
    semaphores = [
        each, each, each, each, each, each, (2, LINE - 1, CHUNKS), (2, LINE - 1, CHUNKS), each, each, (3,), (3,),
        (2, CHUNKS), (2, CHUNKS), (2,), (2,), (2, CHUNKS, 2), (2, CHUNKS, 2), None, None, None, None,
        (3, LINE - 1, 2, 2), (3, LINE - 1, 2, 2), (4,), (4,), (2,), (2,), (4,), (4,),
    ]
    results = pl.pallas_call(
        functools.partial(layer_kernel, length, width, local_hidden),
        out_shape=[jax.ShapeDtypeStruct(shape, dtype) for shape, dtype in shapes],
        in_specs=[smem] * 2 + [vmem] * 8 + [hbm] * 8,
        out_specs=[hbm] * len(shapes),
        scratch_shapes=[pltpu.VMEM(shape, dtype) for shape, dtype in scratch]
        + [dma if shape is None else dma(shape) for shape in semaphores],
        compiler_params=pltpu.CompilerParams(
            collective_id=0, has_side_effects=True, vmem_limit_bytes=62 * 2**20
        ),
    )(
        prefix_lengths,
        cluster_ids,
        token_ids.reshape(1, length),
        embedding,
        cosine,
        sine,
        *norms,
        w_query,
        w_key,
        w_value,
        w_dense,
        w_gate.T,
        w_up.T,
        w_down.T,
        cotangent,
    )
    block_out, table, out_query, out_key, out_value, out_dense, out_gate, out_up, out_down, out_norms = results[:10]
    return (
        block_out,
        table,
        out_query,
        out_key,
        out_value,
        out_dense,
        out_gate.T,
        out_up.T,
        out_down.T,
        out_norms[0],
        out_norms[1],
        out_norms[2],
        out_norms[3],
    )


def solution(mesh):
    fast = mesh.shape["dp"] == 2 * LINE and mesh.shape["mp"] == 4
    return jax.shard_map(
        local_fast if fast else local_general,
        mesh=mesh,
        in_specs=(
            P("dp"),
            P("dp"),
            P(),
            P(),
            P(None, "mp"),
            P(None, "mp"),
            P(None, "mp"),
            P(None, "mp"),
            P(None, "mp"),
            P(None, "mp"),
            P(None, "mp"),
            P(),
            P(),
            P(),
            P(),
            P("dp", None),
        ),
        out_specs=(
            P("dp", None),
            P("dp", None),
            P("dp", "mp"),
            P("dp", "mp"),
            P("dp", "mp"),
            P("dp", "mp"),
            P("dp", "mp"),
            P("dp", "mp"),
            P("dp", "mp"),
            P("dp"),
            P("dp"),
            P("dp"),
            P("dp"),
        ),
        check_vma=False,
    )
```

```python
import functools
import math

import jax
import jax.numpy as jnp
import numpy as np
from jax import lax
from jax.experimental import pallas as pl
from jax.experimental.pallas import tpu as pltpu
from jax.sharding import PartitionSpec as P

HD = 128
FF_USED = 5461


deep_alpha = math.sqrt(48.0)
norm_eps = 1e-05
highest = lax.Precision.HIGHEST


def layer_norm(inputs, norm_gain, norm_bias):
    center = jnp.mean(inputs, axis=-1, keepdims=True)
    centered = inputs - center
    spread = jnp.mean(centered * centered, axis=-1, keepdims=True)
    return centered * lax.rsqrt(spread + norm_eps) * norm_gain + norm_bias


def rotary_tables(length, head_width):
    half_width = head_width // 2
    frequency = jnp.exp(
        jnp.arange(half_width, dtype=jnp.float32) * (-2.0 * math.log(10000.0) / head_width)
    )
    angles = jnp.arange(length, dtype=jnp.float32)[:, None] * frequency[None, :]
    return (jnp.cos(angles), jnp.sin(angles))


def rotate(inputs, cosine, sine):
    half_width = inputs.shape[-1] // 2
    first = inputs[..., :half_width]
    second = inputs[..., half_width:]
    cosine = cosine[:, None, :]
    sine = sine[:, None, :]
    return jnp.concatenate(
        [first * cosine - second * sine, second * cosine + first * sine], axis=-1
    )


def row_mask(row_begin, row_count, length, prefix):
    columns = jnp.arange(length, dtype=jnp.int32)
    row_index = row_begin + jnp.arange(row_count, dtype=jnp.int32)
    return (columns[None, :] < prefix) | (columns[None, :] <= row_index[:, None])


def block_scores(query_block, keys_rot, visible, score_scale):
    scores = (
        jnp.einsum("bhd,khd->hbk", query_block, keys_rot, preferred_element_type=jnp.float32)
        * score_scale
    )
    return jnp.where(visible[None, :, :], scores, -1e30)


def attention_forward(queries, keys_rot, values_in, prefix, row_block):
    length = queries.shape[0]
    score_scale = 1.0 / math.sqrt(HD)

    def one_block(row_begin):
        scores = block_scores(
            queries, keys_rot, row_mask(row_begin, row_block, length, prefix), score_scale
        )
        row_max = jnp.max(scores, axis=-1, keepdims=True)
        weights = jnp.exp(scores - row_max)
        total_weight = jnp.sum(weights, axis=-1, keepdims=True)
        probability = (weights / total_weight).astype(jnp.bfloat16)
        mixed_block = jnp.einsum(
            "hbk,khd->bhd", probability, values_in, preferred_element_type=jnp.float32
        )
        return (mixed_block, row_max + jnp.log(total_weight))

    starts = jnp.arange(length // row_block, dtype=jnp.int32) * row_block
    attended, log_total = lax.map(one_block, starts)
    return (attended.reshape(length, -1), log_total)


def attention_backward(queries, keys_rot, values_in, prefix, row_block, log_total, grad_mixed):
    length = queries.shape[0]
    score_scale = 1.0 / math.sqrt(HD)

    def one_block(carried, inputs):
        grad_keys, grad_values = carried
        row_begin, block_total = inputs
        scores = block_scores(
            queries, keys_rot, row_mask(row_begin, row_block, length, prefix), score_scale
        )
        probability = jnp.exp(scores - block_total)
        prob_low = probability.astype(jnp.bfloat16)
        grad_prob = jnp.einsum(
            "bhd,khd->hbk", grad_mixed, values_in, preferred_element_type=jnp.float32
        )
        centre = jnp.sum(grad_prob * probability, axis=-1, keepdims=True)
        grad_scores = (probability * (grad_prob - centre)).astype(jnp.bfloat16)
        grad_query = (
            jnp.einsum("hbk,khd->bhd", grad_scores, keys_rot, preferred_element_type=jnp.float32)
            * score_scale
        )
        grad_keys = (
            grad_keys
            + jnp.einsum("hbk,bhd->khd", grad_scores, queries, preferred_element_type=jnp.float32)
            * score_scale
        )
        grad_values = grad_values + jnp.einsum(
            "hbk,bhd->khd", prob_low, grad_mixed, preferred_element_type=jnp.float32
        )
        return ((grad_keys, grad_values), grad_query)

    starts = jnp.arange(length // row_block, dtype=jnp.int32) * row_block
    zeros_kv = jnp.zeros(keys_rot.shape, jnp.float32)
    (grad_keys, grad_values), grad_queries = lax.scan(
        one_block, (zeros_kv, zeros_kv), (starts, log_total)
    )
    return (grad_queries.reshape(queries.shape), grad_keys, grad_values)


def local_general(
    token_ids,
    prefix_lengths,
    cluster_ids,
    embedding,
    w_query,
    w_key,
    w_value,
    w_dense,
    w_gate,
    w_up,
    w_down,
    norm1_gain,
    norm1_bias,
    norm2_gain,
    norm2_bias,
    cotangent,
):
    length = token_ids.shape[0]
    vocab_rows = embedding.shape[0]
    row_block = min(512, length)
    local_heads = w_query.shape[1] // HD
    local_hidden = w_gate.shape[1]
    one_hot = (token_ids[:, None] == jnp.arange(vocab_rows, dtype=jnp.int32)[None, :]).astype(
        jnp.bfloat16
    )
    embedded_low = jnp.dot(one_hot, embedding, preferred_element_type=jnp.float32).astype(
        jnp.bfloat16
    )
    embedded = embedded_low.astype(jnp.float32)
    cosine, sine = rotary_tables(length, HD)
    prefix = prefix_lengths[0]
    own_cluster = cluster_ids[lax.axis_index("dp")]
    seq_weight = 1.0 / jnp.sum((cluster_ids == own_cluster).astype(jnp.float32))

    def project(weight_in):
        return jnp.dot(embedded_low, weight_in, preferred_element_type=jnp.float32).reshape(
            length, local_heads, HD
        )

    queries = rotate(project(w_query), cosine, sine).astype(jnp.bfloat16)
    keys_rot = rotate(project(w_key), cosine, sine).astype(jnp.bfloat16)
    values_in = project(w_value).astype(jnp.bfloat16)
    attended, log_total = attention_forward(queries, keys_rot, values_in, prefix, row_block)
    attended_low = attended.astype(jnp.bfloat16)
    branch = lax.psum(
        jnp.einsum("lh,dh->ld", attended_low, w_dense, preferred_element_type=jnp.float32), "mp"
    )
    residual_one = deep_alpha * embedded + branch
    hidden, norm_one_pull = jax.vjp(layer_norm, residual_one, norm1_gain, norm1_bias)
    hidden_low = hidden.astype(jnp.bfloat16)
    gate_proj = jnp.dot(hidden_low, w_gate, preferred_element_type=jnp.float32)
    up_proj = jnp.dot(hidden_low, w_up, preferred_element_type=jnp.float32)
    unit_index = lax.axis_index("mp") * local_hidden + jnp.arange(local_hidden, dtype=jnp.int32)
    used_mask = (unit_index < FF_USED).astype(jnp.float32)

    def gated_unit(gate_in, up_in):
        return jax.nn.gelu(gate_in, approximate=True) * up_in * used_mask

    activation, gated_pull = jax.vjp(gated_unit, gate_proj, up_proj)
    activation_low = activation.astype(jnp.bfloat16)
    branch_two = lax.psum(
        jnp.einsum("lf,df->ld", activation_low, w_down, preferred_element_type=jnp.float32), "mp"
    )
    residual_two = deep_alpha * hidden + branch_two
    final, norm_two_pull = jax.vjp(layer_norm, residual_two, norm2_gain, norm2_bias)
    grad_out = cotangent.astype(jnp.float32) * seq_weight
    grad_two, grad_gain_two, grad_bias_two = norm_two_pull(grad_out)
    grad_branch_two = grad_two.astype(jnp.bfloat16)
    grad_w_down = jnp.einsum(
        "ld,lf->df", grad_branch_two, activation_low, preferred_element_type=jnp.float32
    )
    grad_act = jnp.dot(grad_branch_two, w_down, preferred_element_type=jnp.float32)
    grad_gate, grad_up = gated_pull(grad_act)
    grad_gate_low = grad_gate.astype(jnp.bfloat16)
    grad_up_low = grad_up.astype(jnp.bfloat16)
    grad_w_gate = jnp.einsum(
        "ld,lf->df", hidden_low, grad_gate_low, preferred_element_type=jnp.float32
    )
    grad_w_up = jnp.einsum("ld,lf->df", hidden_low, grad_up_low, preferred_element_type=jnp.float32)
    hidden_part = jnp.einsum(
        "lf,df->ld", grad_gate_low, w_gate, preferred_element_type=jnp.float32
    ) + jnp.einsum("lf,df->ld", grad_up_low, w_up, preferred_element_type=jnp.float32)
    grad_hidden = deep_alpha * grad_two + lax.psum(hidden_part, "mp")
    feed_sums = (
        lax.psum_scatter(grad_w_gate, "dp", scatter_dimension=0, tiled=True),
        lax.psum_scatter(grad_w_up, "dp", scatter_dimension=0, tiled=True),
        lax.psum_scatter(grad_w_down, "dp", scatter_dimension=0, tiled=True),
        lax.psum_scatter(grad_gain_two, "dp", scatter_dimension=0, tiled=True),
        lax.psum_scatter(grad_bias_two, "dp", scatter_dimension=0, tiled=True),
    )
    grad_one, grad_gain_one, grad_bias_one = norm_one_pull(grad_hidden)
    grad_branch = grad_one.astype(jnp.bfloat16)
    grad_w_dense = jnp.einsum(
        "ld,lh->dh", grad_branch, attended_low, preferred_element_type=jnp.float32
    )
    grad_attended = jnp.dot(grad_branch, w_dense, preferred_element_type=jnp.float32).astype(
        jnp.bfloat16
    )
    grad_attended = grad_attended.reshape(length, local_heads, HD)
    grad_queries, grad_keys, grad_values = attention_backward(
        queries, keys_rot, values_in, prefix, row_block, log_total, grad_attended
    )
    grad_query_lin = rotate(grad_queries, cosine, -sine).astype(jnp.bfloat16).reshape(length, -1)
    grad_key_lin = rotate(grad_keys, cosine, -sine).astype(jnp.bfloat16).reshape(length, -1)
    grad_value_lin = grad_values.astype(jnp.bfloat16).reshape(length, -1)
    grad_w_query = jnp.einsum(
        "ld,lh->dh", embedded_low, grad_query_lin, preferred_element_type=jnp.float32
    )
    grad_w_key = jnp.einsum(
        "ld,lh->dh", embedded_low, grad_key_lin, preferred_element_type=jnp.float32
    )
    grad_w_value = jnp.einsum(
        "ld,lh->dh", embedded_low, grad_value_lin, preferred_element_type=jnp.float32
    )
    input_part = (
        jnp.einsum("lh,dh->ld", grad_query_lin, w_query, preferred_element_type=jnp.float32)
        + jnp.einsum("lh,dh->ld", grad_key_lin, w_key, preferred_element_type=jnp.float32)
        + jnp.einsum("lh,dh->ld", grad_value_lin, w_value, preferred_element_type=jnp.float32)
    )
    grad_embedded = deep_alpha * grad_one + lax.psum(input_part, "mp")
    grad_table = 0.1 * jnp.dot(one_hot.astype(jnp.float32).T, grad_embedded, precision=highest)
    attn_sums = (
        lax.psum_scatter(grad_table, "dp", scatter_dimension=0, tiled=True),
        lax.psum_scatter(grad_w_query, "dp", scatter_dimension=0, tiled=True),
        lax.psum_scatter(grad_w_key, "dp", scatter_dimension=0, tiled=True),
        lax.psum_scatter(grad_w_value, "dp", scatter_dimension=0, tiled=True),
        lax.psum_scatter(grad_w_dense, "dp", scatter_dimension=0, tiled=True),
        lax.psum_scatter(grad_gain_one, "dp", scatter_dimension=0, tiled=True),
        lax.psum_scatter(grad_bias_one, "dp", scatter_dimension=0, tiled=True),
    )
    summed = (
        attn_sums[0],
        attn_sums[1],
        attn_sums[2],
        attn_sums[3],
        attn_sums[4],
        feed_sums[0],
        feed_sums[1],
        feed_sums[2],
        attn_sums[5],
        attn_sums[6],
        feed_sums[3],
        feed_sums[4],
    )
    return (
        final.astype(jnp.bfloat16),
        summed[0],
        summed[1],
        summed[2],
        summed[3],
        summed[4],
        summed[5],
        summed[6],
        summed[7],
        summed[8],
        summed[9],
        summed[10],
        summed[11],
    )


LINE = 4
MESH = pl.DeviceIdType.MESH
CHUNKS = 4
AHEAD = 2
LOW = jnp.bfloat16
FULL = jnp.float32
TANH_SCALE = math.sqrt(2.0 / math.pi)


def dot(left, right):
    return jnp.dot(left, right, preferred_element_type=FULL)


def dot_nt(left, right):
    return lax.dot_general(left, right, (((1,), (1,)), ((), ())), preferred_element_type=FULL)


def dot_tn(left, right):
    return lax.dot_general(left, right, (((0,), (0,)), ((), ())), preferred_element_type=FULL)


def split_low(value):
    high = value.astype(LOW)
    return high, (value - high.astype(FULL)).astype(LOW)


def row_mean(value):
    return jnp.mean(value, axis=-1, keepdims=True)


def spread(size, body, tile=512):
    for start in range(0, size, tile):
        body(start, min(tile, size - start))


def tiles(size, body, tile=512):
    whole = size // tile
    lax.fori_loop(0, whole, lambda step, carried: (body(pl.multiple_of(step * tile, tile), tile), carried)[1], 0)
    if size % tile:
        body(whole * tile, size % tile)


def layer_kernel(
    length, width, local_hidden,
    prefix_ref, cluster_ref, ids_row, emb, cos_ref, sin_ref, gain_one, bias_one, gain_two, bias_two, w_query_hbm, w_key_hbm, w_value_hbm, w_dense_hbm,
    w_gate_hbm, w_up_hbm, w_down_hbm, cot_hbm,
    block_out, out_table, out_query, out_key, out_value, out_dense, out_gate, out_up, out_down, out_norms,
    r_act, r_two, r_y, r_cols, r_att, xhat_park, grad_two_park, r_dny, r_rs, r_rsd, r_sums,
    parts, core_in, x_in, back_in, blocks, xbuf, gbuf, obuf, gate_up, grads_low, act_low, send_a, cols_own, cols_send,
    hidden_theirs, two_own, two_send, att_low, att_turned, heads, w_dense, one_hot, hot_turned, rstd_one, vectors, table_core, table_x,
    core_s, core_r, x_s, x_r, back_s, back_r, act_s, act_r, two_s, two_r, fwd_two_s, fwd_two_r, cols_s, cols_r, fwd_s,
    fwd_r, ys_s, ys_r, att_s, att_r, dny_s, dny_r, rs_s, rs_r, sums_s, sums_r, table_s, table_r, load_sem, weight_sem,
):
    dp, mp = lax.axis_index("dp"), lax.axis_index("mp")
    z, y = lax.div(dp, 2), lax.rem(dp, 2)
    x, core = lax.div(mp, 2), lax.rem(mp, 2)
    rows = length // CHUNKS
    heads_here = heads.shape[1]
    inner = heads_here * HD
    vocab = emb.shape[0]
    shift = (local_hidden + 15) // 16 * 16
    near = (local_hidden // 2 + 15) // 16 * 16
    spans = ((0, near), (near, local_hidden - near))
    block = width // (2 * LINE)
    alpha = jnp.float32(deep_alpha)

    def at(z_to=None, y_to=None, x_to=None, core_to=None):
        z_to = z if z_to is None else z_to
        y_to = y if y_to is None else y_to
        x_to = x if x_to is None else x_to
        core_to = core if core_to is None else core_to
        return (2 * z_to + y_to, 2 * x_to + core_to)

    core_peer = at(core_to=1 - core)
    x_peer = at(x_to=1 - x)
    y_peer = at(y_to=1 - y)

    def remote(source, target, send, receive, device):
        return pltpu.make_async_remote_copy(
            src_ref=source, dst_ref=target, send_sem=send, recv_sem=receive,
            device_id=device, device_id_type=MESH,
        )

    def load_all(pairs):
        copies = [
            pltpu.make_async_copy(source, target, load_sem.at[place])
            for place, (source, target) in enumerate(pairs)
        ]
        for copy in copies:
            copy.start()
        return copies

    def moved(pairs):
        for copy in load_all(pairs):
            copy.wait()

    barrier = pltpu.get_barrier_semaphore()
    greeted = [core_peer, x_peer, y_peer] + [at(z_to=lax.rem(z + step, LINE)) for step in range(1, LINE)]
    for device in greeted:
        pl.semaphore_signal(barrier, inc=1, device_id=device, device_id_type=MESH)

    def chunk_rows(chunk):
        return pl.ds(pl.multiple_of(chunk * rows, rows), rows)

    def core_copy(turn, chunk):
        return remote(
            parts.at[chunk, 1 - core], core_in.at[chunk], core_s.at[turn, chunk], core_r.at[turn, chunk], core_peer
        )

    def x_copy(turn, chunk):
        return remote(
            parts.at[chunk, core], x_in.at[turn % 2, chunk], x_s.at[turn, chunk], x_r.at[turn, chunk], x_peer
        )

    def back_copy(turn, chunk):
        return remote(
            parts.at[chunk, core], back_in.at[chunk], back_s.at[turn, chunk], back_r.at[turn, chunk], core_peer
        )

    def put_part(chunk, start, size, value):
        side, first = lax.div(start, width // 2), lax.rem(start, width // 2)
        parts[chunk, side, :, pl.ds(pl.multiple_of(first, size), size)] = value

    def send_part(turn, chunk):
        core_copy(turn, chunk).wait()
        parts[chunk, core] = parts[chunk, core] + core_in[chunk]
        x_copy(turn, chunk).start()

    def take_part(turn, chunk):
        x_copy(turn, chunk).wait()
        parts[chunk, core] = parts[chunk, core] + x_in[turn % 2, chunk]
        back = back_copy(turn, chunk)
        back.start()
        mine = parts[chunk, core]
        back.wait()
        other = back_in[chunk]
        return jnp.concatenate([jnp.where(core == 0, mine, other), jnp.where(core == 0, other, mine)], axis=1)

    def put_blocks(value):
        for place in range(2 * LINE):
            blocks[place] = value[:, place * block : (place + 1) * block]

    def chunk_lanes(chunk):
        return pl.ds(pl.multiple_of(chunk * rows, rows), rows)

    def half_lanes(side):
        return pl.ds(pl.multiple_of(side * block, block), block)

    def keep_columns(own, chunk):
        for place in range(LINE):
            own[place, chunk_rows(chunk), :] = blocks[2 * place + y].astype(LOW)
        for place in range(2):
            cols_send[place, chunk] = blocks[2 * (2 * core + place) + 1 - y]

    def cols_copy(kind, chunk):
        return remote(
            cols_send.at[:, chunk], r_cols.at[kind, pl.ds(2 * core, 2), chunk],
            cols_s.at[kind, chunk], cols_r.at[kind, chunk], y_peer,
        )

    def forward_copy(kind):
        view = r_cols.at[kind, pl.ds(2 * core, 2)]
        return remote(view, view, fwd_s.at[kind], fwd_r.at[kind], core_peer)

    def act_copy(way, hop, chunk):
        goal = jnp.clip(z + 1 - 2 * way, 0, LINE - 1)
        owner = z - hop if way == 0 else z + hop
        active = (owner >= 0) & (z < LINE - 1) if way == 0 else (owner < LINE) & (z > 0)
        owner = jnp.clip(owner, 0, LINE - 1)
        landed = r_act.at[owner, :, chunk_lanes(chunk)]
        source = send_a.at[lax.div(chunk, 2), :, half_chunk(chunk)] if hop == 0 else landed
        return active, remote(
            source, landed, act_s.at[way, hop, chunk], act_r.at[way, hop, chunk], at(z_to=goal)
        )

    def act_landed(way, hop):
        return z - 1 - hop >= 0 if way == 0 else z + 1 + hop < LINE

    def half_chunk(chunk):
        return pl.ds(pl.multiple_of(lax.rem(chunk, 2) * rows, rows), rows)

    def act_send(hop, chunk):
        for way in range(2):
            active, copy = act_copy(way, hop, chunk)
            pl.when(active)(copy.start)

    def act_take(hop, chunk):
        for way in range(2):
            _, copy = act_copy(way, hop, chunk)
            pl.when(act_landed(way, hop))(copy.wait_recv)

    def two_copy(step, chunk):
        goal = lax.rem(z + step, LINE)
        return remote(
            two_send.at[goal, chunk], r_two.at[z, core, chunk],
            two_s.at[step - 1, chunk], two_r.at[step - 1, chunk], at(z_to=goal),
        )

    def two_forward(step):
        view = r_two.at[lax.rem(z + step, LINE), core]
        return remote(view, view, fwd_two_s.at[step - 1], fwd_two_r.at[step - 1], core_peer)

    def pair_copy(which, chunk, part):
        units = pl.ds(*spans[part])
        return remote(
            gate_up.at[which, units, chunk_lanes(chunk)], r_y.at[which, units, chunk_lanes(chunk)],
            ys_s.at[which, chunk, part], ys_r.at[which, chunk, part], y_peer,
        )

    def pair_send(which, chunk):
        for part in range(2):
            pair_copy(which, chunk, part).start()

    def rows_copy():
        return remote(gbuf, r_att, att_s, att_r, y_peer)

    def fetch_columns(kind, target):
        forward = forward_copy(kind)
        forward.start()
        forward.wait()
        for pair in range(2):
            moved(
                [(r_cols.at[kind, 2 * pair + place], blocks.at[pl.ds(CHUNKS * place, CHUNKS)]) for place in range(2)]
            )
            for place in range(2):
                for chunk in range(CHUNKS):
                    piece = blocks[CHUNKS * place + chunk].astype(LOW)
                    target[2 * pair + place, chunk * rows : (chunk + 1) * rows, :] = piece

    def every_chunk(body):
        lax.fori_loop(0, CHUNKS, lambda chunk, carried: (body(chunk), carried)[1], 0)

    score_scale = 1.0 / math.sqrt(HD)

    def probabilities(queries, keys, begin):
        shape = (queries.shape[0], length)
        column = lax.broadcasted_iota(jnp.int32, shape, 1)
        row = lax.broadcasted_iota(jnp.int32, shape, 0) + begin
        visible = (column < prefix_ref[0]) | (column <= row)
        scores = jnp.where(visible, dot_nt(queries, keys) * score_scale, -1e30)
        weights = jnp.exp(scores - jnp.max(scores, axis=-1, keepdims=True))
        return weights / jnp.sum(weights, axis=-1, keepdims=True)

    def turn_by(value, sine):
        return value * cos_ref[...] + pltpu.roll(value, HD // 2, 1) * sine

    def head_lanes(place, offset=0):
        return pl.ds(pl.multiple_of(offset + place * HD, HD), HD)

    def first_scope(w_heads, tab):
        loads = [
            pltpu.make_async_copy(source, target, weight_sem.at[place])
            for place, (source, target) in enumerate(
                (
                    (w_query_hbm, w_heads.at[0]),
                    (w_key_hbm, w_heads.at[1]),
                    (w_value_hbm, w_heads.at[2]),
                    (w_dense_hbm, w_dense),
                )
            )
        ]
        for copy in loads:
            copy.start()
        named = lax.broadcasted_iota(jnp.int32, (vocab, length), 0) == ids_row[...]
        hot = jnp.where(named, 1.0, 0.0)
        hot_turned[...] = hot.astype(LOW)
        one_hot[...] = hot.T.astype(LOW)
        vectors[...] = jnp.zeros_like(vectors)
        for kind in range(3):
            loads[kind].wait()
            table = dot(emb[...], w_heads[kind])
            for place in range(heads_here):
                tab[kind * heads_here + place] = table[:, place * HD : (place + 1) * HD]

        def head_inputs(place, carried):
            hot = one_hot[...]
            lin = []
            for kind in range(3):
                high, rest = split_low(tab[kind * heads_here + place])
                lin.append(dot(hot, high) + dot(hot, rest))
            heads[0, place] = turn_by(lin[0], sin_ref[...]).astype(LOW)
            heads[1, place] = turn_by(lin[1], sin_ref[...]).astype(LOW)
            heads[2, place] = lin[2].astype(LOW)
            return carried

        lax.fori_loop(0, heads_here, head_inputs, 0)

        def attend(chunk):
            for place in range(heads_here):
                queries = heads[0, place, chunk_rows(chunk), :]
                probability = probabilities(queries, heads[1, place], chunk * rows).astype(LOW)
                mixed = dot(probability, heads[2, place]).astype(LOW)
                att_low[chunk_rows(chunk), place * HD : (place + 1) * HD] = mixed
                turned = mixed.astype(FULL).T
                att_turned[place * HD : (place + 1) * HD, chunk_lanes(chunk)] = turned.astype(LOW)
                gbuf[place * HD : (place + 1) * HD, chunk_lanes(chunk)] = turned

        def project(chunk):
            attend(chunk)
            pl.when(chunk == 0)(lambda: loads[3].wait())
            pl.when(chunk == 0)(lambda: pl.semaphore_wait(barrier, len(greeted)))
            mixed = att_low[chunk_rows(chunk), :]

            def columns(start, size):
                put_part(chunk, start, size, dot_nt(mixed, w_dense[pl.ds(start, size), :]))

            spread(width, columns, 256)
            core_copy(0, chunk).start()
            pl.when((chunk > 0) & (chunk <= AHEAD))(lambda: send_part(0, chunk - 1))

        every_chunk(project)
        rows_copy().start()

    pl.run_scoped(first_scope, pltpu.VMEM((3, width, inner), LOW), pltpu.VMEM((3 * heads_here, vocab, HD), FULL))

    def middle_scope(w_gate, w_up, w_down, cotbuf):
        weight_copies = [
            pltpu.make_async_copy(source, target, weight_sem.at[place])
            for place, (source, target) in enumerate(((w_gate_hbm, w_gate), (w_up_hbm, w_up), (w_down_hbm, w_down)))
        ]
        for copy in weight_copies:
            copy.start()
        for copy in weight_copies:
            copy.wait()

        def feed_forward(chunk):
            branch = take_part(0, chunk)
            residual = alpha * dot(one_hot[chunk_rows(chunk), :], emb[...]) + branch
            centered = residual - row_mean(residual)
            rstd = lax.rsqrt(row_mean(centered * centered) + norm_eps)
            xhat = centered * rstd
            rstd_one[chunk] = rstd
            xbuf[...] = xhat
            park = pltpu.make_async_copy(xbuf, xhat_park.at[chunk], load_sem.at[0])
            park.start()
            hidden_low = (xhat * gain_one[...] + bias_one[...]).astype(LOW)
            put_blocks(hidden_low.astype(FULL))
            keep_columns(cols_own, chunk)
            cols_copy(0, chunk).start()

            def units_tile(start, size):
                cut = pl.ds(start, size)
                gate = dot_nt(w_gate[cut, :], hidden_low)
                up = dot_nt(w_up[cut, :], hidden_low)
                units = mp * local_hidden + start + lax.broadcasted_iota(jnp.int32, (size, rows), 0)
                used = jnp.where(units < FF_USED, 1.0, 0.0)
                square = gate * gate
                bend = jnp.tanh(TANH_SCALE * gate * (1.0 + 0.044715 * square))
                gelu = 0.5 * gate * (1.0 + bend) * used
                slope = 0.5 * (1.0 + bend) + 0.5 * gate * (1.0 - bend * bend) * (
                    TANH_SCALE * (1.0 + 3.0 * 0.044715 * square)
                )
                gate_up[0, cut, chunk_lanes(chunk)] = slope * up * used
                gate_up[1, cut, chunk_lanes(chunk)] = gelu
                active = (gelu * up).astype(LOW)
                act_low[cut, chunk_lanes(chunk)] = active
                send_a[lax.div(chunk, 2), cut, half_chunk(chunk)] = active.astype(FULL)

            tiles(local_hidden, units_tile)
            act_send(0, chunk)
            active = send_a[lax.div(chunk, 2), :, half_chunk(chunk)].T.astype(LOW)
            tiles(
                width, lambda start, size: put_part(chunk, start, size, dot(active, w_down[:, pl.ds(start, size)]))
            )
            core_copy(1, chunk).start()
            park.wait()
            send_part(1, chunk)
            pl.when(chunk + AHEAD < CHUNKS)(lambda: send_part(0, chunk + AHEAD))

        same = jnp.int32(0)
        for place in range(2 * LINE):
            same = same + jnp.where(cluster_ref[place] == cluster_ref[dp], 1, 0)
        weight_row = 1.0 / jnp.full((1, width), same, jnp.int32).astype(FULL)

        def feed_backward(chunk):
            loads = load_all(
                ((xhat_park.at[chunk], xbuf), (cot_hbm.at[chunk_rows(chunk)], cotbuf))
            )
            branch = take_part(1, chunk)
            for copy in loads:
                copy.wait()
            residual = alpha * (xbuf[...] * gain_one[...] + bias_one[...]) + branch
            centered = residual - row_mean(residual)
            rstd = lax.rsqrt(row_mean(centered * centered) + norm_eps)
            xhat = centered * rstd
            obuf[...] = (xhat * gain_two[...] + bias_two[...]).astype(LOW)
            grad_out = cotbuf[...].astype(FULL) * weight_row
            vectors[2:3, :] += jnp.sum(grad_out * xhat, axis=0, keepdims=True)
            vectors[3:4, :] += jnp.sum(grad_out, axis=0, keepdims=True)
            grad_x = grad_out * gain_two[...]
            grad_two = (grad_x - row_mean(grad_x) - xhat * row_mean(grad_x * xhat)) * rstd
            for place in range(width // inner):
                gbuf[place * rows : (place + 1) * rows, :] = grad_two[:, place * inner : (place + 1) * inner]
            stores = load_all(
                ((obuf, block_out.at[chunk_rows(chunk)]), (gbuf, grad_two_park.at[chunk]))
            )
            grad_low = grad_two.astype(LOW)
            put_blocks(grad_low.astype(FULL))
            for place in range(2):
                two_own[place, chunk_rows(chunk), :] = blocks[2 * z + place].astype(LOW)
            for place in range(LINE):
                two_send[place, chunk] = blocks[2 * place + core]
            for step in range(1, LINE):
                two_copy(step, chunk).start()

            def units_tile(start, size):
                cut = pl.ds(start, size)
                grad_act = dot_nt(w_down[cut, :], grad_low)
                for which in range(2):
                    low = (grad_act * gate_up[which, cut, chunk_lanes(chunk)]).astype(LOW)
                    grads_low[pl.ds(which * shift + start, size), chunk_lanes(chunk)] = low
                    gate_up[which, cut, chunk_lanes(chunk)] = low.astype(FULL)

            spread(local_hidden, units_tile)
            pair_send(0, chunk)
            for copy in stores:
                copy.wait()

        def hidden_part(pair):
            both = pl.ds(pl.multiple_of(2 * rows * pair, 2 * rows), 2 * rows)
            grad_gate = gate_up[0, :, both].T.astype(LOW)
            grad_up = gate_up[1, :, both].T.astype(LOW)

            def columns(start, size):
                cut = pl.ds(start, size)
                value = dot(grad_gate, w_gate[:, cut]) + dot(grad_up, w_up[:, cut])
                put_part(2 * pair, start, size, value[:rows])
                put_part(2 * pair + 1, start, size, value[rows:])

            tiles(width, columns)
            for place in range(2):
                core_copy(2, 2 * pair + place).start()

        def take_hidden():
            for chunk in range(CHUNKS):
                cols_copy(0, chunk).wait()
            fetch_columns(0, hidden_theirs)

        def step(turn, carried):
            pl.when(turn == CHUNKS - 1)(lambda: hidden_part(0))
            pl.when(turn == CHUNKS)(take_hidden)
            pl.when(turn < CHUNKS)(lambda: feed_forward(turn))
            pl.when(turn == 1)(lambda: rows_copy().wait())
            pl.when(turn > 0)(lambda: feed_backward(turn - 1))
            return carried

        lax.fori_loop(0, CHUNKS + 1, step, 0)

        hidden_part(1)
        every_chunk(lambda chunk: send_part(2, chunk))

    pl.run_scoped(
        middle_scope,
        pltpu.VMEM((local_hidden, width), LOW),
        pltpu.VMEM((local_hidden, width), LOW),
        pltpu.VMEM((local_hidden, width), LOW),
        pltpu.VMEM((rows, width), LOW),
    )

    def last_scope(theirs, late_theirs, two_theirs, att_theirs, send_b, stage, grad_att, grad_one_own, sums, sums_up, sums_down, sums_below, sums_above, late_own):
        def norm_backward(chunk):
            loads = load_all(((xhat_park.at[chunk], xbuf), (grad_two_park.at[chunk], gbuf)))
            branch = take_part(2, chunk)
            for copy in loads:
                copy.wait()
            grad_two = [gbuf[place * rows : (place + 1) * rows, :] for place in range(width // inner)]
            grad_hidden = alpha * jnp.concatenate(grad_two, axis=1) + branch
            xhat = xbuf[...]
            vectors[0:1, :] += jnp.sum(grad_hidden * xhat, axis=0, keepdims=True)
            vectors[1:2, :] += jnp.sum(grad_hidden, axis=0, keepdims=True)
            grad_x = grad_hidden * gain_one[...]
            grad_one = (grad_x - row_mean(grad_x) - xhat * row_mean(grad_x * xhat)) * rstd_one[chunk]
            put_blocks(grad_one)
            for place in range(2):
                grad_one_own[chunk_rows(chunk), place * block : (place + 1) * block] = blocks[2 * mp + place]
            grad_low = grad_one.astype(LOW)
            put_blocks(grad_low.astype(FULL))
            keep_columns(late_own, chunk)
            grad_mixed = dot(grad_low, w_dense[...]).astype(LOW)
            for place in range(heads_here):
                grad_att[place, chunk_rows(chunk), :] = grad_mixed[:, place * HD : (place + 1) * HD]

        def fetch_units(which, part):
            start, size = spans[part]
            for chunk in range(CHUNKS):
                pair_copy(which, chunk, part).wait()
            views = [stage.at[side, pl.ds(start, size)] for side in range(2)]
            moved(
                [(r_y.at[which, pl.ds(start, size), pl.ds(block * side, block)], views[side]) for side in range(2)]
            )
            for side in range(2):
                theirs[1 + which, start : start + size, block * side : block * (side + 1)] = views[side][...].astype(LOW)

        def fetch_rows(source, target):
            size = source.shape[0]
            views = [stage.at[place, pl.ds(0, size)] for place in range(2)]
            moved([(source.at[:, pl.ds(block * place, block)], views[place]) for place in range(2)])
            for place in range(2):
                target[:, block * place : block * (place + 1)] = views[place][...].astype(LOW)

        def outer_product(target, kind, place, own, other):
            right, right_theirs = (cols_own, late_own)[kind][place], (hidden_theirs, late_theirs)[kind][place]

            def rows_tile(start, size):
                cut = pl.ds(start, size)
                target[cut, :] = dot(own[cut, :], right) + dot(other[cut, :], right_theirs)

            tiles(target.shape[0], rows_tile)

        def down_products():
            for step in range(1, LINE):
                for chunk in range(CHUNKS):
                    two_copy(step, chunk).wait()
            for step in range(1, LINE):
                two_forward(step).start()
            for step in range(1, LINE):
                two_forward(step).wait()
            for chunk in range(CHUNKS):
                pl.when(at_end)(lambda: act_take(1, chunk))
                act_take(2, chunk)
            for step in range(LINE):
                owner = lax.rem(z + step, LINE)
                if step:
                    moved(
                        [
                            (r_two.at[owner, place], blocks.at[pl.ds(CHUNKS * place, CHUNKS)])
                            for place in range(2)
                        ]
                    )
                    for place in range(2):
                        for chunk in range(CHUNKS):
                            piece = blocks[CHUNKS * place + chunk].astype(LOW)
                            two_theirs[place, chunk * rows : (chunk + 1) * rows, :] = piece
                    fetch_rows(r_act.at[owner], theirs.at[0])
                left, right = (theirs.at[0], two_theirs) if step else (act_low, two_own)
                for place in range(2):
                    lanes = slice(place * block, (place + 1) * block)

                    def rows_tile(start, size):
                        cut = pl.ds(start, size)
                        product = dot(left[cut, :], right[place])
                        gate_up[0, cut, lanes] = gate_up[0, cut, lanes] + product if step else product

                    tiles(local_hidden, rows_tile)

        def down_copy():
            return remote(gate_up.at[0, :, half_lanes(1 - y)], r_dny, dny_s, dny_r, y_peer)

        def down_end():
            down_copy().wait()
            moved([(r_dny, stage.at[0])])
            stage[0] = stage[0] + gate_up[0, :, half_lanes(y)]
            moved([(stage.at[0], out_down)])
            for chunk in range(CHUNKS):
                for way in range(2):
                    for hop in range(1, LINE - 1):
                        active, copy = act_copy(way, hop, chunk)
                        pl.when(active)(copy.wait_send)

        def goes(slot, way):
            return z < slot if way == 0 else z > LINE - 1 - slot

        def inner_place(way):
            return z > 0 if way == 0 else z < LINE - 1

        def line_goal(way):
            return at(z_to=jnp.clip(z + 1 - 2 * way, 0, LINE - 1))

        def unit_terms(kind):
            return grads_low.at[pl.ds(pl.multiple_of(kind * shift, 16), local_hidden)], theirs.at[1 + kind]

        def count(way):
            return LINE - 1 - z if way == 0 else z

        def order(kind, slot, way):
            return kind * count(way) + slot - (LINE - count(way))

        def turn_of(number, way):
            many = jnp.maximum(count(way), 1)
            return lax.div(number, many) * (LINE - 1) + lax.rem(number, many) + LINE - 1 - count(way)

        def unit_copy(turn, way, part):
            kind, slot = lax.div(turn, LINE - 1), lax.rem(turn, LINE - 1)
            units = pl.ds(*spans[part])
            home = (send_a, send_b)[way].at[lax.rem(jnp.maximum(order(kind, slot + 1, way), 0), 2), units]
            return remote(
                home, r_rs.at[kind, slot, way, units], rs_s.at[kind, slot, way, part], rs_r.at[kind, slot, way, part],
                line_goal(way),
            )

        def unit_sent(number, way):
            for part in range(2):
                unit_copy(turn_of(jnp.maximum(number, 0), way), way, part).wait_send()

        def unit_slot(turn, part):
            kind, slot = lax.div(turn, LINE - 1), lax.rem(turn, LINE - 1) + 1
            own, other = unit_terms(kind)
            start, size = spans[part]
            cut = slice(start, start + size)
            for way in range(2):

                @pl.when(goes(slot, way))
                def _():
                    number = order(kind, slot, way)
                    home = (send_a, send_b)[way].at[lax.rem(jnp.maximum(number, 0), 2)]
                    if part == 0:
                        pl.when(number >= 2)(lambda: unit_sent(number - 2, way))
                    place = LINE - slot + z if way == 0 else slot - LINE + z
                    home[cut, :] = dot(own[cut, :], cols_own[place]) + dot(other[cut, :], hidden_theirs[place])

                    @pl.when((slot > 1) & inner_place(way))
                    def _():
                        before = jnp.maximum(turn - 1, 0)
                        unit_copy(before, way, part).wait_recv()
                        landed = r_rs.at[lax.div(before, LINE - 1), lax.rem(before, LINE - 1), way, pl.ds(start, size)]
                        moved([(landed, stage.at[way, pl.ds(start, size)])])
                        home[cut, :] = home[cut, :] + stage[way, cut, :]

                    unit_copy(turn, way, part).start()

        def unit_end():
            kind = 0
            own, other = unit_terms(kind)
            outer_product(stage.at[0], 0, z, own, other)
            for way in range(2):

                @pl.when(inner_place(way))
                def _():
                    for part in range(2):
                        unit_copy(kind * (LINE - 1) + LINE - 2, way, part).wait_recv()
                    moved([(r_rs.at[kind, LINE - 2, way], stage.at[1])])
                    stage[0] = stage[0] + stage[1]

            moved([(stage.at[0], out_gate)])

        def last_product():
            own, other = unit_terms(1)
            outer_product(stage.at[0], 0, z, own, other)
            moved([(stage.at[0], out_up)])

        def last_landed():
            for way in range(2):
                for part in range(2):
                    pl.when(inner_place(way))(unit_copy(2 * LINE - 3, way, part).wait_recv)

        def late_home(slot, way):
            return parts.at[:, way, :, pl.ds(block * (slot - 1), block)]

        def late_copy(slot, way):
            return remote(
                late_home(slot, way), r_rsd.at[slot - 1, way], rs_s.at[2, slot - 1, way, 0],
                rs_r.at[2, slot - 1, way, 0], line_goal(way),
            )

        def late_product(place, piece):
            cut = slice(piece * rows, (piece + 1) * rows)
            return dot(att_turned[cut, :], late_own[place]) + dot(att_theirs[cut, :], late_theirs[place])

        def late_slot(slot):
            for way in range(2):

                @pl.when(goes(slot, way))
                def _():
                    home = late_home(slot, way)
                    place = LINE - slot + z if way == 0 else slot - LINE + z
                    for piece in range(CHUNKS):
                        home[piece] = late_product(place, piece)
                    if slot > 1:

                        @pl.when(inner_place(way))
                        def _():
                            late_copy(slot - 1, way).wait_recv()
                            arrived = blocks.at[pl.ds(0, CHUNKS)]
                            moved([(r_rsd.at[slot - 2, way], arrived)])
                            home[...] = home[...] + arrived[...]

                    late_copy(slot, way).start()

        def late_end():
            total, arrived = blocks.at[pl.ds(0, CHUNKS)], blocks.at[pl.ds(CHUNKS, CHUNKS)]
            for piece in range(CHUNKS):
                total[piece] = late_product(z, piece)
            for way in range(2):

                @pl.when(inner_place(way))
                def _():
                    late_copy(LINE - 1, way).wait_recv()
                    moved([(r_rsd.at[LINE - 2, way], arrived)])
                    total[...] = total[...] + arrived[...]

            for piece in range(CHUNKS):
                gbuf[0:block, piece * rows : (piece + 1) * rows] = total[piece].T
            moved([(gbuf.at[pl.ds(0, block)], out_dense)])

        def last_sent():
            for way in range(2):
                for slot in range(1, LINE):
                    pl.when(goes(slot, way))(late_copy(slot, way).wait_send)
                pl.when(count(way) > 0)(lambda: unit_sent(2 * count(way) - 1, way))
                pl.when(count(way) > 0)(lambda: unit_sent(2 * count(way) - 2, way))

        def attention_backward(place, carried):
            hot_t = hot_turned[...]
            queries, keys, values = heads[0, place], heads[1, place], heads[2, place]
            grad_mixed = grad_att[place]
            probability = probabilities(queries, keys, 0)
            grad_prob = dot_nt(grad_mixed, values)
            centre = jnp.sum(grad_prob * probability, axis=-1, keepdims=True)
            grad_scores = (probability * (grad_prob - centre)).astype(LOW)
            grad_queries = dot(grad_scores, keys) * score_scale
            grad_keys = dot_tn(grad_scores, queries) * score_scale
            grad_values = dot_tn(probability.astype(LOW), grad_mixed)
            sums[0, 0:vocab, head_lanes(place)] = dot(hot_t, turn_by(grad_queries, -sin_ref[...]).astype(LOW))
            sums[0, 0:vocab, head_lanes(place, inner)] = dot(hot_t, turn_by(grad_keys, -sin_ref[...]).astype(LOW))
            sums[1, 0:vocab, head_lanes(place)] = dot(hot_t, grad_values.astype(LOW))
            return carried

        def small_sums():
            lax.fori_loop(0, heads_here, attention_backward, 0)
            hot_t = hot_turned[...]
            high, rest = split_low(grad_one_own[...])
            sums[1, 0:vocab, heads_here * HD :] = dot(hot_t, high) + dot(hot_t, rest)
            for side in range(2):
                sums[side, vocab:, :] = vectors[:, side * (width // 2) : (side + 1) * (width // 2)]
            sums_pair().start()

        def sums_pair():
            return remote(sums.at[1 - y], r_sums.at[0], sums_s.at[0], sums_r.at[0], y_peer)

        def sums_line(way):
            source = (sums_up, sums_down)[way]
            goal = jnp.clip(z + 1 - 2 * way, 0, LINE - 1)
            return remote(source, r_sums.at[1 + way], sums_s.at[1 + way], sums_r.at[1 + way], at(z_to=goal))

        def sums_back():
            return remote(sums.at[y], r_sums.at[3], sums_s.at[3], sums_r.at[3], y_peer)

        def sums_first():
            sums_pair().wait()
            moved([(r_sums.at[0], sums_below)])
            sums[y] = sums[y] + sums_below[...]

            @pl.when(z == 0)
            def _():
                sums_up[...] = sums[y]
                sums_line(0).start()

            @pl.when(z == LINE - 1)
            def _():
                sums_down[...] = sums[y]
                sums_line(1).start()

        def sums_up_step():
            sums_line(0).wait_recv()
            moved([(r_sums.at[1], sums_below)])
            sums_up[...] = sums[y] + sums_below[...]
            sums_line(0).start()

        def sums_down_step():
            sums_line(1).wait_recv()
            moved([(r_sums.at[2], sums_above)])
            sums_down[...] = sums[y] + sums_above[...]
            sums_line(1).start()

        def sums_near():
            pl.when(z == 1)(sums_up_step)
            pl.when(z == LINE - 2)(sums_down_step)

        def sums_far():
            pl.when(z == LINE - 2)(sums_up_step)
            pl.when(z == 1)(sums_down_step)

        def sums_middle():
            @pl.when(z == LINE - 1)
            def _():
                sums_line(0).wait_recv()
                moved([(r_sums.at[1], sums_below)])

            @pl.when(z == 0)
            def _():
                sums_line(1).wait_recv()
                moved([(r_sums.at[2], sums_above)])

            @pl.when(z > 0)
            def _():
                sums[y] = sums[y] + sums_below[...]

            @pl.when(z < LINE - 1)
            def _():
                sums[y] = sums[y] + sums_above[...]

            sums_back().start()

        def sums_end():
            sums_back().wait()
            pl.when(z < LINE - 1)(sums_line(0).wait_send)
            pl.when(z > 0)(sums_line(1).wait_send)
            moved([(r_sums.at[3], sums.at[1 - y])])
            lanes = pl.ds(pl.multiple_of(lax.rem(dp, LINE) * block, block), block)
            moved([(sums.at[lax.div(dp, LINE), pl.ds(vocab, 8), lanes], out_norms)])

        def by_token(kind, rows_of):
            side, start = ((0, 0), (0, inner), (1, 0), (1, inner))[kind]
            return sums[side, rows_of, start : start + inner]

        def head_gradients():
            own_columns = emb[:, pl.ds(pl.multiple_of(dp * block, block), block)]
            for kind, result in enumerate((out_query, out_key, out_value)):
                high, rest = split_low(by_token(kind, slice(0, vocab)))
                gbuf[0:block, :] = dot_tn(own_columns, high) + dot_tn(own_columns, rest)
                moved([(gbuf.at[pl.ds(0, block)], result)])

        table_rows = vocab // (2 * LINE)
        table_own = pl.ds(pl.multiple_of(dp * table_rows, table_rows), table_rows)

        def table_part():
            for kind, weight in enumerate((w_query_hbm, w_key_hbm, w_value_hbm)):
                moved([(weight, w_dense)])
                pieces = jnp.concatenate(split_low(by_token(kind, table_own)), axis=0)

                def columns(start, size):
                    cut = pl.ds(start, size)
                    both = dot_nt(pieces, w_dense[cut, :])
                    both = both[:table_rows] + both[table_rows:]
                    xbuf[0:table_rows, cut] = both if kind == 0 else xbuf[0:table_rows, cut] + both

                tiles(width, columns)
            quarter = pl.ds(pl.multiple_of(mp * inner, inner), inner)
            xbuf[0:table_rows, quarter] = xbuf[0:table_rows, quarter] + alpha * by_token(3, table_own)
            table_copy(0).start()

        def table_middle():
            table_copy(0).wait()
            xbuf[table_rows : 2 * table_rows, :] = xbuf[0:table_rows, :] + table_core[...]
            table_copy(1).start()

        def table_end():
            table_copy(1).wait()
            xbuf[0:table_rows, :] = 0.1 * (xbuf[table_rows : 2 * table_rows, :] + table_x[...])
            moved([(xbuf.at[pl.ds(0, table_rows)], out_table)])

        def table_copy(turn):
            target, device = ((table_core, core_peer), (table_x, x_peer))[turn]
            return remote(xbuf.at[pl.ds(turn * table_rows, table_rows)], target, table_s.at[turn], table_r.at[turn], device)

        def act_pass():
            for chunk in range(CHUNKS):
                act_take(1, chunk)
                act_send(2, chunk)

        at_end = (z == 0) | (z == LINE - 1)

        for chunk in range(CHUNKS):
            for way in range(2):
                active, copy = act_copy(way, 0, chunk)
                pl.when(active)(copy.wait_send)
        def one_turn(turn, carried):
            for part in range(2):
                pl.when(turn == 0)(lambda: fetch_units(0, part))
                unit_slot(turn, part)

            @pl.when(turn == 0)
            def _():
                pair_send(1, 0)
                pair_send(1, 1)
                for chunk in range(CHUNKS):
                    act_take(0, chunk)
                    act_send(1, chunk)

            @pl.when(turn == 1)
            def _():
                every_chunk(norm_backward)
                small_sums()
                pl.when(~at_end)(act_pass)
                sums_first()
                for chunk in range(CHUNKS):
                    cols_copy(1, chunk).start()
                pair_send(1, 2)
                pair_send(1, 3)

            @pl.when(turn == 2)
            def _():
                sums_near()
                for chunk in range(CHUNKS):
                    cols_copy(1, chunk).wait()
                fetch_columns(1, late_theirs)
                fetch_rows(r_att, att_theirs)
                late_slot(1)

            lately = (turn == 3) & ~at_end | (turn == 2) & at_end
            pl.when(lately)(lambda: late_slot(2))
            pl.when((turn == 3) & ~at_end | (turn == 4) & at_end)(down_products)
            pl.when(lately)(lambda: late_slot(3))

            @pl.when(turn == 2)
            def _():
                for part in range(2):
                    fetch_units(1, part)

            @pl.when((turn == 3) & ~at_end | (turn == 5) & at_end)
            def _():
                sums_far()
                sums_middle()
                down_copy().start()

            @pl.when((turn == 4) & ~at_end | (turn == 5) & at_end)
            def _():
                sums_end()
                head_gradients()
                table_part()

            return carried

        lax.fori_loop(0, 2 * (LINE - 1), one_turn, 0)
        unit_end()
        last_product()
        late_end()
        table_middle()
        table_end()
        down_end()
        last_landed()
        last_sent()

    pl.run_scoped(
        last_scope,
        pltpu.VMEM((3, local_hidden, length), LOW),
        pltpu.VMEM((LINE, length, block), LOW),
        pltpu.VMEM((2, length, block), LOW),
        pltpu.VMEM((inner, length), LOW),
        pltpu.VMEM((2, local_hidden, block), FULL),
        pltpu.VMEM((2, local_hidden, block), FULL),
        pltpu.VMEM((heads_here, length, HD), LOW),
        pltpu.VMEM((length, 2 * block), FULL),
        pltpu.VMEM((2,) + r_sums.shape[1:], FULL),
        pltpu.VMEM(r_sums.shape[1:], FULL),
        pltpu.VMEM(r_sums.shape[1:], FULL),
        pltpu.VMEM(r_sums.shape[1:], FULL),
        pltpu.VMEM(r_sums.shape[1:], FULL),
        pltpu.VMEM(cols_own.shape, LOW),
    )


def write_kernel(*refs):
    count = 10
    late = 7
    sources, landed = refs[:count], refs[count]
    targets = refs[count + 1 : 2 * count + 4]
    rooms, terms, first_sem, second_sem = refs[2 * count + 4 : 3 * count + 4], *refs[3 * count + 4 : 3 * count + 7]
    z = lax.div(lax.axis_index("dp"), 2)
    order = [late] + [place for place in range(count) if place != late]
    loads = {
        place: pltpu.make_async_copy(sources[place], rooms[place], first_sem.at[place]) for place in range(count)
    }
    more = [
        pltpu.make_async_copy(landed.at[1, LINE - 2, way], terms.at[way], first_sem.at[count + way]) for way in range(2)
    ]
    for copy in more:
        copy.start()
    for place in order:
        loads[place].start()
    stores = []
    for copy in more:
        copy.wait()
    for place in order:
        loads[place].wait()
        room = rooms[place]
        if place == late:
            for way, active in ((0, z > 0), (1, z < LINE - 1)):

                @pl.when(active)
                def _():
                    room[...] = room[...] + terms[way]

        if place < count - 1:
            stores.append(pltpu.make_async_copy(room, targets[place], second_sem.at[place]))
            stores[-1].start()
        else:
            for vector in range(4):
                targets[place + vector][...] = room[vector : vector + 1, :]
    for copy in stores:
        copy.wait()


def write_out(results, landed):
    hbm = pl.BlockSpec(memory_space=pl.ANY)
    rows = jax.ShapeDtypeStruct((1, results[-1].shape[1]), FULL)
    shapes = [jax.ShapeDtypeStruct(value.shape, value.dtype) for value in results[:-1]] + [rows] * 4
    return pl.pallas_call(
        write_kernel,
        out_shape=shapes,
        in_specs=[hbm] * (len(results) + 1),
        out_specs=[hbm] * (len(results) - 1) + [pl.BlockSpec(memory_space=pltpu.VMEM)] * 4,
        scratch_shapes=[pltpu.VMEM(value.shape, value.dtype) for value in results]
        + [pltpu.VMEM((2,) + results[7].shape, FULL)]
        + [pltpu.SemaphoreType.DMA((len(results) + 2,))] * 2,
        compiler_params=pltpu.CompilerParams(vmem_limit_bytes=62 * 2**20),
    )(*results, landed)


def local_fast(
    token_ids,
    prefix_lengths,
    cluster_ids,
    embedding,
    w_query,
    w_key,
    w_value,
    w_dense,
    w_gate,
    w_up,
    w_down,
    norm1_gain,
    norm1_bias,
    norm2_gain,
    norm2_bias,
    cotangent,
):
    length = token_ids.shape[0]
    vocab, width = embedding.shape
    inner = w_query.shape[1]
    heads_here = inner // HD
    local_hidden = w_gate.shape[1]
    rows = length // CHUNKS
    block = width // (2 * LINE)
    shift = (local_hidden + 15) // 16 * 16
    frequency = 10000.0 ** (np.arange(HD // 2) * (-2.0 / HD))
    angles = np.arange(length)[:, None] * frequency[None, :]
    cosine = np.concatenate([np.cos(angles)] * 2, axis=1).astype(np.float32)
    sine = np.concatenate([-np.sin(angles), np.sin(angles)], axis=1).astype(np.float32)
    norms = [vector.reshape(1, width) for vector in (norm1_gain, norm1_bias, norm2_gain, norm2_bias)]

    hbm = pl.BlockSpec(memory_space=pl.ANY)
    vmem = pl.BlockSpec(memory_space=pltpu.VMEM)
    smem = pl.BlockSpec(memory_space=pltpu.SMEM)
    sums_rows = vocab + 8
    table_rows = vocab // (2 * LINE)
    shapes = [
        ((length, width), LOW),
        ((table_rows, width), FULL),
        ((block, inner), FULL),
        ((block, inner), FULL),
        ((block, inner), FULL),
        ((block, inner), FULL),
        ((local_hidden, block), FULL),
        ((local_hidden, block), FULL),
        ((local_hidden, block), FULL),
        ((8, block), FULL),
        ((LINE, local_hidden, length), FULL),
        ((LINE, 2, CHUNKS, rows, block), FULL),
        ((2, local_hidden, length), FULL),
        ((2, LINE, CHUNKS, rows, block), FULL),
        ((inner, length), FULL),
        ((CHUNKS, rows, width), FULL),
        ((CHUNKS, length, inner), FULL),
        ((local_hidden, block), FULL),
        ((2, LINE - 1, 2, local_hidden, block), FULL),
        ((LINE - 1, 2, CHUNKS, rows, block), FULL),
        ((4, sums_rows, width // 2), FULL),
    ]
    scratch = [
        ((CHUNKS, 2, rows, width // 2), FULL),
        ((CHUNKS, rows, width // 2), FULL),
        ((2, CHUNKS, rows, width // 2), FULL),
        ((CHUNKS, rows, width // 2), FULL),
        ((2 * LINE, rows, block), FULL),
        ((rows, width), FULL),
        ((length, inner), FULL),
        ((rows, width), LOW),
        ((2, local_hidden, length), FULL),
        ((2 * shift, length), LOW),
        ((local_hidden, length), LOW),
        ((2, local_hidden, block), FULL),
        ((LINE, length, block), LOW),
        ((2, CHUNKS, rows, block), FULL),
        ((LINE, length, block), LOW),
        ((2, length, block), LOW),
        ((LINE, CHUNKS, rows, block), FULL),
        ((length, inner), LOW),
        ((inner, length), LOW),
        ((3, heads_here, length, HD), LOW),
        ((width, inner), LOW),
        ((length, vocab), LOW),
        ((vocab, length), LOW),
        ((CHUNKS, rows, 1), FULL),
        ((8, width), FULL),
        ((table_rows, width), FULL),
        ((table_rows, width), FULL),
    ]
    dma = pltpu.SemaphoreType.DMA
    each = (3, CHUNKS)
    semaphores = [
        each, each, each, each, each, each, (2, LINE - 1, CHUNKS), (2, LINE - 1, CHUNKS), each, each, (3,), (3,),
        (2, CHUNKS), (2, CHUNKS), (2,), (2,), (2, CHUNKS, 2), (2, CHUNKS, 2), None, None, None, None,
        (3, LINE - 1, 2, 2), (3, LINE - 1, 2, 2), (4,), (4,), (2,), (2,), (4,), (4,),
    ]
    results = pl.pallas_call(
        functools.partial(layer_kernel, length, width, local_hidden),
        out_shape=[jax.ShapeDtypeStruct(shape, dtype) for shape, dtype in shapes],
        in_specs=[smem] * 2 + [vmem] * 8 + [hbm] * 8,
        out_specs=[hbm] * len(shapes),
        scratch_shapes=[pltpu.VMEM(shape, dtype) for shape, dtype in scratch]
        + [dma if shape is None else dma(shape) for shape in semaphores],
        compiler_params=pltpu.CompilerParams(
            collective_id=0, has_side_effects=True, vmem_limit_bytes=62 * 2**20
        ),
    )(
        prefix_lengths,
        cluster_ids,
        token_ids.reshape(1, length),
        embedding,
        cosine,
        sine,
        *norms,
        w_query,
        w_key,
        w_value,
        w_dense,
        w_gate.T,
        w_up.T,
        w_down.T,
        cotangent,
    )
    written = write_out(results[:10], results[18])
    block_out, table, out_query, out_key, out_value, out_dense, out_gate, out_up, out_down = written[:9]
    out_norms = written[9:]
    return (
        block_out,
        table,
        out_query,
        out_key,
        out_value,
        out_dense,
        out_gate.T,
        out_up.T,
        out_down.T,
        out_norms[0].reshape(width // (2 * LINE)),
        out_norms[1].reshape(width // (2 * LINE)),
        out_norms[2].reshape(width // (2 * LINE)),
        out_norms[3].reshape(width // (2 * LINE)),
    )


def solution(mesh):
    fast = mesh.shape["dp"] == 2 * LINE and mesh.shape["mp"] == 4
    return jax.shard_map(
        local_fast if fast else local_general,
        mesh=mesh,
        in_specs=(
            P("dp"),
            P("dp"),
            P(),
            P(),
            P(None, "mp"),
            P(None, "mp"),
            P(None, "mp"),
            P(None, "mp"),
            P(None, "mp"),
            P(None, "mp"),
            P(None, "mp"),
            P(),
            P(),
            P(),
            P(),
            P("dp", None),
        ),
        out_specs=(
            P("dp", None),
            P("dp", None),
            P("dp", "mp"),
            P("dp", "mp"),
            P("dp", "mp"),
            P("dp", "mp"),
            P("dp", "mp"),
            P("dp", "mp"),
            P("dp", "mp"),
            P("dp"),
            P("dp"),
            P("dp"),
            P("dp"),
        ),
        check_vma=False,
    )
```

```python
import functools
import math

import jax
import jax.numpy as jnp
import numpy as np
from jax import lax
from jax.experimental import pallas as pl
from jax.experimental.pallas import tpu as pltpu
from jax.sharding import PartitionSpec as P

HD = 128
FF_USED = 5461


deep_alpha = math.sqrt(48.0)
norm_eps = 1e-05
highest = lax.Precision.HIGHEST


def layer_norm(inputs, norm_gain, norm_bias):
    center = jnp.mean(inputs, axis=-1, keepdims=True)
    centered = inputs - center
    spread = jnp.mean(centered * centered, axis=-1, keepdims=True)
    return centered * lax.rsqrt(spread + norm_eps) * norm_gain + norm_bias


def rotary_tables(length, head_width):
    half_width = head_width // 2
    frequency = jnp.exp(
        jnp.arange(half_width, dtype=jnp.float32) * (-2.0 * math.log(10000.0) / head_width)
    )
    angles = jnp.arange(length, dtype=jnp.float32)[:, None] * frequency[None, :]
    return (jnp.cos(angles), jnp.sin(angles))


def rotate(inputs, cosine, sine):
    half_width = inputs.shape[-1] // 2
    first = inputs[..., :half_width]
    second = inputs[..., half_width:]
    cosine = cosine[:, None, :]
    sine = sine[:, None, :]
    return jnp.concatenate(
        [first * cosine - second * sine, second * cosine + first * sine], axis=-1
    )


def row_mask(row_begin, row_count, length, prefix):
    columns = jnp.arange(length, dtype=jnp.int32)
    row_index = row_begin + jnp.arange(row_count, dtype=jnp.int32)
    return (columns[None, :] < prefix) | (columns[None, :] <= row_index[:, None])


def block_scores(query_block, keys_rot, visible, score_scale):
    scores = (
        jnp.einsum("bhd,khd->hbk", query_block, keys_rot, preferred_element_type=jnp.float32)
        * score_scale
    )
    return jnp.where(visible[None, :, :], scores, -1e30)


def attention_forward(queries, keys_rot, values_in, prefix, row_block):
    length = queries.shape[0]
    score_scale = 1.0 / math.sqrt(HD)

    def one_block(row_begin):
        scores = block_scores(
            queries, keys_rot, row_mask(row_begin, row_block, length, prefix), score_scale
        )
        row_max = jnp.max(scores, axis=-1, keepdims=True)
        weights = jnp.exp(scores - row_max)
        total_weight = jnp.sum(weights, axis=-1, keepdims=True)
        probability = (weights / total_weight).astype(jnp.bfloat16)
        mixed_block = jnp.einsum(
            "hbk,khd->bhd", probability, values_in, preferred_element_type=jnp.float32
        )
        return (mixed_block, row_max + jnp.log(total_weight))

    starts = jnp.arange(length // row_block, dtype=jnp.int32) * row_block
    attended, log_total = lax.map(one_block, starts)
    return (attended.reshape(length, -1), log_total)


def attention_backward(queries, keys_rot, values_in, prefix, row_block, log_total, grad_mixed):
    length = queries.shape[0]
    score_scale = 1.0 / math.sqrt(HD)

    def one_block(carried, inputs):
        grad_keys, grad_values = carried
        row_begin, block_total = inputs
        scores = block_scores(
            queries, keys_rot, row_mask(row_begin, row_block, length, prefix), score_scale
        )
        probability = jnp.exp(scores - block_total)
        prob_low = probability.astype(jnp.bfloat16)
        grad_prob = jnp.einsum(
            "bhd,khd->hbk", grad_mixed, values_in, preferred_element_type=jnp.float32
        )
        centre = jnp.sum(grad_prob * probability, axis=-1, keepdims=True)
        grad_scores = (probability * (grad_prob - centre)).astype(jnp.bfloat16)
        grad_query = (
            jnp.einsum("hbk,khd->bhd", grad_scores, keys_rot, preferred_element_type=jnp.float32)
            * score_scale
        )
        grad_keys = (
            grad_keys
            + jnp.einsum("hbk,bhd->khd", grad_scores, queries, preferred_element_type=jnp.float32)
            * score_scale
        )
        grad_values = grad_values + jnp.einsum(
            "hbk,bhd->khd", prob_low, grad_mixed, preferred_element_type=jnp.float32
        )
        return ((grad_keys, grad_values), grad_query)

    starts = jnp.arange(length // row_block, dtype=jnp.int32) * row_block
    zeros_kv = jnp.zeros(keys_rot.shape, jnp.float32)
    (grad_keys, grad_values), grad_queries = lax.scan(
        one_block, (zeros_kv, zeros_kv), (starts, log_total)
    )
    return (grad_queries.reshape(queries.shape), grad_keys, grad_values)


def local_general(
    token_ids,
    prefix_lengths,
    cluster_ids,
    embedding,
    w_query,
    w_key,
    w_value,
    w_dense,
    w_gate,
    w_up,
    w_down,
    norm1_gain,
    norm1_bias,
    norm2_gain,
    norm2_bias,
    cotangent,
):
    length = token_ids.shape[0]
    vocab_rows = embedding.shape[0]
    row_block = min(512, length)
    local_heads = w_query.shape[1] // HD
    local_hidden = w_gate.shape[1]
    one_hot = (token_ids[:, None] == jnp.arange(vocab_rows, dtype=jnp.int32)[None, :]).astype(
        jnp.bfloat16
    )
    embedded_low = jnp.dot(one_hot, embedding, preferred_element_type=jnp.float32).astype(
        jnp.bfloat16
    )
    embedded = embedded_low.astype(jnp.float32)
    cosine, sine = rotary_tables(length, HD)
    prefix = prefix_lengths[0]
    own_cluster = cluster_ids[lax.axis_index("dp")]
    seq_weight = 1.0 / jnp.sum((cluster_ids == own_cluster).astype(jnp.float32))

    def project(weight_in):
        return jnp.dot(embedded_low, weight_in, preferred_element_type=jnp.float32).reshape(
            length, local_heads, HD
        )

    queries = rotate(project(w_query), cosine, sine).astype(jnp.bfloat16)
    keys_rot = rotate(project(w_key), cosine, sine).astype(jnp.bfloat16)
    values_in = project(w_value).astype(jnp.bfloat16)
    attended, log_total = attention_forward(queries, keys_rot, values_in, prefix, row_block)
    attended_low = attended.astype(jnp.bfloat16)
    branch = lax.psum(
        jnp.einsum("lh,dh->ld", attended_low, w_dense, preferred_element_type=jnp.float32), "mp"
    )
    residual_one = deep_alpha * embedded + branch
    hidden, norm_one_pull = jax.vjp(layer_norm, residual_one, norm1_gain, norm1_bias)
    hidden_low = hidden.astype(jnp.bfloat16)
    gate_proj = jnp.dot(hidden_low, w_gate, preferred_element_type=jnp.float32)
    up_proj = jnp.dot(hidden_low, w_up, preferred_element_type=jnp.float32)
    unit_index = lax.axis_index("mp") * local_hidden + jnp.arange(local_hidden, dtype=jnp.int32)
    used_mask = (unit_index < FF_USED).astype(jnp.float32)

    def gated_unit(gate_in, up_in):
        return jax.nn.gelu(gate_in, approximate=True) * up_in * used_mask

    activation, gated_pull = jax.vjp(gated_unit, gate_proj, up_proj)
    activation_low = activation.astype(jnp.bfloat16)
    branch_two = lax.psum(
        jnp.einsum("lf,df->ld", activation_low, w_down, preferred_element_type=jnp.float32), "mp"
    )
    residual_two = deep_alpha * hidden + branch_two
    final, norm_two_pull = jax.vjp(layer_norm, residual_two, norm2_gain, norm2_bias)
    grad_out = cotangent.astype(jnp.float32) * seq_weight
    grad_two, grad_gain_two, grad_bias_two = norm_two_pull(grad_out)
    grad_branch_two = grad_two.astype(jnp.bfloat16)
    grad_w_down = jnp.einsum(
        "ld,lf->df", grad_branch_two, activation_low, preferred_element_type=jnp.float32
    )
    grad_act = jnp.dot(grad_branch_two, w_down, preferred_element_type=jnp.float32)
    grad_gate, grad_up = gated_pull(grad_act)
    grad_gate_low = grad_gate.astype(jnp.bfloat16)
    grad_up_low = grad_up.astype(jnp.bfloat16)
    grad_w_gate = jnp.einsum(
        "ld,lf->df", hidden_low, grad_gate_low, preferred_element_type=jnp.float32
    )
    grad_w_up = jnp.einsum("ld,lf->df", hidden_low, grad_up_low, preferred_element_type=jnp.float32)
    hidden_part = jnp.einsum(
        "lf,df->ld", grad_gate_low, w_gate, preferred_element_type=jnp.float32
    ) + jnp.einsum("lf,df->ld", grad_up_low, w_up, preferred_element_type=jnp.float32)
    grad_hidden = deep_alpha * grad_two + lax.psum(hidden_part, "mp")
    feed_sums = (
        lax.psum_scatter(grad_w_gate, "dp", scatter_dimension=0, tiled=True),
        lax.psum_scatter(grad_w_up, "dp", scatter_dimension=0, tiled=True),
        lax.psum_scatter(grad_w_down, "dp", scatter_dimension=0, tiled=True),
        lax.psum_scatter(grad_gain_two, "dp", scatter_dimension=0, tiled=True),
        lax.psum_scatter(grad_bias_two, "dp", scatter_dimension=0, tiled=True),
    )
    grad_one, grad_gain_one, grad_bias_one = norm_one_pull(grad_hidden)
    grad_branch = grad_one.astype(jnp.bfloat16)
    grad_w_dense = jnp.einsum(
        "ld,lh->dh", grad_branch, attended_low, preferred_element_type=jnp.float32
    )
    grad_attended = jnp.dot(grad_branch, w_dense, preferred_element_type=jnp.float32).astype(
        jnp.bfloat16
    )
    grad_attended = grad_attended.reshape(length, local_heads, HD)
    grad_queries, grad_keys, grad_values = attention_backward(
        queries, keys_rot, values_in, prefix, row_block, log_total, grad_attended
    )
    grad_query_lin = rotate(grad_queries, cosine, -sine).astype(jnp.bfloat16).reshape(length, -1)
    grad_key_lin = rotate(grad_keys, cosine, -sine).astype(jnp.bfloat16).reshape(length, -1)
    grad_value_lin = grad_values.astype(jnp.bfloat16).reshape(length, -1)
    grad_w_query = jnp.einsum(
        "ld,lh->dh", embedded_low, grad_query_lin, preferred_element_type=jnp.float32
    )
    grad_w_key = jnp.einsum(
        "ld,lh->dh", embedded_low, grad_key_lin, preferred_element_type=jnp.float32
    )
    grad_w_value = jnp.einsum(
        "ld,lh->dh", embedded_low, grad_value_lin, preferred_element_type=jnp.float32
    )
    input_part = (
        jnp.einsum("lh,dh->ld", grad_query_lin, w_query, preferred_element_type=jnp.float32)
        + jnp.einsum("lh,dh->ld", grad_key_lin, w_key, preferred_element_type=jnp.float32)
        + jnp.einsum("lh,dh->ld", grad_value_lin, w_value, preferred_element_type=jnp.float32)
    )
    grad_embedded = deep_alpha * grad_one + lax.psum(input_part, "mp")
    grad_table = 0.1 * jnp.dot(one_hot.astype(jnp.float32).T, grad_embedded, precision=highest)
    attn_sums = (
        lax.psum_scatter(grad_table, "dp", scatter_dimension=0, tiled=True),
        lax.psum_scatter(grad_w_query, "dp", scatter_dimension=0, tiled=True),
        lax.psum_scatter(grad_w_key, "dp", scatter_dimension=0, tiled=True),
        lax.psum_scatter(grad_w_value, "dp", scatter_dimension=0, tiled=True),
        lax.psum_scatter(grad_w_dense, "dp", scatter_dimension=0, tiled=True),
        lax.psum_scatter(grad_gain_one, "dp", scatter_dimension=0, tiled=True),
        lax.psum_scatter(grad_bias_one, "dp", scatter_dimension=0, tiled=True),
    )
    summed = (
        attn_sums[0],
        attn_sums[1],
        attn_sums[2],
        attn_sums[3],
        attn_sums[4],
        feed_sums[0],
        feed_sums[1],
        feed_sums[2],
        attn_sums[5],
        attn_sums[6],
        feed_sums[3],
        feed_sums[4],
    )
    return (
        final.astype(jnp.bfloat16),
        summed[0],
        summed[1],
        summed[2],
        summed[3],
        summed[4],
        summed[5],
        summed[6],
        summed[7],
        summed[8],
        summed[9],
        summed[10],
        summed[11],
    )


LINE = 4
MESH = pl.DeviceIdType.MESH
CHUNKS = 4
AHEAD = 2
LOW = jnp.bfloat16
FULL = jnp.float32
TANH_SCALE = math.sqrt(2.0 / math.pi)


def dot(left, right):
    return jnp.dot(left, right, preferred_element_type=FULL)


def dot_nt(left, right):
    return lax.dot_general(left, right, (((1,), (1,)), ((), ())), preferred_element_type=FULL)


def dot_tn(left, right):
    return lax.dot_general(left, right, (((0,), (0,)), ((), ())), preferred_element_type=FULL)


def split_low(value):
    high = value.astype(LOW)
    return high, (value - high.astype(FULL)).astype(LOW)


def row_mean(value):
    return jnp.mean(value, axis=-1, keepdims=True)


def spread(size, body, tile=512):
    for start in range(0, size, tile):
        body(start, min(tile, size - start))


def tiles(size, body, tile=512):
    whole = size // tile
    lax.fori_loop(0, whole, lambda step, carried: (body(pl.multiple_of(step * tile, tile), tile), carried)[1], 0)
    if size % tile:
        body(whole * tile, size % tile)


def layer_kernel(
    length, width, local_hidden,
    prefix_ref, cluster_ref, ids_row, emb, cos_ref, sin_ref, gain_one, bias_one, gain_two, bias_two, w_query_hbm, w_key_hbm, w_value_hbm, w_dense_hbm,
    w_gate_hbm, w_up_hbm, w_down_hbm, cot_hbm,
    block_out, out_table, out_query, out_key, out_value, out_dense, out_gate, out_up, out_down, out_norms,
    r_act, r_two, r_y, r_cols, r_att, xhat_park, grad_two_park, r_dny, r_rs, r_late, r_dz, r_dx, r_sums,
    parts, core_in, x_in, back_in, blocks, xbuf, gbuf, obuf, gate_up, grads_low, act_low, send_a, cols_own, cols_send,
    hidden_theirs, two_own, two_send, att_low, att_turned, heads, w_dense, one_hot, hot_turned, rstd_one, vectors, table_core, table_x,
    core_s, core_r, x_s, x_r, back_s, back_r, act_s, act_r, two_s, two_r, fwd_two_s, fwd_two_r, cols_s, cols_r, fwd_s,
    fwd_r, ys_s, ys_r, att_s, att_r, dny_s, dny_r, late_s, late_r, dz_s, dz_r, dx_s, dx_r, rs_s, rs_r, sums_s, sums_r, table_s, table_r, load_sem, weight_sem,
):
    dp, mp = lax.axis_index("dp"), lax.axis_index("mp")
    z, y = lax.div(dp, 2), lax.rem(dp, 2)
    x, core = lax.div(mp, 2), lax.rem(mp, 2)
    rows = length // CHUNKS
    heads_here = heads.shape[1]
    inner = heads_here * HD
    vocab = emb.shape[0]
    shift = (local_hidden + 15) // 16 * 16
    near = (local_hidden // 2 + 15) // 16 * 16
    spans = ((0, near), (near, local_hidden - near))
    block = width // (2 * LINE)
    alpha = jnp.float32(deep_alpha)

    def at(z_to=None, y_to=None, x_to=None, core_to=None):
        z_to = z if z_to is None else z_to
        y_to = y if y_to is None else y_to
        x_to = x if x_to is None else x_to
        core_to = core if core_to is None else core_to
        return (2 * z_to + y_to, 2 * x_to + core_to)

    core_peer = at(core_to=1 - core)
    x_peer = at(x_to=1 - x)
    y_peer = at(y_to=1 - y)
    z_peer = at(z_to=z + 1 - 2 * lax.rem(z, 2))
    at_end = (z == 0) | (z == LINE - 1)

    def remote(source, target, send, receive, device):
        return pltpu.make_async_remote_copy(
            src_ref=source, dst_ref=target, send_sem=send, recv_sem=receive,
            device_id=device, device_id_type=MESH,
        )

    def load_all(pairs):
        copies = [
            pltpu.make_async_copy(source, target, load_sem.at[place])
            for place, (source, target) in enumerate(pairs)
        ]
        for copy in copies:
            copy.start()
        return copies

    def moved(pairs):
        for copy in load_all(pairs):
            copy.wait()

    barrier = pltpu.get_barrier_semaphore()
    greeted = [core_peer, x_peer, y_peer] + [at(z_to=lax.rem(z + step, LINE)) for step in range(1, LINE)]
    for device in greeted:
        pl.semaphore_signal(barrier, inc=1, device_id=device, device_id_type=MESH)

    def chunk_rows(chunk):
        return pl.ds(pl.multiple_of(chunk * rows, rows), rows)

    def core_copy(turn, chunk):
        return remote(
            parts.at[chunk, 1 - core], core_in.at[chunk], core_s.at[turn, chunk], core_r.at[turn, chunk], core_peer
        )

    def x_copy(turn, chunk):
        return remote(
            parts.at[chunk, core], x_in.at[turn % 2, chunk], x_s.at[turn, chunk], x_r.at[turn, chunk], x_peer
        )

    def back_copy(turn, chunk):
        return remote(
            parts.at[chunk, core], back_in.at[chunk], back_s.at[turn, chunk], back_r.at[turn, chunk], core_peer
        )

    def put_part(chunk, start, size, value):
        side, first = lax.div(start, width // 2), lax.rem(start, width // 2)
        parts[chunk, side, :, pl.ds(pl.multiple_of(first, size), size)] = value

    def send_part(turn, chunk):
        core_copy(turn, chunk).wait()
        parts[chunk, core] = parts[chunk, core] + core_in[chunk]
        x_copy(turn, chunk).start()

    def take_part(turn, chunk):
        x_copy(turn, chunk).wait()
        parts[chunk, core] = parts[chunk, core] + x_in[turn % 2, chunk]
        back = back_copy(turn, chunk)
        back.start()
        mine = parts[chunk, core]
        back.wait()
        other = back_in[chunk]
        return jnp.concatenate([jnp.where(core == 0, mine, other), jnp.where(core == 0, other, mine)], axis=1)

    def put_blocks(value):
        for place in range(2 * LINE):
            blocks[place] = value[:, place * block : (place + 1) * block]

    def chunk_lanes(chunk):
        return pl.ds(pl.multiple_of(chunk * rows, rows), rows)

    def half_lanes(side):
        return pl.ds(pl.multiple_of(side * block, block), block)

    def keep_columns(chunk):
        for place in range(LINE):
            cols_own[place, chunk_rows(chunk), :] = blocks[2 * place + y].astype(LOW)
        for place in range(2):
            cols_send[2 * chunk + place] = blocks[2 * (2 * core + place) + 1 - y]

    def cols_copy(chunk):
        return remote(
            cols_send.at[pl.ds(2 * chunk, 2)], r_cols.at[pl.ds(2 * core, 2), chunk],
            cols_s.at[chunk], cols_r.at[chunk], y_peer,
        )

    def forward_copy():
        view = r_cols.at[pl.ds(2 * core, 2)]
        return remote(view, view, fwd_s, fwd_r, core_peer)

    def act_copy(way, hop, chunk):
        goal = jnp.clip(z + 1 - 2 * way, 0, LINE - 1)
        owner = z - hop if way == 0 else z + hop
        active = (owner >= 0) & (z < LINE - 1) if way == 0 else (owner < LINE) & (z > 0)
        owner = jnp.clip(owner, 0, LINE - 1)
        landed = r_act.at[owner, :, chunk_lanes(chunk)]
        source = send_a.at[lax.div(chunk, 2), :, half_chunk(chunk)] if hop == 0 else landed
        return active, remote(
            source, landed, act_s.at[way, hop, chunk], act_r.at[way, hop, chunk], at(z_to=goal)
        )

    def act_landed(way, hop):
        return z - 1 - hop >= 0 if way == 0 else z + 1 + hop < LINE

    def half_chunk(chunk):
        return pl.ds(pl.multiple_of(lax.rem(chunk, 2) * rows, rows), rows)

    def act_send(hop, chunk):
        for way in range(2):
            active, copy = act_copy(way, hop, chunk)
            pl.when(active)(copy.start)

    def act_take(hop, chunk):
        for way in range(2):
            _, copy = act_copy(way, hop, chunk)
            pl.when(act_landed(way, hop))(copy.wait_recv)

    other_x = 2 * (1 - x) + core

    def two_copy(step):
        goal = lax.rem(z + step, LINE)
        return remote(
            two_send.at[pl.ds(2 * goal, 2)], r_two.at[z, pl.ds(2 * mp, 2)],
            two_s.at[step - 1], two_r.at[step - 1], at(z_to=goal),
        )

    def two_spread(turn, step):
        quarter = other_x if turn == 2 else mp
        view = r_two.at[lax.rem(z + step, LINE), pl.ds(2 * quarter, 2)]
        device = x_peer if turn == 1 else core_peer
        return remote(view, view, fwd_two_s.at[turn, step - 1], fwd_two_r.at[turn, step - 1], device)

    def pair_copy(which, chunk, part):
        units = pl.ds(*spans[part])
        return remote(
            gate_up.at[which, units, chunk_lanes(chunk)], r_y.at[which, units, chunk_lanes(chunk)],
            ys_s.at[which, chunk, part], ys_r.at[which, chunk, part], y_peer,
        )

    def pair_send(which, chunk):
        for part in range(2):
            pair_copy(which, chunk, part).start()

    def rows_copy():
        return remote(gbuf, r_att, att_s, att_r, z_peer)

    def fetch_columns(target):
        forward = forward_copy()
        forward.start()
        forward.wait()
        for pair in range(2):
            moved(
                [(r_cols.at[2 * pair + place], blocks.at[pl.ds(CHUNKS * place, CHUNKS)]) for place in range(2)]
            )
            for place in range(2):
                for chunk in range(CHUNKS):
                    piece = blocks[CHUNKS * place + chunk].astype(LOW)
                    target[2 * pair + place, chunk * rows : (chunk + 1) * rows, :] = piece

    def every_chunk(body):
        lax.fori_loop(0, CHUNKS, lambda chunk, carried: (body(chunk), carried)[1], 0)

    score_scale = 1.0 / math.sqrt(HD)

    def probabilities(queries, keys, begin):
        shape = (queries.shape[0], length)
        column = lax.broadcasted_iota(jnp.int32, shape, 1)
        row = lax.broadcasted_iota(jnp.int32, shape, 0) + begin
        visible = (column < prefix_ref[0]) | (column <= row)
        scores = jnp.where(visible, dot_nt(queries, keys) * score_scale, -1e30)
        weights = jnp.exp(scores - jnp.max(scores, axis=-1, keepdims=True))
        return weights / jnp.sum(weights, axis=-1, keepdims=True)

    def turn_by(value, sine):
        return value * cos_ref[...] + pltpu.roll(value, HD // 2, 1) * sine

    def head_lanes(place, offset=0):
        return pl.ds(pl.multiple_of(offset + place * HD, HD), HD)

    def first_scope(w_heads, tab):
        loads = [
            pltpu.make_async_copy(source, target, weight_sem.at[place])
            for place, (source, target) in enumerate(
                (
                    (w_query_hbm, w_heads.at[0]),
                    (w_key_hbm, w_heads.at[1]),
                    (w_value_hbm, w_heads.at[2]),
                    (w_dense_hbm, w_dense),
                )
            )
        ]
        for copy in loads:
            copy.start()
        named = lax.broadcasted_iota(jnp.int32, (vocab, length), 0) == ids_row[...]
        hot = jnp.where(named, 1.0, 0.0)
        hot_turned[...] = hot.astype(LOW)
        one_hot[...] = hot.T.astype(LOW)
        vectors[...] = jnp.zeros_like(vectors)
        for kind in range(3):
            loads[kind].wait()
            table = dot(emb[...], w_heads[kind])
            for place in range(heads_here):
                tab[kind * heads_here + place] = table[:, place * HD : (place + 1) * HD]

        def head_inputs(place, carried):
            hot = one_hot[...]
            lin = []
            for kind in range(3):
                high, rest = split_low(tab[kind * heads_here + place])
                lin.append(dot(hot, high) + dot(hot, rest))
            heads[0, place] = turn_by(lin[0], sin_ref[...]).astype(LOW)
            heads[1, place] = turn_by(lin[1], sin_ref[...]).astype(LOW)
            heads[2, place] = lin[2].astype(LOW)
            return carried

        lax.fori_loop(0, heads_here, head_inputs, 0)

        def attend(chunk):
            for place in range(heads_here):
                queries = heads[0, place, chunk_rows(chunk), :]
                probability = probabilities(queries, heads[1, place], chunk * rows).astype(LOW)
                mixed = dot(probability, heads[2, place]).astype(LOW)
                att_low[chunk_rows(chunk), place * HD : (place + 1) * HD] = mixed
                turned = mixed.astype(FULL).T
                att_turned[place * HD : (place + 1) * HD, chunk_lanes(chunk)] = turned.astype(LOW)
                gbuf[place * HD : (place + 1) * HD, chunk_lanes(chunk)] = turned

        def project(chunk):
            attend(chunk)
            pl.when(chunk == 0)(lambda: loads[3].wait())
            pl.when(chunk == 0)(lambda: pl.semaphore_wait(barrier, len(greeted)))
            mixed = att_low[chunk_rows(chunk), :]

            def columns(start, size):
                put_part(chunk, start, size, dot_nt(mixed, w_dense[pl.ds(start, size), :]))

            spread(width, columns, 256)
            core_copy(0, chunk).start()
            pl.when((chunk > 0) & (chunk <= AHEAD))(lambda: send_part(0, chunk - 1))

        every_chunk(project)
        rows_copy().start()

    pl.run_scoped(first_scope, pltpu.VMEM((3, width, inner), LOW), pltpu.VMEM((3 * heads_here, vocab, HD), FULL))

    def middle_scope(w_gate, w_up, w_down, cotbuf):
        weight_copies = [
            pltpu.make_async_copy(source, target, weight_sem.at[place])
            for place, (source, target) in enumerate(((w_gate_hbm, w_gate), (w_up_hbm, w_up), (w_down_hbm, w_down)))
        ]
        for copy in weight_copies:
            copy.start()
        for copy in weight_copies:
            copy.wait()

        def feed_forward(chunk):
            branch = take_part(0, chunk)
            residual = alpha * dot(one_hot[chunk_rows(chunk), :], emb[...]) + branch
            centered = residual - row_mean(residual)
            rstd = lax.rsqrt(row_mean(centered * centered) + norm_eps)
            xhat = centered * rstd
            rstd_one[chunk] = rstd
            xbuf[...] = xhat
            park = pltpu.make_async_copy(xbuf, xhat_park.at[chunk], load_sem.at[0])
            park.start()
            hidden_low = (xhat * gain_one[...] + bias_one[...]).astype(LOW)
            put_blocks(hidden_low.astype(FULL))
            keep_columns(chunk)
            cols_copy(chunk).start()

            def units_tile(start, size):
                cut = pl.ds(start, size)
                gate = dot_nt(w_gate[cut, :], hidden_low)
                up = dot_nt(w_up[cut, :], hidden_low)
                units = mp * local_hidden + start + lax.broadcasted_iota(jnp.int32, (size, rows), 0)
                used = jnp.where(units < FF_USED, 1.0, 0.0)
                square = gate * gate
                bend = jnp.tanh(TANH_SCALE * gate * (1.0 + 0.044715 * square))
                gelu = 0.5 * gate * (1.0 + bend) * used
                slope = 0.5 * (1.0 + bend) + 0.5 * gate * (1.0 - bend * bend) * (
                    TANH_SCALE * (1.0 + 3.0 * 0.044715 * square)
                )
                gate_up[0, cut, chunk_lanes(chunk)] = slope * up * used
                gate_up[1, cut, chunk_lanes(chunk)] = gelu
                active = (gelu * up).astype(LOW)
                act_low[cut, chunk_lanes(chunk)] = active
                send_a[lax.div(chunk, 2), cut, half_chunk(chunk)] = active.astype(FULL)

            tiles(local_hidden, units_tile)
            act_send(0, chunk)
            active = send_a[lax.div(chunk, 2), :, half_chunk(chunk)].T.astype(LOW)
            tiles(
                width, lambda start, size: put_part(chunk, start, size, dot(active, w_down[:, pl.ds(start, size)]))
            )
            core_copy(1, chunk).start()
            park.wait()
            send_part(1, chunk)
            pl.when(chunk + AHEAD < CHUNKS)(lambda: send_part(0, chunk + AHEAD))

        same = jnp.int32(0)
        for place in range(2 * LINE):
            same = same + jnp.where(cluster_ref[place] == cluster_ref[dp], 1, 0)
        weight_row = 1.0 / jnp.full((1, width), same, jnp.int32).astype(FULL)

        def feed_backward(chunk):
            loads = load_all(
                ((xhat_park.at[chunk], xbuf), (cot_hbm.at[chunk_rows(chunk)], cotbuf))
            )
            branch = take_part(1, chunk)
            for copy in loads:
                copy.wait()
            residual = alpha * (xbuf[...] * gain_one[...] + bias_one[...]) + branch
            centered = residual - row_mean(residual)
            rstd = lax.rsqrt(row_mean(centered * centered) + norm_eps)
            xhat = centered * rstd
            obuf[...] = (xhat * gain_two[...] + bias_two[...]).astype(LOW)
            grad_out = cotbuf[...].astype(FULL) * weight_row
            vectors[2:3, :] += jnp.sum(grad_out * xhat, axis=0, keepdims=True)
            vectors[3:4, :] += jnp.sum(grad_out, axis=0, keepdims=True)
            grad_x = grad_out * gain_two[...]
            grad_two = (grad_x - row_mean(grad_x) - xhat * row_mean(grad_x * xhat)) * rstd
            for place in range(width // inner):
                gbuf[place * rows : (place + 1) * rows, :] = grad_two[:, place * inner : (place + 1) * inner]
            stores = load_all(
                ((obuf, block_out.at[chunk_rows(chunk)]), (gbuf, grad_two_park.at[chunk]))
            )
            grad_low = grad_two.astype(LOW)
            put_blocks(grad_low.astype(FULL))
            for place in range(2):
                two_own[place, chunk_rows(chunk), :] = blocks[2 * z + place].astype(LOW)

            @pl.when(chunk == mp)
            def _():
                two_send[...] = blocks[...]
                for step in range(1, LINE):
                    two_copy(step).start()


            def units_tile(start, size):
                cut = pl.ds(start, size)
                grad_act = dot_nt(w_down[cut, :], grad_low)
                for which in range(2):
                    low = (grad_act * gate_up[which, cut, chunk_lanes(chunk)]).astype(LOW)
                    grads_low[pl.ds(which * shift + start, size), chunk_lanes(chunk)] = low
                    gate_up[which, cut, chunk_lanes(chunk)] = low.astype(FULL)

            spread(local_hidden, units_tile)
            pair_send(0, chunk)
            for copy in stores:
                copy.wait()

        def hidden_part(pair):
            both = pl.ds(pl.multiple_of(2 * rows * pair, 2 * rows), 2 * rows)
            grad_gate = gate_up[0, :, both].T.astype(LOW)
            grad_up = gate_up[1, :, both].T.astype(LOW)

            def columns(start, size):
                cut = pl.ds(start, size)
                value = dot(grad_gate, w_gate[:, cut]) + dot(grad_up, w_up[:, cut])
                put_part(2 * pair, start, size, value[:rows])
                put_part(2 * pair + 1, start, size, value[rows:])

            tiles(width, columns)
            for place in range(2):
                core_copy(2, 2 * pair + place).start()

        def take_hidden():
            for chunk in range(CHUNKS):
                cols_copy(chunk).wait()
            fetch_columns(hidden_theirs)

        def step(turn, carried):
            pl.when(turn == CHUNKS - 1)(lambda: hidden_part(0))
            @pl.when(turn == CHUNKS)
            def _():
                for chunk in range(2):
                    send_part(2, chunk)
                take_hidden()
                for chunk in range(CHUNKS - 1):
                    act_take(0, chunk)
                    act_send(1, chunk)

            pl.when(turn < CHUNKS)(lambda: feed_forward(turn))
            pl.when(turn == 1)(lambda: rows_copy().wait())
            pl.when(turn > 0)(lambda: feed_backward(turn - 1))
            return carried

        lax.fori_loop(0, CHUNKS + 1, step, 0)

        hidden_part(1)
        for chunk in range(2, CHUNKS):
            send_part(2, chunk)

    pl.run_scoped(
        middle_scope,
        pltpu.VMEM((local_hidden, width), LOW),
        pltpu.VMEM((local_hidden, width), LOW),
        pltpu.VMEM((local_hidden, width), LOW),
        pltpu.VMEM((rows, width), LOW),
    )

    def last_scope(theirs, late_theirs, two_theirs, att_theirs, send_b, stage, grad_att, grad_one_own, sums, sums_up, sums_down, sums_below, sums_above, late_own):
        def norm_backward(chunk):
            loads = load_all(((xhat_park.at[chunk], xbuf), (grad_two_park.at[chunk], gbuf)))
            branch = take_part(2, chunk)
            for copy in loads:
                copy.wait()
            grad_two = [gbuf[place * rows : (place + 1) * rows, :] for place in range(width // inner)]
            grad_hidden = alpha * jnp.concatenate(grad_two, axis=1) + branch
            xhat = xbuf[...]
            vectors[0:1, :] += jnp.sum(grad_hidden * xhat, axis=0, keepdims=True)
            vectors[1:2, :] += jnp.sum(grad_hidden, axis=0, keepdims=True)
            grad_x = grad_hidden * gain_one[...]
            grad_one = (grad_x - row_mean(grad_x) - xhat * row_mean(grad_x * xhat)) * rstd_one[chunk]
            put_blocks(grad_one)
            for place in range(2):
                grad_one_own[chunk_rows(chunk), place * block : (place + 1) * block] = blocks[2 * mp + place]
            grad_low = grad_one.astype(LOW)
            put_blocks(grad_low.astype(FULL))
            for place in range(2 * LINE):
                late_own[place, chunk_rows(chunk), :] = blocks[place].astype(LOW)

            @pl.when(chunk == mp)
            def _():
                for place in range(2 * LINE):
                    cols_send[place] = blocks[place]

            grad_mixed = dot(grad_low, w_dense[...]).astype(LOW)
            for place in range(heads_here):
                grad_att[place, chunk_rows(chunk), :] = grad_mixed[:, place * HD : (place + 1) * HD]

        def fetch_units(which, part):
            start, size = spans[part]
            for chunk in range(CHUNKS):
                pair_copy(which, chunk, part).wait()
            views = [stage.at[side, pl.ds(start, size)] for side in range(2)]
            moved(
                [(r_y.at[which, pl.ds(start, size), pl.ds(block * side, block)], views[side]) for side in range(2)]
            )
            for side in range(2):
                theirs[1 + which, start : start + size, block * side : block * (side + 1)] = views[side][...].astype(LOW)

        def fetch_rows(source, target):
            size = source.shape[0]
            views = [stage.at[place, pl.ds(0, size)] for place in range(2)]
            moved([(source.at[:, pl.ds(block * place, block)], views[place]) for place in range(2)])
            for place in range(2):
                target[:, block * place : block * (place + 1)] = views[place][...].astype(LOW)

        def outer_product(target, place, own, other):
            right, right_theirs = cols_own[place], hidden_theirs[place]

            def rows_tile(start, size):
                cut = pl.ds(start, size)
                target[cut, :] = dot(own[cut, :], right) + dot(other[cut, :], right_theirs)

            tiles(target.shape[0], rows_tile)

        def down_products():
            for step in range(1, LINE):
                two_spread(1, step).wait()
                two_spread(2, step).start()
            for step in range(1, LINE):
                two_spread(0, step).wait()
                two_spread(2, step).wait()
            for chunk in range(CHUNKS):
                pl.when(at_end)(lambda: act_take(1, chunk))
                act_take(2, chunk)
            for step in range(LINE):
                owner = lax.rem(z + step, LINE)
                if step:
                    moved([(r_two.at[owner], blocks)])
                    for place in range(2):
                        for chunk in range(CHUNKS):
                            piece = blocks[2 * chunk + place].astype(LOW)
                            two_theirs[place, chunk * rows : (chunk + 1) * rows, :] = piece
                    fetch_rows(r_act.at[owner], theirs.at[0])
                left, right = (theirs.at[0], two_theirs) if step else (act_low, two_own)
                for place in range(2):
                    lanes = slice(place * block, (place + 1) * block)

                    def rows_tile(start, size):
                        cut = pl.ds(start, size)
                        product = dot(left[cut, :], right[place])
                        gate_up[0, cut, lanes] = gate_up[0, cut, lanes] + product if step else product

                    tiles(local_hidden, rows_tile)

        def down_copy():
            return remote(gate_up.at[0, :, half_lanes(1 - y)], r_dny, dny_s, dny_r, y_peer)

        def down_end():
            down_copy().wait()
            moved([(r_dny, stage.at[0])])
            stage[0] = stage[0] + gate_up[0, :, half_lanes(y)]
            moved([(stage.at[0], out_down)])
            for chunk in range(CHUNKS):
                for way in range(2):
                    for hop in range(1, LINE - 1):
                        active, copy = act_copy(way, hop, chunk)
                        pl.when(active)(copy.wait_send)

        def toward(side):
            return jnp.where(z < LINE // 2, side, 1 - side)

        def goes(slot, way):
            return jnp.where(way == 0, z < slot, z > LINE - 1 - slot)

        def inner_place(way):
            return jnp.where(way == 0, z > 0, z < LINE - 1)

        def line_goal(way):
            return at(z_to=jnp.clip(z + 1 - 2 * way, 0, LINE - 1))

        def unit_terms(kind):
            return grads_low.at[pl.ds(pl.multiple_of(kind * shift, 16), local_hidden)], theirs.at[1 + kind]

        def count(way):
            return jnp.where(way == 0, LINE - 1 - z, z)

        def order(kind, slot, way):
            return kind * count(way) + slot - (LINE - count(way))

        def turn_of(number, way):
            many = jnp.maximum(count(way), 1)
            return lax.div(number, many) * (LINE - 1) + lax.rem(number, many) + LINE - 1 - count(way)

        def unit_copy(turn, side, part):
            way = toward(side)
            kind, slot = lax.div(turn, LINE - 1), lax.rem(turn, LINE - 1)
            units = pl.ds(*spans[part])
            home = (send_a, send_b)[side].at[lax.rem(jnp.maximum(order(kind, slot + 1, way), 0), 2), units]
            return remote(
                home, r_rs.at[kind, slot, way, units], rs_s.at[kind, slot, way, part], rs_r.at[kind, slot, way, part],
                line_goal(way),
            )

        def unit_sent(number, side):
            for part in range(2):
                unit_copy(turn_of(jnp.maximum(number, 0), toward(side)), side, part).wait_send()

        def unit_slot(turn, part, side):
            way = toward(side)
            kind, slot = lax.div(turn, LINE - 1), lax.rem(turn, LINE - 1) + 1
            own, other = unit_terms(kind)
            start, size = spans[part]
            cut = slice(start, start + size)

            @pl.when(goes(slot, way))
            def _():
                number = order(kind, slot, way)
                home = (send_a, send_b)[side].at[lax.rem(jnp.maximum(number, 0), 2)]
                if part == 0:
                    pl.when(number >= 2)(lambda: unit_sent(number - 2, side))
                place = jnp.where(way == 0, LINE - slot + z, slot - LINE + z)
                home[cut, :] = dot(own[cut, :], cols_own[place]) + dot(other[cut, :], hidden_theirs[place])

                @pl.when((slot > 1) & inner_place(way))
                def _():
                    before = jnp.maximum(turn - 1, 0)
                    unit_copy(before, side, part).wait_recv()
                    landed = r_rs.at[lax.div(before, LINE - 1), lax.rem(before, LINE - 1), way, pl.ds(start, size)]
                    moved([(landed, stage.at[side, pl.ds(start, size)])])
                    home[cut, :] = home[cut, :] + stage[side, cut, :]

                unit_copy(turn, side, part).start()

        def unit_end():
            own, other = unit_terms(0)
            outer_product(stage.at[0], z, own, other)
            for side in range(2):

                @pl.when(inner_place(toward(side)))
                def _():
                    for part in range(2):
                        unit_copy(LINE - 2, side, part).wait_recv()
                    moved([(r_rs.at[0, LINE - 2, toward(side)], stage.at[1])])
                    stage[0] = stage[0] + stage[1]

            moved([(stage.at[0], out_gate)])

        def last_product():
            own, other = unit_terms(1)
            outer_product(stage.at[0], z, own, other)
            moved([(stage.at[0], out_up)])

        def last_landed():
            for side in range(2):
                for part in range(2):
                    pl.when(inner_place(toward(side)))(unit_copy(2 * LINE - 3, side, part).wait_recv)

        first = jnp.where(z == 1, 2, jnp.where(z == LINE - 1, 2 * LINE - 2, 0))
        peer_first = jnp.where(z == 0, 2, jnp.where(z == 2, 2 * LINE - 2, 0))
        many = 2 * LINE - 2
        def late_copy(begin, size, part):
            span = pl.ds(begin + part * (size // 2), size // 2)
            return remote(cols_send.at[span], r_late.at[mp, span], late_s.at[0, part], late_r.at[0, part], z_peer)

        def late_send():
            for part in range(2):
                pl.when(at_end)(lambda: late_copy(peer_first, many, part).start())
                pl.when(~at_end)(lambda: late_copy(peer_first, 2, part).start())

        def spread_copy(turn, size, part):
            place = other_x if turn == 3 else mp
            view = r_late.at[place, pl.ds(first + part * (size // 2), size // 2)]
            device = x_peer if turn == 2 else core_peer
            return remote(view, view, late_s.at[turn, part], late_r.at[turn, part], device)

        def by_size(body):
            pl.when(at_end)(lambda: body(2))
            pl.when(~at_end)(lambda: body(many))

        def late_take():
            def body(size):
                for part in range(2):
                    late_copy(first, size, part).wait_recv()
                    spread_copy(2, size, part).start()
                    spread_copy(1, size, part).start()
                for part in range(2):
                    spread_copy(2, size, part).wait()
                    spread_copy(3, size, part).start()
                for part in range(2):
                    spread_copy(1, size, part).wait()
                for part in range(2):
                    spread_copy(3, size, part).wait()

            by_size(body)

        def late_slot(number):
            side, lane = lax.div(number, LINE), lax.rem(number, LINE)
            return parts.at[:, side, :, pl.ds(pl.multiple_of(lane * block, block), block)]

        def late_products():
            for quarter in range(CHUNKS):

                def body(size):
                    moved([(r_late.at[quarter, pl.ds(first, size)], blocks.at[pl.ds(0, size)])])
                    for place in range(size):
                        late_theirs[place, quarter * rows : (quarter + 1) * rows, :] = blocks[place].astype(LOW)

                by_size(body)

            def product(number, carried):
                @pl.when((number < 2) | ~at_end)
                def _():
                    home = late_slot(number)
                    for piece in range(CHUNKS):
                        cut = slice(piece * rows, (piece + 1) * rows)
                        home[piece] = dot(att_turned[cut, :], late_own[first + number]) + dot(
                            att_theirs[cut, :], late_theirs[number]
                        )

                return carried

            lax.fori_loop(0, many, product, 0)
            for place in range(LINE - 1):
                pl.when((place == 0) | ~at_end)(lambda: late_pair(place).start())

        def late_pair(place):
            return remote(late_slot(2 * place + 1 - y), r_dz.at[place], dz_s.at[place], dz_r.at[place], y_peer)

        def late_line(place):
            goal = lax.div(first, 2) + place
            return goal != z, remote(late_slot(2 * place + y), r_dx, dx_s.at[place], dx_r, at(z_to=goal))

        def late_sums():
            for place in range(LINE - 1):

                @pl.when((place == 0) | ~at_end)
                def _():
                    late_pair(place).wait()
                    arrived = blocks.at[pl.ds(0, CHUNKS)]
                    moved([(r_dz.at[place], arrived)])
                    home = late_slot(2 * place + y)
                    home[...] = home[...] + arrived[...]
                    leaves, copy = late_line(place)
                    pl.when(leaves)(copy.start)

        def late_end():
            _, copy = late_line(0)
            copy.wait_recv()
            arrived = blocks.at[pl.ds(0, CHUNKS)]
            moved([(r_dx, arrived)])
            total = late_slot(2 * (z - lax.div(first, 2)) + y)
            for piece in range(CHUNKS):
                gbuf[0:block, piece * rows : (piece + 1) * rows] = (total[piece] + arrived[piece]).T
            moved([(gbuf.at[pl.ds(0, block)], out_dense)])
            for place in range(LINE - 1):

                @pl.when((place == 0) | ~at_end)
                def _():
                    leaves, copy = late_line(place)
                    pl.when(leaves)(copy.wait_send)

            for part in range(2):
                pl.when(at_end)(lambda: late_copy(peer_first, many, part).wait_send())
                pl.when(~at_end)(lambda: late_copy(peer_first, 2, part).wait_send())

        def last_sent():
            for side in range(2):
                pl.when(count(toward(side)) > 0)(lambda: unit_sent(2 * count(toward(side)) - 1, side))
                pl.when(count(toward(side)) > 0)(lambda: unit_sent(2 * count(toward(side)) - 2, side))

        def attention_backward(place, carried):
            hot_t = hot_turned[...]
            queries, keys, values = heads[0, place], heads[1, place], heads[2, place]
            grad_mixed = grad_att[place]
            probability = probabilities(queries, keys, 0)
            grad_prob = dot_nt(grad_mixed, values)
            centre = jnp.sum(grad_prob * probability, axis=-1, keepdims=True)
            grad_scores = (probability * (grad_prob - centre)).astype(LOW)
            grad_queries = dot(grad_scores, keys) * score_scale
            grad_keys = dot_tn(grad_scores, queries) * score_scale
            grad_values = dot_tn(probability.astype(LOW), grad_mixed)
            sums[0, 0:vocab, head_lanes(place)] = dot(hot_t, turn_by(grad_queries, -sin_ref[...]).astype(LOW))
            sums[0, 0:vocab, head_lanes(place, inner)] = dot(hot_t, turn_by(grad_keys, -sin_ref[...]).astype(LOW))
            sums[1, 0:vocab, head_lanes(place)] = dot(hot_t, grad_values.astype(LOW))
            return carried

        def small_sums():
            lax.fori_loop(0, heads_here, attention_backward, 0)
            hot_t = hot_turned[...]
            high, rest = split_low(grad_one_own[...])
            sums[1, 0:vocab, heads_here * HD :] = dot(hot_t, high) + dot(hot_t, rest)
            for side in range(2):
                sums[side, vocab:, :] = vectors[:, side * (width // 2) : (side + 1) * (width // 2)]
            sums_pair().start()

        def sums_pair():
            return remote(sums.at[1 - y], r_sums.at[0], sums_s.at[0], sums_r.at[0], y_peer)

        def sums_line(way):
            source = (sums_up, sums_down)[way]
            goal = jnp.clip(z + 1 - 2 * way, 0, LINE - 1)
            return remote(source, r_sums.at[1 + way], sums_s.at[1 + way], sums_r.at[1 + way], at(z_to=goal))

        def sums_back():
            return remote(sums.at[y], r_sums.at[3], sums_s.at[3], sums_r.at[3], y_peer)

        def sums_first():
            sums_pair().wait()
            moved([(r_sums.at[0], sums_below)])
            sums[y] = sums[y] + sums_below[...]

            @pl.when(z == 0)
            def _():
                sums_up[...] = sums[y]
                sums_line(0).start()

            @pl.when(z == LINE - 1)
            def _():
                sums_down[...] = sums[y]
                sums_line(1).start()

        def sums_up_step():
            sums_line(0).wait_recv()
            moved([(r_sums.at[1], sums_below)])
            sums_up[...] = sums[y] + sums_below[...]
            sums_line(0).start()

        def sums_down_step():
            sums_line(1).wait_recv()
            moved([(r_sums.at[2], sums_above)])
            sums_down[...] = sums[y] + sums_above[...]
            sums_line(1).start()

        def sums_near():
            pl.when(z == 1)(sums_up_step)
            pl.when(z == LINE - 2)(sums_down_step)

        def sums_far():
            pl.when(z == LINE - 2)(sums_up_step)
            pl.when(z == 1)(sums_down_step)

        def sums_middle():
            @pl.when(z == LINE - 1)
            def _():
                sums_line(0).wait_recv()
                moved([(r_sums.at[1], sums_below)])

            @pl.when(z == 0)
            def _():
                sums_line(1).wait_recv()
                moved([(r_sums.at[2], sums_above)])

            @pl.when(z > 0)
            def _():
                sums[y] = sums[y] + sums_below[...]

            @pl.when(z < LINE - 1)
            def _():
                sums[y] = sums[y] + sums_above[...]

            sums_back().start()

        def sums_end():
            sums_back().wait()
            pl.when(z < LINE - 1)(sums_line(0).wait_send)
            pl.when(z > 0)(sums_line(1).wait_send)
            moved([(r_sums.at[3], sums.at[1 - y])])
            lanes = pl.ds(pl.multiple_of(lax.rem(dp, LINE) * block, block), block)
            moved([(sums.at[lax.div(dp, LINE), pl.ds(vocab, 8), lanes], out_norms)])

        def by_token(kind, rows_of):
            side, start = ((0, 0), (0, inner), (1, 0), (1, inner))[kind]
            return sums[side, rows_of, start : start + inner]

        def head_gradients():
            own_columns = emb[:, pl.ds(pl.multiple_of(dp * block, block), block)]
            for kind, result in enumerate((out_query, out_key, out_value)):
                high, rest = split_low(by_token(kind, slice(0, vocab)))
                gbuf[0:block, :] = dot_tn(own_columns, high) + dot_tn(own_columns, rest)
                moved([(gbuf.at[pl.ds(0, block)], result)])

        table_rows = vocab // (2 * LINE)
        table_own = pl.ds(pl.multiple_of(dp * table_rows, table_rows), table_rows)

        def table_part():
            for kind, weight in enumerate((w_query_hbm, w_key_hbm, w_value_hbm)):
                moved([(weight, w_dense)])
                pieces = jnp.concatenate(split_low(by_token(kind, table_own)), axis=0)

                def columns(start, size):
                    cut = pl.ds(start, size)
                    both = dot_nt(pieces, w_dense[cut, :])
                    both = both[:table_rows] + both[table_rows:]
                    xbuf[0:table_rows, cut] = both if kind == 0 else xbuf[0:table_rows, cut] + both

                tiles(width, columns)
            quarter = pl.ds(pl.multiple_of(mp * inner, inner), inner)
            xbuf[0:table_rows, quarter] = xbuf[0:table_rows, quarter] + alpha * by_token(3, table_own)
            table_copy(0).start()

        def table_middle():
            table_copy(0).wait()
            xbuf[table_rows : 2 * table_rows, :] = xbuf[0:table_rows, :] + table_core[...]
            table_copy(1).start()

        def table_end():
            table_copy(1).wait()
            xbuf[0:table_rows, :] = 0.1 * (xbuf[table_rows : 2 * table_rows, :] + table_x[...])
            moved([(xbuf.at[pl.ds(0, table_rows)], out_table)])

        def table_copy(turn):
            target, device = ((table_core, core_peer), (table_x, x_peer))[turn]
            return remote(xbuf.at[pl.ds(turn * table_rows, table_rows)], target, table_s.at[turn], table_r.at[turn], device)

        def act_pass(chunks):
            for chunk in chunks:
                act_take(1, chunk)
                act_send(2, chunk)


        for chunk in range(CHUNKS):
            for way in range(2):
                active, copy = act_copy(way, 0, chunk)
                pl.when(active)(copy.wait_send)
        def one_turn(turn, carried):
            for part in range(2):
                pl.when(turn == 0)(lambda: fetch_units(0, part))
                unit_slot(turn, part, 0)

            @pl.when(turn == 0)
            def _():
                pair_send(1, 0)
                pair_send(1, 1)
                act_take(0, CHUNKS - 1)
                act_send(1, CHUNKS - 1)
                fetch_rows(r_att, att_theirs)
                every_chunk(norm_backward)
                late_send()
                for step in range(1, LINE):
                    two_copy(step).wait()
                for step in range(1, LINE):
                    two_spread(1, step).start()
                    two_spread(0, step).start()

            @pl.when(turn == 1)
            def _():
                small_sums()
                pair_send(1, 2)
                pair_send(1, 3)
                pl.when(~at_end)(lambda: act_pass(range(CHUNKS - 1)))

            @pl.when((turn == 1) & ~at_end | (turn == 3) & at_end)
            def _():
                late_take()
                late_products()

            pl.when((turn == 1) & ~at_end)(lambda: act_pass((CHUNKS - 1,)))
            pl.when(turn == 1)(sums_first)

            pl.when(turn == 2)(sums_near)
            pl.when((turn == 2) & ~at_end | (turn == 4) & at_end)(late_sums)

            @pl.when(turn == 2)
            def _():
                for part in range(2):
                    fetch_units(1, part)

            pl.when(turn == 3)(sums_far)

            @pl.when((turn == 3) | (turn == 5))
            def _():
                for part in range(2):
                    unit_slot(jnp.where(turn == 3, 2, 5), part, 1)

            pl.when(turn == 4)(down_products)
            pl.when((turn == 3) & ~at_end | (turn == 4) & at_end)(sums_middle)
            pl.when(turn == 4)(lambda: down_copy().start())

            @pl.when((turn == 4) & ~at_end | (turn == 5) & at_end)
            def _():
                sums_end()
                head_gradients()

            @pl.when(turn == 5)
            def _():
                table_part()
                last_product()
                unit_end()

            return carried

        lax.fori_loop(0, 2 * (LINE - 1), one_turn, 0)
        late_end()
        table_middle()
        table_end()
        down_end()
        last_landed()
        last_sent()

    pl.run_scoped(
        last_scope,
        pltpu.VMEM((3, local_hidden, length), LOW),
        pltpu.VMEM((2 * LINE - 2, length, block), LOW),
        pltpu.VMEM((2, length, block), LOW),
        pltpu.VMEM((inner, length), LOW),
        pltpu.VMEM((2, local_hidden, block), FULL),
        pltpu.VMEM((2, local_hidden, block), FULL),
        pltpu.VMEM((heads_here, length, HD), LOW),
        pltpu.VMEM((length, 2 * block), FULL),
        pltpu.VMEM((2,) + r_sums.shape[1:], FULL),
        pltpu.VMEM(r_sums.shape[1:], FULL),
        pltpu.VMEM(r_sums.shape[1:], FULL),
        pltpu.VMEM(r_sums.shape[1:], FULL),
        pltpu.VMEM(r_sums.shape[1:], FULL),
        pltpu.VMEM((2 * LINE, length, block), LOW),
    )


def write_kernel(*refs):
    count = 10
    late = 7
    sources, landed = refs[:count], refs[count]
    targets = refs[count + 1 : 2 * count + 4]
    rooms, terms, first_sem, second_sem = refs[2 * count + 4 : 3 * count + 4], *refs[3 * count + 4 : 3 * count + 7]
    z = lax.div(lax.axis_index("dp"), 2)
    order = [late] + [place for place in range(count) if place != late]
    loads = {
        place: pltpu.make_async_copy(sources[place], rooms[place], first_sem.at[place]) for place in range(count)
    }
    more = [
        pltpu.make_async_copy(landed.at[1, LINE - 2, way], terms.at[way], first_sem.at[count + way]) for way in range(2)
    ]
    for copy in more:
        copy.start()
    for place in order:
        loads[place].start()
    stores = []
    for copy in more:
        copy.wait()
    for place in order:
        loads[place].wait()
        room = rooms[place]
        if place == late:
            for way, active in ((0, z > 0), (1, z < LINE - 1)):

                @pl.when(active)
                def _():
                    room[...] = room[...] + terms[way]

        if place < count - 1:
            stores.append(pltpu.make_async_copy(room, targets[place], second_sem.at[place]))
            stores[-1].start()
        else:
            for vector in range(4):
                targets[place + vector][...] = room[vector : vector + 1, :]
    for copy in stores:
        copy.wait()


def write_out(results, landed):
    hbm = pl.BlockSpec(memory_space=pl.ANY)
    rows = jax.ShapeDtypeStruct((1, results[-1].shape[1]), FULL)
    shapes = [jax.ShapeDtypeStruct(value.shape, value.dtype) for value in results[:-1]] + [rows] * 4
    return pl.pallas_call(
        write_kernel,
        out_shape=shapes,
        in_specs=[hbm] * (len(results) + 1),
        out_specs=[hbm] * (len(results) - 1) + [pl.BlockSpec(memory_space=pltpu.VMEM)] * 4,
        scratch_shapes=[pltpu.VMEM(value.shape, value.dtype) for value in results]
        + [pltpu.VMEM((2,) + results[7].shape, FULL)]
        + [pltpu.SemaphoreType.DMA((len(results) + 2,))] * 2,
        compiler_params=pltpu.CompilerParams(vmem_limit_bytes=62 * 2**20),
    )(*results, landed)


def local_fast(
    token_ids,
    prefix_lengths,
    cluster_ids,
    embedding,
    w_query,
    w_key,
    w_value,
    w_dense,
    w_gate,
    w_up,
    w_down,
    norm1_gain,
    norm1_bias,
    norm2_gain,
    norm2_bias,
    cotangent,
):
    length = token_ids.shape[0]
    vocab, width = embedding.shape
    inner = w_query.shape[1]
    heads_here = inner // HD
    local_hidden = w_gate.shape[1]
    rows = length // CHUNKS
    block = width // (2 * LINE)
    shift = (local_hidden + 15) // 16 * 16
    frequency = 10000.0 ** (np.arange(HD // 2) * (-2.0 / HD))
    angles = np.arange(length)[:, None] * frequency[None, :]
    cosine = np.concatenate([np.cos(angles)] * 2, axis=1).astype(np.float32)
    sine = np.concatenate([-np.sin(angles), np.sin(angles)], axis=1).astype(np.float32)
    norms = [vector.reshape(1, width) for vector in (norm1_gain, norm1_bias, norm2_gain, norm2_bias)]

    hbm = pl.BlockSpec(memory_space=pl.ANY)
    vmem = pl.BlockSpec(memory_space=pltpu.VMEM)
    smem = pl.BlockSpec(memory_space=pltpu.SMEM)
    sums_rows = vocab + 8
    table_rows = vocab // (2 * LINE)
    shapes = [
        ((length, width), LOW),
        ((table_rows, width), FULL),
        ((block, inner), FULL),
        ((block, inner), FULL),
        ((block, inner), FULL),
        ((block, inner), FULL),
        ((local_hidden, block), FULL),
        ((local_hidden, block), FULL),
        ((local_hidden, block), FULL),
        ((8, block), FULL),
        ((LINE, local_hidden, length), FULL),
        ((LINE, 2 * CHUNKS, rows, block), FULL),
        ((2, local_hidden, length), FULL),
        ((LINE, CHUNKS, rows, block), FULL),
        ((inner, length), FULL),
        ((CHUNKS, rows, width), FULL),
        ((CHUNKS, length, inner), FULL),
        ((local_hidden, block), FULL),
        ((2, LINE - 1, 2, local_hidden, block), FULL),
        ((4, 2 * LINE, rows, block), FULL),
        ((LINE - 1, CHUNKS, rows, block), FULL),
        ((CHUNKS, rows, block), FULL),
        ((4, sums_rows, width // 2), FULL),
    ]
    scratch = [
        ((CHUNKS, 2, rows, width // 2), FULL),
        ((CHUNKS, rows, width // 2), FULL),
        ((2, CHUNKS, rows, width // 2), FULL),
        ((CHUNKS, rows, width // 2), FULL),
        ((2 * LINE, rows, block), FULL),
        ((rows, width), FULL),
        ((length, inner), FULL),
        ((rows, width), LOW),
        ((2, local_hidden, length), FULL),
        ((2 * shift, length), LOW),
        ((local_hidden, length), LOW),
        ((2, local_hidden, block), FULL),
        ((LINE, length, block), LOW),
        ((2 * CHUNKS, rows, block), FULL),
        ((LINE, length, block), LOW),
        ((2, length, block), LOW),
        ((2 * LINE, rows, block), FULL),
        ((length, inner), LOW),
        ((inner, length), LOW),
        ((3, heads_here, length, HD), LOW),
        ((width, inner), LOW),
        ((length, vocab), LOW),
        ((vocab, length), LOW),
        ((CHUNKS, rows, 1), FULL),
        ((8, width), FULL),
        ((table_rows, width), FULL),
        ((table_rows, width), FULL),
    ]
    dma = pltpu.SemaphoreType.DMA
    each = (3, CHUNKS)
    semaphores = [
        each, each, each, each, each, each, (2, LINE - 1, CHUNKS), (2, LINE - 1, CHUNKS), (3,), (3,), (3, 3), (3, 3),
        (CHUNKS,), (CHUNKS,), None, None, (2, CHUNKS, 2), (2, CHUNKS, 2), None, None, None, None, (4, 2), (4, 2),
        (3,), (3,), (3,), None, (2, LINE - 1, 2, 2), (2, LINE - 1, 2, 2), (4,), (4,), (2,), (2,), (4,), (4,),
    ]
    results = pl.pallas_call(
        functools.partial(layer_kernel, length, width, local_hidden),
        out_shape=[jax.ShapeDtypeStruct(shape, dtype) for shape, dtype in shapes],
        in_specs=[smem] * 2 + [vmem] * 8 + [hbm] * 8,
        out_specs=[hbm] * len(shapes),
        scratch_shapes=[pltpu.VMEM(shape, dtype) for shape, dtype in scratch]
        + [dma if shape is None else dma(shape) for shape in semaphores],
        compiler_params=pltpu.CompilerParams(
            collective_id=0, has_side_effects=True, vmem_limit_bytes=62 * 2**20
        ),
    )(
        prefix_lengths,
        cluster_ids,
        token_ids.reshape(1, length),
        embedding,
        cosine,
        sine,
        *norms,
        w_query,
        w_key,
        w_value,
        w_dense,
        w_gate.T,
        w_up.T,
        w_down.T,
        cotangent,
    )
    written = write_out(results[:10], results[18])
    block_out, table, out_query, out_key, out_value, out_dense, out_gate, out_up, out_down = written[:9]
    out_norms = written[9:]
    return (
        block_out,
        table,
        out_query,
        out_key,
        out_value,
        out_dense,
        out_gate.T,
        out_up.T,
        out_down.T,
        out_norms[0].reshape(width // (2 * LINE)),
        out_norms[1].reshape(width // (2 * LINE)),
        out_norms[2].reshape(width // (2 * LINE)),
        out_norms[3].reshape(width // (2 * LINE)),
    )


def solution(mesh):
    fast = mesh.shape["dp"] == 2 * LINE and mesh.shape["mp"] == 4
    return jax.shard_map(
        local_fast if fast else local_general,
        mesh=mesh,
        in_specs=(
            P("dp"),
            P("dp"),
            P(),
            P(),
            P(None, "mp"),
            P(None, "mp"),
            P(None, "mp"),
            P(None, "mp"),
            P(None, "mp"),
            P(None, "mp"),
            P(None, "mp"),
            P(),
            P(),
            P(),
            P(),
            P("dp", None),
        ),
        out_specs=(
            P("dp", None),
            P("dp", None),
            P("dp", "mp"),
            P("dp", "mp"),
            P("dp", "mp"),
            P("dp", "mp"),
            P("dp", "mp"),
            P("dp", "mp"),
            P("dp", "mp"),
            P("dp"),
            P("dp"),
            P("dp"),
            P("dp"),
        ),
        check_vma=False,
    )
```

```python
import functools
import math

import jax
import jax.numpy as jnp
import numpy as np
from jax import lax
from jax.experimental import pallas as pl
from jax.experimental.pallas import tpu as pltpu
from jax.sharding import PartitionSpec as P

HD = 128
FF_USED = 5461


deep_alpha = math.sqrt(48.0)
norm_eps = 1e-05
highest = lax.Precision.HIGHEST


def layer_norm(inputs, norm_gain, norm_bias):
    center = jnp.mean(inputs, axis=-1, keepdims=True)
    centered = inputs - center
    spread = jnp.mean(centered * centered, axis=-1, keepdims=True)
    return centered * lax.rsqrt(spread + norm_eps) * norm_gain + norm_bias


def rotary_tables(length, head_width):
    half_width = head_width // 2
    frequency = jnp.exp(
        jnp.arange(half_width, dtype=jnp.float32) * (-2.0 * math.log(10000.0) / head_width)
    )
    angles = jnp.arange(length, dtype=jnp.float32)[:, None] * frequency[None, :]
    return (jnp.cos(angles), jnp.sin(angles))


def rotate(inputs, cosine, sine):
    half_width = inputs.shape[-1] // 2
    first = inputs[..., :half_width]
    second = inputs[..., half_width:]
    cosine = cosine[:, None, :]
    sine = sine[:, None, :]
    return jnp.concatenate(
        [first * cosine - second * sine, second * cosine + first * sine], axis=-1
    )


def row_mask(row_begin, row_count, length, prefix):
    columns = jnp.arange(length, dtype=jnp.int32)
    row_index = row_begin + jnp.arange(row_count, dtype=jnp.int32)
    return (columns[None, :] < prefix) | (columns[None, :] <= row_index[:, None])


def block_scores(query_block, keys_rot, visible, score_scale):
    scores = (
        jnp.einsum("bhd,khd->hbk", query_block, keys_rot, preferred_element_type=jnp.float32)
        * score_scale
    )
    return jnp.where(visible[None, :, :], scores, -1e30)


def attention_forward(queries, keys_rot, values_in, prefix, row_block):
    length = queries.shape[0]
    score_scale = 1.0 / math.sqrt(HD)

    def one_block(row_begin):
        scores = block_scores(
            queries, keys_rot, row_mask(row_begin, row_block, length, prefix), score_scale
        )
        row_max = jnp.max(scores, axis=-1, keepdims=True)
        weights = jnp.exp(scores - row_max)
        total_weight = jnp.sum(weights, axis=-1, keepdims=True)
        probability = (weights / total_weight).astype(jnp.bfloat16)
        mixed_block = jnp.einsum(
            "hbk,khd->bhd", probability, values_in, preferred_element_type=jnp.float32
        )
        return (mixed_block, row_max + jnp.log(total_weight))

    starts = jnp.arange(length // row_block, dtype=jnp.int32) * row_block
    attended, log_total = lax.map(one_block, starts)
    return (attended.reshape(length, -1), log_total)


def attention_backward(queries, keys_rot, values_in, prefix, row_block, log_total, grad_mixed):
    length = queries.shape[0]
    score_scale = 1.0 / math.sqrt(HD)

    def one_block(carried, inputs):
        grad_keys, grad_values = carried
        row_begin, block_total = inputs
        scores = block_scores(
            queries, keys_rot, row_mask(row_begin, row_block, length, prefix), score_scale
        )
        probability = jnp.exp(scores - block_total)
        prob_low = probability.astype(jnp.bfloat16)
        grad_prob = jnp.einsum(
            "bhd,khd->hbk", grad_mixed, values_in, preferred_element_type=jnp.float32
        )
        centre = jnp.sum(grad_prob * probability, axis=-1, keepdims=True)
        grad_scores = (probability * (grad_prob - centre)).astype(jnp.bfloat16)
        grad_query = (
            jnp.einsum("hbk,khd->bhd", grad_scores, keys_rot, preferred_element_type=jnp.float32)
            * score_scale
        )
        grad_keys = (
            grad_keys
            + jnp.einsum("hbk,bhd->khd", grad_scores, queries, preferred_element_type=jnp.float32)
            * score_scale
        )
        grad_values = grad_values + jnp.einsum(
            "hbk,bhd->khd", prob_low, grad_mixed, preferred_element_type=jnp.float32
        )
        return ((grad_keys, grad_values), grad_query)

    starts = jnp.arange(length // row_block, dtype=jnp.int32) * row_block
    zeros_kv = jnp.zeros(keys_rot.shape, jnp.float32)
    (grad_keys, grad_values), grad_queries = lax.scan(
        one_block, (zeros_kv, zeros_kv), (starts, log_total)
    )
    return (grad_queries.reshape(queries.shape), grad_keys, grad_values)


def local_general(
    token_ids,
    prefix_lengths,
    cluster_ids,
    embedding,
    w_query,
    w_key,
    w_value,
    w_dense,
    w_gate,
    w_up,
    w_down,
    norm1_gain,
    norm1_bias,
    norm2_gain,
    norm2_bias,
    cotangent,
):
    length = token_ids.shape[0]
    vocab_rows = embedding.shape[0]
    row_block = min(512, length)
    local_heads = w_query.shape[1] // HD
    local_hidden = w_gate.shape[1]
    one_hot = (token_ids[:, None] == jnp.arange(vocab_rows, dtype=jnp.int32)[None, :]).astype(
        jnp.bfloat16
    )
    embedded_low = jnp.dot(one_hot, embedding, preferred_element_type=jnp.float32).astype(
        jnp.bfloat16
    )
    embedded = embedded_low.astype(jnp.float32)
    cosine, sine = rotary_tables(length, HD)
    prefix = prefix_lengths[0]
    own_cluster = cluster_ids[lax.axis_index("dp")]
    seq_weight = 1.0 / jnp.sum((cluster_ids == own_cluster).astype(jnp.float32))

    def project(weight_in):
        return jnp.dot(embedded_low, weight_in, preferred_element_type=jnp.float32).reshape(
            length, local_heads, HD
        )

    queries = rotate(project(w_query), cosine, sine).astype(jnp.bfloat16)
    keys_rot = rotate(project(w_key), cosine, sine).astype(jnp.bfloat16)
    values_in = project(w_value).astype(jnp.bfloat16)
    attended, log_total = attention_forward(queries, keys_rot, values_in, prefix, row_block)
    attended_low = attended.astype(jnp.bfloat16)
    branch = lax.psum(
        jnp.einsum("lh,dh->ld", attended_low, w_dense, preferred_element_type=jnp.float32), "mp"
    )
    residual_one = deep_alpha * embedded + branch
    hidden, norm_one_pull = jax.vjp(layer_norm, residual_one, norm1_gain, norm1_bias)
    hidden_low = hidden.astype(jnp.bfloat16)
    gate_proj = jnp.dot(hidden_low, w_gate, preferred_element_type=jnp.float32)
    up_proj = jnp.dot(hidden_low, w_up, preferred_element_type=jnp.float32)
    unit_index = lax.axis_index("mp") * local_hidden + jnp.arange(local_hidden, dtype=jnp.int32)
    used_mask = (unit_index < FF_USED).astype(jnp.float32)

    def gated_unit(gate_in, up_in):
        return jax.nn.gelu(gate_in, approximate=True) * up_in * used_mask

    activation, gated_pull = jax.vjp(gated_unit, gate_proj, up_proj)
    activation_low = activation.astype(jnp.bfloat16)
    branch_two = lax.psum(
        jnp.einsum("lf,df->ld", activation_low, w_down, preferred_element_type=jnp.float32), "mp"
    )
    residual_two = deep_alpha * hidden + branch_two
    final, norm_two_pull = jax.vjp(layer_norm, residual_two, norm2_gain, norm2_bias)
    grad_out = cotangent.astype(jnp.float32) * seq_weight
    grad_two, grad_gain_two, grad_bias_two = norm_two_pull(grad_out)
    grad_branch_two = grad_two.astype(jnp.bfloat16)
    grad_w_down = jnp.einsum(
        "ld,lf->df", grad_branch_two, activation_low, preferred_element_type=jnp.float32
    )
    grad_act = jnp.dot(grad_branch_two, w_down, preferred_element_type=jnp.float32)
    grad_gate, grad_up = gated_pull(grad_act)
    grad_gate_low = grad_gate.astype(jnp.bfloat16)
    grad_up_low = grad_up.astype(jnp.bfloat16)
    grad_w_gate = jnp.einsum(
        "ld,lf->df", hidden_low, grad_gate_low, preferred_element_type=jnp.float32
    )
    grad_w_up = jnp.einsum("ld,lf->df", hidden_low, grad_up_low, preferred_element_type=jnp.float32)
    hidden_part = jnp.einsum(
        "lf,df->ld", grad_gate_low, w_gate, preferred_element_type=jnp.float32
    ) + jnp.einsum("lf,df->ld", grad_up_low, w_up, preferred_element_type=jnp.float32)
    grad_hidden = deep_alpha * grad_two + lax.psum(hidden_part, "mp")
    feed_sums = (
        lax.psum_scatter(grad_w_gate, "dp", scatter_dimension=0, tiled=True),
        lax.psum_scatter(grad_w_up, "dp", scatter_dimension=0, tiled=True),
        lax.psum_scatter(grad_w_down, "dp", scatter_dimension=0, tiled=True),
        lax.psum_scatter(grad_gain_two, "dp", scatter_dimension=0, tiled=True),
        lax.psum_scatter(grad_bias_two, "dp", scatter_dimension=0, tiled=True),
    )
    grad_one, grad_gain_one, grad_bias_one = norm_one_pull(grad_hidden)
    grad_branch = grad_one.astype(jnp.bfloat16)
    grad_w_dense = jnp.einsum(
        "ld,lh->dh", grad_branch, attended_low, preferred_element_type=jnp.float32
    )
    grad_attended = jnp.dot(grad_branch, w_dense, preferred_element_type=jnp.float32).astype(
        jnp.bfloat16
    )
    grad_attended = grad_attended.reshape(length, local_heads, HD)
    grad_queries, grad_keys, grad_values = attention_backward(
        queries, keys_rot, values_in, prefix, row_block, log_total, grad_attended
    )
    grad_query_lin = rotate(grad_queries, cosine, -sine).astype(jnp.bfloat16).reshape(length, -1)
    grad_key_lin = rotate(grad_keys, cosine, -sine).astype(jnp.bfloat16).reshape(length, -1)
    grad_value_lin = grad_values.astype(jnp.bfloat16).reshape(length, -1)
    grad_w_query = jnp.einsum(
        "ld,lh->dh", embedded_low, grad_query_lin, preferred_element_type=jnp.float32
    )
    grad_w_key = jnp.einsum(
        "ld,lh->dh", embedded_low, grad_key_lin, preferred_element_type=jnp.float32
    )
    grad_w_value = jnp.einsum(
        "ld,lh->dh", embedded_low, grad_value_lin, preferred_element_type=jnp.float32
    )
    input_part = (
        jnp.einsum("lh,dh->ld", grad_query_lin, w_query, preferred_element_type=jnp.float32)
        + jnp.einsum("lh,dh->ld", grad_key_lin, w_key, preferred_element_type=jnp.float32)
        + jnp.einsum("lh,dh->ld", grad_value_lin, w_value, preferred_element_type=jnp.float32)
    )
    grad_embedded = deep_alpha * grad_one + lax.psum(input_part, "mp")
    grad_table = 0.1 * jnp.dot(one_hot.astype(jnp.float32).T, grad_embedded, precision=highest)
    attn_sums = (
        lax.psum_scatter(grad_table, "dp", scatter_dimension=0, tiled=True),
        lax.psum_scatter(grad_w_query, "dp", scatter_dimension=0, tiled=True),
        lax.psum_scatter(grad_w_key, "dp", scatter_dimension=0, tiled=True),
        lax.psum_scatter(grad_w_value, "dp", scatter_dimension=0, tiled=True),
        lax.psum_scatter(grad_w_dense, "dp", scatter_dimension=0, tiled=True),
        lax.psum_scatter(grad_gain_one, "dp", scatter_dimension=0, tiled=True),
        lax.psum_scatter(grad_bias_one, "dp", scatter_dimension=0, tiled=True),
    )
    summed = (
        attn_sums[0],
        attn_sums[1],
        attn_sums[2],
        attn_sums[3],
        attn_sums[4],
        feed_sums[0],
        feed_sums[1],
        feed_sums[2],
        attn_sums[5],
        attn_sums[6],
        feed_sums[3],
        feed_sums[4],
    )
    return (
        final.astype(jnp.bfloat16),
        summed[0],
        summed[1],
        summed[2],
        summed[3],
        summed[4],
        summed[5],
        summed[6],
        summed[7],
        summed[8],
        summed[9],
        summed[10],
        summed[11],
    )


LINE = 4
MESH = pl.DeviceIdType.MESH
CHUNKS = 4
AHEAD = 2
LOW = jnp.bfloat16
FULL = jnp.float32
TANH_SCALE = math.sqrt(2.0 / math.pi)


def dot(left, right):
    return jnp.dot(left, right, preferred_element_type=FULL)


def dot_nt(left, right):
    return lax.dot_general(left, right, (((1,), (1,)), ((), ())), preferred_element_type=FULL)


def dot_tn(left, right):
    return lax.dot_general(left, right, (((0,), (0,)), ((), ())), preferred_element_type=FULL)


def split_low(value):
    high = value.astype(LOW)
    return high, (value - high.astype(FULL)).astype(LOW)


def row_mean(value):
    return jnp.mean(value, axis=-1, keepdims=True)


def spread(size, body, tile=512):
    for start in range(0, size, tile):
        body(start, min(tile, size - start))


def tiles(size, body, tile=512):
    whole = size // tile
    lax.fori_loop(0, whole, lambda step, carried: (body(pl.multiple_of(step * tile, tile), tile), carried)[1], 0)
    if size % tile:
        body(whole * tile, size % tile)


def layer_kernel(
    length, width, local_hidden,
    prefix_ref, cluster_ref, ids_row, gain_one, bias_one, gain_two, bias_two, emb_hbm, cos_hbm, sin_hbm, w_query_hbm, w_key_hbm, w_value_hbm, w_dense_hbm,
    w_gate_hbm, w_up_hbm, w_down_hbm, cot_hbm,
    block_out, out_table, out_query, out_key, out_value, out_dense, out_gate, out_up, out_down, out_norms,
    r_act, r_two, r_y, r_cols, r_att, xhat_park, grad_two_park, r_dny, r_rs, r_late, r_dz, r_dx, r_sums,
    emb, cos_ref, sin_ref, parts, core_in, x_in, back_in, blocks, xbuf, gbuf, obuf, gate_up, grads_low, act_low, send_a, cols_own, cols_send,
    hidden_theirs, two_own, two_send, att_low, att_turned, heads, w_dense, one_hot, hot_turned, rstd_one, vectors, table_core, table_x,
    core_s, core_r, x_s, x_r, back_s, back_r, act_s, act_r, two_s, two_r, fwd_two_s, fwd_two_r, cols_s, cols_r, fwd_s,
    fwd_r, ys_s, ys_r, att_s, att_r, dny_s, dny_r, late_s, late_r, dz_s, dz_r, dx_s, dx_r, rs_s, rs_r, sums_s, sums_r, table_s, table_r, load_sem, weight_sem,
):
    dp, mp = lax.axis_index("dp"), lax.axis_index("mp")
    z, y = lax.div(dp, 2), lax.rem(dp, 2)
    x, core = lax.div(mp, 2), lax.rem(mp, 2)
    rows = length // CHUNKS
    heads_here = heads.shape[1]
    inner = heads_here * HD
    vocab = emb.shape[0]
    shift = (local_hidden + 15) // 16 * 16
    near = (local_hidden // 2 + 15) // 16 * 16
    spans = ((0, near), (near, local_hidden - near))
    block = width // (2 * LINE)
    alpha = jnp.float32(deep_alpha)

    def at(z_to=None, y_to=None, x_to=None, core_to=None):
        z_to = z if z_to is None else z_to
        y_to = y if y_to is None else y_to
        x_to = x if x_to is None else x_to
        core_to = core if core_to is None else core_to
        return (2 * z_to + y_to, 2 * x_to + core_to)

    core_peer = at(core_to=1 - core)
    x_peer = at(x_to=1 - x)
    y_peer = at(y_to=1 - y)
    z_peer = at(z_to=z + 1 - 2 * lax.rem(z, 2))
    at_end = (z == 0) | (z == LINE - 1)

    def remote(source, target, send, receive, device):
        return pltpu.make_async_remote_copy(
            src_ref=source, dst_ref=target, send_sem=send, recv_sem=receive,
            device_id=device, device_id_type=MESH,
        )

    def load_all(pairs):
        copies = [
            pltpu.make_async_copy(source, target, load_sem.at[place])
            for place, (source, target) in enumerate(pairs)
        ]
        for copy in copies:
            copy.start()
        return copies

    def moved(pairs):
        for copy in load_all(pairs):
            copy.wait()

    barrier = pltpu.get_barrier_semaphore()
    greeted = [core_peer, x_peer, y_peer] + [at(z_to=lax.rem(z + step, LINE)) for step in range(1, LINE)]
    for device in greeted:
        pl.semaphore_signal(barrier, inc=1, device_id=device, device_id_type=MESH)

    def chunk_rows(chunk):
        return pl.ds(pl.multiple_of(chunk * rows, rows), rows)

    def core_copy(turn, chunk):
        return remote(
            parts.at[chunk, 1 - core], core_in.at[chunk], core_s.at[turn, chunk], core_r.at[turn, chunk], core_peer
        )

    def x_copy(turn, chunk):
        return remote(
            parts.at[chunk, core], x_in.at[turn % 2, chunk], x_s.at[turn, chunk], x_r.at[turn, chunk], x_peer
        )

    def back_copy(turn, chunk):
        return remote(
            parts.at[chunk, core], back_in.at[chunk], back_s.at[turn, chunk], back_r.at[turn, chunk], core_peer
        )

    def put_part(chunk, start, size, value):
        side, first = lax.div(start, width // 2), lax.rem(start, width // 2)
        parts[chunk, side, :, pl.ds(pl.multiple_of(first, size), size)] = value

    def send_part(turn, chunk):
        core_copy(turn, chunk).wait()
        parts[chunk, core] = parts[chunk, core] + core_in[chunk]
        x_copy(turn, chunk).start()

    def take_part(turn, chunk):
        x_copy(turn, chunk).wait()
        parts[chunk, core] = parts[chunk, core] + x_in[turn % 2, chunk]
        back = back_copy(turn, chunk)
        back.start()
        mine = parts[chunk, core]
        back.wait()
        other = back_in[chunk]
        return jnp.concatenate([jnp.where(core == 0, mine, other), jnp.where(core == 0, other, mine)], axis=1)

    def put_blocks(value):
        for place in range(2 * LINE):
            blocks[place] = value[:, place * block : (place + 1) * block]

    def chunk_lanes(chunk):
        return pl.ds(pl.multiple_of(chunk * rows, rows), rows)

    def half_lanes(side):
        return pl.ds(pl.multiple_of(side * block, block), block)

    def keep_columns(chunk):
        for place in range(LINE):
            cols_own[place, chunk_rows(chunk), :] = blocks[2 * place + y].astype(LOW)
        for place in range(2):
            cols_send[2 * chunk + place] = blocks[2 * (2 * core + place) + 1 - y]

    def cols_copy(chunk):
        return remote(
            cols_send.at[pl.ds(2 * chunk, 2)], r_cols.at[pl.ds(2 * core, 2), chunk],
            cols_s.at[chunk], cols_r.at[chunk], y_peer,
        )

    def forward_copy():
        view = r_cols.at[pl.ds(2 * core, 2)]
        return remote(view, view, fwd_s, fwd_r, core_peer)

    def act_copy(way, hop, chunk):
        goal = jnp.clip(z + 1 - 2 * way, 0, LINE - 1)
        owner = z - hop if way == 0 else z + hop
        active = (owner >= 0) & (z < LINE - 1) if way == 0 else (owner < LINE) & (z > 0)
        owner = jnp.clip(owner, 0, LINE - 1)
        landed = r_act.at[owner, :, chunk_lanes(chunk)]
        source = send_a.at[lax.div(chunk, 2), :, half_chunk(chunk)] if hop == 0 else landed
        return active, remote(
            source, landed, act_s.at[way, hop, chunk], act_r.at[way, hop, chunk], at(z_to=goal)
        )

    def act_landed(way, hop):
        return z - 1 - hop >= 0 if way == 0 else z + 1 + hop < LINE

    def half_chunk(chunk):
        return pl.ds(pl.multiple_of(lax.rem(chunk, 2) * rows, rows), rows)

    def act_send(hop, chunk):
        for way in range(2):
            active, copy = act_copy(way, hop, chunk)
            pl.when(active)(copy.start)

    def act_take(hop, chunk):
        for way in range(2):
            _, copy = act_copy(way, hop, chunk)
            pl.when(act_landed(way, hop))(copy.wait_recv)

    other_x = 2 * (1 - x) + core

    def act_pass(chunks):
        for chunk in chunks:
            act_take(1, chunk)
            act_send(2, chunk)

    def two_copy(step):
        goal = lax.rem(z + step, LINE)
        return remote(
            two_send.at[pl.ds(2 * goal, 2)], r_two.at[z, pl.ds(2 * mp, 2)],
            two_s.at[step - 1], two_r.at[step - 1], at(z_to=goal),
        )

    def two_spread(turn, step):
        quarter = other_x if turn == 2 else mp
        view = r_two.at[lax.rem(z + step, LINE), pl.ds(2 * quarter, 2)]
        device = x_peer if turn == 1 else core_peer
        return remote(view, view, fwd_two_s.at[turn, step - 1], fwd_two_r.at[turn, step - 1], device)

    def pair_copy(which, chunk, part):
        units = pl.ds(*spans[part])
        return remote(
            gate_up.at[which, units, chunk_lanes(chunk)], r_y.at[which, units, chunk_lanes(chunk)],
            ys_s.at[which, chunk, part], ys_r.at[which, chunk, part], y_peer,
        )

    def pair_send(which, chunk):
        for part in range(2):
            pair_copy(which, chunk, part).start()

    def rows_copy():
        return remote(gbuf, r_att, att_s, att_r, z_peer)

    def fetch_columns(target):
        forward = forward_copy()
        forward.start()
        forward.wait()
        for pair in range(2):
            moved(
                [(r_cols.at[2 * pair + place], blocks.at[pl.ds(CHUNKS * place, CHUNKS)]) for place in range(2)]
            )
            for place in range(2):
                for chunk in range(CHUNKS):
                    piece = blocks[CHUNKS * place + chunk].astype(LOW)
                    target[2 * pair + place, chunk * rows : (chunk + 1) * rows, :] = piece

    def every_chunk(body):
        lax.fori_loop(0, CHUNKS, lambda chunk, carried: (body(chunk), carried)[1], 0)

    score_scale = 1.0 / math.sqrt(HD)

    def probabilities(queries, keys, begin):
        shape = (queries.shape[0], length)
        column = lax.broadcasted_iota(jnp.int32, shape, 1)
        row = lax.broadcasted_iota(jnp.int32, shape, 0) + begin
        visible = (column < prefix_ref[0]) | (column <= row)
        scores = jnp.where(visible, dot_nt(queries, keys) * score_scale, -1e30)
        weights = jnp.exp(scores - jnp.max(scores, axis=-1, keepdims=True))
        return weights / jnp.sum(weights, axis=-1, keepdims=True)

    def turn_by(value, sine):
        return value * cos_ref[...] + pltpu.roll(value, HD // 2, 1) * sine

    def head_lanes(place, offset=0):
        return pl.ds(pl.multiple_of(offset + place * HD, HD), HD)

    def first_scope(w_heads, tab):
        loads = [
            pltpu.make_async_copy(source, target, weight_sem.at[place])
            for place, (source, target) in enumerate(
                (
                    (emb_hbm, emb),
                    (w_query_hbm, w_heads.at[0]),
                    (w_key_hbm, w_heads.at[1]),
                    (w_value_hbm, w_heads.at[2]),
                    (cos_hbm, cos_ref),
                    (sin_hbm, sin_ref),
                    (w_dense_hbm, w_dense),
                )
            )
        ]
        for copy in loads:
            copy.start()
        named = lax.broadcasted_iota(jnp.int32, (vocab, length), 0) == ids_row[...]
        hot = jnp.where(named, 1.0, 0.0)
        hot_turned[...] = hot.astype(LOW)
        turned_hot = hot.T.astype(LOW)
        one_hot[:, 0:vocab] = turned_hot
        one_hot[:, vocab:] = turned_hot
        vectors[...] = jnp.zeros_like(vectors)
        loads[0].wait()
        for kind in range(3):
            loads[kind + 1].wait()
            pieces = split_low(dot(emb[...], w_heads[kind]))
            for place in range(heads_here):
                for half, piece in enumerate(pieces):
                    tab[place, half * vocab : (half + 1) * vocab, kind * HD : (kind + 1) * HD] = piece[
                        :, place * HD : (place + 1) * HD
                    ]
        loads[4].wait()
        loads[5].wait()

        def head_inputs(place, carried):
            lin = dot(one_hot[...], tab[place])
            heads[0, place] = turn_by(lin[:, 0:HD], sin_ref[...]).astype(LOW)
            heads[1, place] = turn_by(lin[:, HD : 2 * HD], sin_ref[...]).astype(LOW)
            heads[2, place] = lin[:, 2 * HD :].astype(LOW)
            return carried

        lax.fori_loop(0, heads_here, head_inputs, 0)

        def attend(chunk):
            for place in range(heads_here):
                queries = heads[0, place, chunk_rows(chunk), :]
                probability = probabilities(queries, heads[1, place], chunk * rows).astype(LOW)
                mixed = dot(probability, heads[2, place]).astype(LOW)
                att_low[chunk_rows(chunk), place * HD : (place + 1) * HD] = mixed
                turned = mixed.astype(FULL).T
                att_turned[place * HD : (place + 1) * HD, chunk_lanes(chunk)] = turned.astype(LOW)
                gbuf[place * HD : (place + 1) * HD, chunk_lanes(chunk)] = turned

        def project(chunk):
            attend(chunk)
            pl.when(chunk == 0)(lambda: loads[6].wait())
            pl.when(chunk == 0)(lambda: pl.semaphore_wait(barrier, len(greeted)))
            mixed = att_low[chunk_rows(chunk), :]

            def columns(start, size):
                put_part(chunk, start, size, dot_nt(mixed, w_dense[pl.ds(start, size), :]))

            spread(width, columns, 256)
            core_copy(0, chunk).start()
            pl.when(chunk == 0)(lambda: send_part(0, 0))
            pl.when((chunk > 1) & (chunk <= AHEAD))(lambda: send_part(0, chunk - 1))

        every_chunk(project)
        rows_copy().start()

    pl.run_scoped(first_scope, pltpu.VMEM((3, width, inner), LOW), pltpu.VMEM((heads_here, 2 * vocab, 3 * HD), LOW))

    def middle_scope(w_gate, w_up, w_down, cotbuf):
        weight_copies = [
            pltpu.make_async_copy(source, target, weight_sem.at[place])
            for place, (source, target) in enumerate(((w_gate_hbm, w_gate), (w_up_hbm, w_up), (w_down_hbm, w_down)))
        ]
        for copy in weight_copies:
            copy.start()
        for copy in weight_copies:
            copy.wait()

        def feed_forward(chunk):
            branch = take_part(0, chunk)
            residual = alpha * dot(one_hot[chunk_rows(chunk), 0:vocab], emb[...]) + branch
            centered = residual - row_mean(residual)
            rstd = lax.rsqrt(row_mean(centered * centered) + norm_eps)
            xhat = centered * rstd
            rstd_one[chunk] = rstd
            xbuf[...] = xhat
            park = pltpu.make_async_copy(xbuf, xhat_park.at[chunk], load_sem.at[0])
            park.start()
            hidden_low = (xhat * gain_one[...] + bias_one[...]).astype(LOW)
            put_blocks(hidden_low.astype(FULL))
            keep_columns(chunk)
            cols_copy(chunk).start()

            def units_tile(start, size):
                cut = pl.ds(start, size)
                gate = dot_nt(w_gate[cut, :], hidden_low)
                up = dot_nt(w_up[cut, :], hidden_low)
                units = mp * local_hidden + start + lax.broadcasted_iota(jnp.int32, (size, rows), 0)
                used = jnp.where(units < FF_USED, 1.0, 0.0)
                square = gate * gate
                bend = jnp.tanh(TANH_SCALE * gate * (1.0 + 0.044715 * square))
                gelu = 0.5 * gate * (1.0 + bend) * used
                slope = 0.5 * (1.0 + bend) + 0.5 * gate * (1.0 - bend * bend) * (
                    TANH_SCALE * (1.0 + 3.0 * 0.044715 * square)
                )
                gate_up[0, cut, chunk_lanes(chunk)] = slope * up * used
                gate_up[1, cut, chunk_lanes(chunk)] = gelu
                active = (gelu * up).astype(LOW)
                act_low[cut, chunk_lanes(chunk)] = active
                send_a[lax.div(chunk, 2), cut, half_chunk(chunk)] = active.astype(FULL)

            tiles(local_hidden, units_tile)
            act_send(0, chunk)
            active = send_a[lax.div(chunk, 2), :, half_chunk(chunk)].T.astype(LOW)
            tiles(
                width, lambda start, size: put_part(chunk, start, size, dot(active, w_down[:, pl.ds(start, size)]))
            )
            core_copy(1, chunk).start()
            park.wait()
            send_part(1, chunk)
            pl.when(chunk + AHEAD < CHUNKS)(lambda: send_part(0, chunk + AHEAD))

        same = jnp.int32(0)
        for place in range(2 * LINE):
            same = same + jnp.where(cluster_ref[place] == cluster_ref[dp], 1, 0)
        weight_row = 1.0 / jnp.full((1, width), same, jnp.int32).astype(FULL)

        def feed_backward(chunk):
            loads = load_all(
                ((xhat_park.at[chunk], xbuf), (cot_hbm.at[chunk_rows(chunk)], cotbuf))
            )
            branch = take_part(1, chunk)
            for copy in loads:
                copy.wait()
            residual = alpha * (xbuf[...] * gain_one[...] + bias_one[...]) + branch
            centered = residual - row_mean(residual)
            rstd = lax.rsqrt(row_mean(centered * centered) + norm_eps)
            xhat = centered * rstd
            obuf[...] = (xhat * gain_two[...] + bias_two[...]).astype(LOW)
            grad_out = cotbuf[...].astype(FULL) * weight_row
            vectors[2:3, :] += jnp.sum(grad_out * xhat, axis=0, keepdims=True)
            vectors[3:4, :] += jnp.sum(grad_out, axis=0, keepdims=True)
            grad_x = grad_out * gain_two[...]
            grad_two = (grad_x - row_mean(grad_x) - xhat * row_mean(grad_x * xhat)) * rstd
            for place in range(width // inner):
                gbuf[place * rows : (place + 1) * rows, :] = grad_two[:, place * inner : (place + 1) * inner]
            stores = load_all(
                ((obuf, block_out.at[chunk_rows(chunk)]), (gbuf, grad_two_park.at[chunk]))
            )
            grad_low = grad_two.astype(LOW)
            put_blocks(grad_low.astype(FULL))
            for place in range(2):
                two_own[place, chunk_rows(chunk), :] = blocks[2 * z + place].astype(LOW)

            @pl.when(chunk == mp)
            def _():
                two_send[...] = blocks[...]
                for step in range(1, LINE):
                    two_copy(step).start()


            def units_tile(start, size):
                cut = pl.ds(start, size)
                grad_act = dot_nt(w_down[cut, :], grad_low)
                for which in range(2):
                    low = (grad_act * gate_up[which, cut, chunk_lanes(chunk)]).astype(LOW)
                    grads_low[pl.ds(which * shift + start, size), chunk_lanes(chunk)] = low
                    gate_up[which, cut, chunk_lanes(chunk)] = low.astype(FULL)

            spread(local_hidden, units_tile)
            pair_send(0, chunk)
            for copy in stores:
                copy.wait()

        def hidden_part(pair):
            both = pl.ds(pl.multiple_of(2 * rows * pair, 2 * rows), 2 * rows)
            grad_gate = gate_up[0, :, both].T.astype(LOW)
            grad_up = gate_up[1, :, both].T.astype(LOW)

            def columns(start, size):
                cut = pl.ds(start, size)
                value = dot(grad_gate, w_gate[:, cut]) + dot(grad_up, w_up[:, cut])
                put_part(2 * pair, start, size, value[:rows])
                put_part(2 * pair + 1, start, size, value[rows:])

            tiles(width, columns)
            for place in range(2):
                core_copy(2, 2 * pair + place).start()

        def take_hidden():
            for chunk in range(CHUNKS):
                cols_copy(chunk).wait()
            fetch_columns(hidden_theirs)

        def step(turn, carried):
            pl.when(turn == CHUNKS - 1)(lambda: hidden_part(0))
            @pl.when(turn >= 3)
            def _():
                act_take(0, turn - 3)
                act_send(1, turn - 3)

            @pl.when(turn == CHUNKS)
            def _():
                for chunk in range(2):
                    send_part(2, chunk)
                take_hidden()

            pl.when(turn < CHUNKS)(lambda: feed_forward(turn))
            pl.when(turn == 1)(lambda: rows_copy().wait())
            pl.when(turn > 0)(lambda: feed_backward(turn - 1))
            return carried

        lax.fori_loop(0, CHUNKS + 1, step, 0)

        hidden_part(1)
        for chunk in range(2, CHUNKS):
            send_part(2, chunk)
        act_take(0, 2)
        act_send(1, 2)
        pl.when(~at_end)(lambda: act_pass((0,)))

    pl.run_scoped(
        middle_scope,
        pltpu.VMEM((local_hidden, width), LOW),
        pltpu.VMEM((local_hidden, width), LOW),
        pltpu.VMEM((local_hidden, width), LOW),
        pltpu.VMEM((rows, width), LOW),
    )

    def last_scope(theirs, late_theirs, two_theirs, att_theirs, send_b, stage, grad_att, grad_one_own, sums, sums_up, sums_down, sums_below, sums_above, late_own):
        def norm_backward(chunk):
            loads = load_all(((xhat_park.at[chunk], xbuf), (grad_two_park.at[chunk], gbuf)))
            branch = take_part(2, chunk)
            for copy in loads:
                copy.wait()
            grad_two = [gbuf[place * rows : (place + 1) * rows, :] for place in range(width // inner)]
            grad_hidden = alpha * jnp.concatenate(grad_two, axis=1) + branch
            xhat = xbuf[...]
            vectors[0:1, :] += jnp.sum(grad_hidden * xhat, axis=0, keepdims=True)
            vectors[1:2, :] += jnp.sum(grad_hidden, axis=0, keepdims=True)
            grad_x = grad_hidden * gain_one[...]
            grad_one = (grad_x - row_mean(grad_x) - xhat * row_mean(grad_x * xhat)) * rstd_one[chunk]
            put_blocks(grad_one)
            for place in range(2):
                grad_one_own[chunk_rows(chunk), place * block : (place + 1) * block] = blocks[2 * mp + place]
            grad_low = grad_one.astype(LOW)
            put_blocks(grad_low.astype(FULL))
            for place in range(2 * LINE):
                late_own[place, chunk_rows(chunk), :] = blocks[place].astype(LOW)

            @pl.when(chunk == mp)
            def _():
                for place in range(2 * LINE):
                    cols_send[place] = blocks[place]

            grad_mixed = dot(grad_low, w_dense[...]).astype(LOW)
            for place in range(heads_here):
                grad_att[place, chunk_rows(chunk), :] = grad_mixed[:, place * HD : (place + 1) * HD]

        def fetch_units(which, part):
            start, size = spans[part]
            for chunk in range(CHUNKS):
                pair_copy(which, chunk, part).wait()
            views = [stage.at[side, pl.ds(start, size)] for side in range(2)]
            moved(
                [(r_y.at[which, pl.ds(start, size), pl.ds(block * side, block)], views[side]) for side in range(2)]
            )
            for side in range(2):
                theirs[1 + which, start : start + size, block * side : block * (side + 1)] = views[side][...].astype(LOW)

        def fetch_rows(source, target):
            size = source.shape[0]
            views = [stage.at[place, pl.ds(0, size)] for place in range(2)]
            moved([(source.at[:, pl.ds(block * place, block)], views[place]) for place in range(2)])
            for place in range(2):
                target[:, block * place : block * (place + 1)] = views[place][...].astype(LOW)

        def outer_product(target, place, own, other):
            right, right_theirs = cols_own[place], hidden_theirs[place]

            def rows_tile(start, size):
                cut = pl.ds(start, size)
                target[cut, :] = dot(own[cut, :], right) + dot(other[cut, :], right_theirs)

            tiles(target.shape[0], rows_tile)

        def down_products():
            for step in range(1, LINE):
                two_spread(1, step).wait()
                two_spread(2, step).start()
            for step in range(1, LINE):
                two_spread(0, step).wait()
                two_spread(2, step).wait()
            for chunk in range(CHUNKS):
                pl.when(at_end)(lambda: act_take(1, chunk))
                act_take(2, chunk)
            for step in range(LINE):
                owner = lax.rem(z + step, LINE)
                if step:
                    moved([(r_two.at[owner], blocks)])
                    for place in range(2):
                        for chunk in range(CHUNKS):
                            piece = blocks[2 * chunk + place].astype(LOW)
                            two_theirs[place, chunk * rows : (chunk + 1) * rows, :] = piece
                    fetch_rows(r_act.at[owner], theirs.at[0])
                left, right = (theirs.at[0], two_theirs) if step else (act_low, two_own)
                for place in range(2):
                    lanes = slice(place * block, (place + 1) * block)

                    def rows_tile(start, size):
                        cut = pl.ds(start, size)
                        product = dot(left[cut, :], right[place])
                        gate_up[0, cut, lanes] = gate_up[0, cut, lanes] + product if step else product

                    tiles(local_hidden, rows_tile)

        def down_copy():
            return remote(gate_up.at[0, :, half_lanes(1 - y)], r_dny, dny_s, dny_r, y_peer)

        def down_end():
            down_copy().wait()
            moved([(r_dny, stage.at[0])])
            stage[0] = stage[0] + gate_up[0, :, half_lanes(y)]
            moved([(stage.at[0], out_down)])
            for chunk in range(CHUNKS):
                for way in range(2):
                    for hop in range(1, LINE - 1):
                        active, copy = act_copy(way, hop, chunk)
                        pl.when(active)(copy.wait_send)

        def toward(side):
            return jnp.where(z < LINE // 2, side, 1 - side)

        def goes(slot, way):
            return jnp.where(way == 0, z < slot, z > LINE - 1 - slot)

        def inner_place(way):
            return jnp.where(way == 0, z > 0, z < LINE - 1)

        def line_goal(way):
            return at(z_to=jnp.clip(z + 1 - 2 * way, 0, LINE - 1))

        def unit_terms(kind):
            return grads_low.at[pl.ds(pl.multiple_of(kind * shift, 16), local_hidden)], theirs.at[1 + kind]

        def count(way):
            return jnp.where(way == 0, LINE - 1 - z, z)

        def order(kind, slot, way):
            return kind * count(way) + slot - (LINE - count(way))

        def turn_of(number, way):
            many = jnp.maximum(count(way), 1)
            return lax.div(number, many) * (LINE - 1) + lax.rem(number, many) + LINE - 1 - count(way)

        def unit_copy(turn, side, part):
            way = toward(side)
            kind, slot = lax.div(turn, LINE - 1), lax.rem(turn, LINE - 1)
            units = pl.ds(*spans[part])
            home = (send_a, send_b)[side].at[lax.rem(jnp.maximum(order(kind, slot + 1, way), 0), 2), units]
            return remote(
                home, r_rs.at[kind, slot, way, units], rs_s.at[kind, slot, way, part], rs_r.at[kind, slot, way, part],
                line_goal(way),
            )

        def unit_sent(number, side):
            for part in range(2):
                unit_copy(turn_of(jnp.maximum(number, 0), toward(side)), side, part).wait_send()

        def unit_slot(turn, part, side):
            way = toward(side)
            kind, slot = lax.div(turn, LINE - 1), lax.rem(turn, LINE - 1) + 1
            own, other = unit_terms(kind)
            start, size = spans[part]
            cut = slice(start, start + size)

            @pl.when(goes(slot, way))
            def _():
                number = order(kind, slot, way)
                home = (send_a, send_b)[side].at[lax.rem(jnp.maximum(number, 0), 2)]
                if part == 0:
                    pl.when(number >= 2)(lambda: unit_sent(number - 2, side))
                place = jnp.where(way == 0, LINE - slot + z, slot - LINE + z)
                home[cut, :] = dot(own[cut, :], cols_own[place]) + dot(other[cut, :], hidden_theirs[place])

                @pl.when((slot > 1) & inner_place(way))
                def _():
                    before = jnp.maximum(turn - 1, 0)
                    unit_copy(before, side, part).wait_recv()
                    landed = r_rs.at[lax.div(before, LINE - 1), lax.rem(before, LINE - 1), way, pl.ds(start, size)]
                    moved([(landed, stage.at[side, pl.ds(start, size)])])
                    home[cut, :] = home[cut, :] + stage[side, cut, :]

                unit_copy(turn, side, part).start()

        def unit_end():
            own, other = unit_terms(0)
            outer_product(stage.at[0], z, own, other)
            for side in range(2):

                @pl.when(inner_place(toward(side)))
                def _():
                    for part in range(2):
                        unit_copy(LINE - 2, side, part).wait_recv()
                    moved([(r_rs.at[0, LINE - 2, toward(side)], stage.at[1])])
                    stage[0] = stage[0] + stage[1]

            moved([(stage.at[0], out_gate)])

        def last_product():
            own, other = unit_terms(1)
            outer_product(stage.at[0], z, own, other)
            moved([(stage.at[0], out_up)])

        def last_landed():
            for side in range(2):
                for part in range(2):
                    pl.when(inner_place(toward(side)))(unit_copy(2 * LINE - 3, side, part).wait_recv)

        first = jnp.where(z == 1, 2, jnp.where(z == LINE - 1, 2 * LINE - 2, 0))
        peer_first = jnp.where(z == 0, 2, jnp.where(z == 2, 2 * LINE - 2, 0))
        many = 2 * LINE - 2
        def late_copy(begin, size, part):
            span = pl.ds(begin + part * (size // 2), size // 2)
            return remote(cols_send.at[span], r_late.at[mp, span], late_s.at[0, part], late_r.at[0, part], z_peer)

        def late_send():
            for part in range(2):
                pl.when(at_end)(lambda: late_copy(peer_first, many, part).start())
                pl.when(~at_end)(lambda: late_copy(peer_first, 2, part).start())

        def spread_copy(turn, size, part):
            place = other_x if turn == 3 else mp
            view = r_late.at[place, pl.ds(first + part * (size // 2), size // 2)]
            device = x_peer if turn == 2 else core_peer
            return remote(view, view, late_s.at[turn, part], late_r.at[turn, part], device)

        def by_size(body):
            pl.when(at_end)(lambda: body(2))
            pl.when(~at_end)(lambda: body(many))

        def late_take():
            def body(size):
                for part in range(2):
                    late_copy(first, size, part).wait_recv()
                    spread_copy(2, size, part).start()
                    spread_copy(1, size, part).start()
                for part in range(2):
                    spread_copy(2, size, part).wait()
                    spread_copy(3, size, part).start()
                for part in range(2):
                    spread_copy(1, size, part).wait()
                for part in range(2):
                    spread_copy(3, size, part).wait()

            by_size(body)

        def late_slot(number):
            side, lane = lax.div(number, LINE), lax.rem(number, LINE)
            return parts.at[:, side, :, pl.ds(pl.multiple_of(lane * block, block), block)]

        def late_products():
            for quarter in range(CHUNKS):

                def body(size):
                    moved([(r_late.at[quarter, pl.ds(first, size)], blocks.at[pl.ds(0, size)])])
                    for place in range(size):
                        late_theirs[place, quarter * rows : (quarter + 1) * rows, :] = blocks[place].astype(LOW)

                by_size(body)

            def product(number, carried):
                @pl.when((number < 2) | ~at_end)
                def _():
                    home = late_slot(number)
                    for piece in range(CHUNKS):
                        cut = slice(piece * rows, (piece + 1) * rows)
                        home[piece] = dot(att_turned[cut, :], late_own[first + number]) + dot(
                            att_theirs[cut, :], late_theirs[number]
                        )

                return carried

            lax.fori_loop(0, many, product, 0)
            for place in range(LINE - 1):
                pl.when((place == 0) | ~at_end)(lambda: late_pair(place).start())

        def late_pair(place):
            return remote(late_slot(2 * place + 1 - y), r_dz.at[place], dz_s.at[place], dz_r.at[place], y_peer)

        def late_line(place):
            goal = lax.div(first, 2) + place
            return goal != z, remote(late_slot(2 * place + y), r_dx, dx_s.at[place], dx_r, at(z_to=goal))

        def late_sums():
            for place in range(LINE - 1):

                @pl.when((place == 0) | ~at_end)
                def _():
                    late_pair(place).wait()
                    arrived = blocks.at[pl.ds(0, CHUNKS)]
                    moved([(r_dz.at[place], arrived)])
                    home = late_slot(2 * place + y)
                    home[...] = home[...] + arrived[...]
                    leaves, copy = late_line(place)
                    pl.when(leaves)(copy.start)

        def late_end():
            _, copy = late_line(0)
            copy.wait_recv()
            arrived = blocks.at[pl.ds(0, CHUNKS)]
            moved([(r_dx, arrived)])
            total = late_slot(2 * (z - lax.div(first, 2)) + y)
            for piece in range(CHUNKS):
                gbuf[0:block, piece * rows : (piece + 1) * rows] = (total[piece] + arrived[piece]).T
            moved([(gbuf.at[pl.ds(0, block)], out_dense)])
            for place in range(LINE - 1):

                @pl.when((place == 0) | ~at_end)
                def _():
                    leaves, copy = late_line(place)
                    pl.when(leaves)(copy.wait_send)

            for part in range(2):
                pl.when(at_end)(lambda: late_copy(peer_first, many, part).wait_send())
                pl.when(~at_end)(lambda: late_copy(peer_first, 2, part).wait_send())

        def last_sent():
            for side in range(2):
                pl.when(count(toward(side)) > 0)(lambda: unit_sent(2 * count(toward(side)) - 1, side))
                pl.when(count(toward(side)) > 0)(lambda: unit_sent(2 * count(toward(side)) - 2, side))

        def attention_backward(place, carried):
            hot_t = hot_turned[...]
            queries, keys, values = heads[0, place], heads[1, place], heads[2, place]
            grad_mixed = grad_att[place]
            probability = probabilities(queries, keys, 0)
            grad_prob = dot_nt(grad_mixed, values)
            centre = jnp.sum(grad_prob * probability, axis=-1, keepdims=True)
            grad_scores = (probability * (grad_prob - centre)).astype(LOW)
            grad_queries = dot(grad_scores, keys) * score_scale
            grad_keys = dot_tn(grad_scores, queries) * score_scale
            grad_values = dot_tn(probability.astype(LOW), grad_mixed)
            sums[0, 0:vocab, head_lanes(place)] = dot(hot_t, turn_by(grad_queries, -sin_ref[...]).astype(LOW))
            sums[0, 0:vocab, head_lanes(place, inner)] = dot(hot_t, turn_by(grad_keys, -sin_ref[...]).astype(LOW))
            sums[1, 0:vocab, head_lanes(place)] = dot(hot_t, grad_values.astype(LOW))
            return carried

        def small_sums():
            lax.fori_loop(0, heads_here, attention_backward, 0)
            hot_t = hot_turned[...]
            high, rest = split_low(grad_one_own[...])
            sums[1, 0:vocab, heads_here * HD :] = dot(hot_t, high) + dot(hot_t, rest)
            for side in range(2):
                sums[side, vocab:, :] = vectors[:, side * (width // 2) : (side + 1) * (width // 2)]
            sums_pair().start()

        def sums_pair():
            return remote(sums.at[1 - y], r_sums.at[0], sums_s.at[0], sums_r.at[0], y_peer)

        def sums_line(way):
            source = (sums_up, sums_down)[way]
            goal = jnp.clip(z + 1 - 2 * way, 0, LINE - 1)
            return remote(source, r_sums.at[1 + way], sums_s.at[1 + way], sums_r.at[1 + way], at(z_to=goal))

        def sums_back():
            return remote(sums.at[y], r_sums.at[3], sums_s.at[3], sums_r.at[3], y_peer)

        def sums_first():
            sums_pair().wait()
            moved([(r_sums.at[0], sums_below)])
            sums[y] = sums[y] + sums_below[...]

            @pl.when(z == 0)
            def _():
                sums_up[...] = sums[y]
                sums_line(0).start()

            @pl.when(z == LINE - 1)
            def _():
                sums_down[...] = sums[y]
                sums_line(1).start()

        def sums_up_step():
            sums_line(0).wait_recv()
            moved([(r_sums.at[1], sums_below)])
            sums_up[...] = sums[y] + sums_below[...]
            sums_line(0).start()

        def sums_down_step():
            sums_line(1).wait_recv()
            moved([(r_sums.at[2], sums_above)])
            sums_down[...] = sums[y] + sums_above[...]
            sums_line(1).start()

        def sums_near():
            pl.when(z == 1)(sums_up_step)
            pl.when(z == LINE - 2)(sums_down_step)

        def sums_far():
            pl.when(z == LINE - 2)(sums_up_step)
            pl.when(z == 1)(sums_down_step)

        def sums_middle():
            @pl.when(z == LINE - 1)
            def _():
                sums_line(0).wait_recv()
                moved([(r_sums.at[1], sums_below)])

            @pl.when(z == 0)
            def _():
                sums_line(1).wait_recv()
                moved([(r_sums.at[2], sums_above)])

            @pl.when(z > 0)
            def _():
                sums[y] = sums[y] + sums_below[...]

            @pl.when(z < LINE - 1)
            def _():
                sums[y] = sums[y] + sums_above[...]

            sums_back().start()

        def sums_end():
            sums_back().wait()
            pl.when(z < LINE - 1)(sums_line(0).wait_send)
            pl.when(z > 0)(sums_line(1).wait_send)
            moved([(r_sums.at[3], sums.at[1 - y])])
            lanes = pl.ds(pl.multiple_of(lax.rem(dp, LINE) * block, block), block)
            moved([(sums.at[lax.div(dp, LINE), pl.ds(vocab, 8), lanes], out_norms)])

        def by_token(kind, rows_of):
            side, start = ((0, 0), (0, inner), (1, 0), (1, inner))[kind]
            return sums[side, rows_of, start : start + inner]

        def head_gradients():
            own_columns = emb[:, pl.ds(pl.multiple_of(dp * block, block), block)]
            for kind, result in enumerate((out_query, out_key, out_value)):
                high, rest = split_low(by_token(kind, slice(0, vocab)))
                gbuf[0:block, :] = dot_tn(own_columns, high) + dot_tn(own_columns, rest)
                moved([(gbuf.at[pl.ds(0, block)], result)])

        table_rows = vocab // (2 * LINE)
        table_own = pl.ds(pl.multiple_of(dp * table_rows, table_rows), table_rows)

        def table_part():
            for kind, weight in enumerate((w_query_hbm, w_key_hbm, w_value_hbm)):
                moved([(weight, w_dense)])
                pieces = jnp.concatenate(split_low(by_token(kind, table_own)), axis=0)

                def columns(start, size):
                    cut = pl.ds(start, size)
                    both = dot_nt(pieces, w_dense[cut, :])
                    both = both[:table_rows] + both[table_rows:]
                    xbuf[0:table_rows, cut] = both if kind == 0 else xbuf[0:table_rows, cut] + both

                tiles(width, columns)
            quarter = pl.ds(pl.multiple_of(mp * inner, inner), inner)
            xbuf[0:table_rows, quarter] = xbuf[0:table_rows, quarter] + alpha * by_token(3, table_own)
            table_copy(0).start()

        def table_middle():
            table_copy(0).wait()
            xbuf[table_rows : 2 * table_rows, :] = xbuf[0:table_rows, :] + table_core[...]
            table_copy(1).start()

        def table_end():
            table_copy(1).wait()
            xbuf[0:table_rows, :] = 0.1 * (xbuf[table_rows : 2 * table_rows, :] + table_x[...])
            moved([(xbuf.at[pl.ds(0, table_rows)], out_table)])

        def table_copy(turn):
            target, device = ((table_core, core_peer), (table_x, x_peer))[turn]
            return remote(xbuf.at[pl.ds(turn * table_rows, table_rows)], target, table_s.at[turn], table_r.at[turn], device)


        for chunk in range(CHUNKS):
            for way in range(2):
                active, copy = act_copy(way, 0, chunk)
                pl.when(active)(copy.wait_send)
        def one_turn(turn, carried):
            @pl.when((turn == 2) & at_end)
            def _():
                for part in range(2):
                    fetch_units(1, part)

            swapped = jnp.where(at_end & ((turn == 2) | (turn == 3)), 5 - turn, turn)
            for part in range(2):
                pl.when(turn == 0)(lambda: fetch_units(0, part))
                pl.when((turn < 4) | (turn == 4) & ~at_end)(lambda: unit_slot(swapped, part, 0))

            @pl.when(turn == 0)
            def _():
                pair_send(1, 0)
                pair_send(1, 1)
                act_take(0, CHUNKS - 1)
                act_send(1, CHUNKS - 1)
                fetch_rows(r_att, att_theirs)
                every_chunk(norm_backward)
                late_send()
                pl.when(~at_end)(lambda: act_pass((1,)))
                for step in range(1, LINE):
                    two_copy(step).wait()
                for step in range(1, LINE):
                    two_spread(1, step).start()
                    two_spread(0, step).start()

            @pl.when(turn == 1)
            def _():
                small_sums()
                pair_send(1, 2)
                pair_send(1, 3)

            @pl.when((turn == 1) & ~at_end | (turn == 3) & at_end)
            def _():
                late_take()
                late_products()

            pl.when((turn == 1) & ~at_end)(lambda: act_pass((2, 3)))
            pl.when(turn == 1)(sums_first)

            pl.when(turn == 2)(sums_near)
            pl.when((turn == 2) & ~at_end | (turn == 4) & at_end)(late_sums)

            @pl.when((turn == 2) & ~at_end)
            def _():
                for part in range(2):
                    fetch_units(1, part)


            pl.when(turn == 4)(sums_far)

            @pl.when(turn >= 4)
            def _():
                for part in range(2):
                    unit_slot(jnp.where(turn == 4, 2, 5), part, 1)

            pl.when((turn == 4) & ~at_end)(sums_middle)

            pl.when(turn == 4)(down_products)
            pl.when((turn == 4) & at_end)(sums_middle)
            pl.when(turn == 4)(lambda: down_copy().start())

            @pl.when((turn == 4) & at_end | (turn == 5))
            def _():
                for part in range(2):
                    unit_slot(turn, part, 0)

            @pl.when((turn == 4) & ~at_end | (turn == 5) & at_end)
            def _():
                sums_end()
                head_gradients()
                table_part()
                last_product()
                unit_end()

            return carried

        lax.fori_loop(0, 2 * (LINE - 1), one_turn, 0)
        late_end()
        table_middle()
        table_end()
        down_end()
        last_landed()
        last_sent()

    pl.run_scoped(
        last_scope,
        pltpu.VMEM((3, local_hidden, length), LOW),
        pltpu.VMEM((2 * LINE - 2, length, block), LOW),
        pltpu.VMEM((2, length, block), LOW),
        pltpu.VMEM((inner, length), LOW),
        pltpu.VMEM((2, local_hidden, block), FULL),
        pltpu.VMEM((2, local_hidden, block), FULL),
        pltpu.VMEM((heads_here, length, HD), LOW),
        pltpu.VMEM((length, 2 * block), FULL),
        pltpu.VMEM((2,) + r_sums.shape[1:], FULL),
        pltpu.VMEM(r_sums.shape[1:], FULL),
        pltpu.VMEM(r_sums.shape[1:], FULL),
        pltpu.VMEM(r_sums.shape[1:], FULL),
        pltpu.VMEM(r_sums.shape[1:], FULL),
        pltpu.VMEM((2 * LINE, length, block), LOW),
    )


def write_kernel(*refs):
    count = 10
    late = 7
    sources, landed = refs[:count], refs[count]
    targets = refs[count + 1 : 2 * count + 4]
    rooms, terms, first_sem, second_sem = refs[2 * count + 4 : 3 * count + 4], *refs[3 * count + 4 : 3 * count + 7]
    z = lax.div(lax.axis_index("dp"), 2)
    order = [late] + [place for place in range(count) if place != late]
    loads = {
        place: pltpu.make_async_copy(sources[place], rooms[place], first_sem.at[place]) for place in range(count)
    }
    more = [
        pltpu.make_async_copy(landed.at[1, LINE - 2, way], terms.at[way], first_sem.at[count + way]) for way in range(2)
    ]
    for copy in more:
        copy.start()
    for place in order:
        loads[place].start()
    stores = []
    for copy in more:
        copy.wait()
    for place in order:
        loads[place].wait()
        room = rooms[place]
        if place == late:
            for way, active in ((0, z > 0), (1, z < LINE - 1)):

                @pl.when(active)
                def _():
                    room[...] = room[...] + terms[way]

        if place < count - 1:
            stores.append(pltpu.make_async_copy(room, targets[place], second_sem.at[place]))
            stores[-1].start()
        else:
            for vector in range(4):
                targets[place + vector][...] = room[vector : vector + 1, :]
    for copy in stores:
        copy.wait()


def write_out(results, landed):
    hbm = pl.BlockSpec(memory_space=pl.ANY)
    rows = jax.ShapeDtypeStruct((1, results[-1].shape[1]), FULL)
    shapes = [jax.ShapeDtypeStruct(value.shape, value.dtype) for value in results[:-1]] + [rows] * 4
    return pl.pallas_call(
        write_kernel,
        out_shape=shapes,
        in_specs=[hbm] * (len(results) + 1),
        out_specs=[hbm] * (len(results) - 1) + [pl.BlockSpec(memory_space=pltpu.VMEM)] * 4,
        scratch_shapes=[pltpu.VMEM(value.shape, value.dtype) for value in results]
        + [pltpu.VMEM((2,) + results[7].shape, FULL)]
        + [pltpu.SemaphoreType.DMA((len(results) + 2,))] * 2,
        compiler_params=pltpu.CompilerParams(vmem_limit_bytes=62 * 2**20),
    )(*results, landed)


def local_fast(
    token_ids,
    prefix_lengths,
    cluster_ids,
    embedding,
    w_query,
    w_key,
    w_value,
    w_dense,
    w_gate,
    w_up,
    w_down,
    norm1_gain,
    norm1_bias,
    norm2_gain,
    norm2_bias,
    cotangent,
):
    length = token_ids.shape[0]
    vocab, width = embedding.shape
    inner = w_query.shape[1]
    heads_here = inner // HD
    local_hidden = w_gate.shape[1]
    rows = length // CHUNKS
    block = width // (2 * LINE)
    shift = (local_hidden + 15) // 16 * 16
    frequency = 10000.0 ** (np.arange(HD // 2) * (-2.0 / HD))
    angles = np.arange(length)[:, None] * frequency[None, :]
    cosine = np.concatenate([np.cos(angles)] * 2, axis=1).astype(np.float32)
    sine = np.concatenate([-np.sin(angles), np.sin(angles)], axis=1).astype(np.float32)
    norms = [vector.reshape(1, width) for vector in (norm1_gain, norm1_bias, norm2_gain, norm2_bias)]

    hbm = pl.BlockSpec(memory_space=pl.ANY)
    vmem = pl.BlockSpec(memory_space=pltpu.VMEM)
    smem = pl.BlockSpec(memory_space=pltpu.SMEM)
    sums_rows = vocab + 8
    table_rows = vocab // (2 * LINE)
    shapes = [
        ((length, width), LOW),
        ((table_rows, width), FULL),
        ((block, inner), FULL),
        ((block, inner), FULL),
        ((block, inner), FULL),
        ((block, inner), FULL),
        ((local_hidden, block), FULL),
        ((local_hidden, block), FULL),
        ((local_hidden, block), FULL),
        ((8, block), FULL),
        ((LINE, local_hidden, length), FULL),
        ((LINE, 2 * CHUNKS, rows, block), FULL),
        ((2, local_hidden, length), FULL),
        ((LINE, CHUNKS, rows, block), FULL),
        ((inner, length), FULL),
        ((CHUNKS, rows, width), FULL),
        ((CHUNKS, length, inner), FULL),
        ((local_hidden, block), FULL),
        ((2, LINE - 1, 2, local_hidden, block), FULL),
        ((4, 2 * LINE, rows, block), FULL),
        ((LINE - 1, CHUNKS, rows, block), FULL),
        ((CHUNKS, rows, block), FULL),
        ((4, sums_rows, width // 2), FULL),
    ]
    scratch = [
        ((vocab, width), LOW),
        ((length, HD), FULL),
        ((length, HD), FULL),
        ((CHUNKS, 2, rows, width // 2), FULL),
        ((CHUNKS, rows, width // 2), FULL),
        ((2, CHUNKS, rows, width // 2), FULL),
        ((CHUNKS, rows, width // 2), FULL),
        ((2 * LINE, rows, block), FULL),
        ((rows, width), FULL),
        ((length, inner), FULL),
        ((rows, width), LOW),
        ((2, local_hidden, length), FULL),
        ((2 * shift, length), LOW),
        ((local_hidden, length), LOW),
        ((2, local_hidden, block), FULL),
        ((LINE, length, block), LOW),
        ((2 * CHUNKS, rows, block), FULL),
        ((LINE, length, block), LOW),
        ((2, length, block), LOW),
        ((2 * LINE, rows, block), FULL),
        ((length, inner), LOW),
        ((inner, length), LOW),
        ((3, heads_here, length, HD), LOW),
        ((width, inner), LOW),
        ((length, 2 * vocab), LOW),
        ((vocab, length), LOW),
        ((CHUNKS, rows, 1), FULL),
        ((8, width), FULL),
        ((table_rows, width), FULL),
        ((table_rows, width), FULL),
    ]
    dma = pltpu.SemaphoreType.DMA
    each = (3, CHUNKS)
    semaphores = [
        each, each, each, each, each, each, (2, LINE - 1, CHUNKS), (2, LINE - 1, CHUNKS), (3,), (3,), (3, 3), (3, 3),
        (CHUNKS,), (CHUNKS,), None, None, (2, CHUNKS, 2), (2, CHUNKS, 2), None, None, None, None, (4, 2), (4, 2),
        (3,), (3,), (3,), None, (2, LINE - 1, 2, 2), (2, LINE - 1, 2, 2), (4,), (4,), (2,), (2,), (4,), (7,),
    ]
    results = pl.pallas_call(
        functools.partial(layer_kernel, length, width, local_hidden),
        out_shape=[jax.ShapeDtypeStruct(shape, dtype) for shape, dtype in shapes],
        in_specs=[smem] * 2 + [vmem] * 5 + [hbm] * 11,
        out_specs=[hbm] * len(shapes),
        scratch_shapes=[pltpu.VMEM(shape, dtype) for shape, dtype in scratch]
        + [dma if shape is None else dma(shape) for shape in semaphores],
        compiler_params=pltpu.CompilerParams(
            collective_id=0, has_side_effects=True, vmem_limit_bytes=62 * 2**20
        ),
    )(
        prefix_lengths,
        cluster_ids,
        token_ids.reshape(1, length),
        *norms,
        embedding,
        cosine,
        sine,
        w_query,
        w_key,
        w_value,
        w_dense,
        w_gate.T,
        w_up.T,
        w_down.T,
        cotangent,
    )
    written = write_out(results[:10], results[18])
    block_out, table, out_query, out_key, out_value, out_dense, out_gate, out_up, out_down = written[:9]
    out_norms = written[9:]
    return (
        block_out,
        table,
        out_query,
        out_key,
        out_value,
        out_dense,
        out_gate.T,
        out_up.T,
        out_down.T,
        out_norms[0].reshape(width // (2 * LINE)),
        out_norms[1].reshape(width // (2 * LINE)),
        out_norms[2].reshape(width // (2 * LINE)),
        out_norms[3].reshape(width // (2 * LINE)),
    )


def solution(mesh):
    fast = mesh.shape["dp"] == 2 * LINE and mesh.shape["mp"] == 4
    return jax.shard_map(
        local_fast if fast else local_general,
        mesh=mesh,
        in_specs=(
            P("dp"),
            P("dp"),
            P(),
            P(),
            P(None, "mp"),
            P(None, "mp"),
            P(None, "mp"),
            P(None, "mp"),
            P(None, "mp"),
            P(None, "mp"),
            P(None, "mp"),
            P(),
            P(),
            P(),
            P(),
            P("dp", None),
        ),
        out_specs=(
            P("dp", None),
            P("dp", None),
            P("dp", "mp"),
            P("dp", "mp"),
            P("dp", "mp"),
            P("dp", "mp"),
            P("dp", "mp"),
            P("dp", "mp"),
            P("dp", "mp"),
            P("dp"),
            P("dp"),
            P("dp"),
            P("dp"),
        ),
        check_vma=False,
    )
```

```python
import functools
import math

import jax
import jax.numpy as jnp
import numpy as np
from jax import lax
from jax.experimental import pallas as pl
from jax.experimental.pallas import tpu as pltpu
from jax.sharding import PartitionSpec as P

HD = 128
FF_USED = 5461


deep_alpha = math.sqrt(48.0)
norm_eps = 1e-05
highest = lax.Precision.HIGHEST


def layer_norm(inputs, norm_gain, norm_bias):
    center = jnp.mean(inputs, axis=-1, keepdims=True)
    centered = inputs - center
    spread = jnp.mean(centered * centered, axis=-1, keepdims=True)
    return centered * lax.rsqrt(spread + norm_eps) * norm_gain + norm_bias


def rotary_tables(length, head_width):
    half_width = head_width // 2
    frequency = jnp.exp(
        jnp.arange(half_width, dtype=jnp.float32) * (-2.0 * math.log(10000.0) / head_width)
    )
    angles = jnp.arange(length, dtype=jnp.float32)[:, None] * frequency[None, :]
    return (jnp.cos(angles), jnp.sin(angles))


def rotate(inputs, cosine, sine):
    half_width = inputs.shape[-1] // 2
    first = inputs[..., :half_width]
    second = inputs[..., half_width:]
    cosine = cosine[:, None, :]
    sine = sine[:, None, :]
    return jnp.concatenate(
        [first * cosine - second * sine, second * cosine + first * sine], axis=-1
    )


def row_mask(row_begin, row_count, length, prefix):
    columns = jnp.arange(length, dtype=jnp.int32)
    row_index = row_begin + jnp.arange(row_count, dtype=jnp.int32)
    return (columns[None, :] < prefix) | (columns[None, :] <= row_index[:, None])


def block_scores(query_block, keys_rot, visible, score_scale):
    scores = (
        jnp.einsum("bhd,khd->hbk", query_block, keys_rot, preferred_element_type=jnp.float32)
        * score_scale
    )
    return jnp.where(visible[None, :, :], scores, -1e30)


def attention_forward(queries, keys_rot, values_in, prefix, row_block):
    length = queries.shape[0]
    score_scale = 1.0 / math.sqrt(HD)

    def one_block(row_begin):
        scores = block_scores(
            queries, keys_rot, row_mask(row_begin, row_block, length, prefix), score_scale
        )
        row_max = jnp.max(scores, axis=-1, keepdims=True)
        weights = jnp.exp(scores - row_max)
        total_weight = jnp.sum(weights, axis=-1, keepdims=True)
        probability = (weights / total_weight).astype(jnp.bfloat16)
        mixed_block = jnp.einsum(
            "hbk,khd->bhd", probability, values_in, preferred_element_type=jnp.float32
        )
        return (mixed_block, row_max + jnp.log(total_weight))

    starts = jnp.arange(length // row_block, dtype=jnp.int32) * row_block
    attended, log_total = lax.map(one_block, starts)
    return (attended.reshape(length, -1), log_total)


def attention_backward(queries, keys_rot, values_in, prefix, row_block, log_total, grad_mixed):
    length = queries.shape[0]
    score_scale = 1.0 / math.sqrt(HD)

    def one_block(carried, inputs):
        grad_keys, grad_values = carried
        row_begin, block_total = inputs
        scores = block_scores(
            queries, keys_rot, row_mask(row_begin, row_block, length, prefix), score_scale
        )
        probability = jnp.exp(scores - block_total)
        prob_low = probability.astype(jnp.bfloat16)
        grad_prob = jnp.einsum(
            "bhd,khd->hbk", grad_mixed, values_in, preferred_element_type=jnp.float32
        )
        centre = jnp.sum(grad_prob * probability, axis=-1, keepdims=True)
        grad_scores = (probability * (grad_prob - centre)).astype(jnp.bfloat16)
        grad_query = (
            jnp.einsum("hbk,khd->bhd", grad_scores, keys_rot, preferred_element_type=jnp.float32)
            * score_scale
        )
        grad_keys = (
            grad_keys
            + jnp.einsum("hbk,bhd->khd", grad_scores, queries, preferred_element_type=jnp.float32)
            * score_scale
        )
        grad_values = grad_values + jnp.einsum(
            "hbk,bhd->khd", prob_low, grad_mixed, preferred_element_type=jnp.float32
        )
        return ((grad_keys, grad_values), grad_query)

    starts = jnp.arange(length // row_block, dtype=jnp.int32) * row_block
    zeros_kv = jnp.zeros(keys_rot.shape, jnp.float32)
    (grad_keys, grad_values), grad_queries = lax.scan(
        one_block, (zeros_kv, zeros_kv), (starts, log_total)
    )
    return (grad_queries.reshape(queries.shape), grad_keys, grad_values)


def local_general(
    token_ids,
    prefix_lengths,
    cluster_ids,
    embedding,
    w_query,
    w_key,
    w_value,
    w_dense,
    w_gate,
    w_up,
    w_down,
    norm1_gain,
    norm1_bias,
    norm2_gain,
    norm2_bias,
    cotangent,
):
    length = token_ids.shape[0]
    vocab_rows = embedding.shape[0]
    row_block = min(512, length)
    local_heads = w_query.shape[1] // HD
    local_hidden = w_gate.shape[1]
    one_hot = (token_ids[:, None] == jnp.arange(vocab_rows, dtype=jnp.int32)[None, :]).astype(
        jnp.bfloat16
    )
    embedded_low = jnp.dot(one_hot, embedding, preferred_element_type=jnp.float32).astype(
        jnp.bfloat16
    )
    embedded = embedded_low.astype(jnp.float32)
    cosine, sine = rotary_tables(length, HD)
    prefix = prefix_lengths[0]
    own_cluster = cluster_ids[lax.axis_index("dp")]
    seq_weight = 1.0 / jnp.sum((cluster_ids == own_cluster).astype(jnp.float32))

    def project(weight_in):
        return jnp.dot(embedded_low, weight_in, preferred_element_type=jnp.float32).reshape(
            length, local_heads, HD
        )

    queries = rotate(project(w_query), cosine, sine).astype(jnp.bfloat16)
    keys_rot = rotate(project(w_key), cosine, sine).astype(jnp.bfloat16)
    values_in = project(w_value).astype(jnp.bfloat16)
    attended, log_total = attention_forward(queries, keys_rot, values_in, prefix, row_block)
    attended_low = attended.astype(jnp.bfloat16)
    branch = lax.psum(
        jnp.einsum("lh,dh->ld", attended_low, w_dense, preferred_element_type=jnp.float32), "mp"
    )
    residual_one = deep_alpha * embedded + branch
    hidden, norm_one_pull = jax.vjp(layer_norm, residual_one, norm1_gain, norm1_bias)
    hidden_low = hidden.astype(jnp.bfloat16)
    gate_proj = jnp.dot(hidden_low, w_gate, preferred_element_type=jnp.float32)
    up_proj = jnp.dot(hidden_low, w_up, preferred_element_type=jnp.float32)
    unit_index = lax.axis_index("mp") * local_hidden + jnp.arange(local_hidden, dtype=jnp.int32)
    used_mask = (unit_index < FF_USED).astype(jnp.float32)

    def gated_unit(gate_in, up_in):
        return jax.nn.gelu(gate_in, approximate=True) * up_in * used_mask

    activation, gated_pull = jax.vjp(gated_unit, gate_proj, up_proj)
    activation_low = activation.astype(jnp.bfloat16)
    branch_two = lax.psum(
        jnp.einsum("lf,df->ld", activation_low, w_down, preferred_element_type=jnp.float32), "mp"
    )
    residual_two = deep_alpha * hidden + branch_two
    final, norm_two_pull = jax.vjp(layer_norm, residual_two, norm2_gain, norm2_bias)
    grad_out = cotangent.astype(jnp.float32) * seq_weight
    grad_two, grad_gain_two, grad_bias_two = norm_two_pull(grad_out)
    grad_branch_two = grad_two.astype(jnp.bfloat16)
    grad_w_down = jnp.einsum(
        "ld,lf->df", grad_branch_two, activation_low, preferred_element_type=jnp.float32
    )
    grad_act = jnp.dot(grad_branch_two, w_down, preferred_element_type=jnp.float32)
    grad_gate, grad_up = gated_pull(grad_act)
    grad_gate_low = grad_gate.astype(jnp.bfloat16)
    grad_up_low = grad_up.astype(jnp.bfloat16)
    grad_w_gate = jnp.einsum(
        "ld,lf->df", hidden_low, grad_gate_low, preferred_element_type=jnp.float32
    )
    grad_w_up = jnp.einsum("ld,lf->df", hidden_low, grad_up_low, preferred_element_type=jnp.float32)
    hidden_part = jnp.einsum(
        "lf,df->ld", grad_gate_low, w_gate, preferred_element_type=jnp.float32
    ) + jnp.einsum("lf,df->ld", grad_up_low, w_up, preferred_element_type=jnp.float32)
    grad_hidden = deep_alpha * grad_two + lax.psum(hidden_part, "mp")
    feed_sums = (
        lax.psum_scatter(grad_w_gate, "dp", scatter_dimension=0, tiled=True),
        lax.psum_scatter(grad_w_up, "dp", scatter_dimension=0, tiled=True),
        lax.psum_scatter(grad_w_down, "dp", scatter_dimension=0, tiled=True),
        lax.psum_scatter(grad_gain_two, "dp", scatter_dimension=0, tiled=True),
        lax.psum_scatter(grad_bias_two, "dp", scatter_dimension=0, tiled=True),
    )
    grad_one, grad_gain_one, grad_bias_one = norm_one_pull(grad_hidden)
    grad_branch = grad_one.astype(jnp.bfloat16)
    grad_w_dense = jnp.einsum(
        "ld,lh->dh", grad_branch, attended_low, preferred_element_type=jnp.float32
    )
    grad_attended = jnp.dot(grad_branch, w_dense, preferred_element_type=jnp.float32).astype(
        jnp.bfloat16
    )
    grad_attended = grad_attended.reshape(length, local_heads, HD)
    grad_queries, grad_keys, grad_values = attention_backward(
        queries, keys_rot, values_in, prefix, row_block, log_total, grad_attended
    )
    grad_query_lin = rotate(grad_queries, cosine, -sine).astype(jnp.bfloat16).reshape(length, -1)
    grad_key_lin = rotate(grad_keys, cosine, -sine).astype(jnp.bfloat16).reshape(length, -1)
    grad_value_lin = grad_values.astype(jnp.bfloat16).reshape(length, -1)
    grad_w_query = jnp.einsum(
        "ld,lh->dh", embedded_low, grad_query_lin, preferred_element_type=jnp.float32
    )
    grad_w_key = jnp.einsum(
        "ld,lh->dh", embedded_low, grad_key_lin, preferred_element_type=jnp.float32
    )
    grad_w_value = jnp.einsum(
        "ld,lh->dh", embedded_low, grad_value_lin, preferred_element_type=jnp.float32
    )
    input_part = (
        jnp.einsum("lh,dh->ld", grad_query_lin, w_query, preferred_element_type=jnp.float32)
        + jnp.einsum("lh,dh->ld", grad_key_lin, w_key, preferred_element_type=jnp.float32)
        + jnp.einsum("lh,dh->ld", grad_value_lin, w_value, preferred_element_type=jnp.float32)
    )
    grad_embedded = deep_alpha * grad_one + lax.psum(input_part, "mp")
    grad_table = 0.1 * jnp.dot(one_hot.astype(jnp.float32).T, grad_embedded, precision=highest)
    attn_sums = (
        lax.psum_scatter(grad_table, "dp", scatter_dimension=0, tiled=True),
        lax.psum_scatter(grad_w_query, "dp", scatter_dimension=0, tiled=True),
        lax.psum_scatter(grad_w_key, "dp", scatter_dimension=0, tiled=True),
        lax.psum_scatter(grad_w_value, "dp", scatter_dimension=0, tiled=True),
        lax.psum_scatter(grad_w_dense, "dp", scatter_dimension=0, tiled=True),
        lax.psum_scatter(grad_gain_one, "dp", scatter_dimension=0, tiled=True),
        lax.psum_scatter(grad_bias_one, "dp", scatter_dimension=0, tiled=True),
    )
    summed = (
        attn_sums[0],
        attn_sums[1],
        attn_sums[2],
        attn_sums[3],
        attn_sums[4],
        feed_sums[0],
        feed_sums[1],
        feed_sums[2],
        attn_sums[5],
        attn_sums[6],
        feed_sums[3],
        feed_sums[4],
    )
    return (
        final.astype(jnp.bfloat16),
        summed[0],
        summed[1],
        summed[2],
        summed[3],
        summed[4],
        summed[5],
        summed[6],
        summed[7],
        summed[8],
        summed[9],
        summed[10],
        summed[11],
    )


LINE = 4
MESH = pl.DeviceIdType.MESH
CHUNKS = 4
AHEAD = 2
LOW = jnp.bfloat16
FULL = jnp.float32
TANH_SCALE = math.sqrt(2.0 / math.pi)


def dot(left, right):
    return jnp.dot(left, right, preferred_element_type=FULL)


def dot_nt(left, right):
    return lax.dot_general(left, right, (((1,), (1,)), ((), ())), preferred_element_type=FULL)


def dot_tn(left, right):
    return lax.dot_general(left, right, (((0,), (0,)), ((), ())), preferred_element_type=FULL)


def split_low(value):
    high = value.astype(LOW)
    return high, (value - high.astype(FULL)).astype(LOW)


def row_mean(value):
    return jnp.mean(value, axis=-1, keepdims=True)


def spread(size, body, tile=512):
    for start in range(0, size, tile):
        body(start, min(tile, size - start))


def tiles(size, body, tile=512):
    whole = size // tile
    lax.fori_loop(0, whole, lambda step, carried: (body(pl.multiple_of(step * tile, tile), tile), carried)[1], 0)
    if size % tile:
        body(whole * tile, size % tile)


def layer_kernel(
    length, width, local_hidden,
    prefix_ref, cluster_ref, ids_row, gain_one, bias_one, gain_two, bias_two, emb_hbm, cos_hbm, sin_hbm, w_query_hbm, w_key_hbm, w_value_hbm, w_dense_hbm,
    w_gate_hbm, w_up_hbm, w_down_hbm, cot_hbm,
    block_out, out_table, out_query, out_key, out_value, out_dense, out_gate, out_up, out_down, out_norms,
    r_act, r_two, r_y, r_cols, r_att, xhat_park, grad_two_park, r_dny, r_rs, r_late, r_dz, r_dx, r_sums,
    emb, cos_ref, sin_ref, parts, core_in, x_in, back_in, blocks, xbuf, gbuf, obuf, gate_up, grads_low, act_low, send_a, cols_own, cols_send,
    hidden_theirs, gate_theirs, two_own, two_send, att_low, att_turned, heads, w_dense, one_hot, hot_turned, rstd_one, vectors, table_core, table_x, room,
    core_s, core_r, x_s, x_r, back_s, back_r, act_s, act_r, two_s, two_r, fwd_two_s, fwd_two_r, cols_s, cols_r, fwd_s,
    fwd_r, ys_s, ys_r, att_s, att_r, dny_s, dny_r, late_s, late_r, dz_s, dz_r, dx_s, dx_r, rs_s, rs_r, sums_s, sums_r, table_s, table_r, load_sem, weight_sem,
):
    dp, mp = lax.axis_index("dp"), lax.axis_index("mp")
    z, y = lax.div(dp, 2), lax.rem(dp, 2)
    x, core = lax.div(mp, 2), lax.rem(mp, 2)
    rows = length // CHUNKS
    heads_here = heads.shape[1]
    inner = heads_here * HD
    vocab = emb.shape[0]
    shift = (local_hidden + 15) // 16 * 16
    quarter = (local_hidden // 4 + 15) // 16 * 16
    spans = [(start, min(quarter, local_hidden - start)) for start in range(0, local_hidden, quarter)]
    whole = range(len(spans))
    halves = ((0, 2 * quarter), (2 * quarter, local_hidden - 2 * quarter))
    block = width // (2 * LINE)
    alpha = jnp.float32(deep_alpha)

    def at(z_to=None, y_to=None, x_to=None, core_to=None):
        z_to = z if z_to is None else z_to
        y_to = y if y_to is None else y_to
        x_to = x if x_to is None else x_to
        core_to = core if core_to is None else core_to
        return (2 * z_to + y_to, 2 * x_to + core_to)

    core_peer = at(core_to=1 - core)
    x_peer = at(x_to=1 - x)
    y_peer = at(y_to=1 - y)
    z_peer = at(z_to=z + 1 - 2 * lax.rem(z, 2))
    at_end = (z == 0) | (z == LINE - 1)

    def remote(source, target, send, receive, device):
        return pltpu.make_async_remote_copy(
            src_ref=source, dst_ref=target, send_sem=send, recv_sem=receive,
            device_id=device, device_id_type=MESH,
        )

    def load_all(pairs):
        copies = [
            pltpu.make_async_copy(source, target, load_sem.at[place])
            for place, (source, target) in enumerate(pairs)
        ]
        for copy in copies:
            copy.start()
        return copies

    def moved(pairs):
        for copy in load_all(pairs):
            copy.wait()

    barrier = pltpu.get_barrier_semaphore()
    greeted = [core_peer, x_peer, y_peer] + [at(z_to=lax.rem(z + step, LINE)) for step in range(1, LINE)]
    for device in greeted:
        pl.semaphore_signal(barrier, inc=1, device_id=device, device_id_type=MESH)

    def chunk_rows(chunk):
        return pl.ds(pl.multiple_of(chunk * rows, rows), rows)

    def core_copy(turn, chunk):
        return remote(
            parts.at[chunk, 1 - core], core_in.at[chunk], core_s.at[turn, chunk], core_r.at[turn, chunk], core_peer
        )

    def x_copy(turn, chunk):
        return remote(
            parts.at[chunk, core], x_in.at[turn % 2, chunk], x_s.at[turn, chunk], x_r.at[turn, chunk], x_peer
        )

    def back_copy(turn, chunk):
        return remote(
            parts.at[chunk, core], back_in.at[chunk], back_s.at[turn, chunk], back_r.at[turn, chunk], core_peer
        )

    def put_part(chunk, start, size, value):
        side, first = lax.div(start, width // 2), lax.rem(start, width // 2)
        parts[chunk, side, :, pl.ds(pl.multiple_of(first, size), size)] = value

    def send_part(turn, chunk):
        core_copy(turn, chunk).wait()
        parts[chunk, core] = parts[chunk, core] + core_in[chunk]
        x_copy(turn, chunk).start()

    def take_part(turn, chunk):
        x_copy(turn, chunk).wait()
        parts[chunk, core] = parts[chunk, core] + x_in[turn % 2, chunk]
        back = back_copy(turn, chunk)
        back.start()
        mine = parts[chunk, core]
        back.wait()
        other = back_in[chunk]
        return jnp.concatenate([jnp.where(core == 0, mine, other), jnp.where(core == 0, other, mine)], axis=1)

    def put_blocks(value):
        for place in range(2 * LINE):
            blocks[place] = value[:, place * block : (place + 1) * block]

    def chunk_lanes(chunk):
        return pl.ds(pl.multiple_of(chunk * rows, rows), rows)

    def half_lanes(side):
        return pl.ds(pl.multiple_of(side * block, block), block)

    def keep_columns(chunk):
        for place in range(LINE):
            cols_own[place, chunk_rows(chunk), :] = blocks[2 * place + y].astype(LOW)
        for place in range(2):
            cols_send[2 * chunk + place] = blocks[2 * (2 * core + place) + 1 - y]

    def cols_copy(chunk):
        return remote(
            cols_send.at[pl.ds(2 * chunk, 2)], r_cols.at[pl.ds(2 * core, 2), chunk],
            cols_s.at[chunk], cols_r.at[chunk], y_peer,
        )

    def forward_copy():
        view = r_cols.at[pl.ds(2 * core, 2)]
        return remote(view, view, fwd_s, fwd_r, core_peer)

    def act_copy(way, hop, chunk):
        goal = jnp.clip(z + 1 - 2 * way, 0, LINE - 1)
        owner = z - hop if way == 0 else z + hop
        active = (owner >= 0) & (z < LINE - 1) if way == 0 else (owner < LINE) & (z > 0)
        owner = jnp.clip(owner, 0, LINE - 1)
        landed = r_act.at[owner, :, chunk_lanes(chunk)]
        source = send_a.at[lax.div(chunk, 2), :, half_chunk(chunk)] if hop == 0 else landed
        return active, remote(
            source, landed, act_s.at[way, hop, chunk], act_r.at[way, hop, chunk], at(z_to=goal)
        )

    def act_landed(way, hop):
        return z - 1 - hop >= 0 if way == 0 else z + 1 + hop < LINE

    def half_chunk(chunk):
        return pl.ds(pl.multiple_of(lax.rem(chunk, 2) * rows, rows), rows)

    def act_send(hop, chunk):
        for way in range(2):
            active, copy = act_copy(way, hop, chunk)
            pl.when(active)(copy.start)

    def act_take(hop, chunk):
        for way in range(2):
            _, copy = act_copy(way, hop, chunk)
            pl.when(act_landed(way, hop))(copy.wait_recv)

    def chunk_of(place):
        return jnp.where(place == 0, 0, jnp.where(place == 1, CHUNKS - 1, place - 1))

    mine = chunk_of(mp)
    other_x = chunk_of(2 * (1 - x) + core)

    def act_pass(chunks):
        for chunk in chunks:
            act_take(1, chunk)
            act_send(2, chunk)

    def two_copy(step):
        goal = lax.rem(z + step, LINE)
        return remote(
            two_send.at[pl.ds(2 * goal, 2)], r_two.at[z, pl.ds(2 * mine, 2)],
            two_s.at[step - 1], two_r.at[step - 1], at(z_to=goal),
        )

    def two_spread(turn, step):
        quarter = other_x if turn == 2 else mine
        view = r_two.at[lax.rem(z + step, LINE), pl.ds(2 * quarter, 2)]
        device = x_peer if turn == 1 else core_peer
        return remote(view, view, fwd_two_s.at[turn, step - 1], fwd_two_r.at[turn, step - 1], device)

    def pair_copy(which, chunk, part):
        units = pl.ds(*spans[part])
        return remote(
            gate_up.at[which, units, chunk_lanes(chunk)], r_y.at[which, units, chunk_lanes(chunk)],
            ys_s.at[which, chunk, part], ys_r.at[which, chunk, part], y_peer,
        )

    def pair_send(which, chunk):
        for part in whole:
            pair_copy(which, chunk, part).start()

    def rows_copy():
        return remote(gbuf, r_att, att_s, att_r, z_peer)

    def fetch_columns(target):
        forward = forward_copy()
        forward.start()
        forward.wait()
        for pair in range(2):
            moved(
                [(r_cols.at[2 * pair + place], blocks.at[pl.ds(CHUNKS * place, CHUNKS)]) for place in range(2)]
            )
            for place in range(2):
                for chunk in range(CHUNKS):
                    piece = blocks[CHUNKS * place + chunk].astype(LOW)
                    target[2 * pair + place, chunk * rows : (chunk + 1) * rows, :] = piece

    def toward(side):
        return jnp.where(z < LINE // 2, side, 1 - side)

    def goes(slot, way):
        return jnp.where(way == 0, z < slot, z > LINE - 1 - slot)

    def inner_place(way):
        return jnp.where(way == 0, z > 0, z < LINE - 1)

    def line_goal(way):
        return at(z_to=jnp.clip(z + 1 - 2 * way, 0, LINE - 1))

    def first_copy(part):
        way = toward(0)
        units = pl.ds(*spans[part])
        return remote(
            send_a.at[0, units], r_rs.at[0, 0, way, units], rs_s.at[0, 0, way, part], rs_r.at[0, 0, way, part],
            line_goal(way),
        )

    def act_sent(chunks):
        for chunk in chunks:
            for way in range(2):
                active, copy = act_copy(way, 0, chunk)
                pl.when(active)(copy.wait_send)

    def every_chunk(body):
        lax.fori_loop(0, CHUNKS, lambda chunk, carried: (body(chunk), carried)[1], 0)

    score_scale = 1.0 / math.sqrt(HD)

    def probabilities(queries, keys, begin):
        shape = (queries.shape[0], length)
        column = lax.broadcasted_iota(jnp.int32, shape, 1)
        row = lax.broadcasted_iota(jnp.int32, shape, 0) + begin
        visible = (column < prefix_ref[0]) | (column <= row)
        scores = jnp.where(visible, dot_nt(queries, keys) * score_scale, -1e30)
        weights = jnp.exp(scores - jnp.max(scores, axis=-1, keepdims=True))
        return weights / jnp.sum(weights, axis=-1, keepdims=True)

    def turn_by(value, sine):
        return value * cos_ref[...] + pltpu.roll(value, HD // 2, 1) * sine

    def head_lanes(place, offset=0):
        return pl.ds(pl.multiple_of(offset + place * HD, HD), HD)

    def first_scope(w_heads, tab):
        loads = [
            pltpu.make_async_copy(source, target, weight_sem.at[place])
            for place, (source, target) in enumerate(
                (
                    (emb_hbm, emb),
                    (w_query_hbm, w_heads.at[0]),
                    (w_key_hbm, w_heads.at[1]),
                    (w_value_hbm, w_heads.at[2]),
                    (cos_hbm, cos_ref),
                    (sin_hbm, sin_ref),
                    (w_dense_hbm, w_dense),
                )
            )
        ]
        for copy in loads:
            copy.start()
        named = lax.broadcasted_iota(jnp.int32, (vocab, length), 0) == ids_row[...]
        hot = jnp.where(named, 1.0, 0.0)
        hot_turned[...] = hot.astype(LOW)
        turned_hot = hot.T.astype(LOW)
        one_hot[:, 0:vocab] = turned_hot
        one_hot[:, vocab:] = turned_hot
        vectors[...] = jnp.zeros_like(vectors)
        loads[0].wait()
        for kind in range(3):
            loads[kind + 1].wait()
            pieces = split_low(dot(emb[...], w_heads[kind]))
            for place in range(heads_here):
                for half, piece in enumerate(pieces):
                    tab[place, half * vocab : (half + 1) * vocab, kind * HD : (kind + 1) * HD] = piece[
                        :, place * HD : (place + 1) * HD
                    ]
        loads[4].wait()
        loads[5].wait()

        def head_inputs(place, carried):
            lin = dot(one_hot[...], tab[place])
            heads[0, place] = turn_by(lin[:, 0:HD], sin_ref[...]).astype(LOW)
            heads[1, place] = turn_by(lin[:, HD : 2 * HD], sin_ref[...]).astype(LOW)
            heads[2, place] = lin[:, 2 * HD :].astype(LOW)
            return carried

        lax.fori_loop(0, heads_here, head_inputs, 0)

        def attend(chunk):
            for place in range(heads_here):
                queries = heads[0, place, chunk_rows(chunk), :]
                probability = probabilities(queries, heads[1, place], chunk * rows).astype(LOW)
                mixed = dot(probability, heads[2, place]).astype(LOW)
                att_low[chunk_rows(chunk), place * HD : (place + 1) * HD] = mixed
                turned = mixed.astype(FULL).T
                att_turned[place * HD : (place + 1) * HD, chunk_lanes(chunk)] = turned.astype(LOW)
                gbuf[place * HD : (place + 1) * HD, chunk_lanes(chunk)] = turned

        def project(chunk):
            attend(chunk)
            pl.when(chunk == 0)(lambda: loads[6].wait())
            pl.when(chunk == 0)(lambda: pl.semaphore_wait(barrier, len(greeted)))
            mixed = att_low[chunk_rows(chunk), :]

            def columns(start, size):
                put_part(chunk, start, size, dot_nt(mixed, w_dense[pl.ds(start, size), :]))

            spread(width, columns, 256)
            core_copy(0, chunk).start()
            pl.when(chunk == 0)(lambda: send_part(0, 0))
            pl.when((chunk > 1) & (chunk <= AHEAD))(lambda: send_part(0, chunk - 1))

        every_chunk(project)
        rows_copy().start()

    pl.run_scoped(first_scope, pltpu.VMEM((3, width, inner), LOW), pltpu.VMEM((heads_here, 2 * vocab, 3 * HD), LOW))

    def middle_scope(w_gate, w_up, w_down, cotbuf):
        weight_copies = [
            pltpu.make_async_copy(source, target, weight_sem.at[place])
            for place, (source, target) in enumerate(((w_gate_hbm, w_gate), (w_up_hbm, w_up), (w_down_hbm, w_down)))
        ]
        for copy in weight_copies:
            copy.start()
        for copy in weight_copies:
            copy.wait()

        def feed_forward(chunk):
            branch = take_part(0, chunk)
            residual = alpha * dot(one_hot[chunk_rows(chunk), 0:vocab], emb[...]) + branch
            centered = residual - row_mean(residual)
            rstd = lax.rsqrt(row_mean(centered * centered) + norm_eps)
            xhat = centered * rstd
            rstd_one[chunk] = rstd
            xbuf[...] = xhat
            park = pltpu.make_async_copy(xbuf, xhat_park.at[chunk], load_sem.at[0])
            park.start()
            hidden_low = (xhat * gain_one[...] + bias_one[...]).astype(LOW)
            put_blocks(hidden_low.astype(FULL))
            keep_columns(chunk)
            cols_copy(chunk).start()

            def units_tile(start, size):
                cut = pl.ds(start, size)
                gate = dot_nt(w_gate[cut, :], hidden_low)
                up = dot_nt(w_up[cut, :], hidden_low)
                units = mp * local_hidden + start + lax.broadcasted_iota(jnp.int32, (size, rows), 0)
                used = jnp.where(units < FF_USED, 1.0, 0.0)
                square = gate * gate
                bend = jnp.tanh(TANH_SCALE * gate * (1.0 + 0.044715 * square))
                gelu = 0.5 * gate * (1.0 + bend) * used
                slope = 0.5 * (1.0 + bend) + 0.5 * gate * (1.0 - bend * bend) * (
                    TANH_SCALE * (1.0 + 3.0 * 0.044715 * square)
                )
                gate_up[0, cut, chunk_lanes(chunk)] = slope * up * used
                gate_up[1, cut, chunk_lanes(chunk)] = gelu
                active = (gelu * up).astype(LOW)
                act_low[cut, chunk_lanes(chunk)] = active
                send_a[lax.div(chunk, 2), cut, half_chunk(chunk)] = active.astype(FULL)

            tiles(local_hidden, units_tile)
            act_send(0, chunk)
            active = send_a[lax.div(chunk, 2), :, half_chunk(chunk)].T.astype(LOW)
            tiles(
                width, lambda start, size: put_part(chunk, start, size, dot(active, w_down[:, pl.ds(start, size)]))
            )
            core_copy(1, chunk).start()
            park.wait()
            send_part(1, chunk)
            pl.when(chunk + AHEAD < CHUNKS)(lambda: send_part(0, chunk + AHEAD))

        same = jnp.int32(0)
        for place in range(2 * LINE):
            same = same + jnp.where(cluster_ref[place] == cluster_ref[dp], 1, 0)
        weight_row = 1.0 / jnp.full((1, width), same, jnp.int32).astype(FULL)

        def feed_backward(chunk):
            loads = load_all(
                ((xhat_park.at[chunk], xbuf), (cot_hbm.at[chunk_rows(chunk)], cotbuf))
            )
            branch = take_part(1, chunk)
            for copy in loads:
                copy.wait()
            residual = alpha * (xbuf[...] * gain_one[...] + bias_one[...]) + branch
            centered = residual - row_mean(residual)
            rstd = lax.rsqrt(row_mean(centered * centered) + norm_eps)
            xhat = centered * rstd
            obuf[...] = (xhat * gain_two[...] + bias_two[...]).astype(LOW)
            grad_out = cotbuf[...].astype(FULL) * weight_row
            vectors[2:3, :] += jnp.sum(grad_out * xhat, axis=0, keepdims=True)
            vectors[3:4, :] += jnp.sum(grad_out, axis=0, keepdims=True)
            grad_x = grad_out * gain_two[...]
            grad_two = (grad_x - row_mean(grad_x) - xhat * row_mean(grad_x * xhat)) * rstd
            for place in range(width // inner):
                gbuf[place * rows : (place + 1) * rows, :] = grad_two[:, place * inner : (place + 1) * inner]
            stores = load_all(
                ((obuf, block_out.at[chunk_rows(chunk)]), (gbuf, grad_two_park.at[chunk]))
            )
            grad_low = grad_two.astype(LOW)
            put_blocks(grad_low.astype(FULL))
            for place in range(2):
                two_own[place, chunk_rows(chunk), :] = blocks[2 * z + place].astype(LOW)

            @pl.when(chunk == mine)
            def _():
                two_send[...] = blocks[...]
                for step in range(1, LINE):
                    two_copy(step).start()


            def units_tile(start, size):
                cut = pl.ds(start, size)
                grad_act = dot_nt(w_down[cut, :], grad_low)
                for which in range(2):
                    low = (grad_act * gate_up[which, cut, chunk_lanes(chunk)]).astype(LOW)
                    grads_low[pl.ds(which * shift + start, size), chunk_lanes(chunk)] = low
                    gate_up[which, cut, chunk_lanes(chunk)] = low.astype(FULL)

            spread(local_hidden, units_tile)
            pair_send(0, chunk)
            for copy in stores:
                copy.wait()

        def hidden_part(pair):
            both = pl.ds(pl.multiple_of(2 * rows * pair, 2 * rows), 2 * rows)
            grad_gate = gate_up[0, :, both].T.astype(LOW)
            grad_up = gate_up[1, :, both].T.astype(LOW)

            def columns(start, size):
                cut = pl.ds(start, size)
                value = dot(grad_gate, w_gate[:, cut]) + dot(grad_up, w_up[:, cut])
                put_part(2 * pair, start, size, value[:rows])
                put_part(2 * pair + 1, start, size, value[rows:])

            tiles(width, columns)
            for place in range(2):
                core_copy(2, 2 * pair + place).start()

        def take_hidden():
            for chunk in range(CHUNKS):
                cols_copy(chunk).wait()
            fetch_columns(hidden_theirs)

        def step(turn, carried):
            pl.when(turn == CHUNKS - 1)(lambda: hidden_part(0))
            @pl.when(turn >= 3)
            def _():
                act_take(0, turn - 3)
                act_send(1, turn - 3)

            @pl.when(turn == CHUNKS)
            def _():
                for chunk in range(2):
                    send_part(2, chunk)
                take_hidden()
                act_sent(range(2))
                for chunk in range(2):
                    for part in whole:
                        pair_copy(0, chunk, part).wait()
                moved([(r_y.at[0, :, pl.ds(0, block)], send_a.at[0])])
                gate_theirs[:, 0:block] = send_a[0].astype(LOW)

            pl.when(turn < CHUNKS)(lambda: feed_forward(turn))
            pl.when(turn == 1)(lambda: rows_copy().wait())
            pl.when(turn > 0)(lambda: feed_backward(turn - 1))
            return carried

        lax.fori_loop(0, CHUNKS + 1, step, 0)

        for chunk in range(CHUNKS - 1):
            pair_send(1, chunk)
        hidden_part(1)
        for chunk in range(2, CHUNKS):
            send_part(2, chunk)
        for part in whole:
            for chunk in range(2, CHUNKS):
                pair_copy(0, chunk, part).wait()
            start, size = spans[part]
            cut = slice(start, start + size)
            arrived = room.at[pl.ds(0, size)]
            moved([(r_y.at[0, pl.ds(start, size), pl.ds(block, block)], arrived)])
            gate_theirs[cut, block:] = arrived[...].astype(LOW)

            @pl.when(at_end)
            def _():
                place = jnp.where(z == 0, LINE - 1, 0)
                send_a[0, cut, :] = dot(grads_low[cut, :], cols_own[place]) + dot(
                    gate_theirs[cut, :], hidden_theirs[place]
                )
                first_copy(part).start()

        act_take(0, 2)
        act_send(1, 2)
        pl.when(~at_end)(lambda: act_pass((0,)))

    pl.run_scoped(
        middle_scope,
        pltpu.VMEM((local_hidden, width), LOW),
        pltpu.VMEM((local_hidden, width), LOW),
        pltpu.VMEM((local_hidden, width), LOW),
        pltpu.VMEM((rows, width), LOW),
    )

    def last_scope(theirs, late_theirs, two_theirs, att_theirs, send_b, stage, grad_att, grad_one_own, sums, sums_up, sums_down, sums_below, sums_above, late_own):
        def norm_backward(chunk):
            loads = load_all(((xhat_park.at[chunk], xbuf), (grad_two_park.at[chunk], gbuf)))
            branch = take_part(2, chunk)
            for copy in loads:
                copy.wait()
            grad_two = [gbuf[place * rows : (place + 1) * rows, :] for place in range(width // inner)]
            grad_hidden = alpha * jnp.concatenate(grad_two, axis=1) + branch
            xhat = xbuf[...]
            vectors[0:1, :] += jnp.sum(grad_hidden * xhat, axis=0, keepdims=True)
            vectors[1:2, :] += jnp.sum(grad_hidden, axis=0, keepdims=True)
            grad_x = grad_hidden * gain_one[...]
            grad_one = (grad_x - row_mean(grad_x) - xhat * row_mean(grad_x * xhat)) * rstd_one[chunk]
            put_blocks(grad_one)
            for place in range(2):
                grad_one_own[chunk_rows(chunk), place * block : (place + 1) * block] = blocks[2 * mp + place]
            grad_low = grad_one.astype(LOW)
            put_blocks(grad_low.astype(FULL))
            for place in range(2 * LINE):
                late_own[place, chunk_rows(chunk), :] = blocks[place].astype(LOW)

            @pl.when(chunk == mine)
            def _():
                for place in range(2 * LINE):
                    cols_send[place] = blocks[place]
                late_send()

            grad_mixed = dot(grad_low, w_dense[...]).astype(LOW)
            for place in range(heads_here):
                grad_att[place, chunk_rows(chunk), :] = grad_mixed[:, place * HD : (place + 1) * HD]

        def fetch_up():
            for chunk in range(CHUNKS):
                for part in whole:
                    pair_copy(1, chunk, part).wait()
            fetch_rows(r_y.at[1], theirs.at[1])

        def fetch_rows(source, target):
            size = source.shape[0]
            views = [stage.at[place, pl.ds(0, size)] for place in range(2)]
            moved([(source.at[:, pl.ds(block * place, block)], views[place]) for place in range(2)])
            for place in range(2):
                target[:, block * place : block * (place + 1)] = views[place][...].astype(LOW)

        def outer_product(target, place, own, other):
            right, right_theirs = cols_own[place], hidden_theirs[place]

            def rows_tile(start, size):
                cut = pl.ds(start, size)
                target[cut, :] = dot(own[cut, :], right) + dot(other(cut), right_theirs)

            tiles(target.shape[0], rows_tile)

        def down_products():
            for step in range(1, LINE):
                two_spread(1, step).wait()
                two_spread(2, step).start()
            for step in range(1, LINE):
                two_spread(0, step).wait()
                two_spread(2, step).wait()
            for chunk in range(CHUNKS):
                pl.when(at_end)(lambda: act_take(1, chunk))
                act_take(2, chunk)
            for step in range(LINE):
                owner = lax.rem(z + step, LINE)
                if step:
                    moved([(r_two.at[owner], blocks)])
                    for place in range(2):
                        for chunk in range(CHUNKS):
                            piece = blocks[2 * chunk + place].astype(LOW)
                            two_theirs[place, chunk * rows : (chunk + 1) * rows, :] = piece
                    fetch_rows(r_act.at[owner], theirs.at[0])
                left, right = (theirs.at[0], two_theirs) if step else (act_low, two_own)
                for place in range(2):
                    lanes = slice(place * block, (place + 1) * block)

                    def rows_tile(start, size):
                        cut = pl.ds(start, size)
                        product = dot(left[cut, :], right[place])
                        gate_up[0, cut, lanes] = gate_up[0, cut, lanes] + product if step else product

                    tiles(local_hidden, rows_tile)

        def down_copy():
            return remote(gate_up.at[0, :, half_lanes(1 - y)], r_dny, dny_s, dny_r, y_peer)

        def down_end():
            down_copy().wait()
            moved([(r_dny, stage.at[0])])
            stage[0] = stage[0] + gate_up[0, :, half_lanes(y)]
            moved([(stage.at[0], out_down)])
            for chunk in range(CHUNKS):
                for way in range(2):
                    for hop in range(1, LINE - 1):
                        active, copy = act_copy(way, hop, chunk)
                        pl.when(active)(copy.wait_send)

        def unit_terms(kind):
            own = grads_low.at[pl.ds(pl.multiple_of(kind * shift, 16), local_hidden)]

            def other(cut):
                if isinstance(kind, int):
                    return theirs[1, cut, :] if kind else gate_theirs[cut, :]
                return jnp.where(kind == 0, gate_theirs[cut, :], theirs[1, cut, :])

            return own, other

        def count(way):
            return jnp.where(way == 0, LINE - 1 - z, z)

        def order(kind, slot, way):
            return kind * count(way) + slot - (LINE - count(way))

        def turn_of(number, way):
            many = jnp.maximum(count(way), 1)
            return lax.div(number, many) * (LINE - 1) + lax.rem(number, many) + LINE - 1 - count(way)

        def unit_copy(turn, side, part):
            way = toward(side)
            kind, slot = lax.div(turn, LINE - 1), lax.rem(turn, LINE - 1)
            units = pl.ds(*halves[part])
            home = (send_a, send_b)[side].at[lax.rem(jnp.maximum(order(kind, slot + 1, way), 0), 2), units]
            return remote(
                home, r_rs.at[kind, slot, way, units], rs_s.at[kind, slot, way, part], rs_r.at[kind, slot, way, part],
                line_goal(way),
            )

        def unit_sent(number, side):
            turn = turn_of(jnp.maximum(number, 0), toward(side))

            @pl.when(turn == 0)
            def _():
                for part in whole:
                    first_copy(part).wait_send()

            @pl.when(turn > 0)
            def _():
                for part in range(2):
                    unit_copy(turn, side, part).wait_send()

        def unit_slot(turn, part, side):
            way = toward(side)
            kind, slot = lax.div(turn, LINE - 1), lax.rem(turn, LINE - 1) + 1
            own, other = unit_terms(kind)
            start, size = halves[part]
            cut = slice(start, start + size)

            @pl.when(goes(slot, way))
            def _():
                number = order(kind, slot, way)
                home = (send_a, send_b)[side].at[lax.rem(jnp.maximum(number, 0), 2)]
                if part == 0:
                    pl.when(number >= 2)(lambda: unit_sent(number - 2, side))
                place = jnp.where(way == 0, LINE - slot + z, slot - LINE + z)
                home[cut, :] = dot(own[cut, :], cols_own[place]) + dot(other(cut), hidden_theirs[place])

                @pl.when((slot > 1) & inner_place(way))
                def _():
                    before = jnp.maximum(turn - 1, 0)

                    @pl.when(before == 0)
                    def _():
                        for piece in (2 * part, 2 * part + 1):
                            first_copy(piece).wait_recv()

                    pl.when(before > 0)(lambda: unit_copy(before, side, part).wait_recv())
                    landed = r_rs.at[lax.div(before, LINE - 1), lax.rem(before, LINE - 1), way, pl.ds(start, size)]
                    moved([(landed, stage.at[side, pl.ds(start, size)])])
                    home[cut, :] = home[cut, :] + stage[side, cut, :]

                unit_copy(turn, side, part).start()

        def unit_end():
            own, other = unit_terms(0)
            outer_product(stage.at[0], z, own, other)
            for side in range(2):

                @pl.when(inner_place(toward(side)))
                def _():
                    for part in range(2):
                        unit_copy(LINE - 2, side, part).wait_recv()
                    moved([(r_rs.at[0, LINE - 2, toward(side)], stage.at[1])])
                    stage[0] = stage[0] + stage[1]

            moved([(stage.at[0], out_gate)])

        def last_product():
            own, other = unit_terms(1)
            outer_product(stage.at[0], z, own, other)
            moved([(stage.at[0], out_up)])

        def last_landed():
            for side in range(2):
                for part in range(2):
                    pl.when(inner_place(toward(side)))(unit_copy(2 * LINE - 3, side, part).wait_recv)

        first = jnp.where(z == 1, 2, jnp.where(z == LINE - 1, 2 * LINE - 2, 0))
        peer_first = jnp.where(z == 0, 2, jnp.where(z == 2, 2 * LINE - 2, 0))
        many = 2 * LINE - 2
        def late_copy(begin, size, part):
            span = pl.ds(begin + part * (size // 2), size // 2)
            return remote(cols_send.at[span], r_late.at[mine, span], late_s.at[0, part], late_r.at[0, part], z_peer)

        def late_send():
            for part in range(2):
                pl.when(at_end)(lambda: late_copy(peer_first, many, part).start())
                pl.when(~at_end)(lambda: late_copy(peer_first, 2, part).start())

        def spread_copy(turn, size, part):
            place = other_x if turn == 3 else mine
            view = r_late.at[place, pl.ds(first + part * (size // 2), size // 2)]
            device = x_peer if turn == 2 else core_peer
            return remote(view, view, late_s.at[turn, part], late_r.at[turn, part], device)

        def by_size(body):
            pl.when(at_end)(lambda: body(2))
            pl.when(~at_end)(lambda: body(many))

        def late_take():
            def body(size):
                for part in range(2):
                    late_copy(first, size, part).wait_recv()
                    spread_copy(2, size, part).start()
                    spread_copy(1, size, part).start()
                for part in range(2):
                    spread_copy(2, size, part).wait()
                    spread_copy(3, size, part).start()
                for part in range(2):
                    spread_copy(1, size, part).wait()
                for part in range(2):
                    spread_copy(3, size, part).wait()

            by_size(body)

        def late_slot(number):
            side, lane = lax.div(number, LINE), lax.rem(number, LINE)
            return parts.at[:, side, :, pl.ds(pl.multiple_of(lane * block, block), block)]

        def late_products():
            for quarter in range(CHUNKS):

                def body(size):
                    moved([(r_late.at[quarter, pl.ds(first, size)], blocks.at[pl.ds(0, size)])])
                    for place in range(size):
                        late_theirs[place, quarter * rows : (quarter + 1) * rows, :] = blocks[place].astype(LOW)

                by_size(body)

            def product(number, carried):
                @pl.when((number < 2) | ~at_end)
                def _():
                    home = late_slot(number)
                    for piece in range(CHUNKS):
                        cut = slice(piece * rows, (piece + 1) * rows)
                        home[piece] = dot(att_turned[cut, :], late_own[first + number]) + dot(
                            att_theirs[cut, :], late_theirs[number]
                        )

                return carried

            lax.fori_loop(0, many, product, 0)
            for place in range(LINE - 1):
                pl.when((place == 0) | ~at_end)(lambda: late_pair(place).start())

        def late_pair(place):
            return remote(late_slot(2 * place + 1 - y), r_dz.at[place], dz_s.at[place], dz_r.at[place], y_peer)

        def late_line(place):
            goal = lax.div(first, 2) + place
            return goal != z, remote(late_slot(2 * place + y), r_dx, dx_s.at[place], dx_r, at(z_to=goal))

        def late_sums():
            for place in range(LINE - 1):

                @pl.when((place == 0) | ~at_end)
                def _():
                    late_pair(place).wait()
                    arrived = blocks.at[pl.ds(0, CHUNKS)]
                    moved([(r_dz.at[place], arrived)])
                    home = late_slot(2 * place + y)
                    home[...] = home[...] + arrived[...]
                    leaves, copy = late_line(place)
                    pl.when(leaves)(copy.start)

        def late_end():
            _, copy = late_line(0)
            copy.wait_recv()
            arrived = blocks.at[pl.ds(0, CHUNKS)]
            moved([(r_dx, arrived)])
            total = late_slot(2 * (z - lax.div(first, 2)) + y)
            for piece in range(CHUNKS):
                gbuf[0:block, piece * rows : (piece + 1) * rows] = (total[piece] + arrived[piece]).T
            moved([(gbuf.at[pl.ds(0, block)], out_dense)])
            for place in range(LINE - 1):

                @pl.when((place == 0) | ~at_end)
                def _():
                    leaves, copy = late_line(place)
                    pl.when(leaves)(copy.wait_send)

            for part in range(2):
                pl.when(at_end)(lambda: late_copy(peer_first, many, part).wait_send())
                pl.when(~at_end)(lambda: late_copy(peer_first, 2, part).wait_send())

        def last_sent():
            for side in range(2):
                pl.when(count(toward(side)) > 0)(lambda: unit_sent(2 * count(toward(side)) - 1, side))
                pl.when(count(toward(side)) > 0)(lambda: unit_sent(2 * count(toward(side)) - 2, side))

        def attention_backward(place, carried):
            hot_t = hot_turned[...]
            queries, keys, values = heads[0, place], heads[1, place], heads[2, place]
            grad_mixed = grad_att[place]
            probability = probabilities(queries, keys, 0)
            grad_prob = dot_nt(grad_mixed, values)
            centre = jnp.sum(grad_prob * probability, axis=-1, keepdims=True)
            grad_scores = (probability * (grad_prob - centre)).astype(LOW)
            grad_queries = dot(grad_scores, keys) * score_scale
            grad_keys = dot_tn(grad_scores, queries) * score_scale
            grad_values = dot_tn(probability.astype(LOW), grad_mixed)
            sums[0, 0:vocab, head_lanes(place)] = dot(hot_t, turn_by(grad_queries, -sin_ref[...]).astype(LOW))
            sums[0, 0:vocab, head_lanes(place, inner)] = dot(hot_t, turn_by(grad_keys, -sin_ref[...]).astype(LOW))
            sums[1, 0:vocab, head_lanes(place)] = dot(hot_t, grad_values.astype(LOW))
            return carried

        def small_sums():
            lax.fori_loop(0, heads_here, attention_backward, 0)
            hot_t = hot_turned[...]
            high, rest = split_low(grad_one_own[...])
            sums[1, 0:vocab, heads_here * HD :] = dot(hot_t, high) + dot(hot_t, rest)
            for side in range(2):
                sums[side, vocab:, :] = vectors[:, side * (width // 2) : (side + 1) * (width // 2)]
            sums_pair().start()

        def sums_pair():
            return remote(sums.at[1 - y], r_sums.at[0], sums_s.at[0], sums_r.at[0], y_peer)

        def sums_line(way):
            source = (sums_up, sums_down)[way]
            goal = jnp.clip(z + 1 - 2 * way, 0, LINE - 1)
            return remote(source, r_sums.at[1 + way], sums_s.at[1 + way], sums_r.at[1 + way], at(z_to=goal))

        def sums_back():
            return remote(sums.at[y], r_sums.at[3], sums_s.at[3], sums_r.at[3], y_peer)

        def sums_first():
            sums_pair().wait()
            moved([(r_sums.at[0], sums_below)])
            sums[y] = sums[y] + sums_below[...]

            @pl.when(z == 0)
            def _():
                sums_up[...] = sums[y]
                sums_line(0).start()

            @pl.when(z == LINE - 1)
            def _():
                sums_down[...] = sums[y]
                sums_line(1).start()

        def sums_up_step():
            sums_line(0).wait_recv()
            moved([(r_sums.at[1], sums_below)])
            sums_up[...] = sums[y] + sums_below[...]
            sums_line(0).start()

        def sums_down_step():
            sums_line(1).wait_recv()
            moved([(r_sums.at[2], sums_above)])
            sums_down[...] = sums[y] + sums_above[...]
            sums_line(1).start()

        def sums_near():
            pl.when(z == 1)(sums_up_step)
            pl.when(z == LINE - 2)(sums_down_step)

        def sums_far():
            pl.when(z == LINE - 2)(sums_up_step)
            pl.when(z == 1)(sums_down_step)

        def sums_middle():
            @pl.when(z == LINE - 1)
            def _():
                sums_line(0).wait_recv()
                moved([(r_sums.at[1], sums_below)])

            @pl.when(z == 0)
            def _():
                sums_line(1).wait_recv()
                moved([(r_sums.at[2], sums_above)])

            @pl.when(z > 0)
            def _():
                sums[y] = sums[y] + sums_below[...]

            @pl.when(z < LINE - 1)
            def _():
                sums[y] = sums[y] + sums_above[...]

            sums_back().start()

        def sums_end():
            sums_back().wait()
            pl.when(z < LINE - 1)(sums_line(0).wait_send)
            pl.when(z > 0)(sums_line(1).wait_send)
            moved([(r_sums.at[3], sums.at[1 - y])])
            lanes = pl.ds(pl.multiple_of(lax.rem(dp, LINE) * block, block), block)
            moved([(sums.at[lax.div(dp, LINE), pl.ds(vocab, 8), lanes], out_norms)])

        def by_token(kind, rows_of):
            side, start = ((0, 0), (0, inner), (1, 0), (1, inner))[kind]
            return sums[side, rows_of, start : start + inner]

        def head_gradients():
            own_columns = emb[:, pl.ds(pl.multiple_of(dp * block, block), block)]
            for kind, result in enumerate((out_query, out_key, out_value)):
                high, rest = split_low(by_token(kind, slice(0, vocab)))
                gbuf[0:block, :] = dot_tn(own_columns, high) + dot_tn(own_columns, rest)
                moved([(gbuf.at[pl.ds(0, block)], result)])

        table_rows = vocab // (2 * LINE)
        table_own = pl.ds(pl.multiple_of(dp * table_rows, table_rows), table_rows)

        def table_part():
            for kind, weight in enumerate((w_query_hbm, w_key_hbm, w_value_hbm)):
                moved([(weight, w_dense)])
                pieces = jnp.concatenate(split_low(by_token(kind, table_own)), axis=0)

                def columns(start, size):
                    cut = pl.ds(start, size)
                    both = dot_nt(pieces, w_dense[cut, :])
                    both = both[:table_rows] + both[table_rows:]
                    xbuf[0:table_rows, cut] = both if kind == 0 else xbuf[0:table_rows, cut] + both

                tiles(width, columns)
            quarter = pl.ds(pl.multiple_of(mp * inner, inner), inner)
            xbuf[0:table_rows, quarter] = xbuf[0:table_rows, quarter] + alpha * by_token(3, table_own)
            table_copy(0).start()

        def table_middle():
            table_copy(0).wait()
            xbuf[table_rows : 2 * table_rows, :] = xbuf[0:table_rows, :] + table_core[...]
            table_copy(1).start()

        def table_end():
            table_copy(1).wait()
            xbuf[0:table_rows, :] = 0.1 * (xbuf[table_rows : 2 * table_rows, :] + table_x[...])
            moved([(xbuf.at[pl.ds(0, table_rows)], out_table)])

        def table_copy(turn):
            target, device = ((table_core, core_peer), (table_x, x_peer))[turn]
            return remote(xbuf.at[pl.ds(turn * table_rows, table_rows)], target, table_s.at[turn], table_r.at[turn], device)


        def one_turn(turn, carried):
            @pl.when((turn == 2) & at_end)
            def _():
                fetch_up()

            swapped = jnp.where(at_end & ((turn == 2) | (turn == 3)), 5 - turn, turn)
            for part in range(2):
                pl.when((turn > 0) & (turn < 4) | (turn == 4) & ~at_end)(lambda: unit_slot(swapped, part, 0))

            @pl.when(turn == 0)
            def _():
                act_take(0, CHUNKS - 1)
                act_send(1, CHUNKS - 1)
                fetch_rows(r_att, att_theirs)
                every_chunk(norm_backward)
                act_sent(range(2, CHUNKS))
                pl.when(~at_end)(lambda: act_pass((1,)))
                for step in range(1, LINE):
                    two_copy(step).wait()
                for step in range(1, LINE):
                    two_spread(1, step).start()
                    two_spread(0, step).start()

            @pl.when(turn == 1)
            def _():
                small_sums()
                pair_send(1, CHUNKS - 1)

            @pl.when((turn == 1) & ~at_end | (turn == 3) & at_end)
            def _():
                late_take()
                late_products()

            pl.when((turn == 1) & ~at_end)(lambda: act_pass((2, 3)))
            pl.when(turn == 1)(sums_first)

            pl.when(turn == 2)(sums_near)
            pl.when((turn == 2) & ~at_end | (turn == 4) & at_end)(late_sums)

            @pl.when((turn == 2) & ~at_end)
            def _():
                fetch_up()


            pl.when(turn == 4)(sums_far)

            @pl.when(turn == 4)
            def _():
                for part in range(2):
                    unit_slot(2, part, 1)

            pl.when((turn == 4) & ~at_end)(sums_middle)
            pl.when(turn == 4)(down_products)

            @pl.when((turn == 4) & ~at_end)
            def _():
                down_copy().start()
                sums_end()
                head_gradients()

            @pl.when((turn == 4) & at_end)
            def _():
                for part in range(2):
                    unit_slot(4, part, 0)
                sums_middle()
                down_copy().start()

            @pl.when(turn == 5)
            def _():
                for part in range(2):
                    for side in range(2):
                        unit_slot(5, part, side)
                    if part == 0:
                        pl.when(~at_end)(table_part)

                @pl.when(at_end)
                def _():
                    sums_end()
                    head_gradients()
                    table_part()

                last_product()
                unit_end()

            return carried

        lax.fori_loop(0, 2 * (LINE - 1), one_turn, 0)
        late_end()
        table_middle()
        table_end()
        down_end()
        last_landed()
        last_sent()

    pl.run_scoped(
        last_scope,
        pltpu.VMEM((2, local_hidden, length), LOW),
        pltpu.VMEM((2 * LINE - 2, length, block), LOW),
        pltpu.VMEM((2, length, block), LOW),
        pltpu.VMEM((inner, length), LOW),
        pltpu.VMEM((2, local_hidden, block), FULL),
        pltpu.VMEM((2, local_hidden, block), FULL),
        pltpu.VMEM((heads_here, length, HD), LOW),
        pltpu.VMEM((length, 2 * block), FULL),
        pltpu.VMEM((2,) + r_sums.shape[1:], FULL),
        pltpu.VMEM(r_sums.shape[1:], FULL),
        pltpu.VMEM(r_sums.shape[1:], FULL),
        pltpu.VMEM(r_sums.shape[1:], FULL),
        pltpu.VMEM(r_sums.shape[1:], FULL),
        pltpu.VMEM((2 * LINE, length, block), LOW),
    )


def write_kernel(*refs):
    count = 10
    late = 7
    sources, landed = refs[:count], refs[count]
    targets = refs[count + 1 : 2 * count + 4]
    rooms, terms, first_sem, second_sem = refs[2 * count + 4 : 3 * count + 4], *refs[3 * count + 4 : 3 * count + 7]
    z = lax.div(lax.axis_index("dp"), 2)
    order = [late] + [place for place in range(count) if place != late]
    loads = {
        place: pltpu.make_async_copy(sources[place], rooms[place], first_sem.at[place]) for place in range(count)
    }
    more = [
        pltpu.make_async_copy(landed.at[1, LINE - 2, way], terms.at[way], first_sem.at[count + way]) for way in range(2)
    ]
    for copy in more:
        copy.start()
    for place in order:
        loads[place].start()
    stores = []
    for copy in more:
        copy.wait()
    for place in order:
        loads[place].wait()
        room = rooms[place]
        if place == late:
            for way, active in ((0, z > 0), (1, z < LINE - 1)):

                @pl.when(active)
                def _():
                    room[...] = room[...] + terms[way]

        if place < count - 1:
            stores.append(pltpu.make_async_copy(room, targets[place], second_sem.at[place]))
            stores[-1].start()
        else:
            for vector in range(4):
                targets[place + vector][...] = room[vector : vector + 1, :]
    for copy in stores:
        copy.wait()


def write_out(results, landed):
    hbm = pl.BlockSpec(memory_space=pl.ANY)
    rows = jax.ShapeDtypeStruct((1, results[-1].shape[1]), FULL)
    shapes = [jax.ShapeDtypeStruct(value.shape, value.dtype) for value in results[:-1]] + [rows] * 4
    return pl.pallas_call(
        write_kernel,
        out_shape=shapes,
        in_specs=[hbm] * (len(results) + 1),
        out_specs=[hbm] * (len(results) - 1) + [pl.BlockSpec(memory_space=pltpu.VMEM)] * 4,
        scratch_shapes=[pltpu.VMEM(value.shape, value.dtype) for value in results]
        + [pltpu.VMEM((2,) + results[7].shape, FULL)]
        + [pltpu.SemaphoreType.DMA((len(results) + 2,))] * 2,
        compiler_params=pltpu.CompilerParams(vmem_limit_bytes=62 * 2**20),
    )(*results, landed)


def local_fast(
    token_ids,
    prefix_lengths,
    cluster_ids,
    embedding,
    w_query,
    w_key,
    w_value,
    w_dense,
    w_gate,
    w_up,
    w_down,
    norm1_gain,
    norm1_bias,
    norm2_gain,
    norm2_bias,
    cotangent,
):
    length = token_ids.shape[0]
    vocab, width = embedding.shape
    inner = w_query.shape[1]
    heads_here = inner // HD
    local_hidden = w_gate.shape[1]
    rows = length // CHUNKS
    block = width // (2 * LINE)
    shift = (local_hidden + 15) // 16 * 16
    frequency = 10000.0 ** (np.arange(HD // 2) * (-2.0 / HD))
    angles = np.arange(length)[:, None] * frequency[None, :]
    cosine = np.concatenate([np.cos(angles)] * 2, axis=1).astype(np.float32)
    sine = np.concatenate([-np.sin(angles), np.sin(angles)], axis=1).astype(np.float32)
    norms = [vector.reshape(1, width) for vector in (norm1_gain, norm1_bias, norm2_gain, norm2_bias)]

    hbm = pl.BlockSpec(memory_space=pl.ANY)
    vmem = pl.BlockSpec(memory_space=pltpu.VMEM)
    smem = pl.BlockSpec(memory_space=pltpu.SMEM)
    sums_rows = vocab + 8
    table_rows = vocab // (2 * LINE)
    shapes = [
        ((length, width), LOW),
        ((table_rows, width), FULL),
        ((block, inner), FULL),
        ((block, inner), FULL),
        ((block, inner), FULL),
        ((block, inner), FULL),
        ((local_hidden, block), FULL),
        ((local_hidden, block), FULL),
        ((local_hidden, block), FULL),
        ((8, block), FULL),
        ((LINE, local_hidden, length), FULL),
        ((LINE, 2 * CHUNKS, rows, block), FULL),
        ((2, local_hidden, length), FULL),
        ((LINE, CHUNKS, rows, block), FULL),
        ((inner, length), FULL),
        ((CHUNKS, rows, width), FULL),
        ((CHUNKS, length, inner), FULL),
        ((local_hidden, block), FULL),
        ((2, LINE - 1, 2, local_hidden, block), FULL),
        ((4, 2 * LINE, rows, block), FULL),
        ((LINE - 1, CHUNKS, rows, block), FULL),
        ((CHUNKS, rows, block), FULL),
        ((4, sums_rows, width // 2), FULL),
    ]
    scratch = [
        ((vocab, width), LOW),
        ((length, HD), FULL),
        ((length, HD), FULL),
        ((CHUNKS, 2, rows, width // 2), FULL),
        ((CHUNKS, rows, width // 2), FULL),
        ((2, CHUNKS, rows, width // 2), FULL),
        ((CHUNKS, rows, width // 2), FULL),
        ((2 * LINE, rows, block), FULL),
        ((rows, width), FULL),
        ((length, inner), FULL),
        ((rows, width), LOW),
        ((2, local_hidden, length), FULL),
        ((2 * shift, length), LOW),
        ((local_hidden, length), LOW),
        ((2, local_hidden, block), FULL),
        ((LINE, length, block), LOW),
        ((2 * CHUNKS, rows, block), FULL),
        ((LINE, length, block), LOW),
        ((local_hidden, length), LOW),
        ((2, length, block), LOW),
        ((2 * LINE, rows, block), FULL),
        ((length, inner), LOW),
        ((inner, length), LOW),
        ((3, heads_here, length, HD), LOW),
        ((width, inner), LOW),
        ((length, 2 * vocab), LOW),
        ((vocab, length), LOW),
        ((CHUNKS, rows, 1), FULL),
        ((8, width), FULL),
        ((table_rows, width), FULL),
        ((table_rows, width), FULL),
        (((local_hidden // 4 + 15) // 16 * 16, block), FULL),
    ]
    dma = pltpu.SemaphoreType.DMA
    each = (3, CHUNKS)
    semaphores = [
        each, each, each, each, each, each, (2, LINE - 1, CHUNKS), (2, LINE - 1, CHUNKS), (3,), (3,), (3, 3), (3, 3),
        (CHUNKS,), (CHUNKS,), None, None, (2, CHUNKS, 4), (2, CHUNKS, 4), None, None, None, None, (4, 2), (4, 2),
        (3,), (3,), (3,), None, (2, LINE - 1, 2, 4), (2, LINE - 1, 2, 4), (4,), (4,), (2,), (2,), (4,), (7,),
    ]
    results = pl.pallas_call(
        functools.partial(layer_kernel, length, width, local_hidden),
        out_shape=[jax.ShapeDtypeStruct(shape, dtype) for shape, dtype in shapes],
        in_specs=[smem] * 2 + [vmem] * 5 + [hbm] * 11,
        out_specs=[hbm] * len(shapes),
        scratch_shapes=[pltpu.VMEM(shape, dtype) for shape, dtype in scratch]
        + [dma if shape is None else dma(shape) for shape in semaphores],
        compiler_params=pltpu.CompilerParams(
            collective_id=0, has_side_effects=True, vmem_limit_bytes=62 * 2**20
        ),
    )(
        prefix_lengths,
        cluster_ids,
        token_ids.reshape(1, length),
        *norms,
        embedding,
        cosine,
        sine,
        w_query,
        w_key,
        w_value,
        w_dense,
        w_gate.T,
        w_up.T,
        w_down.T,
        cotangent,
    )
    written = write_out(results[:10], results[18])
    block_out, table, out_query, out_key, out_value, out_dense, out_gate, out_up, out_down = written[:9]
    out_norms = written[9:]
    return (
        block_out,
        table,
        out_query,
        out_key,
        out_value,
        out_dense,
        out_gate.T,
        out_up.T,
        out_down.T,
        out_norms[0].reshape(width // (2 * LINE)),
        out_norms[1].reshape(width // (2 * LINE)),
        out_norms[2].reshape(width // (2 * LINE)),
        out_norms[3].reshape(width // (2 * LINE)),
    )


def solution(mesh):
    fast = mesh.shape["dp"] == 2 * LINE and mesh.shape["mp"] == 4
    return jax.shard_map(
        local_fast if fast else local_general,
        mesh=mesh,
        in_specs=(
            P("dp"),
            P("dp"),
            P(),
            P(),
            P(None, "mp"),
            P(None, "mp"),
            P(None, "mp"),
            P(None, "mp"),
            P(None, "mp"),
            P(None, "mp"),
            P(None, "mp"),
            P(),
            P(),
            P(),
            P(),
            P("dp", None),
        ),
        out_specs=(
            P("dp", None),
            P("dp", None),
            P("dp", "mp"),
            P("dp", "mp"),
            P("dp", "mp"),
            P("dp", "mp"),
            P("dp", "mp"),
            P("dp", "mp"),
            P("dp", "mp"),
            P("dp"),
            P("dp"),
            P("dp"),
            P("dp"),
        ),
        check_vma=False,
    )
```

```python
import functools
import math

import jax
import jax.numpy as jnp
import numpy as np
from jax import lax
from jax.experimental import pallas as pl
from jax.experimental.pallas import tpu as pltpu
from jax.sharding import PartitionSpec as P

HD = 128
FF_USED = 5461


deep_alpha = math.sqrt(48.0)
norm_eps = 1e-05
highest = lax.Precision.HIGHEST


def layer_norm(inputs, norm_gain, norm_bias):
    center = jnp.mean(inputs, axis=-1, keepdims=True)
    centered = inputs - center
    spread = jnp.mean(centered * centered, axis=-1, keepdims=True)
    return centered * lax.rsqrt(spread + norm_eps) * norm_gain + norm_bias


def rotary_tables(length, head_width):
    half_width = head_width // 2
    frequency = jnp.exp(
        jnp.arange(half_width, dtype=jnp.float32) * (-2.0 * math.log(10000.0) / head_width)
    )
    angles = jnp.arange(length, dtype=jnp.float32)[:, None] * frequency[None, :]
    return (jnp.cos(angles), jnp.sin(angles))


def rotate(inputs, cosine, sine):
    half_width = inputs.shape[-1] // 2
    first = inputs[..., :half_width]
    second = inputs[..., half_width:]
    cosine = cosine[:, None, :]
    sine = sine[:, None, :]
    return jnp.concatenate(
        [first * cosine - second * sine, second * cosine + first * sine], axis=-1
    )


def row_mask(row_begin, row_count, length, prefix):
    columns = jnp.arange(length, dtype=jnp.int32)
    row_index = row_begin + jnp.arange(row_count, dtype=jnp.int32)
    return (columns[None, :] < prefix) | (columns[None, :] <= row_index[:, None])


def block_scores(query_block, keys_rot, visible, score_scale):
    scores = (
        jnp.einsum("bhd,khd->hbk", query_block, keys_rot, preferred_element_type=jnp.float32)
        * score_scale
    )
    return jnp.where(visible[None, :, :], scores, -1e30)


def attention_forward(queries, keys_rot, values_in, prefix, row_block):
    length = queries.shape[0]
    score_scale = 1.0 / math.sqrt(HD)

    def one_block(row_begin):
        scores = block_scores(
            queries, keys_rot, row_mask(row_begin, row_block, length, prefix), score_scale
        )
        row_max = jnp.max(scores, axis=-1, keepdims=True)
        weights = jnp.exp(scores - row_max)
        total_weight = jnp.sum(weights, axis=-1, keepdims=True)
        probability = (weights / total_weight).astype(jnp.bfloat16)
        mixed_block = jnp.einsum(
            "hbk,khd->bhd", probability, values_in, preferred_element_type=jnp.float32
        )
        return (mixed_block, row_max + jnp.log(total_weight))

    starts = jnp.arange(length // row_block, dtype=jnp.int32) * row_block
    attended, log_total = lax.map(one_block, starts)
    return (attended.reshape(length, -1), log_total)


def attention_backward(queries, keys_rot, values_in, prefix, row_block, log_total, grad_mixed):
    length = queries.shape[0]
    score_scale = 1.0 / math.sqrt(HD)

    def one_block(carried, inputs):
        grad_keys, grad_values = carried
        row_begin, block_total = inputs
        scores = block_scores(
            queries, keys_rot, row_mask(row_begin, row_block, length, prefix), score_scale
        )
        probability = jnp.exp(scores - block_total)
        prob_low = probability.astype(jnp.bfloat16)
        grad_prob = jnp.einsum(
            "bhd,khd->hbk", grad_mixed, values_in, preferred_element_type=jnp.float32
        )
        centre = jnp.sum(grad_prob * probability, axis=-1, keepdims=True)
        grad_scores = (probability * (grad_prob - centre)).astype(jnp.bfloat16)
        grad_query = (
            jnp.einsum("hbk,khd->bhd", grad_scores, keys_rot, preferred_element_type=jnp.float32)
            * score_scale
        )
        grad_keys = (
            grad_keys
            + jnp.einsum("hbk,bhd->khd", grad_scores, queries, preferred_element_type=jnp.float32)
            * score_scale
        )
        grad_values = grad_values + jnp.einsum(
            "hbk,bhd->khd", prob_low, grad_mixed, preferred_element_type=jnp.float32
        )
        return ((grad_keys, grad_values), grad_query)

    starts = jnp.arange(length // row_block, dtype=jnp.int32) * row_block
    zeros_kv = jnp.zeros(keys_rot.shape, jnp.float32)
    (grad_keys, grad_values), grad_queries = lax.scan(
        one_block, (zeros_kv, zeros_kv), (starts, log_total)
    )
    return (grad_queries.reshape(queries.shape), grad_keys, grad_values)


def local_general(
    token_ids,
    prefix_lengths,
    cluster_ids,
    embedding,
    w_query,
    w_key,
    w_value,
    w_dense,
    w_gate,
    w_up,
    w_down,
    norm1_gain,
    norm1_bias,
    norm2_gain,
    norm2_bias,
    cotangent,
):
    length = token_ids.shape[0]
    vocab_rows = embedding.shape[0]
    row_block = min(512, length)
    local_heads = w_query.shape[1] // HD
    local_hidden = w_gate.shape[1]
    one_hot = (token_ids[:, None] == jnp.arange(vocab_rows, dtype=jnp.int32)[None, :]).astype(
        jnp.bfloat16
    )
    embedded_low = jnp.dot(one_hot, embedding, preferred_element_type=jnp.float32).astype(
        jnp.bfloat16
    )
    embedded = embedded_low.astype(jnp.float32)
    cosine, sine = rotary_tables(length, HD)
    prefix = prefix_lengths[0]
    own_cluster = cluster_ids[lax.axis_index("dp")]
    seq_weight = 1.0 / jnp.sum((cluster_ids == own_cluster).astype(jnp.float32))

    def project(weight_in):
        return jnp.dot(embedded_low, weight_in, preferred_element_type=jnp.float32).reshape(
            length, local_heads, HD
        )

    queries = rotate(project(w_query), cosine, sine).astype(jnp.bfloat16)
    keys_rot = rotate(project(w_key), cosine, sine).astype(jnp.bfloat16)
    values_in = project(w_value).astype(jnp.bfloat16)
    attended, log_total = attention_forward(queries, keys_rot, values_in, prefix, row_block)
    attended_low = attended.astype(jnp.bfloat16)
    branch = lax.psum(
        jnp.einsum("lh,dh->ld", attended_low, w_dense, preferred_element_type=jnp.float32), "mp"
    )
    residual_one = deep_alpha * embedded + branch
    hidden, norm_one_pull = jax.vjp(layer_norm, residual_one, norm1_gain, norm1_bias)
    hidden_low = hidden.astype(jnp.bfloat16)
    gate_proj = jnp.dot(hidden_low, w_gate, preferred_element_type=jnp.float32)
    up_proj = jnp.dot(hidden_low, w_up, preferred_element_type=jnp.float32)
    unit_index = lax.axis_index("mp") * local_hidden + jnp.arange(local_hidden, dtype=jnp.int32)
    used_mask = (unit_index < FF_USED).astype(jnp.float32)

    def gated_unit(gate_in, up_in):
        return jax.nn.gelu(gate_in, approximate=True) * up_in * used_mask

    activation, gated_pull = jax.vjp(gated_unit, gate_proj, up_proj)
    activation_low = activation.astype(jnp.bfloat16)
    branch_two = lax.psum(
        jnp.einsum("lf,df->ld", activation_low, w_down, preferred_element_type=jnp.float32), "mp"
    )
    residual_two = deep_alpha * hidden + branch_two
    final, norm_two_pull = jax.vjp(layer_norm, residual_two, norm2_gain, norm2_bias)
    grad_out = cotangent.astype(jnp.float32) * seq_weight
    grad_two, grad_gain_two, grad_bias_two = norm_two_pull(grad_out)
    grad_branch_two = grad_two.astype(jnp.bfloat16)
    grad_w_down = jnp.einsum(
        "ld,lf->df", grad_branch_two, activation_low, preferred_element_type=jnp.float32
    )
    grad_act = jnp.dot(grad_branch_two, w_down, preferred_element_type=jnp.float32)
    grad_gate, grad_up = gated_pull(grad_act)
    grad_gate_low = grad_gate.astype(jnp.bfloat16)
    grad_up_low = grad_up.astype(jnp.bfloat16)
    grad_w_gate = jnp.einsum(
        "ld,lf->df", hidden_low, grad_gate_low, preferred_element_type=jnp.float32
    )
    grad_w_up = jnp.einsum("ld,lf->df", hidden_low, grad_up_low, preferred_element_type=jnp.float32)
    hidden_part = jnp.einsum(
        "lf,df->ld", grad_gate_low, w_gate, preferred_element_type=jnp.float32
    ) + jnp.einsum("lf,df->ld", grad_up_low, w_up, preferred_element_type=jnp.float32)
    grad_hidden = deep_alpha * grad_two + lax.psum(hidden_part, "mp")
    feed_sums = (
        lax.psum_scatter(grad_w_gate, "dp", scatter_dimension=0, tiled=True),
        lax.psum_scatter(grad_w_up, "dp", scatter_dimension=0, tiled=True),
        lax.psum_scatter(grad_w_down, "dp", scatter_dimension=0, tiled=True),
        lax.psum_scatter(grad_gain_two, "dp", scatter_dimension=0, tiled=True),
        lax.psum_scatter(grad_bias_two, "dp", scatter_dimension=0, tiled=True),
    )
    grad_one, grad_gain_one, grad_bias_one = norm_one_pull(grad_hidden)
    grad_branch = grad_one.astype(jnp.bfloat16)
    grad_w_dense = jnp.einsum(
        "ld,lh->dh", grad_branch, attended_low, preferred_element_type=jnp.float32
    )
    grad_attended = jnp.dot(grad_branch, w_dense, preferred_element_type=jnp.float32).astype(
        jnp.bfloat16
    )
    grad_attended = grad_attended.reshape(length, local_heads, HD)
    grad_queries, grad_keys, grad_values = attention_backward(
        queries, keys_rot, values_in, prefix, row_block, log_total, grad_attended
    )
    grad_query_lin = rotate(grad_queries, cosine, -sine).astype(jnp.bfloat16).reshape(length, -1)
    grad_key_lin = rotate(grad_keys, cosine, -sine).astype(jnp.bfloat16).reshape(length, -1)
    grad_value_lin = grad_values.astype(jnp.bfloat16).reshape(length, -1)
    grad_w_query = jnp.einsum(
        "ld,lh->dh", embedded_low, grad_query_lin, preferred_element_type=jnp.float32
    )
    grad_w_key = jnp.einsum(
        "ld,lh->dh", embedded_low, grad_key_lin, preferred_element_type=jnp.float32
    )
    grad_w_value = jnp.einsum(
        "ld,lh->dh", embedded_low, grad_value_lin, preferred_element_type=jnp.float32
    )
    input_part = (
        jnp.einsum("lh,dh->ld", grad_query_lin, w_query, preferred_element_type=jnp.float32)
        + jnp.einsum("lh,dh->ld", grad_key_lin, w_key, preferred_element_type=jnp.float32)
        + jnp.einsum("lh,dh->ld", grad_value_lin, w_value, preferred_element_type=jnp.float32)
    )
    grad_embedded = deep_alpha * grad_one + lax.psum(input_part, "mp")
    grad_table = 0.1 * jnp.dot(one_hot.astype(jnp.float32).T, grad_embedded, precision=highest)
    attn_sums = (
        lax.psum_scatter(grad_table, "dp", scatter_dimension=0, tiled=True),
        lax.psum_scatter(grad_w_query, "dp", scatter_dimension=0, tiled=True),
        lax.psum_scatter(grad_w_key, "dp", scatter_dimension=0, tiled=True),
        lax.psum_scatter(grad_w_value, "dp", scatter_dimension=0, tiled=True),
        lax.psum_scatter(grad_w_dense, "dp", scatter_dimension=0, tiled=True),
        lax.psum_scatter(grad_gain_one, "dp", scatter_dimension=0, tiled=True),
        lax.psum_scatter(grad_bias_one, "dp", scatter_dimension=0, tiled=True),
    )
    summed = (
        attn_sums[0],
        attn_sums[1],
        attn_sums[2],
        attn_sums[3],
        attn_sums[4],
        feed_sums[0],
        feed_sums[1],
        feed_sums[2],
        attn_sums[5],
        attn_sums[6],
        feed_sums[3],
        feed_sums[4],
    )
    return (
        final.astype(jnp.bfloat16),
        summed[0],
        summed[1],
        summed[2],
        summed[3],
        summed[4],
        summed[5],
        summed[6],
        summed[7],
        summed[8],
        summed[9],
        summed[10],
        summed[11],
    )


LINE = 4
MESH = pl.DeviceIdType.MESH
CHUNKS = 4
AHEAD = 3
LOW = jnp.bfloat16
FULL = jnp.float32
TANH_SCALE = math.sqrt(2.0 / math.pi)


def dot(left, right):
    return jnp.dot(left, right, preferred_element_type=FULL)


def dot_nt(left, right):
    return lax.dot_general(left, right, (((1,), (1,)), ((), ())), preferred_element_type=FULL)


def dot_tn(left, right):
    return lax.dot_general(left, right, (((0,), (0,)), ((), ())), preferred_element_type=FULL)


def split_low(value):
    high = value.astype(LOW)
    return high, (value - high.astype(FULL)).astype(LOW)


def row_mean(value):
    return jnp.mean(value, axis=-1, keepdims=True)


def spread(size, body, tile=512):
    for start in range(0, size, tile):
        body(start, min(tile, size - start))


def tiles(size, body, tile=512):
    whole = size // tile
    lax.fori_loop(0, whole, lambda step, carried: (body(pl.multiple_of(step * tile, tile), tile), carried)[1], 0)
    if size % tile:
        body(whole * tile, size % tile)


def layer_kernel(
    length, width, local_hidden,
    prefix_ref, cluster_ref, ids_row, gain_one, bias_one, gain_two, bias_two, emb_hbm, cos_hbm, sin_hbm, w_query_hbm, w_key_hbm, w_value_hbm, w_dense_hbm,
    w_gate_hbm, w_up_hbm, w_down_hbm, cot_hbm,
    block_out, out_table, out_query, out_key, out_value, out_dense, out_gate, out_up, out_down, out_norms,
    r_act, r_two, r_y, r_cols, r_att, xhat_park, grad_two_park, r_dny, r_rs, r_late, r_dz, r_dx, r_sums,
    emb, cos_ref, sin_ref, parts, core_in, x_in, back_in, blocks, xbuf, gbuf, obuf, gate_up, grads_low, act_low, send_a, cols_own, cols_send,
    hidden_theirs, gate_theirs, two_own, two_send, att_low, att_turned, heads, w_dense, one_hot, hot_turned, rstd_one, vectors, table_core, table_x, room,
    core_s, core_r, x_s, x_r, back_s, back_r, act_s, act_r, two_s, two_r, fwd_two_s, fwd_two_r, cols_s, cols_r, fwd_s,
    fwd_r, ys_s, ys_r, att_s, att_r, dny_s, dny_r, late_s, late_r, dz_s, dz_r, dx_s, dx_r, rs_s, rs_r, sums_s, sums_r, table_s, table_r, load_sem, weight_sem,
):
    dp, mp = lax.axis_index("dp"), lax.axis_index("mp")
    z, y = lax.div(dp, 2), lax.rem(dp, 2)
    x, core = lax.div(mp, 2), lax.rem(mp, 2)
    rows = length // CHUNKS
    heads_here = heads.shape[1]
    inner = heads_here * HD
    vocab = emb.shape[0]
    shift = (local_hidden + 15) // 16 * 16
    quarter = (local_hidden // 4 + 15) // 16 * 16
    spans = [(start, min(quarter, local_hidden - start)) for start in range(0, local_hidden, quarter)]
    whole = range(len(spans))
    halves = ((0, 2 * quarter), (2 * quarter, local_hidden - 2 * quarter))
    block = width // (2 * LINE)
    alpha = jnp.float32(deep_alpha)

    def at(z_to=None, y_to=None, x_to=None, core_to=None):
        z_to = z if z_to is None else z_to
        y_to = y if y_to is None else y_to
        x_to = x if x_to is None else x_to
        core_to = core if core_to is None else core_to
        return (2 * z_to + y_to, 2 * x_to + core_to)

    core_peer = at(core_to=1 - core)
    x_peer = at(x_to=1 - x)
    y_peer = at(y_to=1 - y)
    z_peer = at(z_to=z + 1 - 2 * lax.rem(z, 2))
    at_end = (z == 0) | (z == LINE - 1)

    def remote(source, target, send, receive, device):
        return pltpu.make_async_remote_copy(
            src_ref=source, dst_ref=target, send_sem=send, recv_sem=receive,
            device_id=device, device_id_type=MESH,
        )

    def load_all(pairs):
        copies = [
            pltpu.make_async_copy(source, target, load_sem.at[place])
            for place, (source, target) in enumerate(pairs)
        ]
        for copy in copies:
            copy.start()
        return copies

    def moved(pairs):
        for copy in load_all(pairs):
            copy.wait()

    barrier = pltpu.get_barrier_semaphore()
    greeted = [core_peer, x_peer, y_peer] + [at(z_to=lax.rem(z + step, LINE)) for step in range(1, LINE)]
    for device in greeted:
        pl.semaphore_signal(barrier, inc=1, device_id=device, device_id_type=MESH)

    def chunk_rows(chunk):
        return pl.ds(pl.multiple_of(chunk * rows, rows), rows)

    def core_copy(turn, chunk):
        return remote(
            parts.at[chunk, 1 - core], core_in.at[chunk], core_s.at[turn, chunk], core_r.at[turn, chunk], core_peer
        )

    def x_copy(turn, chunk):
        return remote(
            parts.at[chunk, core], x_in.at[turn % 2, chunk], x_s.at[turn, chunk], x_r.at[turn, chunk], x_peer
        )

    def back_copy(turn, chunk):
        return remote(
            parts.at[chunk, core], back_in.at[chunk], back_s.at[turn, chunk], back_r.at[turn, chunk], core_peer
        )

    def put_part(chunk, start, size, value):
        side, first = lax.div(start, width // 2), lax.rem(start, width // 2)
        parts[chunk, side, :, pl.ds(pl.multiple_of(first, size), size)] = value

    def send_part(turn, chunk):
        core_copy(turn, chunk).wait()
        parts[chunk, core] = parts[chunk, core] + core_in[chunk]
        x_copy(turn, chunk).start()

    def take_part(turn, chunk):
        x_copy(turn, chunk).wait()
        parts[chunk, core] = parts[chunk, core] + x_in[turn % 2, chunk]
        back = back_copy(turn, chunk)
        back.start()
        mine = parts[chunk, core]
        back.wait()
        other = back_in[chunk]
        return jnp.concatenate([jnp.where(core == 0, mine, other), jnp.where(core == 0, other, mine)], axis=1)

    def put_blocks(value):
        for place in range(2 * LINE):
            blocks[place] = value[:, place * block : (place + 1) * block]

    def chunk_lanes(chunk):
        return pl.ds(pl.multiple_of(chunk * rows, rows), rows)

    def half_lanes(side):
        return pl.ds(pl.multiple_of(side * block, block), block)

    def keep_columns(chunk):
        for place in range(LINE):
            cols_own[place, chunk_rows(chunk), :] = blocks[2 * place + y].astype(LOW)
        for place in range(2):
            cols_send[2 * chunk + place] = blocks[2 * (2 * core + place) + 1 - y]

    def cols_copy(chunk):
        return remote(
            cols_send.at[pl.ds(2 * chunk, 2)], r_cols.at[pl.ds(2 * core, 2), chunk],
            cols_s.at[chunk], cols_r.at[chunk], y_peer,
        )

    def forward_copy():
        view = r_cols.at[pl.ds(2 * core, 2)]
        return remote(view, view, fwd_s, fwd_r, core_peer)

    def act_copy(way, hop, chunk):
        goal = jnp.clip(z + 1 - 2 * way, 0, LINE - 1)
        owner = z - hop if way == 0 else z + hop
        active = (owner >= 0) & (z < LINE - 1) if way == 0 else (owner < LINE) & (z > 0)
        owner = jnp.clip(owner, 0, LINE - 1)
        landed = r_act.at[owner, :, chunk_lanes(chunk)]
        source = send_a.at[lax.div(chunk, 2), :, half_chunk(chunk)] if hop == 0 else landed
        return active, remote(
            source, landed, act_s.at[way, hop, chunk], act_r.at[way, hop, chunk], at(z_to=goal)
        )

    def act_landed(way, hop):
        return z - 1 - hop >= 0 if way == 0 else z + 1 + hop < LINE

    def half_chunk(chunk):
        return pl.ds(pl.multiple_of(lax.rem(chunk, 2) * rows, rows), rows)

    def act_send(hop, chunk):
        for way in range(2):
            active, copy = act_copy(way, hop, chunk)
            pl.when(active)(copy.start)

    def act_take(hop, chunk):
        for way in range(2):
            _, copy = act_copy(way, hop, chunk)
            pl.when(act_landed(way, hop))(copy.wait_recv)

    def chunk_of(place):
        return jnp.where(place == 0, 0, jnp.where(place == 1, CHUNKS - 1, place - 1))

    mine = chunk_of(mp)
    other_x = chunk_of(2 * (1 - x) + core)

    def act_pass(chunks):
        for chunk in chunks:
            act_take(1, chunk)
            act_send(2, chunk)

    def two_copy(step):
        goal = lax.rem(z + step, LINE)
        return remote(
            two_send.at[pl.ds(2 * goal, 2)], r_two.at[z, pl.ds(2 * mine, 2)],
            two_s.at[step - 1], two_r.at[step - 1], at(z_to=goal),
        )

    def two_spread(turn, step):
        quarter = other_x if turn == 2 else mine
        view = r_two.at[lax.rem(z + step, LINE), pl.ds(2 * quarter, 2)]
        device = x_peer if turn == 1 else core_peer
        return remote(view, view, fwd_two_s.at[turn, step - 1], fwd_two_r.at[turn, step - 1], device)

    def pair_copy(which, chunk, part):
        units = pl.ds(*spans[part])
        return remote(
            gate_up.at[which, units, chunk_lanes(chunk)], r_y.at[which, units, chunk_lanes(chunk)],
            ys_s.at[which, chunk, part], ys_r.at[which, chunk, part], y_peer,
        )

    def pair_send(which, chunk):
        for part in whole:
            pair_copy(which, chunk, part).start()

    def rows_copy():
        return remote(gbuf, r_att, att_s, att_r, z_peer)

    def fetch_columns(target):
        forward = forward_copy()
        forward.start()
        forward.wait()
        for pair in range(2):
            moved(
                [(r_cols.at[2 * pair + place], blocks.at[pl.ds(CHUNKS * place, CHUNKS)]) for place in range(2)]
            )
            for place in range(2):
                for chunk in range(CHUNKS):
                    piece = blocks[CHUNKS * place + chunk].astype(LOW)
                    target[2 * pair + place, chunk * rows : (chunk + 1) * rows, :] = piece

    def toward(side):
        return jnp.where(z < LINE // 2, side, 1 - side)

    def goes(slot, way):
        return jnp.where(way == 0, z < slot, z > LINE - 1 - slot)

    def inner_place(way):
        return jnp.where(way == 0, z > 0, z < LINE - 1)

    def line_goal(way):
        return at(z_to=jnp.clip(z + 1 - 2 * way, 0, LINE - 1))

    def first_copy(part):
        way = toward(0)
        units = pl.ds(*spans[part])
        return remote(
            send_a.at[0, units], r_rs.at[0, 0, way, units], rs_s.at[0, 0, way, part], rs_r.at[0, 0, way, part],
            line_goal(way),
        )

    def act_sent(chunks):
        for chunk in chunks:
            for way in range(2):
                active, copy = act_copy(way, 0, chunk)
                pl.when(active)(copy.wait_send)

    def every_chunk(body):
        lax.fori_loop(0, CHUNKS, lambda chunk, carried: (body(chunk), carried)[1], 0)

    score_scale = 1.0 / math.sqrt(HD)

    def probabilities(queries, keys, begin):
        shape = (queries.shape[0], length)
        column = lax.broadcasted_iota(jnp.int32, shape, 1)
        row = lax.broadcasted_iota(jnp.int32, shape, 0) + begin
        visible = (column < prefix_ref[0]) | (column <= row)
        scores = jnp.where(visible, dot_nt(queries, keys) * score_scale, -1e30)
        weights = jnp.exp(scores - jnp.max(scores, axis=-1, keepdims=True))
        return weights / jnp.sum(weights, axis=-1, keepdims=True)

    def turn_by(value, sine):
        return value * cos_ref[...] + pltpu.roll(value, HD // 2, 1) * sine

    def head_lanes(place, offset=0):
        return pl.ds(pl.multiple_of(offset + place * HD, HD), HD)

    def first_scope(w_heads, tab):
        loads = [
            pltpu.make_async_copy(source, target, weight_sem.at[place])
            for place, (source, target) in enumerate(
                (
                    (emb_hbm, emb),
                    (w_query_hbm, w_heads.at[0]),
                    (w_key_hbm, w_heads.at[1]),
                    (w_value_hbm, w_heads.at[2]),
                    (cos_hbm, cos_ref),
                    (sin_hbm, sin_ref),
                    (w_dense_hbm, w_dense),
                )
            )
        ]
        for copy in loads:
            copy.start()
        named = lax.broadcasted_iota(jnp.int32, (vocab, length), 0) == ids_row[...]
        hot = jnp.where(named, 1.0, 0.0)
        hot_turned[...] = hot.astype(LOW)
        turned_hot = hot.T.astype(LOW)
        one_hot[:, 0:vocab] = turned_hot
        one_hot[:, vocab:] = turned_hot
        vectors[...] = jnp.zeros_like(vectors)
        loads[0].wait()
        for kind in range(3):
            loads[kind + 1].wait()
            pieces = split_low(dot(emb[...], w_heads[kind]))
            for place in range(heads_here):
                for half, piece in enumerate(pieces):
                    tab[place, half * vocab : (half + 1) * vocab, kind * HD : (kind + 1) * HD] = piece[
                        :, place * HD : (place + 1) * HD
                    ]
        loads[4].wait()
        loads[5].wait()

        def head_inputs(place, carried):
            lin = dot(one_hot[...], tab[place])
            heads[0, place] = turn_by(lin[:, 0:HD], sin_ref[...]).astype(LOW)
            heads[1, place] = turn_by(lin[:, HD : 2 * HD], sin_ref[...]).astype(LOW)
            heads[2, place] = lin[:, 2 * HD :].astype(LOW)
            return carried

        lax.fori_loop(0, heads_here, head_inputs, 0)

        def attend(chunk):
            for place in range(heads_here):
                queries = heads[0, place, chunk_rows(chunk), :]
                probability = probabilities(queries, heads[1, place], chunk * rows).astype(LOW)
                mixed = dot(probability, heads[2, place]).astype(LOW)
                att_low[chunk_rows(chunk), place * HD : (place + 1) * HD] = mixed
                turned = mixed.astype(FULL).T
                att_turned[place * HD : (place + 1) * HD, chunk_lanes(chunk)] = turned.astype(LOW)
                gbuf[place * HD : (place + 1) * HD, chunk_lanes(chunk)] = turned

        def project(chunk):
            attend(chunk)
            pl.when(chunk == 0)(lambda: loads[6].wait())
            pl.when(chunk == 0)(lambda: pl.semaphore_wait(barrier, len(greeted)))
            mixed = att_low[chunk_rows(chunk), :]

            def columns(start, size):
                put_part(chunk, start, size, dot_nt(mixed, w_dense[pl.ds(start, size), :]))

            spread(width, columns, 256)
            core_copy(0, chunk).start()
            pl.when(chunk == 0)(lambda: send_part(0, 0))
            pl.when((chunk > 1) & (chunk <= AHEAD))(lambda: send_part(0, chunk - 1))

        every_chunk(project)
        rows_copy().start()

    pl.run_scoped(first_scope, pltpu.VMEM((3, width, inner), LOW), pltpu.VMEM((heads_here, 2 * vocab, 3 * HD), LOW))

    def middle_scope(w_gate, w_up, w_down, cotbuf):
        weight_copies = [
            pltpu.make_async_copy(source, target, weight_sem.at[place])
            for place, (source, target) in enumerate(((w_gate_hbm, w_gate), (w_up_hbm, w_up), (w_down_hbm, w_down)))
        ]
        for copy in weight_copies:
            copy.start()
        for copy in weight_copies:
            copy.wait()

        def feed_forward(chunk):
            branch = take_part(0, chunk)
            residual = alpha * dot(one_hot[chunk_rows(chunk), 0:vocab], emb[...]) + branch
            centered = residual - row_mean(residual)
            rstd = lax.rsqrt(row_mean(centered * centered) + norm_eps)
            xhat = centered * rstd
            rstd_one[chunk] = rstd
            xbuf[...] = xhat
            park = pltpu.make_async_copy(xbuf, xhat_park.at[chunk], load_sem.at[0])
            park.start()
            hidden_low = (xhat * gain_one[...] + bias_one[...]).astype(LOW)
            put_blocks(hidden_low.astype(FULL))
            keep_columns(chunk)
            cols_copy(chunk).start()

            def units_tile(start, size):
                cut = pl.ds(start, size)
                gate = dot_nt(w_gate[cut, :], hidden_low)
                up = dot_nt(w_up[cut, :], hidden_low)
                units = mp * local_hidden + start + lax.broadcasted_iota(jnp.int32, (size, rows), 0)
                used = jnp.where(units < FF_USED, 1.0, 0.0)
                square = gate * gate
                bend = jnp.tanh(TANH_SCALE * gate * (1.0 + 0.044715 * square))
                gelu = 0.5 * gate * (1.0 + bend) * used
                slope = 0.5 * (1.0 + bend) + 0.5 * gate * (1.0 - bend * bend) * (
                    TANH_SCALE * (1.0 + 3.0 * 0.044715 * square)
                )
                gate_up[0, cut, chunk_lanes(chunk)] = slope * up * used
                gate_up[1, cut, chunk_lanes(chunk)] = gelu
                active = (gelu * up).astype(LOW)
                act_low[cut, chunk_lanes(chunk)] = active
                send_a[lax.div(chunk, 2), cut, half_chunk(chunk)] = active.astype(FULL)

            tiles(local_hidden, units_tile)
            act_send(0, chunk)
            active = send_a[lax.div(chunk, 2), :, half_chunk(chunk)].T.astype(LOW)
            tiles(
                width, lambda start, size: put_part(chunk, start, size, dot(active, w_down[:, pl.ds(start, size)]))
            )
            core_copy(1, chunk).start()
            park.wait()
            send_part(1, chunk)
            pl.when(chunk + AHEAD < CHUNKS)(lambda: send_part(0, chunk + AHEAD))

        same = jnp.int32(0)
        for place in range(2 * LINE):
            same = same + jnp.where(cluster_ref[place] == cluster_ref[dp], 1, 0)
        weight_row = 1.0 / jnp.full((1, width), same, jnp.int32).astype(FULL)

        def feed_backward(chunk):
            loads = load_all(
                ((xhat_park.at[chunk], xbuf), (cot_hbm.at[chunk_rows(chunk)], cotbuf))
            )
            branch = take_part(1, chunk)
            for copy in loads:
                copy.wait()
            residual = alpha * (xbuf[...] * gain_one[...] + bias_one[...]) + branch
            centered = residual - row_mean(residual)
            rstd = lax.rsqrt(row_mean(centered * centered) + norm_eps)
            xhat = centered * rstd
            obuf[...] = (xhat * gain_two[...] + bias_two[...]).astype(LOW)
            grad_out = cotbuf[...].astype(FULL) * weight_row
            vectors[2:3, :] += jnp.sum(grad_out * xhat, axis=0, keepdims=True)
            vectors[3:4, :] += jnp.sum(grad_out, axis=0, keepdims=True)
            grad_x = grad_out * gain_two[...]
            grad_two = (grad_x - row_mean(grad_x) - xhat * row_mean(grad_x * xhat)) * rstd
            for place in range(width // inner):
                gbuf[place * rows : (place + 1) * rows, :] = grad_two[:, place * inner : (place + 1) * inner]
            stores = load_all(
                ((obuf, block_out.at[chunk_rows(chunk)]), (gbuf, grad_two_park.at[chunk]))
            )
            grad_low = grad_two.astype(LOW)
            put_blocks(grad_low.astype(FULL))
            for place in range(2):
                two_own[place, chunk_rows(chunk), :] = blocks[2 * z + place].astype(LOW)

            @pl.when(chunk == mine)
            def _():
                two_send[...] = blocks[...]
                for step in range(1, LINE):
                    two_copy(step).start()


            def units_tile(start, size):
                cut = pl.ds(start, size)
                grad_act = dot_nt(w_down[cut, :], grad_low)
                for which in range(2):
                    low = (grad_act * gate_up[which, cut, chunk_lanes(chunk)]).astype(LOW)
                    grads_low[pl.ds(which * shift + start, size), chunk_lanes(chunk)] = low
                    gate_up[which, cut, chunk_lanes(chunk)] = low.astype(FULL)

            spread(local_hidden, units_tile)
            pair_send(0, chunk)
            for copy in stores:
                copy.wait()

        def hidden_part(pair):
            both = pl.ds(pl.multiple_of(2 * rows * pair, 2 * rows), 2 * rows)
            grad_gate = gate_up[0, :, both].T.astype(LOW)
            grad_up = gate_up[1, :, both].T.astype(LOW)

            def columns(start, size):
                cut = pl.ds(start, size)
                value = dot(grad_gate, w_gate[:, cut]) + dot(grad_up, w_up[:, cut])
                put_part(2 * pair, start, size, value[:rows])
                put_part(2 * pair + 1, start, size, value[rows:])

            tiles(width, columns)
            for place in range(2):
                core_copy(2, 2 * pair + place).start()

        def take_hidden():
            for chunk in range(CHUNKS):
                cols_copy(chunk).wait()
            fetch_columns(hidden_theirs)

        lag = AHEAD - 1

        def step(turn, carried):
            pl.when(turn == CHUNKS - 2 + lag)(lambda: hidden_part(0))
            @pl.when(turn >= 3)
            def _():
                act_take(0, turn - 3)
                act_send(1, turn - 3)

            @pl.when(turn == CHUNKS - 1 + lag)
            def _():
                for chunk in range(2):
                    send_part(2, chunk)
                take_hidden()
                act_sent(range(2))
                for chunk in range(2):
                    for part in whole:
                        pair_copy(0, chunk, part).wait()
                moved([(r_y.at[0, :, pl.ds(0, block)], send_a.at[0])])
                gate_theirs[:, 0:block] = send_a[0].astype(LOW)

            pl.when(turn < CHUNKS)(lambda: feed_forward(turn))
            pl.when(turn == lag)(lambda: rows_copy().wait())
            pl.when(turn >= lag)(lambda: feed_backward(turn - lag))
            return carried

        lax.fori_loop(0, CHUNKS + lag, step, 0)

        for chunk in range(CHUNKS - 1):
            pair_send(1, chunk)
        hidden_part(1)
        for chunk in range(2, CHUNKS):
            send_part(2, chunk)
        for part in whole:
            for chunk in range(2, CHUNKS):
                pair_copy(0, chunk, part).wait()
            start, size = spans[part]
            cut = slice(start, start + size)
            arrived = room.at[pl.ds(0, size)]
            moved([(r_y.at[0, pl.ds(start, size), pl.ds(block, block)], arrived)])
            gate_theirs[cut, block:] = arrived[...].astype(LOW)

            @pl.when(at_end)
            def _():
                place = jnp.where(z == 0, LINE - 1, 0)
                send_a[0, cut, :] = dot(grads_low[cut, :], cols_own[place]) + dot(
                    gate_theirs[cut, :], hidden_theirs[place]
                )
                first_copy(part).start()

        pl.when(~at_end)(lambda: act_pass((0,)))

    pl.run_scoped(
        middle_scope,
        pltpu.VMEM((local_hidden, width), LOW),
        pltpu.VMEM((local_hidden, width), LOW),
        pltpu.VMEM((local_hidden, width), LOW),
        pltpu.VMEM((rows, width), LOW),
    )

    def last_scope(theirs, late_theirs, two_theirs, att_theirs, send_b, stage, grad_att, grad_one_own, sums, sums_up, sums_down, sums_below, sums_above, late_own):
        def norm_backward(chunk):
            loads = load_all(((xhat_park.at[chunk], xbuf), (grad_two_park.at[chunk], gbuf)))
            branch = take_part(2, chunk)
            for copy in loads:
                copy.wait()
            grad_two = [gbuf[place * rows : (place + 1) * rows, :] for place in range(width // inner)]
            grad_hidden = alpha * jnp.concatenate(grad_two, axis=1) + branch
            xhat = xbuf[...]
            vectors[0:1, :] += jnp.sum(grad_hidden * xhat, axis=0, keepdims=True)
            vectors[1:2, :] += jnp.sum(grad_hidden, axis=0, keepdims=True)
            grad_x = grad_hidden * gain_one[...]
            grad_one = (grad_x - row_mean(grad_x) - xhat * row_mean(grad_x * xhat)) * rstd_one[chunk]
            put_blocks(grad_one)
            for place in range(2):
                grad_one_own[chunk_rows(chunk), place * block : (place + 1) * block] = blocks[2 * mp + place]
            grad_low = grad_one.astype(LOW)
            put_blocks(grad_low.astype(FULL))
            for place in range(2 * LINE):
                late_own[place, chunk_rows(chunk), :] = blocks[place].astype(LOW)

            @pl.when(chunk == mine)
            def _():
                for place in range(2 * LINE):
                    cols_send[place] = blocks[place]
                late_send()

            grad_mixed = dot(grad_low, w_dense[...]).astype(LOW)
            for place in range(heads_here):
                grad_att[place, chunk_rows(chunk), :] = grad_mixed[:, place * HD : (place + 1) * HD]

        def fetch_up():
            for chunk in range(CHUNKS):
                for part in whole:
                    pair_copy(1, chunk, part).wait()
            fetch_rows(r_y.at[1], theirs.at[1])

        def fetch_rows(source, target):
            size = source.shape[0]
            views = [stage.at[place, pl.ds(0, size)] for place in range(2)]
            moved([(source.at[:, pl.ds(block * place, block)], views[place]) for place in range(2)])
            for place in range(2):
                target[:, block * place : block * (place + 1)] = views[place][...].astype(LOW)

        def outer_product(target, place, own, other):
            right, right_theirs = cols_own[place], hidden_theirs[place]

            def rows_tile(start, size):
                cut = pl.ds(start, size)
                target[cut, :] = dot(own[cut, :], right) + dot(other(cut), right_theirs)

            tiles(target.shape[0], rows_tile)

        def down_products():
            for step in range(1, LINE):
                two_spread(1, step).wait()
                two_spread(2, step).start()
            for step in range(1, LINE):
                two_spread(0, step).wait()
                two_spread(2, step).wait()
            for chunk in range(CHUNKS):
                pl.when(at_end)(lambda: act_take(1, chunk))
                act_take(2, chunk)
            for step in range(LINE):
                owner = lax.rem(z + step, LINE)
                if step:
                    moved([(r_two.at[owner], blocks)])
                    for place in range(2):
                        for chunk in range(CHUNKS):
                            piece = blocks[2 * chunk + place].astype(LOW)
                            two_theirs[place, chunk * rows : (chunk + 1) * rows, :] = piece
                    fetch_rows(r_act.at[owner], theirs.at[0])
                left, right = (theirs.at[0], two_theirs) if step else (act_low, two_own)
                for place in range(2):
                    lanes = slice(place * block, (place + 1) * block)

                    def rows_tile(start, size):
                        cut = pl.ds(start, size)
                        product = dot(left[cut, :], right[place])
                        gate_up[0, cut, lanes] = gate_up[0, cut, lanes] + product if step else product

                    tiles(local_hidden, rows_tile)

        def down_copy():
            return remote(gate_up.at[0, :, half_lanes(1 - y)], r_dny, dny_s, dny_r, y_peer)

        def down_end():
            down_copy().wait()
            moved([(r_dny, stage.at[0])])
            stage[0] = stage[0] + gate_up[0, :, half_lanes(y)]
            moved([(stage.at[0], out_down)])
            for chunk in range(CHUNKS):
                for way in range(2):
                    for hop in range(1, LINE - 1):
                        active, copy = act_copy(way, hop, chunk)
                        pl.when(active)(copy.wait_send)

        def unit_terms(kind):
            own = grads_low.at[pl.ds(pl.multiple_of(kind * shift, 16), local_hidden)]

            def other(cut):
                if isinstance(kind, int):
                    return theirs[1, cut, :] if kind else gate_theirs[cut, :]
                return jnp.where(kind == 0, gate_theirs[cut, :], theirs[1, cut, :])

            return own, other

        def count(way):
            return jnp.where(way == 0, LINE - 1 - z, z)

        def order(kind, slot, way):
            return kind * count(way) + slot - (LINE - count(way))

        def turn_of(number, way):
            many = jnp.maximum(count(way), 1)
            return lax.div(number, many) * (LINE - 1) + lax.rem(number, many) + LINE - 1 - count(way)

        def unit_copy(turn, side, part):
            way = toward(side)
            kind, slot = lax.div(turn, LINE - 1), lax.rem(turn, LINE - 1)
            units = pl.ds(*halves[part])
            home = (send_a, send_b)[side].at[lax.rem(jnp.maximum(order(kind, slot + 1, way), 0), 2), units]
            return remote(
                home, r_rs.at[kind, slot, way, units], rs_s.at[kind, slot, way, part], rs_r.at[kind, slot, way, part],
                line_goal(way),
            )

        def unit_sent(number, side):
            turn = turn_of(jnp.maximum(number, 0), toward(side))

            @pl.when(turn == 0)
            def _():
                for part in whole:
                    first_copy(part).wait_send()

            @pl.when(turn > 0)
            def _():
                for part in range(2):
                    unit_copy(turn, side, part).wait_send()

        def unit_slot(turn, part, side):
            way = toward(side)
            kind, slot = lax.div(turn, LINE - 1), lax.rem(turn, LINE - 1) + 1
            own, other = unit_terms(kind)
            start, size = halves[part]
            cut = slice(start, start + size)

            @pl.when(goes(slot, way))
            def _():
                number = order(kind, slot, way)
                home = (send_a, send_b)[side].at[lax.rem(jnp.maximum(number, 0), 2)]
                if part == 0:
                    pl.when(number >= 2)(lambda: unit_sent(number - 2, side))
                place = jnp.where(way == 0, LINE - slot + z, slot - LINE + z)
                home[cut, :] = dot(own[cut, :], cols_own[place]) + dot(other(cut), hidden_theirs[place])

                @pl.when((slot > 1) & inner_place(way))
                def _():
                    before = jnp.maximum(turn - 1, 0)

                    @pl.when(before == 0)
                    def _():
                        for piece in (2 * part, 2 * part + 1):
                            first_copy(piece).wait_recv()

                    pl.when(before > 0)(lambda: unit_copy(before, side, part).wait_recv())
                    landed = r_rs.at[lax.div(before, LINE - 1), lax.rem(before, LINE - 1), way, pl.ds(start, size)]
                    moved([(landed, stage.at[side, pl.ds(start, size)])])
                    home[cut, :] = home[cut, :] + stage[side, cut, :]

                unit_copy(turn, side, part).start()

        def unit_end():
            own, other = unit_terms(0)
            outer_product(stage.at[0], z, own, other)
            for side in range(2):

                @pl.when(inner_place(toward(side)))
                def _():
                    for part in range(2):
                        unit_copy(LINE - 2, side, part).wait_recv()
                    moved([(r_rs.at[0, LINE - 2, toward(side)], stage.at[1])])
                    stage[0] = stage[0] + stage[1]

            moved([(stage.at[0], out_gate)])

        def last_product():
            own, other = unit_terms(1)
            outer_product(stage.at[0], z, own, other)
            moved([(stage.at[0], out_up)])

        def last_landed():
            for side in range(2):
                for part in range(2):
                    pl.when(inner_place(toward(side)))(unit_copy(2 * LINE - 3, side, part).wait_recv)

        first = jnp.where(z == 1, 2, jnp.where(z == LINE - 1, 2 * LINE - 2, 0))
        peer_first = jnp.where(z == 0, 2, jnp.where(z == 2, 2 * LINE - 2, 0))
        many = 2 * LINE - 2
        def late_copy(begin, size, part):
            span = pl.ds(begin + part * (size // 2), size // 2)
            return remote(cols_send.at[span], r_late.at[mine, span], late_s.at[0, part], late_r.at[0, part], z_peer)

        def late_send():
            for part in range(2):
                pl.when(at_end)(lambda: late_copy(peer_first, many, part).start())
                pl.when(~at_end)(lambda: late_copy(peer_first, 2, part).start())

        def spread_copy(turn, size, part):
            place = other_x if turn == 3 else mine
            view = r_late.at[place, pl.ds(first + part * (size // 2), size // 2)]
            device = x_peer if turn == 2 else core_peer
            return remote(view, view, late_s.at[turn, part], late_r.at[turn, part], device)

        def by_size(body):
            pl.when(at_end)(lambda: body(2))
            pl.when(~at_end)(lambda: body(many))

        def late_take():
            def body(size):
                for part in range(2):
                    late_copy(first, size, part).wait_recv()
                    spread_copy(2, size, part).start()
                    spread_copy(1, size, part).start()
                for part in range(2):
                    spread_copy(2, size, part).wait()
                    spread_copy(3, size, part).start()
                for part in range(2):
                    spread_copy(1, size, part).wait()
                for part in range(2):
                    spread_copy(3, size, part).wait()

            by_size(body)

        def late_slot(number):
            side, lane = lax.div(number, LINE), lax.rem(number, LINE)
            return parts.at[:, side, :, pl.ds(pl.multiple_of(lane * block, block), block)]

        def late_products():
            for quarter in range(CHUNKS):

                def body(size):
                    moved([(r_late.at[quarter, pl.ds(first, size)], blocks.at[pl.ds(0, size)])])
                    for place in range(size):
                        late_theirs[place, quarter * rows : (quarter + 1) * rows, :] = blocks[place].astype(LOW)

                by_size(body)

            def product(number, carried):
                @pl.when((number < 2) | ~at_end)
                def _():
                    home = late_slot(number)
                    for piece in range(CHUNKS):
                        cut = slice(piece * rows, (piece + 1) * rows)
                        home[piece] = dot(att_turned[cut, :], late_own[first + number]) + dot(
                            att_theirs[cut, :], late_theirs[number]
                        )

                return carried

            lax.fori_loop(0, many, product, 0)
            for place in range(LINE - 1):
                pl.when((place == 0) | ~at_end)(lambda: late_pair(place).start())

        def late_pair(place):
            return remote(late_slot(2 * place + 1 - y), r_dz.at[place], dz_s.at[place], dz_r.at[place], y_peer)

        def late_line(place):
            goal = lax.div(first, 2) + place
            return goal != z, remote(late_slot(2 * place + y), r_dx, dx_s.at[place], dx_r, at(z_to=goal))

        def late_sums():
            for place in range(LINE - 1):

                @pl.when((place == 0) | ~at_end)
                def _():
                    late_pair(place).wait()
                    arrived = blocks.at[pl.ds(0, CHUNKS)]
                    moved([(r_dz.at[place], arrived)])
                    home = late_slot(2 * place + y)
                    home[...] = home[...] + arrived[...]
                    leaves, copy = late_line(place)
                    pl.when(leaves)(copy.start)

        def late_end():
            _, copy = late_line(0)
            copy.wait_recv()
            arrived = blocks.at[pl.ds(0, CHUNKS)]
            moved([(r_dx, arrived)])
            total = late_slot(2 * (z - lax.div(first, 2)) + y)
            for piece in range(CHUNKS):
                gbuf[0:block, piece * rows : (piece + 1) * rows] = (total[piece] + arrived[piece]).T
            moved([(gbuf.at[pl.ds(0, block)], out_dense)])
            for place in range(LINE - 1):

                @pl.when((place == 0) | ~at_end)
                def _():
                    leaves, copy = late_line(place)
                    pl.when(leaves)(copy.wait_send)

            for part in range(2):
                pl.when(at_end)(lambda: late_copy(peer_first, many, part).wait_send())
                pl.when(~at_end)(lambda: late_copy(peer_first, 2, part).wait_send())

        def last_sent():
            for side in range(2):
                pl.when(count(toward(side)) > 0)(lambda: unit_sent(2 * count(toward(side)) - 1, side))
                pl.when(count(toward(side)) > 0)(lambda: unit_sent(2 * count(toward(side)) - 2, side))

        def attention_backward(place, carried):
            hot_t = hot_turned[...]
            queries, keys, values = heads[0, place], heads[1, place], heads[2, place]
            grad_mixed = grad_att[place]
            probability = probabilities(queries, keys, 0)
            grad_prob = dot_nt(grad_mixed, values)
            centre = jnp.sum(grad_prob * probability, axis=-1, keepdims=True)
            grad_scores = (probability * (grad_prob - centre)).astype(LOW)
            grad_queries = dot(grad_scores, keys) * score_scale
            grad_keys = dot_tn(grad_scores, queries) * score_scale
            grad_values = dot_tn(probability.astype(LOW), grad_mixed)
            sums[0, 0:vocab, head_lanes(place)] = dot(hot_t, turn_by(grad_queries, -sin_ref[...]).astype(LOW))
            sums[0, 0:vocab, head_lanes(place, inner)] = dot(hot_t, turn_by(grad_keys, -sin_ref[...]).astype(LOW))
            sums[1, 0:vocab, head_lanes(place)] = dot(hot_t, grad_values.astype(LOW))
            return carried

        def small_sums():
            lax.fori_loop(0, heads_here, attention_backward, 0)
            hot_t = hot_turned[...]
            high, rest = split_low(grad_one_own[...])
            sums[1, 0:vocab, heads_here * HD :] = dot(hot_t, high) + dot(hot_t, rest)
            for side in range(2):
                sums[side, vocab:, :] = vectors[:, side * (width // 2) : (side + 1) * (width // 2)]
            sums_pair().start()

        def sums_pair():
            return remote(sums.at[1 - y], r_sums.at[0], sums_s.at[0], sums_r.at[0], y_peer)

        def sums_line(way):
            source = (sums_up, sums_down)[way]
            goal = jnp.clip(z + 1 - 2 * way, 0, LINE - 1)
            return remote(source, r_sums.at[1 + way], sums_s.at[1 + way], sums_r.at[1 + way], at(z_to=goal))

        def sums_back():
            return remote(sums.at[y], r_sums.at[3], sums_s.at[3], sums_r.at[3], y_peer)

        def sums_first():
            sums_pair().wait()
            moved([(r_sums.at[0], sums_below)])
            sums[y] = sums[y] + sums_below[...]

            @pl.when(z == 0)
            def _():
                sums_up[...] = sums[y]
                sums_line(0).start()

            @pl.when(z == LINE - 1)
            def _():
                sums_down[...] = sums[y]
                sums_line(1).start()

        def sums_up_step():
            sums_line(0).wait_recv()
            moved([(r_sums.at[1], sums_below)])
            sums_up[...] = sums[y] + sums_below[...]
            sums_line(0).start()

        def sums_down_step():
            sums_line(1).wait_recv()
            moved([(r_sums.at[2], sums_above)])
            sums_down[...] = sums[y] + sums_above[...]
            sums_line(1).start()

        def sums_near():
            pl.when(z == 1)(sums_up_step)
            pl.when(z == LINE - 2)(sums_down_step)

        def sums_far():
            pl.when(z == LINE - 2)(sums_up_step)
            pl.when(z == 1)(sums_down_step)

        def sums_middle():
            @pl.when(z == LINE - 1)
            def _():
                sums_line(0).wait_recv()
                moved([(r_sums.at[1], sums_below)])

            @pl.when(z == 0)
            def _():
                sums_line(1).wait_recv()
                moved([(r_sums.at[2], sums_above)])

            @pl.when(z > 0)
            def _():
                sums[y] = sums[y] + sums_below[...]

            @pl.when(z < LINE - 1)
            def _():
                sums[y] = sums[y] + sums_above[...]

            sums_back().start()

        def sums_end():
            sums_back().wait()
            pl.when(z < LINE - 1)(sums_line(0).wait_send)
            pl.when(z > 0)(sums_line(1).wait_send)
            moved([(r_sums.at[3], sums.at[1 - y])])
            lanes = pl.ds(pl.multiple_of(lax.rem(dp, LINE) * block, block), block)
            moved([(sums.at[lax.div(dp, LINE), pl.ds(vocab, 8), lanes], out_norms)])

        def by_token(kind, rows_of):
            side, start = ((0, 0), (0, inner), (1, 0), (1, inner))[kind]
            return sums[side, rows_of, start : start + inner]

        def head_gradients():
            own_columns = emb[:, pl.ds(pl.multiple_of(dp * block, block), block)]
            for kind, result in enumerate((out_query, out_key, out_value)):
                high, rest = split_low(by_token(kind, slice(0, vocab)))
                gbuf[0:block, :] = dot_tn(own_columns, high) + dot_tn(own_columns, rest)
                moved([(gbuf.at[pl.ds(0, block)], result)])

        table_rows = vocab // (2 * LINE)
        table_own = pl.ds(pl.multiple_of(dp * table_rows, table_rows), table_rows)

        def table_part():
            for kind, weight in enumerate((w_query_hbm, w_key_hbm, w_value_hbm)):
                moved([(weight, w_dense)])
                pieces = jnp.concatenate(split_low(by_token(kind, table_own)), axis=0)

                def columns(start, size):
                    cut = pl.ds(start, size)
                    both = dot_nt(pieces, w_dense[cut, :])
                    both = both[:table_rows] + both[table_rows:]
                    xbuf[0:table_rows, cut] = both if kind == 0 else xbuf[0:table_rows, cut] + both

                tiles(width, columns)
            quarter = pl.ds(pl.multiple_of(mp * inner, inner), inner)
            xbuf[0:table_rows, quarter] = xbuf[0:table_rows, quarter] + alpha * by_token(3, table_own)
            table_copy(0).start()

        def table_middle():
            table_copy(0).wait()
            xbuf[table_rows : 2 * table_rows, :] = xbuf[0:table_rows, :] + table_core[...]
            table_copy(1).start()

        def table_end():
            table_copy(1).wait()
            xbuf[0:table_rows, :] = 0.1 * (xbuf[table_rows : 2 * table_rows, :] + table_x[...])
            moved([(xbuf.at[pl.ds(0, table_rows)], out_table)])

        def table_copy(turn):
            target, device = ((table_core, core_peer), (table_x, x_peer))[turn]
            return remote(xbuf.at[pl.ds(turn * table_rows, table_rows)], target, table_s.at[turn], table_r.at[turn], device)


        def one_turn(turn, carried):
            @pl.when((turn == 2) & at_end)
            def _():
                fetch_up()

            swapped = jnp.where(at_end & ((turn == 2) | (turn == 3)), 5 - turn, turn)
            for part in range(2):
                pl.when((turn > 0) & (turn < 4) | (turn == 4) & ~at_end)(lambda: unit_slot(swapped, part, 0))

            @pl.when(turn == 0)
            def _():
                act_take(0, CHUNKS - 1)
                act_send(1, CHUNKS - 1)
                fetch_rows(r_att, att_theirs)
                every_chunk(norm_backward)
                act_sent(range(2, CHUNKS))
                pl.when(~at_end)(lambda: act_pass((1,)))
                for step in range(1, LINE):
                    two_copy(step).wait()
                for step in range(1, LINE):
                    two_spread(1, step).start()
                    two_spread(0, step).start()

            @pl.when(turn == 1)
            def _():
                small_sums()
                pair_send(1, CHUNKS - 1)

            @pl.when((turn == 1) & ~at_end | (turn == 3) & at_end)
            def _():
                late_take()
                late_products()

            pl.when((turn == 1) & ~at_end)(lambda: act_pass((2, 3)))
            pl.when(turn == 1)(sums_first)

            pl.when(turn == 2)(sums_near)
            pl.when((turn == 2) & ~at_end | (turn == 4) & at_end)(late_sums)

            @pl.when((turn == 2) & ~at_end)
            def _():
                fetch_up()


            pl.when(turn == 4)(sums_far)

            @pl.when(turn == 4)
            def _():
                for part in range(2):
                    unit_slot(2, part, 1)

            pl.when((turn == 4) & ~at_end)(sums_middle)
            pl.when(turn == 4)(down_products)

            @pl.when((turn == 4) & ~at_end)
            def _():
                down_copy().start()
                sums_end()
                head_gradients()

            @pl.when((turn == 4) & at_end)
            def _():
                for part in range(2):
                    unit_slot(4, part, 0)
                sums_middle()
                down_copy().start()

            @pl.when(turn == 5)
            def _():
                for part in range(2):
                    for side in range(2):
                        unit_slot(5, part, side)
                    if part == 0:
                        pl.when(~at_end)(table_part)

                @pl.when(at_end)
                def _():
                    sums_end()
                    head_gradients()
                    table_part()

                last_product()
                unit_end()

            return carried

        lax.fori_loop(0, 2 * (LINE - 1), one_turn, 0)
        late_end()
        table_middle()
        table_end()
        down_end()
        last_landed()
        last_sent()

    pl.run_scoped(
        last_scope,
        pltpu.VMEM((2, local_hidden, length), LOW),
        pltpu.VMEM((2 * LINE - 2, length, block), LOW),
        pltpu.VMEM((2, length, block), LOW),
        pltpu.VMEM((inner, length), LOW),
        pltpu.VMEM((2, local_hidden, block), FULL),
        pltpu.VMEM((2, local_hidden, block), FULL),
        pltpu.VMEM((heads_here, length, HD), LOW),
        pltpu.VMEM((length, 2 * block), FULL),
        pltpu.VMEM((2,) + r_sums.shape[1:], FULL),
        pltpu.VMEM(r_sums.shape[1:], FULL),
        pltpu.VMEM(r_sums.shape[1:], FULL),
        pltpu.VMEM(r_sums.shape[1:], FULL),
        pltpu.VMEM(r_sums.shape[1:], FULL),
        pltpu.VMEM((2 * LINE, length, block), LOW),
    )


def write_kernel(*refs):
    count = 10
    late = 7
    sources, landed = refs[:count], refs[count]
    targets = refs[count + 1 : 2 * count + 4]
    rooms, terms, first_sem, second_sem = refs[2 * count + 4 : 3 * count + 4], *refs[3 * count + 4 : 3 * count + 7]
    z = lax.div(lax.axis_index("dp"), 2)
    order = [late] + [place for place in range(count) if place != late]
    loads = {
        place: pltpu.make_async_copy(sources[place], rooms[place], first_sem.at[place]) for place in range(count)
    }
    more = [
        pltpu.make_async_copy(landed.at[1, LINE - 2, way], terms.at[way], first_sem.at[count + way]) for way in range(2)
    ]
    for copy in more:
        copy.start()
    for place in order:
        loads[place].start()
    stores = []
    for copy in more:
        copy.wait()
    for place in order:
        loads[place].wait()
        room = rooms[place]
        if place == late:
            for way, active in ((0, z > 0), (1, z < LINE - 1)):

                @pl.when(active)
                def _():
                    room[...] = room[...] + terms[way]

        if place < count - 1:
            stores.append(pltpu.make_async_copy(room, targets[place], second_sem.at[place]))
            stores[-1].start()
        else:
            for vector in range(4):
                targets[place + vector][...] = room[vector : vector + 1, :]
    for copy in stores:
        copy.wait()


def write_out(results, landed):
    hbm = pl.BlockSpec(memory_space=pl.ANY)
    rows = jax.ShapeDtypeStruct((1, results[-1].shape[1]), FULL)
    shapes = [jax.ShapeDtypeStruct(value.shape, value.dtype) for value in results[:-1]] + [rows] * 4
    return pl.pallas_call(
        write_kernel,
        out_shape=shapes,
        in_specs=[hbm] * (len(results) + 1),
        out_specs=[hbm] * (len(results) - 1) + [pl.BlockSpec(memory_space=pltpu.VMEM)] * 4,
        scratch_shapes=[pltpu.VMEM(value.shape, value.dtype) for value in results]
        + [pltpu.VMEM((2,) + results[7].shape, FULL)]
        + [pltpu.SemaphoreType.DMA((len(results) + 2,))] * 2,
        compiler_params=pltpu.CompilerParams(vmem_limit_bytes=62 * 2**20),
    )(*results, landed)


def local_fast(
    token_ids,
    prefix_lengths,
    cluster_ids,
    embedding,
    w_query,
    w_key,
    w_value,
    w_dense,
    w_gate,
    w_up,
    w_down,
    norm1_gain,
    norm1_bias,
    norm2_gain,
    norm2_bias,
    cotangent,
):
    length = token_ids.shape[0]
    vocab, width = embedding.shape
    inner = w_query.shape[1]
    heads_here = inner // HD
    local_hidden = w_gate.shape[1]
    rows = length // CHUNKS
    block = width // (2 * LINE)
    shift = (local_hidden + 15) // 16 * 16
    frequency = 10000.0 ** (np.arange(HD // 2) * (-2.0 / HD))
    angles = np.arange(length)[:, None] * frequency[None, :]
    cosine = np.concatenate([np.cos(angles)] * 2, axis=1).astype(np.float32)
    sine = np.concatenate([-np.sin(angles), np.sin(angles)], axis=1).astype(np.float32)
    norms = [vector.reshape(1, width) for vector in (norm1_gain, norm1_bias, norm2_gain, norm2_bias)]

    hbm = pl.BlockSpec(memory_space=pl.ANY)
    vmem = pl.BlockSpec(memory_space=pltpu.VMEM)
    smem = pl.BlockSpec(memory_space=pltpu.SMEM)
    sums_rows = vocab + 8
    table_rows = vocab // (2 * LINE)
    shapes = [
        ((length, width), LOW),
        ((table_rows, width), FULL),
        ((block, inner), FULL),
        ((block, inner), FULL),
        ((block, inner), FULL),
        ((block, inner), FULL),
        ((local_hidden, block), FULL),
        ((local_hidden, block), FULL),
        ((local_hidden, block), FULL),
        ((8, block), FULL),
        ((LINE, local_hidden, length), FULL),
        ((LINE, 2 * CHUNKS, rows, block), FULL),
        ((2, local_hidden, length), FULL),
        ((LINE, CHUNKS, rows, block), FULL),
        ((inner, length), FULL),
        ((CHUNKS, rows, width), FULL),
        ((CHUNKS, length, inner), FULL),
        ((local_hidden, block), FULL),
        ((2, LINE - 1, 2, local_hidden, block), FULL),
        ((4, 2 * LINE, rows, block), FULL),
        ((LINE - 1, CHUNKS, rows, block), FULL),
        ((CHUNKS, rows, block), FULL),
        ((4, sums_rows, width // 2), FULL),
    ]
    scratch = [
        ((vocab, width), LOW),
        ((length, HD), FULL),
        ((length, HD), FULL),
        ((CHUNKS, 2, rows, width // 2), FULL),
        ((CHUNKS, rows, width // 2), FULL),
        ((2, CHUNKS, rows, width // 2), FULL),
        ((CHUNKS, rows, width // 2), FULL),
        ((2 * LINE, rows, block), FULL),
        ((rows, width), FULL),
        ((length, inner), FULL),
        ((rows, width), LOW),
        ((2, local_hidden, length), FULL),
        ((2 * shift, length), LOW),
        ((local_hidden, length), LOW),
        ((2, local_hidden, block), FULL),
        ((LINE, length, block), LOW),
        ((2 * CHUNKS, rows, block), FULL),
        ((LINE, length, block), LOW),
        ((local_hidden, length), LOW),
        ((2, length, block), LOW),
        ((2 * LINE, rows, block), FULL),
        ((length, inner), LOW),
        ((inner, length), LOW),
        ((3, heads_here, length, HD), LOW),
        ((width, inner), LOW),
        ((length, 2 * vocab), LOW),
        ((vocab, length), LOW),
        ((CHUNKS, rows, 1), FULL),
        ((8, width), FULL),
        ((table_rows, width), FULL),
        ((table_rows, width), FULL),
        (((local_hidden // 4 + 15) // 16 * 16, block), FULL),
    ]
    dma = pltpu.SemaphoreType.DMA
    each = (3, CHUNKS)
    semaphores = [
        each, each, each, each, each, each, (2, LINE - 1, CHUNKS), (2, LINE - 1, CHUNKS), (3,), (3,), (3, 3), (3, 3),
        (CHUNKS,), (CHUNKS,), None, None, (2, CHUNKS, 4), (2, CHUNKS, 4), None, None, None, None, (4, 2), (4, 2),
        (3,), (3,), (3,), None, (2, LINE - 1, 2, 4), (2, LINE - 1, 2, 4), (4,), (4,), (2,), (2,), (4,), (7,),
    ]
    results = pl.pallas_call(
        functools.partial(layer_kernel, length, width, local_hidden),
        out_shape=[jax.ShapeDtypeStruct(shape, dtype) for shape, dtype in shapes],
        in_specs=[smem] * 2 + [vmem] * 5 + [hbm] * 11,
        out_specs=[hbm] * len(shapes),
        scratch_shapes=[pltpu.VMEM(shape, dtype) for shape, dtype in scratch]
        + [dma if shape is None else dma(shape) for shape in semaphores],
        compiler_params=pltpu.CompilerParams(
            collective_id=0, has_side_effects=True, vmem_limit_bytes=62 * 2**20
        ),
    )(
        prefix_lengths,
        cluster_ids,
        token_ids.reshape(1, length),
        *norms,
        embedding,
        cosine,
        sine,
        w_query,
        w_key,
        w_value,
        w_dense,
        w_gate.T,
        w_up.T,
        w_down.T,
        cotangent,
    )
    written = write_out(results[:10], results[18])
    block_out, table, out_query, out_key, out_value, out_dense, out_gate, out_up, out_down = written[:9]
    out_norms = written[9:]
    return (
        block_out,
        table,
        out_query,
        out_key,
        out_value,
        out_dense,
        out_gate.T,
        out_up.T,
        out_down.T,
        out_norms[0].reshape(width // (2 * LINE)),
        out_norms[1].reshape(width // (2 * LINE)),
        out_norms[2].reshape(width // (2 * LINE)),
        out_norms[3].reshape(width // (2 * LINE)),
    )


def solution(mesh):
    fast = mesh.shape["dp"] == 2 * LINE and mesh.shape["mp"] == 4
    return jax.shard_map(
        local_fast if fast else local_general,
        mesh=mesh,
        in_specs=(
            P("dp"),
            P("dp"),
            P(),
            P(),
            P(None, "mp"),
            P(None, "mp"),
            P(None, "mp"),
            P(None, "mp"),
            P(None, "mp"),
            P(None, "mp"),
            P(None, "mp"),
            P(),
            P(),
            P(),
            P(),
            P("dp", None),
        ),
        out_specs=(
            P("dp", None),
            P("dp", None),
            P("dp", "mp"),
            P("dp", "mp"),
            P("dp", "mp"),
            P("dp", "mp"),
            P("dp", "mp"),
            P("dp", "mp"),
            P("dp", "mp"),
            P("dp"),
            P("dp"),
            P("dp"),
            P("dp"),
        ),
        check_vma=False,
    )
```

```python
import functools
import math

import jax
import jax.numpy as jnp
import numpy as np
from jax import lax
from jax.experimental import pallas as pl
from jax.experimental.pallas import tpu as pltpu
from jax.sharding import PartitionSpec as P

HD = 128
FF_USED = 5461


deep_alpha = math.sqrt(48.0)
norm_eps = 1e-05
highest = lax.Precision.HIGHEST


def layer_norm(inputs, norm_gain, norm_bias):
    center = jnp.mean(inputs, axis=-1, keepdims=True)
    centered = inputs - center
    spread = jnp.mean(centered * centered, axis=-1, keepdims=True)
    return centered * lax.rsqrt(spread + norm_eps) * norm_gain + norm_bias


def rotary_tables(length, head_width):
    half_width = head_width // 2
    frequency = jnp.exp(
        jnp.arange(half_width, dtype=jnp.float32) * (-2.0 * math.log(10000.0) / head_width)
    )
    angles = jnp.arange(length, dtype=jnp.float32)[:, None] * frequency[None, :]
    return (jnp.cos(angles), jnp.sin(angles))


def rotate(inputs, cosine, sine):
    half_width = inputs.shape[-1] // 2
    first = inputs[..., :half_width]
    second = inputs[..., half_width:]
    cosine = cosine[:, None, :]
    sine = sine[:, None, :]
    return jnp.concatenate(
        [first * cosine - second * sine, second * cosine + first * sine], axis=-1
    )


def row_mask(row_begin, row_count, length, prefix):
    columns = jnp.arange(length, dtype=jnp.int32)
    row_index = row_begin + jnp.arange(row_count, dtype=jnp.int32)
    return (columns[None, :] < prefix) | (columns[None, :] <= row_index[:, None])


def block_scores(query_block, keys_rot, visible, score_scale):
    scores = (
        jnp.einsum("bhd,khd->hbk", query_block, keys_rot, preferred_element_type=jnp.float32)
        * score_scale
    )
    return jnp.where(visible[None, :, :], scores, -1e30)


def attention_forward(queries, keys_rot, values_in, prefix, row_block):
    length = queries.shape[0]
    score_scale = 1.0 / math.sqrt(HD)

    def one_block(row_begin):
        scores = block_scores(
            queries, keys_rot, row_mask(row_begin, row_block, length, prefix), score_scale
        )
        row_max = jnp.max(scores, axis=-1, keepdims=True)
        weights = jnp.exp(scores - row_max)
        total_weight = jnp.sum(weights, axis=-1, keepdims=True)
        probability = (weights / total_weight).astype(jnp.bfloat16)
        mixed_block = jnp.einsum(
            "hbk,khd->bhd", probability, values_in, preferred_element_type=jnp.float32
        )
        return (mixed_block, row_max + jnp.log(total_weight))

    starts = jnp.arange(length // row_block, dtype=jnp.int32) * row_block
    attended, log_total = lax.map(one_block, starts)
    return (attended.reshape(length, -1), log_total)


def attention_backward(queries, keys_rot, values_in, prefix, row_block, log_total, grad_mixed):
    length = queries.shape[0]
    score_scale = 1.0 / math.sqrt(HD)

    def one_block(carried, inputs):
        grad_keys, grad_values = carried
        row_begin, block_total = inputs
        scores = block_scores(
            queries, keys_rot, row_mask(row_begin, row_block, length, prefix), score_scale
        )
        probability = jnp.exp(scores - block_total)
        prob_low = probability.astype(jnp.bfloat16)
        grad_prob = jnp.einsum(
            "bhd,khd->hbk", grad_mixed, values_in, preferred_element_type=jnp.float32
        )
        centre = jnp.sum(grad_prob * probability, axis=-1, keepdims=True)
        grad_scores = (probability * (grad_prob - centre)).astype(jnp.bfloat16)
        grad_query = (
            jnp.einsum("hbk,khd->bhd", grad_scores, keys_rot, preferred_element_type=jnp.float32)
            * score_scale
        )
        grad_keys = (
            grad_keys
            + jnp.einsum("hbk,bhd->khd", grad_scores, queries, preferred_element_type=jnp.float32)
            * score_scale
        )
        grad_values = grad_values + jnp.einsum(
            "hbk,bhd->khd", prob_low, grad_mixed, preferred_element_type=jnp.float32
        )
        return ((grad_keys, grad_values), grad_query)

    starts = jnp.arange(length // row_block, dtype=jnp.int32) * row_block
    zeros_kv = jnp.zeros(keys_rot.shape, jnp.float32)
    (grad_keys, grad_values), grad_queries = lax.scan(
        one_block, (zeros_kv, zeros_kv), (starts, log_total)
    )
    return (grad_queries.reshape(queries.shape), grad_keys, grad_values)


def local_general(
    token_ids,
    prefix_lengths,
    cluster_ids,
    embedding,
    w_query,
    w_key,
    w_value,
    w_dense,
    w_gate,
    w_up,
    w_down,
    norm1_gain,
    norm1_bias,
    norm2_gain,
    norm2_bias,
    cotangent,
):
    length = token_ids.shape[0]
    vocab_rows = embedding.shape[0]
    row_block = min(512, length)
    local_heads = w_query.shape[1] // HD
    local_hidden = w_gate.shape[1]
    one_hot = (token_ids[:, None] == jnp.arange(vocab_rows, dtype=jnp.int32)[None, :]).astype(
        jnp.bfloat16
    )
    embedded_low = jnp.dot(one_hot, embedding, preferred_element_type=jnp.float32).astype(
        jnp.bfloat16
    )
    embedded = embedded_low.astype(jnp.float32)
    cosine, sine = rotary_tables(length, HD)
    prefix = prefix_lengths[0]
    own_cluster = cluster_ids[lax.axis_index("dp")]
    seq_weight = 1.0 / jnp.sum((cluster_ids == own_cluster).astype(jnp.float32))

    def project(weight_in):
        return jnp.dot(embedded_low, weight_in, preferred_element_type=jnp.float32).reshape(
            length, local_heads, HD
        )

    queries = rotate(project(w_query), cosine, sine).astype(jnp.bfloat16)
    keys_rot = rotate(project(w_key), cosine, sine).astype(jnp.bfloat16)
    values_in = project(w_value).astype(jnp.bfloat16)
    attended, log_total = attention_forward(queries, keys_rot, values_in, prefix, row_block)
    attended_low = attended.astype(jnp.bfloat16)
    branch = lax.psum(
        jnp.einsum("lh,dh->ld", attended_low, w_dense, preferred_element_type=jnp.float32), "mp"
    )
    residual_one = deep_alpha * embedded + branch
    hidden, norm_one_pull = jax.vjp(layer_norm, residual_one, norm1_gain, norm1_bias)
    hidden_low = hidden.astype(jnp.bfloat16)
    gate_proj = jnp.dot(hidden_low, w_gate, preferred_element_type=jnp.float32)
    up_proj = jnp.dot(hidden_low, w_up, preferred_element_type=jnp.float32)
    unit_index = lax.axis_index("mp") * local_hidden + jnp.arange(local_hidden, dtype=jnp.int32)
    used_mask = (unit_index < FF_USED).astype(jnp.float32)

    def gated_unit(gate_in, up_in):
        return jax.nn.gelu(gate_in, approximate=True) * up_in * used_mask

    activation, gated_pull = jax.vjp(gated_unit, gate_proj, up_proj)
    activation_low = activation.astype(jnp.bfloat16)
    branch_two = lax.psum(
        jnp.einsum("lf,df->ld", activation_low, w_down, preferred_element_type=jnp.float32), "mp"
    )
    residual_two = deep_alpha * hidden + branch_two
    final, norm_two_pull = jax.vjp(layer_norm, residual_two, norm2_gain, norm2_bias)
    grad_out = cotangent.astype(jnp.float32) * seq_weight
    grad_two, grad_gain_two, grad_bias_two = norm_two_pull(grad_out)
    grad_branch_two = grad_two.astype(jnp.bfloat16)
    grad_w_down = jnp.einsum(
        "ld,lf->df", grad_branch_two, activation_low, preferred_element_type=jnp.float32
    )
    grad_act = jnp.dot(grad_branch_two, w_down, preferred_element_type=jnp.float32)
    grad_gate, grad_up = gated_pull(grad_act)
    grad_gate_low = grad_gate.astype(jnp.bfloat16)
    grad_up_low = grad_up.astype(jnp.bfloat16)
    grad_w_gate = jnp.einsum(
        "ld,lf->df", hidden_low, grad_gate_low, preferred_element_type=jnp.float32
    )
    grad_w_up = jnp.einsum("ld,lf->df", hidden_low, grad_up_low, preferred_element_type=jnp.float32)
    hidden_part = jnp.einsum(
        "lf,df->ld", grad_gate_low, w_gate, preferred_element_type=jnp.float32
    ) + jnp.einsum("lf,df->ld", grad_up_low, w_up, preferred_element_type=jnp.float32)
    grad_hidden = deep_alpha * grad_two + lax.psum(hidden_part, "mp")
    feed_sums = (
        lax.psum_scatter(grad_w_gate, "dp", scatter_dimension=0, tiled=True),
        lax.psum_scatter(grad_w_up, "dp", scatter_dimension=0, tiled=True),
        lax.psum_scatter(grad_w_down, "dp", scatter_dimension=0, tiled=True),
        lax.psum_scatter(grad_gain_two, "dp", scatter_dimension=0, tiled=True),
        lax.psum_scatter(grad_bias_two, "dp", scatter_dimension=0, tiled=True),
    )
    grad_one, grad_gain_one, grad_bias_one = norm_one_pull(grad_hidden)
    grad_branch = grad_one.astype(jnp.bfloat16)
    grad_w_dense = jnp.einsum(
        "ld,lh->dh", grad_branch, attended_low, preferred_element_type=jnp.float32
    )
    grad_attended = jnp.dot(grad_branch, w_dense, preferred_element_type=jnp.float32).astype(
        jnp.bfloat16
    )
    grad_attended = grad_attended.reshape(length, local_heads, HD)
    grad_queries, grad_keys, grad_values = attention_backward(
        queries, keys_rot, values_in, prefix, row_block, log_total, grad_attended
    )
    grad_query_lin = rotate(grad_queries, cosine, -sine).astype(jnp.bfloat16).reshape(length, -1)
    grad_key_lin = rotate(grad_keys, cosine, -sine).astype(jnp.bfloat16).reshape(length, -1)
    grad_value_lin = grad_values.astype(jnp.bfloat16).reshape(length, -1)
    grad_w_query = jnp.einsum(
        "ld,lh->dh", embedded_low, grad_query_lin, preferred_element_type=jnp.float32
    )
    grad_w_key = jnp.einsum(
        "ld,lh->dh", embedded_low, grad_key_lin, preferred_element_type=jnp.float32
    )
    grad_w_value = jnp.einsum(
        "ld,lh->dh", embedded_low, grad_value_lin, preferred_element_type=jnp.float32
    )
    input_part = (
        jnp.einsum("lh,dh->ld", grad_query_lin, w_query, preferred_element_type=jnp.float32)
        + jnp.einsum("lh,dh->ld", grad_key_lin, w_key, preferred_element_type=jnp.float32)
        + jnp.einsum("lh,dh->ld", grad_value_lin, w_value, preferred_element_type=jnp.float32)
    )
    grad_embedded = deep_alpha * grad_one + lax.psum(input_part, "mp")
    grad_table = 0.1 * jnp.dot(one_hot.astype(jnp.float32).T, grad_embedded, precision=highest)
    attn_sums = (
        lax.psum_scatter(grad_table, "dp", scatter_dimension=0, tiled=True),
        lax.psum_scatter(grad_w_query, "dp", scatter_dimension=0, tiled=True),
        lax.psum_scatter(grad_w_key, "dp", scatter_dimension=0, tiled=True),
        lax.psum_scatter(grad_w_value, "dp", scatter_dimension=0, tiled=True),
        lax.psum_scatter(grad_w_dense, "dp", scatter_dimension=0, tiled=True),
        lax.psum_scatter(grad_gain_one, "dp", scatter_dimension=0, tiled=True),
        lax.psum_scatter(grad_bias_one, "dp", scatter_dimension=0, tiled=True),
    )
    summed = (
        attn_sums[0],
        attn_sums[1],
        attn_sums[2],
        attn_sums[3],
        attn_sums[4],
        feed_sums[0],
        feed_sums[1],
        feed_sums[2],
        attn_sums[5],
        attn_sums[6],
        feed_sums[3],
        feed_sums[4],
    )
    return (
        final.astype(jnp.bfloat16),
        summed[0],
        summed[1],
        summed[2],
        summed[3],
        summed[4],
        summed[5],
        summed[6],
        summed[7],
        summed[8],
        summed[9],
        summed[10],
        summed[11],
    )


LINE = 4
MESH = pl.DeviceIdType.MESH
CHUNKS = 4
AHEAD = 3
LOW = jnp.bfloat16
FULL = jnp.float32
TANH_SCALE = math.sqrt(2.0 / math.pi)


def dot(left, right):
    return jnp.dot(left, right, preferred_element_type=FULL)


def dot_nt(left, right):
    return lax.dot_general(left, right, (((1,), (1,)), ((), ())), preferred_element_type=FULL)


def dot_tn(left, right):
    return lax.dot_general(left, right, (((0,), (0,)), ((), ())), preferred_element_type=FULL)


def split_low(value):
    high = value.astype(LOW)
    return high, (value - high.astype(FULL)).astype(LOW)


def row_mean(value):
    return jnp.mean(value, axis=-1, keepdims=True)


def spread(size, body, tile=512):
    for start in range(0, size, tile):
        body(start, min(tile, size - start))


def tiles(size, body, tile=512):
    whole = size // tile
    lax.fori_loop(0, whole, lambda step, carried: (body(pl.multiple_of(step * tile, tile), tile), carried)[1], 0)
    if size % tile:
        body(whole * tile, size % tile)


def layer_kernel(
    length, width, local_hidden,
    prefix_ref, cluster_ref, ids_row, gain_one, bias_one, gain_two, bias_two, emb_hbm, cos_hbm, sin_hbm, w_query_hbm, w_key_hbm, w_value_hbm, w_dense_hbm,
    w_gate_hbm, w_up_hbm, w_down_hbm, cot_hbm,
    block_out, out_table, out_query, out_key, out_value, out_dense, out_gate, out_up, out_down, out_norms,
    r_act, r_two, r_y, r_cols, r_att, xhat_park, grad_two_park, r_dny, r_rs, r_late, r_dz, r_dx, r_sums,
    emb, cos_ref, sin_ref, parts, core_in, x_in, back_in, blocks, xbuf, gbuf, obuf, gate_up, grads_low, act_low, send_a, cols_own, cols_send,
    hidden_theirs, gate_theirs, two_own, two_send, att_low, att_turned, heads, w_dense, one_hot, hot_turned, rstd_one, vectors, table_core, table_x, room,
    core_s, core_r, x_s, x_r, back_s, back_r, act_s, act_r, two_s, two_r, fwd_two_s, fwd_two_r, cols_s, cols_r, fwd_s,
    fwd_r, ys_s, ys_r, att_s, att_r, dny_s, dny_r, late_s, late_r, dz_s, dz_r, dx_s, dx_r, rs_s, rs_r, sums_s, sums_r, table_s, table_r, load_sem, weight_sem,
):
    dp, mp = lax.axis_index("dp"), lax.axis_index("mp")
    z, y = lax.div(dp, 2), lax.rem(dp, 2)
    x, core = lax.div(mp, 2), lax.rem(mp, 2)
    rows = length // CHUNKS
    heads_here = heads.shape[1]
    inner = heads_here * HD
    vocab = emb.shape[0]
    shift = (local_hidden + 15) // 16 * 16
    quarter = (local_hidden // 4 + 15) // 16 * 16
    spans = [(start, min(quarter, local_hidden - start)) for start in range(0, local_hidden, quarter)]
    whole = range(len(spans))
    halves = ((0, 2 * quarter), (2 * quarter, local_hidden - 2 * quarter))
    block = width // (2 * LINE)
    alpha = jnp.float32(deep_alpha)

    def at(z_to=None, y_to=None, x_to=None, core_to=None):
        z_to = z if z_to is None else z_to
        y_to = y if y_to is None else y_to
        x_to = x if x_to is None else x_to
        core_to = core if core_to is None else core_to
        return (2 * z_to + y_to, 2 * x_to + core_to)

    core_peer = at(core_to=1 - core)
    x_peer = at(x_to=1 - x)
    y_peer = at(y_to=1 - y)
    z_peer = at(z_to=z + 1 - 2 * lax.rem(z, 2))
    at_end = (z == 0) | (z == LINE - 1)

    def remote(source, target, send, receive, device):
        return pltpu.make_async_remote_copy(
            src_ref=source, dst_ref=target, send_sem=send, recv_sem=receive,
            device_id=device, device_id_type=MESH,
        )

    def load_all(pairs):
        copies = [
            pltpu.make_async_copy(source, target, load_sem.at[place])
            for place, (source, target) in enumerate(pairs)
        ]
        for copy in copies:
            copy.start()
        return copies

    def moved(pairs):
        for copy in load_all(pairs):
            copy.wait()

    barrier = pltpu.get_barrier_semaphore()
    greeted = [core_peer, x_peer, y_peer] + [at(z_to=lax.rem(z + step, LINE)) for step in range(1, LINE)]
    for device in greeted:
        pl.semaphore_signal(barrier, inc=1, device_id=device, device_id_type=MESH)

    def chunk_rows(chunk):
        return pl.ds(pl.multiple_of(chunk * rows, rows), rows)

    def core_copy(turn, chunk):
        return remote(
            parts.at[chunk, 1 - core], core_in.at[chunk], core_s.at[turn, chunk], core_r.at[turn, chunk], core_peer
        )

    def x_copy(turn, chunk):
        return remote(
            parts.at[chunk, core], x_in.at[turn % 2, chunk], x_s.at[turn, chunk], x_r.at[turn, chunk], x_peer
        )

    def back_copy(turn, chunk):
        return remote(
            parts.at[chunk, core], back_in.at[chunk], back_s.at[turn, chunk], back_r.at[turn, chunk], core_peer
        )

    def put_part(chunk, start, size, value):
        side, first = lax.div(start, width // 2), lax.rem(start, width // 2)
        parts[chunk, side, :, pl.ds(pl.multiple_of(first, size), size)] = value

    def send_part(turn, chunk):
        core_copy(turn, chunk).wait()
        parts[chunk, core] = parts[chunk, core] + core_in[chunk]
        x_copy(turn, chunk).start()

    def take_part(turn, chunk):
        x_copy(turn, chunk).wait()
        parts[chunk, core] = parts[chunk, core] + x_in[turn % 2, chunk]
        back = back_copy(turn, chunk)
        back.start()
        mine = parts[chunk, core]
        back.wait()
        other = back_in[chunk]
        return jnp.concatenate([jnp.where(core == 0, mine, other), jnp.where(core == 0, other, mine)], axis=1)

    def put_blocks(value):
        for place in range(2 * LINE):
            blocks[place] = value[:, place * block : (place + 1) * block]

    def chunk_lanes(chunk):
        return pl.ds(pl.multiple_of(chunk * rows, rows), rows)

    def half_lanes(side):
        return pl.ds(pl.multiple_of(side * block, block), block)

    def keep_columns(chunk):
        for place in range(LINE):
            cols_own[place, chunk_rows(chunk), :] = blocks[2 * place + y].astype(LOW)
        for place in range(2):
            cols_send[2 * chunk + place] = blocks[2 * (2 * core + place) + 1 - y]

    def cols_copy(chunk):
        return remote(
            cols_send.at[pl.ds(2 * chunk, 2)], r_cols.at[pl.ds(2 * core, 2), chunk],
            cols_s.at[chunk], cols_r.at[chunk], y_peer,
        )

    def forward_copy():
        view = r_cols.at[pl.ds(2 * core, 2)]
        return remote(view, view, fwd_s, fwd_r, core_peer)

    def act_copy(way, hop, chunk):
        goal = jnp.clip(z + 1 - 2 * way, 0, LINE - 1)
        owner = z - hop if way == 0 else z + hop
        active = (owner >= 0) & (z < LINE - 1) if way == 0 else (owner < LINE) & (z > 0)
        owner = jnp.clip(owner, 0, LINE - 1)
        landed = r_act.at[owner, :, chunk_lanes(chunk)]
        source = send_a.at[lax.div(chunk, 2), :, half_chunk(chunk)] if hop == 0 else landed
        return active, remote(
            source, landed, act_s.at[way, hop, chunk], act_r.at[way, hop, chunk], at(z_to=goal)
        )

    def act_landed(way, hop):
        return z - 1 - hop >= 0 if way == 0 else z + 1 + hop < LINE

    def half_chunk(chunk):
        return pl.ds(pl.multiple_of(lax.rem(chunk, 2) * rows, rows), rows)

    def act_send(hop, chunk):
        for way in range(2):
            active, copy = act_copy(way, hop, chunk)
            pl.when(active)(copy.start)

    def act_take(hop, chunk):
        for way in range(2):
            _, copy = act_copy(way, hop, chunk)
            pl.when(act_landed(way, hop))(copy.wait_recv)

    def chunk_of(place):
        return jnp.where(place == 0, 0, jnp.where(place == 1, CHUNKS - 1, place - 1))

    mine = chunk_of(mp)
    other_x = chunk_of(2 * (1 - x) + core)

    def act_pass(chunks):
        for chunk in chunks:
            act_take(1, chunk)
            act_send(2, chunk)

    def two_copy(step):
        goal = lax.rem(z + step, LINE)
        return remote(
            two_send.at[pl.ds(2 * goal, 2)], r_two.at[z, pl.ds(2 * mine, 2)],
            two_s.at[step - 1], two_r.at[step - 1], at(z_to=goal),
        )

    def two_spread(turn, step):
        quarter = other_x if turn == 2 else mine
        view = r_two.at[lax.rem(z + step, LINE), pl.ds(2 * quarter, 2)]
        device = x_peer if turn == 1 else core_peer
        return remote(view, view, fwd_two_s.at[turn, step - 1], fwd_two_r.at[turn, step - 1], device)

    def pair_copy(which, chunk, part):
        units = pl.ds(*spans[part])
        return remote(
            gate_up.at[which, units, chunk_lanes(chunk)], r_y.at[which, units, chunk_lanes(chunk)],
            ys_s.at[which, chunk, part], ys_r.at[which, chunk, part], y_peer,
        )

    def pair_send(which, chunk):
        for part in whole:
            pair_copy(which, chunk, part).start()

    def rows_copy():
        return remote(gbuf, r_att, att_s, att_r, z_peer)

    def fetch_columns(target):
        forward = forward_copy()
        forward.start()
        forward.wait()
        for pair in range(2):
            moved(
                [(r_cols.at[2 * pair + place], blocks.at[pl.ds(CHUNKS * place, CHUNKS)]) for place in range(2)]
            )
            for place in range(2):
                for chunk in range(CHUNKS):
                    piece = blocks[CHUNKS * place + chunk].astype(LOW)
                    target[2 * pair + place, chunk * rows : (chunk + 1) * rows, :] = piece

    def toward(side):
        return jnp.where(z < LINE // 2, side, 1 - side)

    def goes(slot, way):
        return jnp.where(way == 0, z < slot, z > LINE - 1 - slot)

    def inner_place(way):
        return jnp.where(way == 0, z > 0, z < LINE - 1)

    def line_goal(way):
        return at(z_to=jnp.clip(z + 1 - 2 * way, 0, LINE - 1))

    def first_copy(part):
        way = toward(0)
        units = pl.ds(*spans[part])
        return remote(
            send_a.at[0, units], r_rs.at[0, 0, way, units], rs_s.at[0, 0, way, part], rs_r.at[0, 0, way, part],
            line_goal(way),
        )

    def act_sent(chunks):
        for chunk in chunks:
            for way in range(2):
                active, copy = act_copy(way, 0, chunk)
                pl.when(active)(copy.wait_send)

    def every_chunk(body):
        lax.fori_loop(0, CHUNKS, lambda chunk, carried: (body(chunk), carried)[1], 0)

    score_scale = 1.0 / math.sqrt(HD)

    def probabilities(queries, keys, begin):
        shape = (queries.shape[0], length)
        column = lax.broadcasted_iota(jnp.int32, shape, 1)
        row = lax.broadcasted_iota(jnp.int32, shape, 0) + begin
        visible = (column < prefix_ref[0]) | (column <= row)
        scores = jnp.where(visible, dot_nt(queries, keys) * score_scale, -1e30)
        weights = jnp.exp(scores - jnp.max(scores, axis=-1, keepdims=True))
        return weights / jnp.sum(weights, axis=-1, keepdims=True)

    def turn_by(value, sine):
        return value * cos_ref[...] + pltpu.roll(value, HD // 2, 1) * sine

    def head_lanes(place, offset=0):
        return pl.ds(pl.multiple_of(offset + place * HD, HD), HD)

    def first_scope(w_heads, tab):
        loads = [
            pltpu.make_async_copy(source, target, weight_sem.at[place])
            for place, (source, target) in enumerate(
                (
                    (emb_hbm, emb),
                    (w_query_hbm, w_heads.at[0]),
                    (w_key_hbm, w_heads.at[1]),
                    (w_value_hbm, w_heads.at[2]),
                    (cos_hbm, cos_ref),
                    (sin_hbm, sin_ref),
                    (w_dense_hbm, w_dense),
                )
            )
        ]
        for copy in loads:
            copy.start()
        named = lax.broadcasted_iota(jnp.int32, (vocab, length), 0) == ids_row[...]
        hot = jnp.where(named, 1.0, 0.0)
        hot_turned[...] = hot.astype(LOW)
        turned_hot = hot.T.astype(LOW)
        one_hot[:, 0:vocab] = turned_hot
        one_hot[:, vocab:] = turned_hot
        vectors[...] = jnp.zeros_like(vectors)
        loads[0].wait()
        for kind in range(3):
            loads[kind + 1].wait()
            pieces = split_low(dot(emb[...], w_heads[kind]))
            for place in range(heads_here):
                for half, piece in enumerate(pieces):
                    tab[place, half * vocab : (half + 1) * vocab, kind * HD : (kind + 1) * HD] = piece[
                        :, place * HD : (place + 1) * HD
                    ]
        loads[4].wait()
        loads[5].wait()

        def head_inputs(place, carried):
            lin = dot(one_hot[...], tab[place])
            heads[0, place] = turn_by(lin[:, 0:HD], sin_ref[...]).astype(LOW)
            heads[1, place] = turn_by(lin[:, HD : 2 * HD], sin_ref[...]).astype(LOW)
            heads[2, place] = lin[:, 2 * HD :].astype(LOW)
            return carried

        lax.fori_loop(0, heads_here, head_inputs, 0)

        def attend(chunk):
            for place in range(heads_here):
                queries = heads[0, place, chunk_rows(chunk), :]
                probability = probabilities(queries, heads[1, place], chunk * rows).astype(LOW)
                mixed = dot(probability, heads[2, place]).astype(LOW)
                att_low[chunk_rows(chunk), place * HD : (place + 1) * HD] = mixed
                turned = mixed.astype(FULL).T
                att_turned[place * HD : (place + 1) * HD, chunk_lanes(chunk)] = turned.astype(LOW)
                gbuf[place * HD : (place + 1) * HD, chunk_lanes(chunk)] = turned

        def project(chunk):
            attend(chunk)
            pl.when(chunk == 0)(lambda: loads[6].wait())
            pl.when(chunk == 0)(lambda: pl.semaphore_wait(barrier, len(greeted)))
            mixed = att_low[chunk_rows(chunk), :]

            def columns(start, size):
                put_part(chunk, start, size, dot_nt(mixed, w_dense[pl.ds(start, size), :]))

            spread(width, columns, 256)
            core_copy(0, chunk).start()
            pl.when(chunk == 0)(lambda: send_part(0, 0))
            pl.when((chunk > 1) & (chunk <= AHEAD))(lambda: send_part(0, chunk - 1))

        every_chunk(project)
        rows_copy().start()

    pl.run_scoped(first_scope, pltpu.VMEM((3, width, inner), LOW), pltpu.VMEM((heads_here, 2 * vocab, 3 * HD), LOW))

    def middle_scope(w_gate, w_up, w_down, cotbuf):
        weight_copies = [
            pltpu.make_async_copy(source, target, weight_sem.at[place])
            for place, (source, target) in enumerate(((w_gate_hbm, w_gate), (w_up_hbm, w_up), (w_down_hbm, w_down)))
        ]
        for copy in weight_copies:
            copy.start()
        for copy in weight_copies:
            copy.wait()

        def feed_forward(chunk):
            branch = take_part(0, chunk)
            residual = alpha * dot(one_hot[chunk_rows(chunk), 0:vocab], emb[...]) + branch
            centered = residual - row_mean(residual)
            rstd = lax.rsqrt(row_mean(centered * centered) + norm_eps)
            xhat = centered * rstd
            rstd_one[chunk] = rstd
            xbuf[...] = xhat
            park = pltpu.make_async_copy(xbuf, xhat_park.at[chunk], load_sem.at[0])
            park.start()
            hidden_low = (xhat * gain_one[...] + bias_one[...]).astype(LOW)
            put_blocks(hidden_low.astype(FULL))
            keep_columns(chunk)
            cols_copy(chunk).start()

            def units_tile(start, size):
                cut = pl.ds(start, size)
                gate = dot_nt(w_gate[cut, :], hidden_low)
                up = dot_nt(w_up[cut, :], hidden_low)
                units = mp * local_hidden + start + lax.broadcasted_iota(jnp.int32, (size, rows), 0)
                used = jnp.where(units < FF_USED, 1.0, 0.0)
                square = gate * gate
                bend = jnp.tanh(TANH_SCALE * gate * (1.0 + 0.044715 * square))
                gelu = 0.5 * gate * (1.0 + bend) * used
                slope = 0.5 * (1.0 + bend) + 0.5 * gate * (1.0 - bend * bend) * (
                    TANH_SCALE * (1.0 + 3.0 * 0.044715 * square)
                )
                gate_up[0, cut, chunk_lanes(chunk)] = slope * up * used
                gate_up[1, cut, chunk_lanes(chunk)] = gelu
                active = (gelu * up).astype(LOW)
                act_low[cut, chunk_lanes(chunk)] = active
                send_a[lax.div(chunk, 2), cut, half_chunk(chunk)] = active.astype(FULL)

            tiles(local_hidden, units_tile)
            act_send(0, chunk)
            active = send_a[lax.div(chunk, 2), :, half_chunk(chunk)].T.astype(LOW)
            tiles(
                width, lambda start, size: put_part(chunk, start, size, dot(active, w_down[:, pl.ds(start, size)]))
            )
            core_copy(1, chunk).start()
            park.wait()
            send_part(1, chunk)
            pl.when(chunk + AHEAD < CHUNKS)(lambda: send_part(0, chunk + AHEAD))

        same = jnp.int32(0)
        for place in range(2 * LINE):
            same = same + jnp.where(cluster_ref[place] == cluster_ref[dp], 1, 0)
        weight_row = 1.0 / jnp.full((1, width), same, jnp.int32).astype(FULL)

        def feed_backward(chunk):
            loads = load_all(
                ((xhat_park.at[chunk], xbuf), (cot_hbm.at[chunk_rows(chunk)], cotbuf))
            )
            branch = take_part(1, chunk)
            for copy in loads:
                copy.wait()
            residual = alpha * (xbuf[...] * gain_one[...] + bias_one[...]) + branch
            centered = residual - row_mean(residual)
            rstd = lax.rsqrt(row_mean(centered * centered) + norm_eps)
            xhat = centered * rstd
            obuf[...] = (xhat * gain_two[...] + bias_two[...]).astype(LOW)
            grad_out = cotbuf[...].astype(FULL) * weight_row
            vectors[2:3, :] += jnp.sum(grad_out * xhat, axis=0, keepdims=True)
            vectors[3:4, :] += jnp.sum(grad_out, axis=0, keepdims=True)
            grad_x = grad_out * gain_two[...]
            grad_two = (grad_x - row_mean(grad_x) - xhat * row_mean(grad_x * xhat)) * rstd
            for place in range(width // inner):
                gbuf[place * rows : (place + 1) * rows, :] = grad_two[:, place * inner : (place + 1) * inner]
            stores = load_all(
                ((obuf, block_out.at[chunk_rows(chunk)]), (gbuf, grad_two_park.at[chunk]))
            )
            grad_low = grad_two.astype(LOW)
            put_blocks(grad_low.astype(FULL))
            for place in range(2):
                two_own[place, chunk_rows(chunk), :] = blocks[2 * z + place].astype(LOW)

            @pl.when(chunk == mine)
            def _():
                two_send[...] = blocks[...]
                for step in range(1, LINE):
                    two_copy(step).start()


            def units_tile(start, size):
                cut = pl.ds(start, size)
                grad_act = dot_nt(w_down[cut, :], grad_low)
                for which in range(2):
                    low = (grad_act * gate_up[which, cut, chunk_lanes(chunk)]).astype(LOW)
                    grads_low[pl.ds(which * shift + start, size), chunk_lanes(chunk)] = low
                    gate_up[which, cut, chunk_lanes(chunk)] = low.astype(FULL)

            spread(local_hidden, units_tile)
            pair_send(0, chunk)
            for copy in stores:
                copy.wait()

        def hidden_part(pair):
            both = pl.ds(pl.multiple_of(2 * rows * pair, 2 * rows), 2 * rows)
            grad_gate = gate_up[0, :, both].T.astype(LOW)
            grad_up = gate_up[1, :, both].T.astype(LOW)

            def columns(start, size):
                cut = pl.ds(start, size)
                value = dot(grad_gate, w_gate[:, cut]) + dot(grad_up, w_up[:, cut])
                put_part(2 * pair, start, size, value[:rows])
                put_part(2 * pair + 1, start, size, value[rows:])

            tiles(width, columns)
            for place in range(2):
                core_copy(2, 2 * pair + place).start()

        def take_hidden():
            for chunk in range(CHUNKS):
                cols_copy(chunk).wait()
            fetch_columns(hidden_theirs)

        lag = AHEAD - 1

        def step(turn, carried):
            pl.when(turn == CHUNKS - 2 + lag)(lambda: hidden_part(0))
            @pl.when(turn >= 3)
            def _():
                act_take(0, turn - 3)
                act_send(1, turn - 3)

            @pl.when(turn == CHUNKS - 1 + lag)
            def _():
                for chunk in range(2):
                    send_part(2, chunk)
                take_hidden()
                act_sent(range(2))
                for chunk in range(2):
                    for part in whole:
                        pair_copy(0, chunk, part).wait()
                moved([(r_y.at[0, :, pl.ds(0, block)], send_a.at[0])])
                gate_theirs[:, 0:block] = send_a[0].astype(LOW)

            pl.when(turn < CHUNKS)(lambda: feed_forward(turn))
            pl.when(turn == lag)(lambda: rows_copy().wait())
            pl.when(turn >= lag)(lambda: feed_backward(turn - lag))
            return carried

        lax.fori_loop(0, CHUNKS + lag, step, 0)

        for chunk in range(CHUNKS - 1):
            pair_send(1, chunk)
        hidden_part(1)
        for chunk in range(2, CHUNKS):
            send_part(2, chunk)
        for part in whole:
            for chunk in range(2, CHUNKS):
                pair_copy(0, chunk, part).wait()
            start, size = spans[part]
            cut = slice(start, start + size)
            arrived = room.at[pl.ds(0, size)]
            moved([(r_y.at[0, pl.ds(start, size), pl.ds(block, block)], arrived)])
            gate_theirs[cut, block:] = arrived[...].astype(LOW)

            @pl.when(at_end)
            def _():
                place = jnp.where(z == 0, LINE - 1, 0)
                send_a[0, cut, :] = dot(grads_low[cut, :], cols_own[place]) + dot(
                    gate_theirs[cut, :], hidden_theirs[place]
                )
                first_copy(part).start()

        pl.when(~at_end)(lambda: act_pass((0,)))

    pl.run_scoped(
        middle_scope,
        pltpu.VMEM((local_hidden, width), LOW),
        pltpu.VMEM((local_hidden, width), LOW),
        pltpu.VMEM((local_hidden, width), LOW),
        pltpu.VMEM((rows, width), LOW),
    )

    def last_scope(theirs, late_theirs, two_theirs, att_theirs, send_b, stage, grad_att, grad_one_own, sums, sums_up, sums_down, sums_below, sums_above, late_own):
        def norm_backward(chunk):
            loads = load_all(((xhat_park.at[chunk], xbuf), (grad_two_park.at[chunk], gbuf)))
            branch = take_part(2, chunk)
            for copy in loads:
                copy.wait()
            grad_two = [gbuf[place * rows : (place + 1) * rows, :] for place in range(width // inner)]
            grad_hidden = alpha * jnp.concatenate(grad_two, axis=1) + branch
            xhat = xbuf[...]
            vectors[0:1, :] += jnp.sum(grad_hidden * xhat, axis=0, keepdims=True)
            vectors[1:2, :] += jnp.sum(grad_hidden, axis=0, keepdims=True)
            grad_x = grad_hidden * gain_one[...]
            grad_one = (grad_x - row_mean(grad_x) - xhat * row_mean(grad_x * xhat)) * rstd_one[chunk]
            put_blocks(grad_one)
            for place in range(2):
                grad_one_own[chunk_rows(chunk), place * block : (place + 1) * block] = blocks[2 * mp + place]
            grad_low = grad_one.astype(LOW)
            put_blocks(grad_low.astype(FULL))
            for place in range(2 * LINE):
                late_own[place, chunk_rows(chunk), :] = blocks[place].astype(LOW)

            @pl.when(chunk == mine)
            def _():
                for place in range(2 * LINE):
                    cols_send[place] = blocks[place]
                late_send()

            grad_mixed = dot(grad_low, w_dense[...]).astype(LOW)
            for place in range(heads_here):
                grad_att[place, chunk_rows(chunk), :] = grad_mixed[:, place * HD : (place + 1) * HD]

        def fetch_up():
            for chunk in range(CHUNKS):
                for part in whole:
                    pair_copy(1, chunk, part).wait()
            fetch_rows(r_y.at[1], theirs.at[1])

        def fetch_rows(source, target):
            size = source.shape[0]
            views = [stage.at[place, pl.ds(0, size)] for place in range(2)]
            moved([(source.at[:, pl.ds(block * place, block)], views[place]) for place in range(2)])
            for place in range(2):
                target[:, block * place : block * (place + 1)] = views[place][...].astype(LOW)

        def outer_product(target, place, own, other):
            right, right_theirs = cols_own[place], hidden_theirs[place]

            def rows_tile(start, size):
                cut = pl.ds(start, size)
                target[cut, :] = dot(own[cut, :], right) + dot(other(cut), right_theirs)

            tiles(target.shape[0], rows_tile)

        def down_products():
            for step in range(1, LINE):
                two_spread(1, step).wait()
                two_spread(2, step).start()
            for step in range(1, LINE):
                two_spread(0, step).wait()
                two_spread(2, step).wait()
            for chunk in range(CHUNKS):
                pl.when(at_end)(lambda: act_take(1, chunk))
                act_take(2, chunk)
            for step in range(LINE):
                owner = lax.rem(z + step, LINE)
                if step:
                    moved([(r_two.at[owner], blocks)])
                    for place in range(2):
                        for chunk in range(CHUNKS):
                            piece = blocks[2 * chunk + place].astype(LOW)
                            two_theirs[place, chunk * rows : (chunk + 1) * rows, :] = piece
                    fetch_rows(r_act.at[owner], theirs.at[0])
                left, right = (theirs.at[0], two_theirs) if step else (act_low, two_own)
                for place in range(2):
                    lanes = slice(place * block, (place + 1) * block)

                    def rows_tile(start, size):
                        cut = pl.ds(start, size)
                        product = dot(left[cut, :], right[place])
                        gate_up[0, cut, lanes] = gate_up[0, cut, lanes] + product if step else product

                    tiles(local_hidden, rows_tile)

        def down_copy():
            return remote(gate_up.at[0, :, half_lanes(1 - y)], r_dny, dny_s, dny_r, y_peer)

        def down_end():
            down_copy().wait()
            moved([(r_dny, stage.at[0])])
            stage[0] = stage[0] + gate_up[0, :, half_lanes(y)]
            moved([(stage.at[0], out_down)])
            for chunk in range(CHUNKS):
                for way in range(2):
                    for hop in range(1, LINE - 1):
                        active, copy = act_copy(way, hop, chunk)
                        pl.when(active)(copy.wait_send)

        def unit_terms(kind):
            own = grads_low.at[pl.ds(pl.multiple_of(kind * shift, 16), local_hidden)]

            def other(cut):
                if isinstance(kind, int):
                    return theirs[1, cut, :] if kind else gate_theirs[cut, :]
                return jnp.where(kind == 0, gate_theirs[cut, :], theirs[1, cut, :])

            return own, other

        def count(way):
            return jnp.where(way == 0, LINE - 1 - z, z)

        def order(kind, slot, way):
            return kind * count(way) + slot - (LINE - count(way))

        def turn_of(number, way):
            many = jnp.maximum(count(way), 1)
            return lax.div(number, many) * (LINE - 1) + lax.rem(number, many) + LINE - 1 - count(way)

        def unit_copy(turn, side, part):
            way = toward(side)
            kind, slot = lax.div(turn, LINE - 1), lax.rem(turn, LINE - 1)
            units = pl.ds(*halves[part])
            home = (send_a, send_b)[side].at[lax.rem(jnp.maximum(order(kind, slot + 1, way), 0), 2), units]
            return remote(
                home, r_rs.at[kind, slot, way, units], rs_s.at[kind, slot, way, part], rs_r.at[kind, slot, way, part],
                line_goal(way),
            )

        def unit_sent(number, side):
            turn = turn_of(jnp.maximum(number, 0), toward(side))

            @pl.when(turn == 0)
            def _():
                for part in whole:
                    first_copy(part).wait_send()

            @pl.when(turn > 0)
            def _():
                for part in range(2):
                    unit_copy(turn, side, part).wait_send()

        def unit_slot(turn, part, side):
            way = toward(side)
            kind, slot = lax.div(turn, LINE - 1), lax.rem(turn, LINE - 1) + 1
            own, other = unit_terms(kind)
            start, size = halves[part]
            cut = slice(start, start + size)

            @pl.when(goes(slot, way))
            def _():
                number = order(kind, slot, way)
                home = (send_a, send_b)[side].at[lax.rem(jnp.maximum(number, 0), 2)]
                if part == 0:
                    pl.when(number >= 2)(lambda: unit_sent(number - 2, side))
                place = jnp.where(way == 0, LINE - slot + z, slot - LINE + z)
                home[cut, :] = dot(own[cut, :], cols_own[place]) + dot(other(cut), hidden_theirs[place])

                @pl.when((slot > 1) & inner_place(way))
                def _():
                    before = jnp.maximum(turn - 1, 0)

                    @pl.when(before == 0)
                    def _():
                        for piece in (2 * part, 2 * part + 1):
                            first_copy(piece).wait_recv()

                    pl.when(before > 0)(lambda: unit_copy(before, side, part).wait_recv())
                    landed = r_rs.at[lax.div(before, LINE - 1), lax.rem(before, LINE - 1), way, pl.ds(start, size)]
                    moved([(landed, stage.at[side, pl.ds(start, size)])])
                    home[cut, :] = home[cut, :] + stage[side, cut, :]

                unit_copy(turn, side, part).start()

        def unit_end():
            own, other = unit_terms(0)
            outer_product(stage.at[0], z, own, other)
            for side in range(2):

                @pl.when(inner_place(toward(side)))
                def _():
                    for part in range(2):
                        unit_copy(LINE - 2, side, part).wait_recv()
                    moved([(r_rs.at[0, LINE - 2, toward(side)], stage.at[1])])
                    stage[0] = stage[0] + stage[1]

            moved([(stage.at[0], out_gate)])

        def last_product():
            own, other = unit_terms(1)
            outer_product(stage.at[0], z, own, other)
            moved([(stage.at[0], out_up)])

        def last_landed():
            for side in range(2):
                for part in range(2):
                    pl.when(inner_place(toward(side)))(unit_copy(2 * LINE - 3, side, part).wait_recv)

        first = jnp.where(z == 1, 2, jnp.where(z == LINE - 1, 2 * LINE - 2, 0))
        peer_first = jnp.where(z == 0, 2, jnp.where(z == 2, 2 * LINE - 2, 0))
        many = 2 * LINE - 2
        def late_copy(begin, size, part):
            span = pl.ds(begin + part * (size // 2), size // 2)
            return remote(cols_send.at[span], r_late.at[mine, span], late_s.at[0, part], late_r.at[0, part], z_peer)

        def late_send():
            for part in range(2):
                pl.when(at_end)(lambda: late_copy(peer_first, many, part).start())
                pl.when(~at_end)(lambda: late_copy(peer_first, 2, part).start())

        def spread_copy(turn, size, part):
            place = other_x if turn == 3 else mine
            view = r_late.at[place, pl.ds(first + part * (size // 2), size // 2)]
            device = x_peer if turn == 2 else core_peer
            return remote(view, view, late_s.at[turn, part], late_r.at[turn, part], device)

        def by_size(body):
            pl.when(at_end)(lambda: body(2))
            pl.when(~at_end)(lambda: body(many))

        def late_take():
            def body(size):
                for part in range(2):
                    late_copy(first, size, part).wait_recv()
                    spread_copy(2, size, part).start()
                    spread_copy(1, size, part).start()
                for part in range(2):
                    spread_copy(2, size, part).wait()
                    spread_copy(3, size, part).start()
                for part in range(2):
                    spread_copy(1, size, part).wait()
                for part in range(2):
                    spread_copy(3, size, part).wait()

            by_size(body)

        def late_slot(number):
            side, lane = lax.div(number, LINE), lax.rem(number, LINE)
            return parts.at[:, side, :, pl.ds(pl.multiple_of(lane * block, block), block)]

        def late_products():
            for quarter in range(CHUNKS):

                def body(size):
                    moved([(r_late.at[quarter, pl.ds(first, size)], blocks.at[pl.ds(0, size)])])
                    for place in range(size):
                        late_theirs[place, quarter * rows : (quarter + 1) * rows, :] = blocks[place].astype(LOW)

                by_size(body)

            def product(number, carried):
                @pl.when((number < 2) | ~at_end)
                def _():
                    home = late_slot(number)
                    for piece in range(CHUNKS):
                        cut = slice(piece * rows, (piece + 1) * rows)
                        home[piece] = dot(att_turned[cut, :], late_own[first + number]) + dot(
                            att_theirs[cut, :], late_theirs[number]
                        )

                return carried

            lax.fori_loop(0, many, product, 0)
            for place in range(LINE - 1):
                pl.when((place == 0) | ~at_end)(lambda: late_pair(place).start())

        def late_pair(place):
            return remote(late_slot(2 * place + 1 - y), r_dz.at[place], dz_s.at[place], dz_r.at[place], y_peer)

        def late_line(place):
            goal = lax.div(first, 2) + place
            return goal != z, remote(late_slot(2 * place + y), r_dx, dx_s.at[place], dx_r, at(z_to=goal))

        def late_sums():
            for place in range(LINE - 1):

                @pl.when((place == 0) | ~at_end)
                def _():
                    late_pair(place).wait()
                    arrived = blocks.at[pl.ds(0, CHUNKS)]
                    moved([(r_dz.at[place], arrived)])
                    home = late_slot(2 * place + y)
                    home[...] = home[...] + arrived[...]
                    leaves, copy = late_line(place)
                    pl.when(leaves)(copy.start)

        def late_end():
            _, copy = late_line(0)
            copy.wait_recv()
            arrived = blocks.at[pl.ds(0, CHUNKS)]
            moved([(r_dx, arrived)])
            total = late_slot(2 * (z - lax.div(first, 2)) + y)
            for piece in range(CHUNKS):
                gbuf[0:block, piece * rows : (piece + 1) * rows] = (total[piece] + arrived[piece]).T
            moved([(gbuf.at[pl.ds(0, block)], out_dense)])
            for place in range(LINE - 1):

                @pl.when((place == 0) | ~at_end)
                def _():
                    leaves, copy = late_line(place)
                    pl.when(leaves)(copy.wait_send)

            for part in range(2):
                pl.when(at_end)(lambda: late_copy(peer_first, many, part).wait_send())
                pl.when(~at_end)(lambda: late_copy(peer_first, 2, part).wait_send())

        def last_sent():
            for side in range(2):
                pl.when(count(toward(side)) > 0)(lambda: unit_sent(2 * count(toward(side)) - 1, side))
                pl.when(count(toward(side)) > 0)(lambda: unit_sent(2 * count(toward(side)) - 2, side))

        def attention_backward(place, carried):
            hot_t = hot_turned[...]
            queries, keys, values = heads[0, place], heads[1, place], heads[2, place]
            grad_mixed = grad_att[place]
            probability = probabilities(queries, keys, 0)
            grad_prob = dot_nt(grad_mixed, values)
            centre = jnp.sum(grad_prob * probability, axis=-1, keepdims=True)
            grad_scores = (probability * (grad_prob - centre)).astype(LOW)
            grad_queries = dot(grad_scores, keys) * score_scale
            grad_keys = dot_tn(grad_scores, queries) * score_scale
            grad_values = dot_tn(probability.astype(LOW), grad_mixed)
            sums[0, 0:vocab, head_lanes(place)] = dot(hot_t, turn_by(grad_queries, -sin_ref[...]).astype(LOW))
            sums[0, 0:vocab, head_lanes(place, inner)] = dot(hot_t, turn_by(grad_keys, -sin_ref[...]).astype(LOW))
            sums[1, 0:vocab, head_lanes(place)] = dot(hot_t, grad_values.astype(LOW))
            return carried

        def small_sums():
            lax.fori_loop(0, heads_here, attention_backward, 0)
            hot_t = hot_turned[...]
            high, rest = split_low(grad_one_own[...])
            sums[1, 0:vocab, heads_here * HD :] = dot(hot_t, high) + dot(hot_t, rest)
            for side in range(2):
                sums[side, vocab:, :] = vectors[:, side * (width // 2) : (side + 1) * (width // 2)]
            sums_pair().start()

        def sums_pair():
            return remote(sums.at[1 - y], r_sums.at[0], sums_s.at[0], sums_r.at[0], y_peer)

        def sums_line(way):
            source = (sums_up, sums_down)[way]
            goal = jnp.clip(z + 1 - 2 * way, 0, LINE - 1)
            return remote(source, r_sums.at[1 + way], sums_s.at[1 + way], sums_r.at[1 + way], at(z_to=goal))

        def sums_back():
            return remote(sums.at[y], r_sums.at[3], sums_s.at[3], sums_r.at[3], y_peer)

        def sums_first():
            sums_pair().wait()
            moved([(r_sums.at[0], sums_below)])
            sums[y] = sums[y] + sums_below[...]

            @pl.when(z == 0)
            def _():
                sums_up[...] = sums[y]
                sums_line(0).start()

            @pl.when(z == LINE - 1)
            def _():
                sums_down[...] = sums[y]
                sums_line(1).start()

        def sums_up_step():
            sums_line(0).wait_recv()
            moved([(r_sums.at[1], sums_below)])
            sums_up[...] = sums[y] + sums_below[...]
            sums_line(0).start()

        def sums_down_step():
            sums_line(1).wait_recv()
            moved([(r_sums.at[2], sums_above)])
            sums_down[...] = sums[y] + sums_above[...]
            sums_line(1).start()

        def sums_near():
            pl.when(z == 1)(sums_up_step)
            pl.when(z == LINE - 2)(sums_down_step)

        def sums_far():
            pl.when(z == LINE - 2)(sums_up_step)
            pl.when(z == 1)(sums_down_step)

        def sums_middle():
            @pl.when(z == LINE - 1)
            def _():
                sums_line(0).wait_recv()
                moved([(r_sums.at[1], sums_below)])

            @pl.when(z == 0)
            def _():
                sums_line(1).wait_recv()
                moved([(r_sums.at[2], sums_above)])

            @pl.when(z > 0)
            def _():
                sums[y] = sums[y] + sums_below[...]

            @pl.when(z < LINE - 1)
            def _():
                sums[y] = sums[y] + sums_above[...]

            sums_back().start()

        def sums_end():
            sums_back().wait()
            pl.when(z < LINE - 1)(sums_line(0).wait_send)
            pl.when(z > 0)(sums_line(1).wait_send)
            moved([(r_sums.at[3], sums.at[1 - y])])
            lanes = pl.ds(pl.multiple_of(lax.rem(dp, LINE) * block, block), block)
            moved([(sums.at[lax.div(dp, LINE), pl.ds(vocab, 8), lanes], out_norms)])

        def by_token(kind, rows_of):
            side, start = ((0, 0), (0, inner), (1, 0), (1, inner))[kind]
            return sums[side, rows_of, start : start + inner]

        def head_gradients():
            own_columns = emb[:, pl.ds(pl.multiple_of(dp * block, block), block)]
            for kind, result in enumerate((out_query, out_key, out_value)):
                high, rest = split_low(by_token(kind, slice(0, vocab)))
                gbuf[0:block, :] = dot_tn(own_columns, high) + dot_tn(own_columns, rest)
                moved([(gbuf.at[pl.ds(0, block)], result)])

        table_rows = vocab // (2 * LINE)
        table_own = pl.ds(pl.multiple_of(dp * table_rows, table_rows), table_rows)

        def table_part():
            for kind, weight in enumerate((w_query_hbm, w_key_hbm, w_value_hbm)):
                moved([(weight, w_dense)])
                pieces = jnp.concatenate(split_low(by_token(kind, table_own)), axis=0)

                def columns(start, size):
                    cut = pl.ds(start, size)
                    both = dot_nt(pieces, w_dense[cut, :])
                    both = both[:table_rows] + both[table_rows:]
                    xbuf[0:table_rows, cut] = both if kind == 0 else xbuf[0:table_rows, cut] + both

                tiles(width, columns)
            quarter = pl.ds(pl.multiple_of(mp * inner, inner), inner)
            xbuf[0:table_rows, quarter] = xbuf[0:table_rows, quarter] + alpha * by_token(3, table_own)
            table_copy(0).start()

        def table_middle():
            table_copy(0).wait()
            xbuf[table_rows : 2 * table_rows, :] = xbuf[0:table_rows, :] + table_core[...]
            table_copy(1).start()

        def table_end():
            table_copy(1).wait()
            xbuf[0:table_rows, :] = 0.1 * (xbuf[table_rows : 2 * table_rows, :] + table_x[...])
            moved([(xbuf.at[pl.ds(0, table_rows)], out_table)])

        def table_copy(turn):
            target, device = ((table_core, core_peer), (table_x, x_peer))[turn]
            return remote(xbuf.at[pl.ds(turn * table_rows, table_rows)], target, table_s.at[turn], table_r.at[turn], device)


        def one_turn(turn, carried):
            @pl.when((turn == 2) & at_end)
            def _():
                fetch_up()

            swapped = jnp.where(at_end & ((turn == 2) | (turn == 3)), 5 - turn, turn)
            for part in range(2):
                pl.when((turn > 0) & (turn < 4) | (turn == 4) & ~at_end)(lambda: unit_slot(swapped, part, 0))

            @pl.when(turn == 0)
            def _():
                act_take(0, CHUNKS - 1)
                act_send(1, CHUNKS - 1)
                fetch_rows(r_att, att_theirs)
                every_chunk(norm_backward)
                act_sent(range(2, CHUNKS))
                pl.when(~at_end)(lambda: act_pass((1,)))
                for step in range(1, LINE):
                    two_copy(step).wait()
                for step in range(1, LINE):
                    two_spread(1, step).start()
                    two_spread(0, step).start()

            @pl.when(turn == 1)
            def _():
                small_sums()
                pair_send(1, CHUNKS - 1)

            @pl.when((turn == 1) & ~at_end | (turn == 3) & at_end)
            def _():
                late_take()
                late_products()

            pl.when((turn == 1) & ~at_end)(lambda: act_pass((2, 3)))
            pl.when(turn == 1)(sums_first)

            pl.when(turn == 2)(sums_near)
            pl.when((turn == 2) & ~at_end | (turn == 4) & at_end)(late_sums)

            @pl.when((turn == 2) & ~at_end)
            def _():
                fetch_up()


            pl.when(turn == 4)(sums_far)

            @pl.when(turn == 4)
            def _():
                for part in range(2):
                    unit_slot(2, part, 1)

            pl.when((turn == 4) & ~at_end)(sums_middle)
            pl.when(turn == 4)(down_products)

            @pl.when((turn == 4) & ~at_end)
            def _():
                down_copy().start()
                sums_end()
                head_gradients()

            @pl.when((turn == 4) & at_end)
            def _():
                for part in range(2):
                    unit_slot(4, part, 0)
                sums_middle()
                down_copy().start()

            @pl.when(turn == 5)
            def _():
                for part in range(2):
                    for side in range(2):
                        unit_slot(5, part, side)
                    if part == 0:
                        pl.when(~at_end)(table_part)

                @pl.when(at_end)
                def _():
                    sums_end()
                    head_gradients()
                    table_part()

                last_product()
                unit_end()

            return carried

        lax.fori_loop(0, 2 * (LINE - 1), one_turn, 0)
        late_end()
        table_middle()
        table_end()
        down_end()
        last_landed()
        last_sent()

    pl.run_scoped(
        last_scope,
        pltpu.VMEM((2, local_hidden, length), LOW),
        pltpu.VMEM((2 * LINE - 2, length, block), LOW),
        pltpu.VMEM((2, length, block), LOW),
        pltpu.VMEM((inner, length), LOW),
        pltpu.VMEM((2, local_hidden, block), FULL),
        pltpu.VMEM((2, local_hidden, block), FULL),
        pltpu.VMEM((heads_here, length, HD), LOW),
        pltpu.VMEM((length, 2 * block), FULL),
        pltpu.VMEM((2,) + r_sums.shape[1:], FULL),
        pltpu.VMEM(r_sums.shape[1:], FULL),
        pltpu.VMEM(r_sums.shape[1:], FULL),
        pltpu.VMEM(r_sums.shape[1:], FULL),
        pltpu.VMEM(r_sums.shape[1:], FULL),
        pltpu.VMEM((2 * LINE, length, block), LOW),
    )


def write_kernel(*refs):
    count = 10
    late = 7
    sources, landed = refs[:count], refs[count]
    targets = refs[count + 1 : 2 * count + 4]
    rooms, terms, first_sem, second_sem = refs[2 * count + 4 : 3 * count + 4], *refs[3 * count + 4 : 3 * count + 7]
    z = lax.div(lax.axis_index("dp"), 2)
    order = [late] + [place for place in range(count) if place != late]
    loads = {
        place: pltpu.make_async_copy(sources[place], rooms[place], first_sem.at[place]) for place in range(count)
    }
    more = [
        pltpu.make_async_copy(landed.at[1, LINE - 2, way], terms.at[way], first_sem.at[count + way]) for way in range(2)
    ]
    lands = (z > 0, z < LINE - 1)
    for way in range(2):
        pl.when(lands[way])(more[way].start)
    for place in order:
        loads[place].start()
    stores = []
    for way in range(2):
        pl.when(lands[way])(more[way].wait)
    for place in order:
        loads[place].wait()
        room = rooms[place]
        if place == late:
            for way, active in ((0, z > 0), (1, z < LINE - 1)):

                @pl.when(active)
                def _():
                    room[...] = room[...] + terms[way]

        if place < count - 1:
            stores.append(pltpu.make_async_copy(room, targets[place], second_sem.at[place]))
            stores[-1].start()
        else:
            for vector in range(4):
                targets[place + vector][...] = room[vector : vector + 1, :]
    for copy in stores:
        copy.wait()


def write_out(results, landed):
    hbm = pl.BlockSpec(memory_space=pl.ANY)
    rows = jax.ShapeDtypeStruct((1, results[-1].shape[1]), FULL)
    shapes = [jax.ShapeDtypeStruct(value.shape, value.dtype) for value in results[:-1]] + [rows] * 4
    return pl.pallas_call(
        write_kernel,
        out_shape=shapes,
        in_specs=[hbm] * (len(results) + 1),
        out_specs=[hbm] * (len(results) - 1) + [pl.BlockSpec(memory_space=pltpu.VMEM)] * 4,
        scratch_shapes=[pltpu.VMEM(value.shape, value.dtype) for value in results]
        + [pltpu.VMEM((2,) + results[7].shape, FULL)]
        + [pltpu.SemaphoreType.DMA((len(results) + 2,))] * 2,
        compiler_params=pltpu.CompilerParams(vmem_limit_bytes=62 * 2**20),
    )(*results, landed)


def local_fast(
    token_ids,
    prefix_lengths,
    cluster_ids,
    embedding,
    w_query,
    w_key,
    w_value,
    w_dense,
    w_gate,
    w_up,
    w_down,
    norm1_gain,
    norm1_bias,
    norm2_gain,
    norm2_bias,
    cotangent,
):
    length = token_ids.shape[0]
    vocab, width = embedding.shape
    inner = w_query.shape[1]
    heads_here = inner // HD
    local_hidden = w_gate.shape[1]
    rows = length // CHUNKS
    block = width // (2 * LINE)
    shift = (local_hidden + 15) // 16 * 16
    frequency = 10000.0 ** (np.arange(HD // 2) * (-2.0 / HD))
    angles = np.arange(length)[:, None] * frequency[None, :]
    cosine = np.concatenate([np.cos(angles)] * 2, axis=1).astype(np.float32)
    sine = np.concatenate([-np.sin(angles), np.sin(angles)], axis=1).astype(np.float32)
    norms = [vector.reshape(1, width) for vector in (norm1_gain, norm1_bias, norm2_gain, norm2_bias)]

    hbm = pl.BlockSpec(memory_space=pl.ANY)
    vmem = pl.BlockSpec(memory_space=pltpu.VMEM)
    smem = pl.BlockSpec(memory_space=pltpu.SMEM)
    sums_rows = vocab + 8
    table_rows = vocab // (2 * LINE)
    shapes = [
        ((length, width), LOW),
        ((table_rows, width), FULL),
        ((block, inner), FULL),
        ((block, inner), FULL),
        ((block, inner), FULL),
        ((block, inner), FULL),
        ((local_hidden, block), FULL),
        ((local_hidden, block), FULL),
        ((local_hidden, block), FULL),
        ((8, block), FULL),
        ((LINE, local_hidden, length), FULL),
        ((LINE, 2 * CHUNKS, rows, block), FULL),
        ((2, local_hidden, length), FULL),
        ((LINE, CHUNKS, rows, block), FULL),
        ((inner, length), FULL),
        ((CHUNKS, rows, width), FULL),
        ((CHUNKS, length, inner), FULL),
        ((local_hidden, block), FULL),
        ((2, LINE - 1, 2, local_hidden, block), FULL),
        ((4, 2 * LINE, rows, block), FULL),
        ((LINE - 1, CHUNKS, rows, block), FULL),
        ((CHUNKS, rows, block), FULL),
        ((4, sums_rows, width // 2), FULL),
    ]
    scratch = [
        ((vocab, width), LOW),
        ((length, HD), FULL),
        ((length, HD), FULL),
        ((CHUNKS, 2, rows, width // 2), FULL),
        ((CHUNKS, rows, width // 2), FULL),
        ((2, CHUNKS, rows, width // 2), FULL),
        ((CHUNKS, rows, width // 2), FULL),
        ((2 * LINE, rows, block), FULL),
        ((rows, width), FULL),
        ((length, inner), FULL),
        ((rows, width), LOW),
        ((2, local_hidden, length), FULL),
        ((2 * shift, length), LOW),
        ((local_hidden, length), LOW),
        ((2, local_hidden, block), FULL),
        ((LINE, length, block), LOW),
        ((2 * CHUNKS, rows, block), FULL),
        ((LINE, length, block), LOW),
        ((local_hidden, length), LOW),
        ((2, length, block), LOW),
        ((2 * LINE, rows, block), FULL),
        ((length, inner), LOW),
        ((inner, length), LOW),
        ((3, heads_here, length, HD), LOW),
        ((width, inner), LOW),
        ((length, 2 * vocab), LOW),
        ((vocab, length), LOW),
        ((CHUNKS, rows, 1), FULL),
        ((8, width), FULL),
        ((table_rows, width), FULL),
        ((table_rows, width), FULL),
        (((local_hidden // 4 + 15) // 16 * 16, block), FULL),
    ]
    dma = pltpu.SemaphoreType.DMA
    each = (3, CHUNKS)
    semaphores = [
        each, each, each, each, each, each, (2, LINE - 1, CHUNKS), (2, LINE - 1, CHUNKS), (3,), (3,), (3, 3), (3, 3),
        (CHUNKS,), (CHUNKS,), None, None, (2, CHUNKS, 4), (2, CHUNKS, 4), None, None, None, None, (4, 2), (4, 2),
        (3,), (3,), (3,), None, (2, LINE - 1, 2, 4), (2, LINE - 1, 2, 4), (4,), (4,), (2,), (2,), (4,), (7,),
    ]
    results = pl.pallas_call(
        functools.partial(layer_kernel, length, width, local_hidden),
        out_shape=[jax.ShapeDtypeStruct(shape, dtype) for shape, dtype in shapes],
        in_specs=[smem] * 2 + [vmem] * 5 + [hbm] * 11,
        out_specs=[hbm] * len(shapes),
        scratch_shapes=[pltpu.VMEM(shape, dtype) for shape, dtype in scratch]
        + [dma if shape is None else dma(shape) for shape in semaphores],
        compiler_params=pltpu.CompilerParams(
            collective_id=0, has_side_effects=True, vmem_limit_bytes=62 * 2**20
        ),
    )(
        prefix_lengths,
        cluster_ids,
        token_ids.reshape(1, length),
        *norms,
        embedding,
        cosine,
        sine,
        w_query,
        w_key,
        w_value,
        w_dense,
        w_gate.T,
        w_up.T,
        w_down.T,
        cotangent,
    )
    written = write_out(results[:10], results[18])
    block_out, table, out_query, out_key, out_value, out_dense, out_gate, out_up, out_down = written[:9]
    out_norms = written[9:]
    return (
        block_out,
        table,
        out_query,
        out_key,
        out_value,
        out_dense,
        out_gate.T,
        out_up.T,
        out_down.T,
        out_norms[0].reshape(width // (2 * LINE)),
        out_norms[1].reshape(width // (2 * LINE)),
        out_norms[2].reshape(width // (2 * LINE)),
        out_norms[3].reshape(width // (2 * LINE)),
    )


def solution(mesh):
    fast = mesh.shape["dp"] == 2 * LINE and mesh.shape["mp"] == 4
    return jax.shard_map(
        local_fast if fast else local_general,
        mesh=mesh,
        in_specs=(
            P("dp"),
            P("dp"),
            P(),
            P(),
            P(None, "mp"),
            P(None, "mp"),
            P(None, "mp"),
            P(None, "mp"),
            P(None, "mp"),
            P(None, "mp"),
            P(None, "mp"),
            P(),
            P(),
            P(),
            P(),
            P("dp", None),
        ),
        out_specs=(
            P("dp", None),
            P("dp", None),
            P("dp", "mp"),
            P("dp", "mp"),
            P("dp", "mp"),
            P("dp", "mp"),
            P("dp", "mp"),
            P("dp", "mp"),
            P("dp", "mp"),
            P("dp"),
            P("dp"),
            P("dp"),
            P("dp"),
        ),
        check_vma=False,
    )
```
